32 devices in a mesh: section: 2 (over x), rep: 16 (over z, y, core).
Axes of the slice: x: 2, y: 2, z: 4, core: 2. Of those that a mesh axis runs over, the one named last changes fastest.
Arguments:
- ends_in: bfloat16 [2, 8192, 768], P('section', 'rep'), may hold values from -6 to 6
- lengths: int32 [16, 2, 4], P('rep'), may hold values from 0 to 256, as said below
- times: int32 [16, 2, 4], P('rep'), may hold values from 0 to 999
- norm_gain: bfloat16 [2, 768], P('section'), may hold values from 0.099609375 to 1.8984375
- attend_in: bfloat16 [2, 768, 2304], P('section'), may hold values from -0.21875 to 0.21875
- attend_out: bfloat16 [2, 768, 768], P('section'), may hold values from -1.25 to 1.25
- time_weight: bfloat16 [2, 128, 2304], P('section'), may hold values from -0.5 to 0.5
- time_bias: bfloat16 [2, 2304], P('section'), may hold values from -3 to 3
- expand_weight: bfloat16 [2, 768, 3072], P('section'), may hold values from -0.21875 to 0.21875
- expand_bias: bfloat16 [2, 3072], P('section'), may hold values from -3 to 3
- reduce_weight: bfloat16 [2, 3072, 768], P('section'), may hold values from -0.109375 to 0.109375
- reduce_bias: bfloat16 [2, 768], P('section'), may hold values from -3 to 3
Outputs:
- ends_out: bfloat16 [2, 8192, 768], P('section', 'rep')
- grad_norm_gain: float32 [2, 768], P('section', 'rep')
- grad_attend_in: float32 [2, 768, 2304], P('section', 'rep')
- grad_attend_out: float32 [2, 768, 768], P('section', 'rep')
- grad_time_weight: float32 [2, 128, 2304], P('section', 'rep')
- grad_time_bias: float32 [2, 2304], P('section', 'rep')
- grad_expand_weight: float32 [2, 768, 3072], P('section', 'rep')
- grad_expand_bias: float32 [2, 3072], P('section', 'rep')
- grad_reduce_weight: float32 [2, 3072, 768], P('section', 'rep')
- grad_reduce_bias: float32 [2, 768], P('section', 'rep')
The draws below stay inside these ranges and needn't reach their ends.
Inputs may be any that keep to these rules, and one draw needn't show every extreme that they name: Each micro-batch's 4 lengths sum to 256: either one sequence of 256 tokens followed by zeros, or 4 sequences of 64 tokens; some micro-batch of some replica holds one sequence.
All inputs are finite; a program needn't handle non-finite values.
Results may differ from the reference program's by a relative error of at most 0.019.
Values may be sent and summed in bfloat16 or wider, within the bound.
No kernel may reach another device: no remote copies, remote signals or barrier semaphores. Data moves between devices by JAX's collectives and lax.ppermute only.
A program may use at most 192 MiB of HBM per device.

```python
import math
import jax
import jax.numpy as jnp
from jax import lax

D = 768
HEADS = 12
HEAD = 64
FF = 3072
EMB = 128
SEGS = 4
MB = 2
MB_TOK = 256
REPLICAS = 16
SECTIONS = 2
TOKENS = 8192


def draw_lengths(key, part):
    key = jax.random.fold_in(key, 7)
    key_bucket, key_replica, key_micro = jax.random.split(key, 3)
    single = jax.random.randint(key_bucket, (REPLICAS, MB), 0, 3) == 0
    chosen_replica = jax.random.randint(key_replica, (), 0, REPLICAS)
    chosen_micro = jax.random.randint(key_micro, (), 0, MB)
    forced = (jnp.arange(REPLICAS)[:, None] == chosen_replica) & (jnp.arange(MB)[None, :] == chosen_micro)
    single = single | forced
    whole_row = jnp.concatenate([jnp.full((1,), MB_TOK, jnp.int32), jnp.zeros((SEGS - 1,), jnp.int32)])
    split_row = jnp.full((SEGS,), MB_TOK // SEGS, jnp.int32)
    return jnp.where(single[:, :, None], whole_row[None, None, :], split_row[None, None, :]).astype(jnp.int32)


def set_ends(entries, own_key, low, top_value):
    longest = entries.shape.index(max(entries.shape))
    spots = []
    for shift in (0, 1):
        where = [jax.random.randint(jax.random.fold_in(own_key, axis), (), 0, length) for axis, length in enumerate(entries.shape)]
        where[longest] = (where[longest] + shift) % entries.shape[longest]
        spots.append(tuple(where))
    return entries.at[spots[0]].set(low).at[spots[1]].set(top_value)


def steps_of(stream_key, shape, pieces, least, high):
    level = 1.0
    for dim, parts in pieces:
        draws = jax.random.uniform(jax.random.fold_in(jax.random.fold_in(stream_key, 6), dim), (parts,), jnp.float32, least / len(pieces), high / len(pieces))
        level = level * jnp.repeat(jnp.exp(draws), shape[dim] // parts).reshape((-1,) + (1,) * (len(shape) - 1 - dim))
    return level


def bell_draw(own_key, dims, scale, limit, cuts=(), held_as=jnp.bfloat16):
    level = steps_of(own_key, dims, cuts, -0.22, 0.18) if cuts else 1.0
    values = jax.random.normal(own_key, dims, jnp.float32) * scale * level
    return jnp.minimum(jnp.maximum(values, -limit), limit).astype(held_as)


def setup_inputs(seed: int = 0) -> dict:
    streams_of = jax.random.split(jax.random.key(seed), 13)
    ends_in = bell_draw(streams_of[0], (2, TOKENS, D), 1.0, 6.0, ((0, 2), (1, 16)))
    lengths = draw_lengths(jax.random.fold_in(streams_of[12], 71), 0)
    times = set_ends(jax.random.randint(streams_of[2], (REPLICAS, MB, SEGS), 0, 1000), jax.random.fold_in(streams_of[2], 1), 0, 999).astype(jnp.int32)
    norm_gain = jnp.clip(1.0 + 0.18 * jax.random.normal(streams_of[3], (SECTIONS, D), jnp.float32), 0.099609375, 1.8984375).astype(jnp.bfloat16)
    attend_in = bell_draw(streams_of[4], (SECTIONS, D, 3 * D), D ** -0.5, 0.21875, ((0, 2),))
    attend_out = bell_draw(streams_of[5], (SECTIONS, D, D), (D // 32) ** -0.5, 1.25, ((0, 2),))
    time_weight = bell_draw(streams_of[6], (SECTIONS, EMB, 3 * D), EMB ** -0.5, 0.5, ((0, 2),))
    time_bias = bell_draw(streams_of[7], (SECTIONS, 3 * D), 0.5, 3.0, ((0, 2),))
    expand_weight = bell_draw(streams_of[8], (SECTIONS, D, FF), D ** -0.5, 0.21875, ((0, 2),))
    expand_bias = bell_draw(streams_of[9], (SECTIONS, FF), 0.5, 3.0, ((0, 2),))
    reduce_weight = bell_draw(streams_of[10], (SECTIONS, FF, D), FF ** -0.5, 0.109375, ((0, 2),))
    reduce_bias = bell_draw(streams_of[11], (SECTIONS, D), 0.5, 3.0, ((0, 2),))
    return dict(ends_in=ends_in, lengths=lengths, times=times, norm_gain=norm_gain, attend_in=attend_in, attend_out=attend_out, time_weight=time_weight, time_bias=time_bias, expand_weight=expand_weight, expand_bias=expand_bias, reduce_weight=reduce_weight, reduce_bias=reduce_bias)


@jax.custom_vjp
def low(v):
    return lax.optimization_barrier(v.astype(jnp.bfloat16)).astype(jnp.float32)

@jax.custom_vjp
def low_back(v):
    return v

def low_keep(v):
    return (low(v), None)

def low_pass(kept, grad):
    return (grad,)

def back_keep(v):
    return (v, None)

def back_low(kept, grad):
    return (low(grad),)
low.defvjp(low_keep, low_pass)
low_back.defvjp(back_keep, back_low)

def rounded(values):
    return low_back(low(values))

def matmul(left, right):
    return jnp.dot(left, right, precision=lax.Precision.HIGHEST)

def normalize(values):
    center = values - lax.optimization_barrier(jnp.mean(values, axis=-1, keepdims=True))
    spread = lax.optimization_barrier(jnp.mean(center * center, axis=-1, keepdims=True))
    return center * lax.rsqrt(spread + 1e-05)

def segment_table(lengths_row, times_row, span):
    finish = jnp.cumsum(lengths_row).astype(jnp.int32)
    begin = (finish - lengths_row).astype(jnp.int32)
    position = jnp.arange(span, dtype=jnp.int32)
    owner = lax.optimization_barrier(jnp.sum((position[:, None] >= finish[None, :]).astype(jnp.int32), axis=1)).astype(jnp.int32)
    member = owner[:, None] == jnp.arange(SEGS, dtype=jnp.int32)[None, :]
    onehot = member.astype(jnp.float32)
    offset = lax.optimization_barrier(jnp.sum(jnp.where(member, begin[None, :], 0), axis=1)).astype(jnp.int32)
    place = (position - offset).astype(jnp.float32)
    same = owner[:, None] == owner[None, :]
    freqs = jnp.exp(-math.log(10000.0) * jnp.arange(EMB // 2, dtype=jnp.float32) / (EMB // 2))
    phase = times_row.astype(jnp.float32)[:, None] * freqs[None, :]
    embed = jnp.concatenate([jnp.cos(phase), jnp.sin(phase)], axis=1)
    return (onehot, place, same, embed)

def angles(place):
    half_size = HEAD // 2
    freqs = jnp.exp(-math.log(10000.0) * jnp.arange(half_size, dtype=jnp.float32) / half_size)
    phase = place[:, None, None] * freqs[None, None, :]
    return (jnp.cos(phase), jnp.sin(phase))

def rotate(values, cos_part, sin_part):
    half_size = values.shape[-1] // 2
    first_half = values[..., :half_size]
    second_half = values[..., half_size:]
    return jnp.concatenate([first_half * cos_part - second_half * sin_part, second_half * cos_part + first_half * sin_part], axis=-1)

def block(values, params, table):
    gain, attend_in, attend_out, time_weight, time_bias, expand_weight, expand_bias, reduce_weight, reduce_bias = params
    onehot, place, same, embed = table
    span = values.shape[0]
    normed = normalize(values) * gain
    joint = low_back(matmul(rounded(normed), attend_in))
    query = joint[:, :D].reshape(span, HEADS, HEAD) * 0.125
    keys = joint[:, D:2 * D].reshape(span, HEADS, HEAD)
    vals = joint[:, 2 * D:].reshape(span, HEADS, HEAD)
    cos_part, sin_part = angles(place)
    query16 = rounded(rotate(query, cos_part, sin_part))
    key16 = rounded(rotate(keys, cos_part, sin_part))
    value16 = rounded(vals)
    scores = low_back(jnp.einsum('thd,uhd->htu', query16, key16, precision=lax.Precision.HIGHEST))
    scores = jnp.where(same[None], scores, -1e+30)
    probs = jax.nn.softmax(scores, axis=-1)
    mixed = jnp.einsum('htu,uhd->thd', rounded(probs), value16, precision=lax.Precision.HIGHEST).reshape(span, D)
    middle = values + low_back(matmul(rounded(mixed), attend_out))
    modulation = matmul(embed, time_weight) + time_bias
    per_token = matmul(onehot, modulation)
    scale = per_token[:, :D]
    shift = per_token[:, D:2 * D]
    gate = per_token[:, 2 * D:]
    modded = normalize(middle) * (1.0 + scale) + shift
    preact = low_back(matmul(rounded(modded), expand_weight) + expand_bias)
    active = jax.nn.gelu(preact, approximate=False)
    branch = low_back(matmul(rounded(active), reduce_weight) + reduce_bias)
    return middle + gate * branch

def reference(ends_in, lengths, times, norm_gain, attend_in, attend_out, time_weight, time_bias, expand_weight, expand_bias, reduce_weight, reduce_bias):
    weights = tuple((item.astype(jnp.float32) for item in (norm_gain, attend_in, attend_out, time_weight, time_bias, expand_weight, expand_bias, reduce_weight, reduce_bias)))
    inputs = ends_in[0].astype(jnp.float32).reshape(-1, MB_TOK, D)
    cotans = ends_in[1].astype(jnp.float32).reshape(-1, MB_TOK, D)
    span_rows = lengths.reshape(-1, SEGS)
    stamp_rows = times.reshape(-1, SEGS)

    def micro_step(totals, item):
        entering, cotan, span_row, stamp_row = item
        table = segment_table(span_row, stamp_row, MB_TOK)

        def two_layers(values, params):
            first_out = block(values, tuple((piece[0] for piece in params)), table)
            return block(low_back(low(first_out)), tuple((piece[1] for piece in params)), table)
        result, pull = jax.vjp(two_layers, entering, weights)
        input_grad, weight_grads = pull(cotan)
        totals = tuple((total + term for total, term in zip(totals, weight_grads)))
        return (totals, (result.astype(jnp.bfloat16), input_grad.astype(jnp.bfloat16)))
    start = tuple((jnp.zeros_like(item) for item in weights))
    totals, (results, input_grads) = lax.scan(micro_step, start, (inputs, cotans, span_rows, stamp_rows))
    ends_out = jnp.stack([input_grads.reshape(-1, D), results.reshape(-1, D)])
    return (ends_out, totals[0], totals[1], totals[2], totals[3], totals[4], totals[5], totals[6], totals[7], totals[8])
```

```python
from functools import partial
import math

import jax
import jax.numpy as jnp
from jax import lax
from jax.sharding import PartitionSpec as P

HEADS = 12
HEAD = 64
EMB = 128
SEGS = 4


def from_behind(block, axis, distance):
    devices = range(lax.axis_size(axis))
    route = [(i - distance, i) for i in devices if i - distance in devices]
    return lax.ppermute(block, axis, route)


def normalize(values):
    center = values - jnp.mean(values, axis=-1, keepdims=True)
    spread = jnp.mean(center * center, axis=-1, keepdims=True)
    return center * lax.rsqrt(spread + 1e-05)


def segment_table(lengths_row, times_row, span):
    finish = jnp.cumsum(lengths_row)
    begin = finish - lengths_row
    position = jnp.arange(span, dtype=jnp.int32)
    owner = jnp.sum((position[:, None] >= finish[None, :]).astype(jnp.int32), axis=1)
    member = owner[:, None] == jnp.arange(SEGS, dtype=jnp.int32)[None, :]
    onehot = member.astype(jnp.float32)
    offset = jnp.sum(jnp.where(member, begin[None, :], 0), axis=1)
    place = (position - offset).astype(jnp.float32)
    same = owner[:, None] == owner[None, :]
    freqs = jnp.exp(-math.log(10000.0) * jnp.arange(EMB // 2, dtype=jnp.float32) / (EMB // 2))
    phase = times_row.astype(jnp.float32)[:, None] * freqs[None, :]
    embed = jnp.concatenate([jnp.cos(phase), jnp.sin(phase)], axis=1)
    return (onehot, place, same, embed)


def angles(place):
    half_size = HEAD // 2
    freqs = jnp.exp(-math.log(10000.0) * jnp.arange(half_size, dtype=jnp.float32) / half_size)
    phase = place[:, None, None] * freqs[None, None, :]
    return (jnp.cos(phase), jnp.sin(phase))


def rotate(values, cos_part, sin_part):
    half_size = values.shape[-1] // 2
    first_half = values[..., :half_size]
    second_half = values[..., half_size:]
    return jnp.concatenate(
        [
            first_half * cos_part - second_half * sin_part,
            second_half * cos_part + first_half * sin_part,
        ],
        axis=-1,
    )


def modulation(time_weight, time_bias, onehot, embed, width):
    per_seq = jnp.dot(
        embed, time_weight.astype(jnp.float32), precision=lax.Precision.HIGHEST
    ) + time_bias.astype(jnp.float32)
    per_token = jnp.dot(onehot, per_seq, precision=lax.Precision.HIGHEST)
    return (per_token[:, :width], per_token[:, width : 2 * width], per_token[:, 2 * width :])


def modnorm(middle, scale, shift):
    return normalize(middle) * (1.0 + scale) + shift


def forward(entering, weights, table):
    (
        gain,
        attend_in,
        attend_out,
        time_weight,
        time_bias,
        expand_weight,
        expand_bias,
        reduce_weight,
        reduce_bias,
    ) = weights
    onehot, place, same, embed = table
    span, width = entering.shape
    inputs = entering.astype(jnp.float32)
    normed16 = (normalize(inputs) * gain.astype(jnp.float32)).astype(jnp.bfloat16)
    joint = jnp.dot(normed16, attend_in, preferred_element_type=jnp.float32)
    cos_part, sin_part = angles(place)
    query = joint[:, :width].reshape(span, HEADS, HEAD) * 0.125
    query16 = rotate(query, cos_part, sin_part).astype(jnp.bfloat16)
    key16 = rotate(
        joint[:, width : 2 * width].reshape(span, HEADS, HEAD), cos_part, sin_part
    ).astype(jnp.bfloat16)
    value16 = joint[:, 2 * width :].reshape(span, HEADS, HEAD).astype(jnp.bfloat16)
    scores = jnp.einsum("thd,uhd->htu", query16, key16, preferred_element_type=jnp.float32)
    scores = jnp.where(same[None], scores, -1e30)
    probs = jax.nn.softmax(scores, axis=-1)
    mixed16 = (
        jnp.einsum(
            "htu,uhd->thd", probs.astype(jnp.bfloat16), value16, preferred_element_type=jnp.float32
        )
        .reshape(span, width)
        .astype(jnp.bfloat16)
    )
    middle = inputs + jnp.dot(mixed16, attend_out, preferred_element_type=jnp.float32)
    scale, shift, gate = modulation(time_weight, time_bias, onehot, embed, width)
    modded16 = modnorm(middle, scale, shift).astype(jnp.bfloat16)
    preact = jnp.dot(
        modded16, expand_weight, preferred_element_type=jnp.float32
    ) + expand_bias.astype(jnp.float32)
    active16 = jax.nn.gelu(preact, approximate=False).astype(jnp.bfloat16)
    branch = jnp.dot(
        active16, reduce_weight, preferred_element_type=jnp.float32
    ) + reduce_bias.astype(jnp.float32)
    result = middle + gate * branch
    return (
        result,
        (
            entering,
            normed16,
            query16,
            key16,
            value16,
            probs,
            mixed16,
            middle,
            modded16,
            preact,
            active16,
            branch,
        ),
    )


def input_chain(cotan, saved, weights, table):
    (
        gain,
        attend_in,
        attend_out,
        time_weight,
        time_bias,
        expand_weight,
        expand_bias,
        reduce_weight,
        reduce_bias,
    ) = weights
    (
        entering,
        normed16,
        query16,
        key16,
        value16,
        probs,
        mixed16,
        middle,
        modded16,
        preact,
        active16,
        branch,
    ) = saved
    onehot, place, same, embed = table
    span, width = entering.shape
    scale, shift, gate = modulation(time_weight, time_bias, onehot, embed, width)
    branch_grad = (cotan * gate).astype(jnp.bfloat16)
    gate_grad = cotan * branch
    grad_rbias = jnp.sum(branch_grad.astype(jnp.float32), axis=0)
    active_grad = jnp.einsum(
        "td,fd->tf", branch_grad, reduce_weight, preferred_element_type=jnp.float32
    ).astype(jnp.bfloat16)
    gelu_out, gelu_pull = jax.vjp(partial(jax.nn.gelu, approximate=False), preact)
    preact_grad = gelu_pull(active_grad.astype(jnp.float32))[0].astype(jnp.bfloat16)
    grad_ebias = jnp.sum(preact_grad.astype(jnp.float32), axis=0)
    modded_grad = (
        jnp.einsum("tf,df->td", preact_grad, expand_weight, preferred_element_type=jnp.float32)
        .astype(jnp.bfloat16)
        .astype(jnp.float32)
    )
    mod_out, mod_pull = jax.vjp(modnorm, middle, scale, shift)
    middle_part, scale_grad, shift_grad = mod_pull(modded_grad)
    middle_grad = cotan + middle_part
    token_grad = jnp.concatenate([scale_grad, shift_grad, gate_grad], axis=1)
    seq_grad = jnp.dot(onehot.T, token_grad, precision=lax.Precision.HIGHEST)
    grad_tbias = jnp.sum(seq_grad, axis=0)
    attn_grad = middle_grad.astype(jnp.bfloat16)
    mixed_grad = (
        jnp.einsum("te,de->td", attn_grad, attend_out, preferred_element_type=jnp.float32)
        .astype(jnp.bfloat16)
        .reshape(span, HEADS, HEAD)
    )
    prob_grad = (
        jnp.einsum("thd,uhd->htu", mixed_grad, value16, preferred_element_type=jnp.float32)
        .astype(jnp.bfloat16)
        .astype(jnp.float32)
    )
    value_grad = jnp.einsum(
        "htu,thd->uhd", probs.astype(jnp.bfloat16), mixed_grad, preferred_element_type=jnp.float32
    ).astype(jnp.bfloat16)
    score_grad = probs * (prob_grad - jnp.sum(probs * prob_grad, axis=-1, keepdims=True))
    score_grad = jnp.where(same[None], score_grad, 0.0).astype(jnp.bfloat16)
    query_grad = (
        jnp.einsum("htu,uhd->thd", score_grad, key16, preferred_element_type=jnp.float32)
        .astype(jnp.bfloat16)
        .astype(jnp.float32)
    )
    key_grad = (
        jnp.einsum("htu,thd->uhd", score_grad, query16, preferred_element_type=jnp.float32)
        .astype(jnp.bfloat16)
        .astype(jnp.float32)
    )
    cos_part, sin_part = angles(place)
    rot_out, rot_pull = jax.vjp(lambda values: rotate(values, cos_part, sin_part), query_grad)
    query_grad = rot_pull(query_grad)[0] * 0.125
    key_grad = rot_pull(key_grad)[0]
    joint_grad = jnp.concatenate(
        [
            query_grad.reshape(span, width),
            key_grad.reshape(span, width),
            value_grad.astype(jnp.float32).reshape(span, width),
        ],
        axis=1,
    ).astype(jnp.bfloat16)
    normed_grad = (
        jnp.einsum("te,de->td", joint_grad, attend_in, preferred_element_type=jnp.float32)
        .astype(jnp.bfloat16)
        .astype(jnp.float32)
    )
    norm_out, norm_pull = jax.vjp(
        lambda values, scaler: normalize(values) * scaler,
        entering.astype(jnp.float32),
        gain.astype(jnp.float32),
    )
    input_part, grad_gain = norm_pull(normed_grad)
    input_grad = middle_grad + input_part
    small_terms = (grad_gain, grad_tbias, grad_ebias, grad_rbias)
    operands = (
        active16,
        branch_grad,
        modded16,
        preact_grad,
        mixed16,
        attn_grad,
        normed16,
        joint_grad,
        seq_grad,
    )
    return (input_grad, small_terms, operands)


def weight_products(operands, embed):
    (
        active16,
        branch_grad,
        modded16,
        preact_grad,
        mixed16,
        attn_grad,
        normed16,
        joint_grad,
        seq_grad,
    ) = operands
    grad_rweight = jnp.einsum(
        "tf,td->fd", active16, branch_grad, preferred_element_type=jnp.float32
    )
    grad_eweight = jnp.einsum(
        "td,tf->df", modded16, preact_grad, preferred_element_type=jnp.float32
    )
    grad_oweight = jnp.einsum("td,te->de", mixed16, attn_grad, preferred_element_type=jnp.float32)
    grad_iweight = jnp.einsum("td,te->de", normed16, joint_grad, preferred_element_type=jnp.float32)
    grad_tweight = jnp.dot(embed.T, seq_grad, precision=lax.Precision.HIGHEST)
    return (grad_iweight, grad_oweight, grad_tweight, grad_eweight, grad_rweight)

def bits_of(count):
    bits = count.bit_length() - 1
    assert 1 << bits == count
    return bits


def halve_sum(terms, axis, order):
    count = terms.shape[0]
    bits = bits_of(count)
    me = lax.axis_index(axis)
    view = terms.reshape((2,) * bits + terms.shape[1:])
    left = list(range(bits - 1, -1, -1))
    for step, bit in enumerate(order):
        spot = left.index(bit)
        own = (me >> bit) & 1
        keep = lax.dynamic_index_in_dim(view, own, spot, keepdims=False)
        send = lax.dynamic_index_in_dim(view, 1 - own, spot, keepdims=False)
        came = lax.ppermute(send, axis, [(i, i ^ (1 << bit)) for i in range(count)])
        view = keep.astype(jnp.float32) + came.astype(jnp.float32)
        if step < bits - 1:
            view = view.astype(jnp.bfloat16)
        left.remove(bit)
    return view


def per_device(
    ends_in,
    lengths,
    times,
    norm_gain,
    attend_in,
    attend_out,
    time_weight,
    time_bias,
    expand_weight,
    expand_bias,
    reduce_weight,
    reduce_bias,
):
    weights = tuple(
        (
            piece[0]
            for piece in (
                norm_gain,
                attend_in,
                attend_out,
                time_weight,
                time_bias,
                expand_weight,
                expand_bias,
                reduce_weight,
                reduce_bias,
            )
        )
    )
    local = ends_in[0]
    micro = lengths.shape[1]
    assert micro == 2
    width = local.shape[1]
    span = local.shape[0] // micro
    section = lax.axis_index("section")
    leading = section == 0
    tables = [segment_table(lengths[0, slot], times[0, slot], span) for slot in range(micro)]
    rows = [local[slot * span : (slot + 1) * span] for slot in range(micro)]

    def first_half(slot, entering):
        return forward(entering, weights, tables[slot])[0].astype(jnp.bfloat16)

    def both_halves(slot, entering, cotan):
        result, saved = forward(entering, weights, tables[slot])
        input_grad, small_terms, operands = input_chain(
            cotan.astype(jnp.float32), saved, weights, tables[slot]
        )
        return (
            result.astype(jnp.bfloat16),
            input_grad.astype(jnp.bfloat16),
            small_terms,
            operands,
        )

    shapes = jax.eval_shape(lambda a, b: both_halves(0, a, b), rows[0], rows[0])
    blank = jax.tree.map(lambda s: jnp.zeros(s.shape, s.dtype), shapes)
    swap = [(0, 1), (1, 0)]
    out0 = lax.cond(
        leading, lambda: first_half(0, rows[0]), lambda: jnp.zeros((span, width), jnp.bfloat16)
    )
    came0 = lax.ppermute(out0, "section", [(0, 1)])
    phase_b = lax.cond(
        leading,
        lambda: (blank[0], first_half(1, rows[1]), blank[2], blank[3]),
        lambda: both_halves(0, came0, rows[0]),
    )
    came1 = lax.ppermute(phase_b[1], "section", swap)
    pick0 = lambda a, b: jax.tree.map(lambda x, y: jnp.where(leading, x, y), a, b)
    slot_tab = pick0(tables[0], tables[1])
    result_c, saved = forward(jnp.where(leading, rows[0], came1), weights, slot_tab)
    grad_c, small_c, operands_c = input_chain(
        jnp.where(leading, came1, rows[1]).astype(jnp.float32), saved, weights, slot_tab
    )
    phase_c = (result_c.astype(jnp.bfloat16), grad_c.astype(jnp.bfloat16), small_c, operands_c)
    came2 = lax.ppermute(phase_c[1], "section", [(1, 0)])
    phase_d = lax.cond(
        leading,
        lambda: both_halves(1, rows[1], came2),
        lambda: phase_b,
    )
    ends_out = jnp.where(
        leading,
        jnp.concatenate([phase_c[1], phase_d[1]]),
        jnp.concatenate([phase_b[0], phase_c[0]]),
    )[None]
    small = jax.tree.map(lambda x, y: x + y, phase_c[2], phase_d[2])
    operands = jax.tree.map(lambda x, y: jnp.concatenate([x, y]), phase_c[3], phase_d[3])
    embed = jnp.concatenate(
        [slot_tab[3], jnp.where(leading, tables[1][3], tables[0][3])]
    )
    grad_iweight, grad_oweight, grad_tweight, grad_eweight, grad_rweight = weight_products(
        operands, embed
    )
    grad_gain, grad_tbias, grad_ebias, grad_rbias = small
    count = lax.axis_size("rep")

    def block(grad):
        return grad.reshape((count, grad.shape[0] // count) + grad.shape[1:]).astype(jnp.bfloat16)

    tail_parts = [
        grad_oweight.reshape(count, -1, width),
        grad_tweight.reshape(count, -1, width),
    ]
    smalls = jnp.concatenate(
        [piece.reshape(count, -1) for piece in (grad_gain, grad_tbias, grad_ebias, grad_rbias)], 1
    )
    small_width = smalls.shape[1]
    smalls = jnp.pad(smalls, ((0, 0), (0, width - small_width)))[:, None]
    tail = jnp.concatenate(tail_parts + [smalls], axis=1)
    pad = -tail.shape[1] % 16
    tail = jnp.pad(tail, ((0, 0), (0, pad), (0, 0))).astype(jnp.bfloat16)
    bits = bits_of(count)
    plain = list(range(bits))
    turned = plain if bits < 3 else [0, 2, 1] + plain[3:]
    share_r = halve_sum(block(grad_rweight), "rep", plain)
    share_e = halve_sum(block(grad_eweight), "rep", plain)
    share_i = halve_sum(block(grad_iweight), "rep", turned)
    share_t = halve_sum(tail, "rep", plain)
    rows_o = width // count
    rows_t = EMB // count
    share_o = share_t[:rows_o]
    share_w = share_t[rows_o : rows_o + 3 * rows_t].reshape(rows_t, 3 * width)
    line = share_t[rows_o + 3 * rows_t]
    cuts = [width // count, 3 * width // count, expand_bias.shape[1] // count, width // count]
    spots = [sum(cuts[:i]) for i in range(5)]
    share_gain, share_tb, share_eb, share_rb = (line[spots[i] : spots[i + 1]] for i in range(4))
    results = (
        share_gain,
        share_i,
        share_o,
        share_w,
        share_tb,
        share_e,
        share_eb,
        share_r,
        share_rb,
    )
    return (ends_out,) + tuple(piece[None] for piece in results)


def solution(mesh):
    return jax.shard_map(
        per_device,
        mesh=mesh,
        in_specs=(
            P("section", "rep", None),
            P("rep", None, None),
            P("rep", None, None),
            P("section", None),
            P("section", None, None),
            P("section", None, None),
            P("section", None, None),
            P("section", None),
            P("section", None, None),
            P("section", None),
            P("section", None, None),
            P("section", None),
        ),
        out_specs=(
            P("section", "rep", None),
            P("section", "rep"),
            P("section", "rep", None),
            P("section", "rep", None),
            P("section", "rep", None),
            P("section", "rep"),
            P("section", "rep", None),
            P("section", "rep"),
            P("section", "rep", None),
            P("section", "rep"),
        ),
        check_vma=False,
    )
```

```python
from functools import partial
import math

import jax
import jax.numpy as jnp
from jax import lax
from jax.experimental import pallas as pl
from jax.experimental.pallas import tpu as pltpu
from jax.sharding import PartitionSpec as P

HEADS = 12
HEAD = 64
EMB = 128
SEGS = 4

ANY = pl.ANY
VMEM = pltpu.MemorySpace.VMEM
SMEM = pltpu.MemorySpace.SMEM
F32 = jnp.float32
BF16 = jnp.bfloat16
ROOT_HALF = 0.7071067811865476
ROOT_TAU = 0.3989422804014327


def dot(left, right, left_dim=1, right_dim=0):
    return lax.dot_general(
        left, right, (((left_dim,), (right_dim,)), ((), ())), preferred_element_type=F32
    )


def lane_blocks(values, size=128):
    return [values[:, i : i + size] for i in range(0, values.shape[1], size)]


def swap_halves(values, low_half):
    forth = pltpu.roll(values, 128 - HEAD // 2, 1)
    back = pltpu.roll(values, HEAD // 2, 1)
    return jnp.where(low_half, forth, back)


def norm_parts(values):
    center = values - jnp.mean(values, axis=-1, keepdims=True)
    spread = jnp.mean(center * center, axis=-1, keepdims=True)
    factor = lax.rsqrt(spread + 1e-05)
    return center * factor, factor


def norm_back(grad, unit, factor):
    return factor * (
        grad
        - jnp.mean(grad, axis=-1, keepdims=True)
        - unit * jnp.mean(grad * unit, axis=-1, keepdims=True)
    )


OPERANDS = ("normed", "mixed", "modded", "active", "bgrad", "pgrad", "agrad", "jgrad")


def relay_kernel(span, width, hidden, with_back, carried_count, *refs):
    refs = list(refs)
    flags, local, came, mods, trig, gain, ebias, rbias = refs[:8]
    big_hbm = refs[8:12]
    pos = 12 + carried_count
    leave = refs[pos]
    pos += 1
    if with_back:
        ends, small_out = refs[pos : pos + 2]
        ops_out = dict(zip(OPERANDS, refs[pos + 2 : pos + 2 + len(OPERANDS)]))
        pos += 2 + len(OPERANDS)
    (
        xv, dyv, win, wout, wex, wre, qkv, probs, middle, slope, branch, mixed_grad,
        middle_grad, acc, bias, leave_v, small, *rest,
    ) = refs[pos:]
    ops = dict(zip(OPERANDS, rest[: len(OPERANDS)]))
    result_v, in_sem, out_sem = rest[len(OPERANDS) :]
    mode, slot, first, single = flags[0], flags[1], flags[2], flags[3]
    pairs = width // 128
    seg = span // SEGS
    step = 512
    tiles = hidden // step
    low_half = lax.broadcasted_iota(jnp.int32, (span, 128), 1) % HEAD < HEAD // 2
    low_head = lax.broadcasted_iota(jnp.int32, (span, 128), 1) < HEAD
    head_row = [
        (lax.broadcasted_iota(jnp.int32, (1, 128), 1) // HEAD == i).astype(F32).astype(BF16)
        for i in range(2)
    ]

    def trig_pair():
        cos_all, sin_all = trig[0], trig[1]
        cos_cut = jnp.concatenate([cos_all[:seg]] * SEGS, axis=0)
        sin_cut = jnp.concatenate([sin_all[:seg]] * SEGS, axis=0)
        whole = single == 1
        return jnp.where(whole, cos_all, cos_cut), jnp.where(whole, sin_all, sin_cut)

    def mod_row(block, part):
        row = jnp.where(single == 1, 0, block)
        return mods[slot, pl.ds(row, 1), part * width : (part + 1) * width]

    own = local.at[pl.ds(pl.multiple_of(slot * span, span), span)]
    big = (win, wout, wex, wre)
    loads = [
        pltpu.make_async_copy(source, target, in_sem.at[i])
        for i, (source, target) in enumerate(zip(big_hbm, big))
    ]

    def token_loads():
        mine = first == 1

        @pl.when(mine)
        def _():
            pltpu.make_async_copy(own, xv, in_sem.at[4]).start()

        @pl.when(jnp.logical_not(mine))
        def _():
            pltpu.make_async_copy(came, xv, in_sem.at[4]).start()

        if with_back:

            @pl.when(mine & (mode == 2))
            def _():
                pltpu.make_async_copy(came, dyv, in_sem.at[5]).start()

            @pl.when(jnp.logical_not(mine) & (mode == 2))
            def _():
                pltpu.make_async_copy(own, dyv, in_sem.at[5]).start()

    def forward_part():
        token_loads()
        for load in loads:
            load.start()
        pltpu.make_async_copy(came, xv, in_sem.at[4]).wait()
        unit, _ = norm_parts(xv[...].astype(F32))
        ops["normed"][...] = (unit * gain[...].astype(F32)).astype(BF16)
        across = lax.broadcasted_iota(jnp.int32, (span, span), 0) // seg
        down = lax.broadcasted_iota(jnp.int32, (span, span), 1) // seg
        bias[...] = jnp.where((across == down) | (single == 1), 0.0, -1e30)
        loads[0].wait()

        def turned(tile, factor):
            cos_part, sin_part = trig_pair()

            def body(i, _):
                at = pl.ds(pl.multiple_of(tile * width + i * 256, 256), 256)
                joint = dot(ops["normed"][...], win[:, at])
                outs = []
                for piece in lane_blocks(joint):
                    outs.append(piece * cos_part + swap_halves(piece, low_half) * sin_part)
                whole = jnp.concatenate(outs, axis=1)
                qkv[:, at] = (whole * factor if factor != 1.0 else whole).astype(BF16)
                return _

            lax.fori_loop(0, width // 256, body, 0)

        turned(0, 0.125)
        turned(1, 1.0)
        qkv[:, 2 * width :] = dot(ops["normed"][...], win[:, 2 * width :]).astype(BF16)

        def heads(i, _):
            at = [pl.ds(pl.multiple_of(p * width + i * 128, 128), 128) for p in range(3)]
            query, key, value = (qkv[:, a] for a in at)
            outs = []
            for h in range(2):
                scores = dot(key * head_row[h], query, 1, 1) + bias[...]
                top = jnp.max(scores, axis=0, keepdims=True)
                raised = jnp.exp(scores - top)
                total = jnp.sum(raised, axis=0, keepdims=True)
                prob = raised * (1.0 / total)
                probs[2 * i + h] = prob
                outs.append(dot(prob.astype(BF16), value, 0, 0))
            ops["mixed"][:, at[0]] = jnp.where(low_head, outs[0], outs[1]).astype(BF16)
            return _

        lax.fori_loop(0, pairs, heads, 0)
        loads[1].wait()
        middle[...] = xv[...].astype(F32) + dot(ops["mixed"][...], wout[...])
        for b in range(SEGS):
            rows = slice(b * seg, (b + 1) * seg)
            unit, _ = norm_parts(middle[rows])
            ops["modded"][rows] = (unit * (1.0 + mod_row(b, 0)) + mod_row(b, 1)).astype(BF16)
        loads[2].wait()
        loads[3].wait()
        branch[...] = jnp.broadcast_to(rbias[...].astype(F32), (span, width))

        def feed(j, _):
            at = pl.ds(pl.multiple_of(j * step, step), step)
            pre = dot(ops["modded"][...], wex[:, at]) + ebias[:, at].astype(F32)
            area = 0.5 + 0.5 * lax.erf(pre * ROOT_HALF)
            active = (pre * area).astype(BF16)
            if with_back:
                slope[:, at] = area + pre * (jnp.exp(pre * pre * -0.5) * ROOT_TAU)
            ops["active"][:, at] = active
            branch[...] += dot(active, wre[at, :])
            return _

        lax.fori_loop(0, tiles, feed, 0)
        for b in range(SEGS):
            rows = slice(b * seg, (b + 1) * seg)
            result = (middle[rows] + mod_row(b, 2) * branch[rows]).astype(BF16)
            result_v[rows] = result

    def send_out(name, index):
        return pltpu.make_async_copy(ops[name], ops_out[name], out_sem.at[index])

    def backward_part():
        outs = {name: send_out(name, i) for i, name in enumerate(OPERANDS)}
        for name in ("normed", "mixed", "modded", "active"):
            outs[name].start()
        pltpu.make_async_copy(came, dyv, in_sem.at[5]).wait()
        small[...] = jnp.zeros(small.shape, F32)
        whole = single == 1

        def add_segment(block, part, sums):
            row = jnp.where(whole, 0, block)
            at = (pl.ds(SEGS + row, 1), slice(part * width, (part + 1) * width))
            small[at] = small[at] + sums

        total = jnp.zeros((1, width), F32)
        for b in range(SEGS):
            rows = slice(b * seg, (b + 1) * seg)
            cotan = dyv[rows].astype(F32)
            grad = (cotan * mod_row(b, 2)).astype(BF16)
            ops["bgrad"][rows] = grad
            total += jnp.sum(grad.astype(F32), axis=0, keepdims=True)
            add_segment(b, 2, jnp.sum(cotan * branch[rows], axis=0, keepdims=True))
        small[1:2, width : 2 * width] = total
        outs["bgrad"].start()
        acc[...] = jnp.zeros(acc.shape, F32)

        def feed(j, _):
            at = pl.ds(pl.multiple_of(j * step, step), step)
            grad = dot(ops["bgrad"][...], wre[at, :], 1, 1).astype(BF16).astype(F32)
            pre_grad = (slope[:, at] * grad).astype(BF16)
            ops["pgrad"][:, at] = pre_grad
            small[0:1, at] = jnp.sum(pre_grad.astype(F32), axis=0, keepdims=True)
            acc[...] += dot(pre_grad, wex[:, at], 1, 1)
            return _

        lax.fori_loop(0, tiles, feed, 0)
        outs["pgrad"].start()
        for b in range(SEGS):
            rows = slice(b * seg, (b + 1) * seg)
            grad = acc[rows].astype(BF16).astype(F32)
            unit, factor = norm_parts(middle[rows])
            add_segment(b, 0, jnp.sum(grad * unit, axis=0, keepdims=True))
            add_segment(b, 1, jnp.sum(grad, axis=0, keepdims=True))
            back = norm_back(grad * (1.0 + mod_row(b, 0)), unit, factor)
            full = dyv[rows].astype(F32) + back
            middle_grad[rows] = full
            ops["agrad"][rows] = full.astype(BF16)
        outs["agrad"].start()
        mixed_grad[...] = dot(ops["agrad"][...], wout[...], 1, 1).astype(BF16)
        cos_part, sin_part = trig_pair()

        def heads(i, _):
            at = [pl.ds(pl.multiple_of(p * width + i * 128, 128), 128) for p in range(3)]
            query, key, value = (qkv[:, a] for a in at)
            out_grad = mixed_grad[:, at[0]]
            parts = []
            for h in range(2):
                prob = probs[2 * i + h]
                pull = dot(value * head_row[h], out_grad, 1, 1).astype(BF16).astype(F32)
                shared = jnp.sum(prob * pull, axis=0, keepdims=True)
                score_grad = (prob * (pull - shared)).astype(BF16)
                parts.append(
                    (
                        dot(score_grad, key, 0, 0),
                        dot(score_grad, query),
                        dot(prob.astype(BF16), out_grad),
                    )
                )
            for p in range(3):
                grad = jnp.where(low_head, parts[0][p], parts[1][p])
                if p < 2:
                    grad = grad.astype(BF16).astype(F32)
                    grad = grad * cos_part - swap_halves(grad, low_half) * sin_part
                    if p == 0:
                        grad = grad * 0.125
                ops["jgrad"][:, at[p]] = grad.astype(BF16)
            return _

        lax.fori_loop(0, pairs, heads, 0)
        outs["jgrad"].start()
        acc[...] = dot(ops["jgrad"][...], win[...], 1, 1)
        total = jnp.zeros((1, width), F32)
        for b in range(SEGS):
            rows = slice(b * seg, (b + 1) * seg)
            grad = acc[rows].astype(BF16).astype(F32)
            unit, factor = norm_parts(xv[rows].astype(F32))
            total += jnp.sum(grad * unit, axis=0, keepdims=True)
            back = norm_back(grad * gain[...].astype(F32), unit, factor)
            leave_v[rows] = (middle_grad[rows] + back).astype(BF16)
        small[1:2, 0:width] = total
        end_rows = ends.at[pl.ds(pl.multiple_of(slot * span, span), span)]
        mine = first == 1

        @pl.when(mine)
        def _():
            pltpu.make_async_copy(leave_v, end_rows, out_sem.at[8]).start()

        @pl.when(jnp.logical_not(mine))
        def _():
            pltpu.make_async_copy(result_v, end_rows, out_sem.at[8]).start()

        away = pltpu.make_async_copy(leave_v, leave, out_sem.at[9])
        away.start()
        rest_out = pltpu.make_async_copy(small, small_out, out_sem.at[10])
        rest_out.start()
        for name in OPERANDS:
            outs[name].wait()
        pltpu.make_async_copy(leave_v, end_rows, out_sem.at[8]).wait()
        away.wait()
        rest_out.wait()

    @pl.when(mode >= 1)
    def _():
        forward_part()

    @pl.when(mode == 1)
    def _():
        away = pltpu.make_async_copy(result_v, leave, out_sem.at[9])
        away.start()
        away.wait()

    if with_back:

        @pl.when(mode == 2)
        def _():
            backward_part()


def relay_call(flags, local, came, mods, trig, rows, big, carried, with_back):
    span = came.shape[0]
    width = came.shape[1]
    hidden = big[2].shape[1]
    shapes = {
        "normed": width,
        "mixed": width,
        "modded": width,
        "active": hidden,
        "bgrad": width,
        "pgrad": hidden,
        "agrad": width,
        "jgrad": 3 * width,
    }
    tok = lambda cols, kind=BF16: jax.ShapeDtypeStruct((span, cols), kind)
    outs = [tok(width)]
    if with_back:
        outs += [
            jax.ShapeDtypeStruct(local.shape, BF16),
            jax.ShapeDtypeStruct((2 * SEGS, hidden), F32),
        ]
        outs += [tok(shapes[name]) for name in OPERANDS]
    in_specs = [pl.BlockSpec(memory_space=SMEM), pl.BlockSpec(memory_space=ANY)]
    in_specs += [pl.BlockSpec(memory_space=ANY)]
    in_specs += [pl.BlockSpec(memory_space=VMEM)] * 5
    in_specs += [pl.BlockSpec(memory_space=ANY)] * 4
    args = [flags, local, came, mods, trig, *rows, *big]
    aliases = {}
    for i, item in enumerate(carried):
        aliases[len(args)] = 1 + i
        args.append(item)
        in_specs.append(pl.BlockSpec(memory_space=ANY))
    scratch = lambda cols, kind=BF16: pltpu.VMEM((span, cols), kind)
    scratch_shapes = [
        scratch(width),
        scratch(width),
        *[pltpu.VMEM(item.shape, BF16) for item in big],
        scratch(3 * width),
        pltpu.VMEM((HEADS, span, span), F32),
        scratch(width, F32),
        scratch(hidden, F32),
        scratch(width, F32),
        scratch(width),
        scratch(width, F32),
        scratch(width, F32),
        scratch(span, F32),
        scratch(width),
        pltpu.VMEM((2 * SEGS, hidden), F32),
        *[scratch(shapes[name]) for name in OPERANDS],
        scratch(width),
        pltpu.SemaphoreType.DMA((6,)),
        pltpu.SemaphoreType.DMA((11,)),
    ]
    return pl.pallas_call(
        partial(relay_kernel, span, width, hidden, with_back, len(carried)),
        out_shape=outs,
        in_specs=in_specs,
        out_specs=[pl.BlockSpec(memory_space=ANY)] * len(outs),
        input_output_aliases=aliases,
        scratch_shapes=scratch_shapes,
        compiler_params=pltpu.CompilerParams(
            vmem_limit_bytes=56 * 1024 * 1024
        ),
        name="relay_both" if with_back else "relay_forward",
    )(*args)


def term_kernel(lines, core, left_x, left_y, right_x, right_y, send, keep):
    term = dot(left_x[...], right_x[...], 0, 0) + dot(left_y[...], right_y[...], 0, 0)
    low = core[0] == 0
    for p in range(send.shape[0]):
        even = term[2 * p * lines : (2 * p + 1) * lines]
        odd = term[(2 * p + 1) * lines : (2 * p + 2) * lines]
        send[p] = jnp.where(low, odd, even).astype(BF16)
        keep[p] = jnp.where(low, even, odd)


def weight_term(core, left, right, count, name):
    span, rows = left[0].shape
    cols = right[0].shape[1]
    lines = rows // count
    high, wide = 384, 768
    if lines % 16 or high % (2 * lines):
        term = dot(left[0], right[0], 0, 0) + dot(left[1], right[1], 0, 0)
        view = term.reshape(count // 2, 2, lines, cols)
        own = lax.dynamic_index_in_dim(view, core, 1, keepdims=False)
        other = lax.dynamic_index_in_dim(view, 1 - core, 1, keepdims=False)
        return other.astype(BF16), own
    group = high // (2 * lines)
    left_spec = pl.BlockSpec((span, high), lambda i, j: (0, i))
    right_spec = pl.BlockSpec((span, wide), lambda i, j: (0, j))
    out_spec = pl.BlockSpec((group, lines, wide), lambda i, j: (i, 0, j))
    shape = (count // 2, lines, cols)
    return pl.pallas_call(
        partial(term_kernel, lines),
        grid=(rows // high, cols // wide),
        out_shape=[jax.ShapeDtypeStruct(shape, BF16), jax.ShapeDtypeStruct(shape, F32)],
        in_specs=[
            pl.BlockSpec(memory_space=SMEM),
            left_spec,
            left_spec,
            right_spec,
            right_spec,
        ],
        out_specs=[out_spec, out_spec],
        cost_estimate=pl.CostEstimate(
            flops=4 * span * rows * cols, bytes_accessed=6 * rows * cols, transcendentals=0
        ),
        compiler_params=pltpu.CompilerParams(vmem_limit_bytes=32 * 1024 * 1024),
        name=name,
    )(core.reshape(1), left[0], left[1], right[0], right[1])


def bits_of(count):
    bits = count.bit_length() - 1
    assert 1 << bits == count
    return bits


def halve_sum(send, keep, axis, order):
    count = 2 * keep.shape[0]
    bits = bits_of(count)
    me = lax.axis_index(axis)
    left = list(range(bits - 1, 0, -1))
    terms = [keep.reshape((2,) * (bits - 1) + keep.shape[1:])]
    for step, bit in enumerate(order):
        route = [(i, i ^ (1 << bit)) for i in range(count)]
        if step:
            spot = left.index(bit)
            own = (me >> bit) & 1
            cut = lambda item, at: lax.dynamic_index_in_dim(item, at, spot, keepdims=False)
            send = sum(cut(term, 1 - own).astype(F32) for term in terms).astype(BF16)
            terms = [cut(term, own) for term in terms]
            left.remove(bit)
        came = lax.ppermute(send, axis, route)
        terms.append(came.reshape((2,) * len(left) + keep.shape[1:]))
    return sum(term.astype(F32) for term in terms)


def per_device(
    ends_in,
    lengths,
    times,
    norm_gain,
    attend_in,
    attend_out,
    time_weight,
    time_bias,
    expand_weight,
    expand_bias,
    reduce_weight,
    reduce_bias,
):
    local = ends_in[0]
    micro = lengths.shape[1]
    assert micro == 2
    width = local.shape[1]
    span = local.shape[0] // micro
    hidden = expand_weight.shape[2]
    count = lax.axis_size("rep")
    section = lax.axis_index("section")
    core = lax.axis_index("rep") & 1
    first = 1 - section
    half = HEAD // 2
    freqs = jnp.exp(-math.log(10000.0) * jnp.arange(half, dtype=F32) / half)
    phase = jnp.arange(span, dtype=F32)[:, None] * freqs[None, :]
    cos_part, sin_part = jnp.cos(phase), jnp.sin(phase)
    trig = jnp.stack(
        [
            jnp.concatenate([cos_part] * 4, axis=1),
            jnp.concatenate([-sin_part, sin_part] * 2, axis=1),
        ]
    )
    steps = jnp.exp(-math.log(10000.0) * jnp.arange(EMB // 2, dtype=F32) / (EMB // 2))
    turn = times[0].astype(F32)[:, :, None] * steps
    embed = jnp.concatenate([jnp.cos(turn), jnp.sin(turn)], axis=2)
    mods = jnp.dot(
        embed.reshape(micro * SEGS, EMB),
        time_weight[0].astype(F32),
        precision=lax.Precision.HIGHEST,
    ) + time_bias.astype(F32)
    mods = mods.reshape(micro, SEGS, 3 * width)
    single = (lengths[0, :, 0] == span).astype(jnp.int32)
    rows = (norm_gain, expand_bias, reduce_bias)
    big = (attend_in[0], attend_out[0], expand_weight[0], reduce_weight[0])

    def phase_call(mode, slot, came, carried, with_back=True):
        flags = jnp.stack([mode, slot, first, single[slot]]).astype(jnp.int32)
        return relay_call(flags, local, came, mods, trig, rows, big, carried, with_back)

    zero = jnp.int32(0)
    (out_a,) = phase_call(first, zero, local[:span], (), False)
    came_a = lax.ppermute(out_a, "section", [(0, 1)])
    out_b, ends, *held_y = phase_call(1 + section, first, came_a, ())
    came_b = lax.ppermute(out_b, "section", [(0, 1), (1, 0)])
    out_c, ends, *held_x = phase_call(zero + 2, section, came_b, (ends,))
    came_c = lax.ppermute(out_c, "section", [(1, 0)])
    _, ends, *held_y = phase_call(2 * first, zero + 1, came_c, (ends, *held_y))
    small_x, *ops_x = held_x
    small_y, *ops_y = held_y
    ops = {name: (a, b) for name, a, b in zip(OPERANDS, ops_x, ops_y)}
    bits = bits_of(count)
    plain = list(range(bits))
    turned = plain if bits < 3 else [0, 2, 1] + plain[3:]

    def share(left, right, name, order):
        send, keep = weight_term(core, ops[left], ops[right], count, name)
        return halve_sum(send, keep, "rep", order)

    share_r = share("active", "bgrad", "term_reduce", plain)
    share_e = share("modded", "pgrad", "term_expand", plain)
    share_i = share("normed", "jgrad", "term_attend_in", turned)
    share_o = share("mixed", "agrad", "term_attend_out", plain)
    seq = jnp.concatenate([small_x[SEGS:, : 3 * width], small_y[SEGS:, : 3 * width]])
    swapped = jnp.where(first == 1, embed, embed[::-1]).reshape(micro * SEGS, EMB)
    grad_t = lax.dot_general(
        swapped, seq, (((0,), (0,)), ((), ())), precision=lax.Precision.HIGHEST
    )
    small = small_x + small_y
    pieces = [
        small[1, :width],
        jnp.sum(small[SEGS:, : 3 * width], axis=0),
        small[0],
        small[1, width : 2 * width],
    ]
    line = jnp.concatenate([piece.reshape(count, -1) for piece in pieces], 1)
    cuts = [piece.shape[0] // count for piece in pieces]
    deep = EMB // count
    line = jnp.pad(line, ((0, 0), (0, -line.shape[1] % 128)))
    flat = jnp.pad(line[:, None], ((0, 0), (0, deep - 1), (0, 0)))
    tail = jnp.concatenate([grad_t.reshape(count, deep, 3 * width), flat], axis=2)
    tail = tail.reshape((count // 2, 2) + tail.shape[1:])
    share_t = halve_sum(
        lax.dynamic_index_in_dim(tail, 1 - core, 1, keepdims=False).astype(BF16),
        lax.dynamic_index_in_dim(tail, core, 1, keepdims=False),
        "rep",
        plain,
    )
    share_w = share_t[:, : 3 * width]
    share_s = share_t[0, 3 * width :]
    spots = [sum(cuts[:i]) for i in range(5)]
    share_gain, share_tb, share_eb, share_rb = (share_s[spots[i] : spots[i + 1]] for i in range(4))
    results = (
        share_gain,
        share_i,
        share_o,
        share_w,
        share_tb,
        share_e,
        share_eb,
        share_r,
        share_rb,
    )
    return (ends[None],) + tuple(piece[None] for piece in results)


def solution(mesh):
    return jax.shard_map(
        per_device,
        mesh=mesh,
        in_specs=(
            P("section", "rep", None),
            P("rep", None, None),
            P("rep", None, None),
            P("section", None),
            P("section", None, None),
            P("section", None, None),
            P("section", None, None),
            P("section", None),
            P("section", None, None),
            P("section", None),
            P("section", None, None),
            P("section", None),
        ),
        out_specs=(
            P("section", "rep", None),
            P("section", "rep"),
            P("section", "rep", None),
            P("section", "rep", None),
            P("section", "rep", None),
            P("section", "rep"),
            P("section", "rep", None),
            P("section", "rep"),
            P("section", "rep", None),
            P("section", "rep"),
        ),
        check_vma=False,
    )
```

```python
from functools import partial
import math

import jax
import jax.numpy as jnp
import numpy as np
from jax import lax
from jax.experimental import pallas as pl
from jax.experimental.pallas import tpu as pltpu
from jax.sharding import PartitionSpec as P

HEADS = 12
HEAD = 64
EMB = 128
SEGS = 4

ANY = pl.ANY
VMEM = pltpu.MemorySpace.VMEM
SMEM = pltpu.MemorySpace.SMEM
F32 = jnp.float32
BF16 = jnp.bfloat16
ROOT_HALF = 0.7071067811865476
ROOT_TAU = 0.3989422804014327


def dot(left, right, left_dim=1, right_dim=0):
    return lax.dot_general(
        left, right, (((left_dim,), (right_dim,)), ((), ())), preferred_element_type=F32
    )


def repeat(count, body):
    for i in range(count):
        body(i, 0)


def halves(count, body):
    def both(i, _):
        body(2 * i, 0)
        body(2 * i + 1, 0)
        return _

    lax.fori_loop(0, count // 2, both, 0)


def lanes(index, size, start=0):
    if isinstance(index, int):
        return slice(start + index * size, start + (index + 1) * size)
    return pl.ds(pl.multiple_of(start + index * size, size), size)


def lane_blocks(values, size=128):
    return [values[:, i : i + size] for i in range(0, values.shape[1], size)]


def swap_halves(values, low_half):
    forth = pltpu.roll(values, 128 - HEAD // 2, 1)
    back = pltpu.roll(values, HEAD // 2, 1)
    return jnp.where(low_half, forth, back)


def norm_parts(values):
    center = values - jnp.mean(values, axis=-1, keepdims=True)
    spread = jnp.mean(center * center, axis=-1, keepdims=True)
    factor = lax.rsqrt(spread + 1e-05)
    return center * factor, factor


def norm_back(grad, unit, factor):
    return factor * (
        grad
        - jnp.mean(grad, axis=-1, keepdims=True)
        - unit * jnp.mean(grad * unit, axis=-1, keepdims=True)
    )


OPERANDS = ("normed", "mixed", "modded", "active", "bgrad", "pgrad", "agrad", "jgrad")
SMALLS = ("small_out", "small_mlp", "small_in")
KEPT = ("slope", "branch", "middle", "probs", "qkv")
BIG = ("win", "wout", "wex", "wre")
LIGHT = pl.CostEstimate(flops=1, bytes_accessed=1, transcendentals=0)


def scratch_shapes_of(span, width, hidden):
    tok = lambda cols, kind=BF16: ((span, cols), kind)
    return dict(
        xv=tok(width),
        dyv=tok(width),
        win=((width, 3 * width), BF16),
        wout=((width, width), BF16),
        wex=((width, hidden), BF16),
        wre=((hidden, width), BF16),
        normed=tok(width),
        qkv=tok(3 * width),
        probs=((HEADS, span, span), F32),
        mixed=tok(width),
        middle=tok(width, F32),
        modded=tok(width),
        slope=tok(hidden, F32),
        active=tok(hidden),
        branch=tok(width, F32),
        result=tok(width),
        bgrad=tok(width),
        pgrad=tok(hidden),
        agrad=tok(width),
        jgrad=tok(3 * width),
        mixed_grad=tok(width),
        middle_grad=tok(width, F32),
        leave=tok(width),
        acc=tok(width, F32),
        bias=tok(span, F32),
        small_out=((2 * SEGS, width), F32),
        small_mlp=((2 * SEGS, hidden), F32),
        small_in=((2 * SEGS, width), F32),
    )


USES = dict(
    forward=(
        "xv",
        "win",
        "wout",
        "wex",
        "wre",
        "normed",
        "qkv",
        "probs",
        "mixed",
        "middle",
        "modded",
        "slope",
        "active",
        "branch",
        "result",
        "bias",
    ),
    output=(
        "dyv",
        "branch",
        "bgrad",
        "small_out",
    ),
    mlp=(
        "wre",
        "wex",
        "bgrad",
        "slope",
        "middle",
        "dyv",
        "pgrad",
        "agrad",
        "middle_grad",
        "small_mlp",
        "acc",
    ),
    attend=(
        "wout",
        "win",
        "agrad",
        "probs",
        "qkv",
        "xv",
        "middle_grad",
        "jgrad",
        "leave",
        "small_in",
        "mixed_grad",
        "acc",
    ),
)
TERMS = dict(
    reduce=("active", "bgrad"),
    expand=("modded", "pgrad"),
    attend_in=("normed", "jgrad"),
    attend_out=("mixed", "agrad"),
)
TILE = 384


def chunk_cols(term, cols):
    parts = dict(reduce=(2, 2), expand=(2, 4, 4), attend_in=(1,), attend_out=(1,))[term]
    sizes = [cols // part for part in parts]
    return [(sum(sizes[:n]), size) for n, size in enumerate(sizes)]


class Held:
    def __init__(self, bufs, loads, stores, sems):
        self.bufs = bufs
        self.loads = loads
        self.stores = stores
        self.sems = sems
        self.spots = {name: n for n, name in enumerate(loads)}
        self.pending = set(loads)
        self.leaving = {}

    def load(self, name):
        return pltpu.make_async_copy(
            self.loads[name], self.bufs[name], self.sems.at[self.spots[name]]
        )

    def store(self, name):
        return pltpu.make_async_copy(
            self.bufs[name], self.stores[name], self.sems.at[self.leaving[name]]
        )

    def start(self):
        for name in self.loads:
            self.load(name).start()

    def need(self, *names):
        for name in names:
            if name in self.pending:
                self.pending.remove(name)
                self.load(name).wait()

    def done(self, *names):
        for name in names:
            if name in self.stores:
                self.leaving[name] = len(self.loads) + len(self.leaving)
                self.store(name).start()

    def finish(self):
        for name in self.leaving:
            self.store(name).wait()


def stage_kernel(sizes, parts, terms, who, slot, plan, *refs):
    span, width, hidden, lines = sizes
    lengths, section, core, mods, trig, gain, ebias, rbias = refs[:8]
    in_names, in_rows, carried, out_names, out_rows, buf_names, shared = plan
    spots = refs[8:]
    cut = lambda ref, row: ref if row is None else ref.at[pl.ds(row, span)]
    sources = {name: cut(ref, row) for name, row, ref in zip(in_names, in_rows, spots)}
    spots = spots[len(in_names) + carried :]
    stores = {name: cut(ref, row) for name, row, ref in zip(out_names, out_rows, spots)}
    spots = spots[len(out_names) :]
    bufs = dict(zip(buf_names, spots))
    loads = {name: ref for name, ref in sources.items() if name not in shared}
    held = Held(bufs, loads, stores, spots[-1])
    single = lengths[slot, 0] == span
    pairs = width // 128
    seg = span // SEGS
    step = 512
    tiles = hidden // step
    low_half = lax.broadcasted_iota(jnp.int32, (span, 128), 1) % HEAD < HEAD // 2
    low_head = lax.broadcasted_iota(jnp.int32, (span, 128), 1) < HEAD
    head_row = [
        (lax.broadcasted_iota(jnp.int32, (1, 128), 1) // HEAD == i).astype(F32).astype(BF16)
        for i in range(2)
    ]
    blocks = [(b, slice(b * seg, (b + 1) * seg)) for b in range(SEGS)]

    def trig_pair():
        cos_all, sin_all = trig[0], trig[1]
        cos_cut = jnp.concatenate([cos_all[:seg]] * SEGS, axis=0)
        sin_cut = jnp.concatenate([sin_all[:seg]] * SEGS, axis=0)
        return jnp.where(single, cos_all, cos_cut), jnp.where(single, sin_all, sin_cut)

    def mod_row(block, part):
        row = slot * SEGS + jnp.where(single, 0, block)
        return mods[pl.ds(row, 1), part * width : (part + 1) * width]

    def add_segment(small, block, at, sums):
        row = SEGS + jnp.where(single, 0, block)
        small[pl.ds(row, 1), at * width : (at + 1) * width] += sums

    def forward(
        xv, win, wout, wex, wre, normed, qkv, probs, mixed, middle, modded, slope, active, branch,
        result, bias,
    ):
        held.need("xv")
        unit, _ = norm_parts(xv[...].astype(F32))
        normed[...] = (unit * gain[...].astype(F32)).astype(BF16)
        held.done("normed")
        across = lax.broadcasted_iota(jnp.int32, (span, span), 0) // seg
        down = lax.broadcasted_iota(jnp.int32, (span, span), 1) // seg
        bias[...] = jnp.where((across == down) | single, 0.0, -1e30)
        held.need("win")

        def turned(tile, factor):
            cos_part, sin_part = trig_pair()

            def body(i, _):
                at = lanes(i, 256, tile * width)
                joint = dot(normed[...], win[:, at])
                outs = []
                for piece in lane_blocks(joint):
                    outs.append(piece * cos_part + swap_halves(piece, low_half) * sin_part)
                whole = jnp.concatenate(outs, axis=1)
                qkv[:, at] = (whole * factor if factor != 1.0 else whole).astype(BF16)
                return _

            repeat(width // 256, body)

        turned(0, 0.125)
        turned(1, 1.0)
        qkv[:, 2 * width :] = dot(normed[...], win[:, 2 * width :]).astype(BF16)
        held.done("qkv")

        def heads(i, _):
            at = [lanes(i, 128, p * width) for p in range(3)]
            query, key, value = (qkv[:, a] for a in at)
            outs = []
            for h in range(2):
                scores = dot(key * head_row[h], query, 1, 1) + bias[...]
                top = jnp.max(scores, axis=0, keepdims=True)
                raised = jnp.exp(scores - top)
                total = jnp.sum(raised, axis=0, keepdims=True)
                prob = raised * (1.0 / total)
                probs[2 * i + h] = prob
                outs.append(dot(prob.astype(BF16), value, 0, 0))
            mixed[:, at[0]] = jnp.where(low_head, outs[0], outs[1]).astype(BF16)
            return _

        halves(pairs, heads)
        held.done("probs", "mixed")
        held.need("wout")
        middle[...] = xv[...].astype(F32) + dot(mixed[...], wout[...])
        held.done("middle")
        for b, rows in blocks:
            unit, _ = norm_parts(middle[rows])
            modded[rows] = (unit * (1.0 + mod_row(b, 0)) + mod_row(b, 1)).astype(BF16)
        held.done("modded")
        held.need("wex", "wre")
        branch[...] = jnp.broadcast_to(rbias[...].astype(F32), (span, width))

        def feed(j, _):
            at = lanes(j, step)
            pre = dot(modded[...], wex[:, at]) + ebias[:, at].astype(F32)
            area = 0.5 + 0.5 * lax.erf(pre * ROOT_HALF)
            out = (pre * area).astype(BF16)
            slope[:, at] = area + pre * (jnp.exp(pre * pre * -0.5) * ROOT_TAU)
            active[:, at] = out
            branch[...] += dot(out, wre[at, :])
            return _

        repeat(tiles, feed)
        held.done("slope", "active", "branch")
        for b, rows in blocks:
            result[rows] = (middle[rows] + mod_row(b, 2) * branch[rows]).astype(BF16)
        held.done("result")

    def output(dyv, branch, bgrad, small_out):
        held.need("dyv", "branch")
        small_out[...] = jnp.zeros(small_out.shape, F32)
        total = jnp.zeros((1, width), F32)
        for b, rows in blocks:
            cotan = dyv[rows].astype(F32)
            grad = (cotan * mod_row(b, 2)).astype(BF16)
            bgrad[rows] = grad
            total += jnp.sum(grad.astype(F32), axis=0, keepdims=True)
            add_segment(small_out, b, 0, jnp.sum(cotan * branch[rows], axis=0, keepdims=True))
        small_out[0:1, :] = total
        held.done("bgrad", "small_out")

    def mlp(wre, wex, bgrad, slope, middle, dyv, pgrad, agrad, middle_grad, small_mlp, acc):
        small_mlp[...] = jnp.zeros(small_mlp.shape, F32)
        acc[...] = jnp.zeros(acc.shape, F32)
        held.need("bgrad", "wre", "slope", "wex")

        def feed(j, _):
            at = lanes(j, step)
            grad = dot(bgrad[...], wre[at, :], 1, 1).astype(BF16).astype(F32)
            pre_grad = (slope[:, at] * grad).astype(BF16)
            pgrad[:, at] = pre_grad
            small_mlp[0:1, at] = jnp.sum(pre_grad.astype(F32), axis=0, keepdims=True)
            acc[...] += dot(pre_grad, wex[:, at], 1, 1)
            return _

        repeat(tiles, feed)
        held.done("pgrad")
        held.need("middle", "dyv")
        for b, rows in blocks:
            grad = acc[rows].astype(BF16).astype(F32)
            unit, factor = norm_parts(middle[rows])
            add_segment(small_mlp, b, 0, jnp.sum(grad * unit, axis=0, keepdims=True))
            add_segment(small_mlp, b, 1, jnp.sum(grad, axis=0, keepdims=True))
            back = norm_back(grad * (1.0 + mod_row(b, 0)), unit, factor)
            full = dyv[rows].astype(F32) + back
            middle_grad[rows] = full
            agrad[rows] = full.astype(BF16)
        held.done("agrad", "middle_grad", "small_mlp")

    def attend(
        wout, win, agrad, probs, qkv, xv, middle_grad, jgrad, leave, small_in, mixed_grad, acc
    ):
        held.need("agrad", "wout")
        mixed_grad[...] = dot(agrad[...], wout[...], 1, 1).astype(BF16)
        held.need("probs", "qkv")
        cos_part, sin_part = trig_pair()

        def heads(i, _):
            at = [lanes(i, 128, p * width) for p in range(3)]
            query, key, value = (qkv[:, a] for a in at)
            out_grad = mixed_grad[:, at[0]]
            parts = []
            for h in range(2):
                prob = probs[2 * i + h]
                pull = dot(value * head_row[h], out_grad, 1, 1).astype(BF16).astype(F32)
                shared = jnp.sum(prob * pull, axis=0, keepdims=True)
                score_grad = (prob * (pull - shared)).astype(BF16)
                parts.append(
                    (
                        dot(score_grad, key, 0, 0),
                        dot(score_grad, query),
                        dot(prob.astype(BF16), out_grad),
                    )
                )
            for p in range(3):
                grad = jnp.where(low_head, parts[0][p], parts[1][p])
                if p < 2:
                    grad = grad.astype(BF16).astype(F32)
                    grad = grad * cos_part - swap_halves(grad, low_half) * sin_part
                    if p == 0:
                        grad = grad * 0.125
                jgrad[:, at[p]] = grad.astype(BF16)
            return _

        halves(pairs, heads)
        held.done("jgrad")
        held.need("win", "xv", "middle_grad")
        acc[...] = dot(jgrad[...], win[...], 1, 1)
        small_in[...] = jnp.zeros(small_in.shape, F32)
        total = jnp.zeros((1, width), F32)
        for b, rows in blocks:
            grad = acc[rows].astype(BF16).astype(F32)
            unit, factor = norm_parts(xv[rows].astype(F32))
            total += jnp.sum(grad * unit, axis=0, keepdims=True)
            back = norm_back(grad * gain[...].astype(F32), unit, factor)
            leave[rows] = (middle_grad[rows] + back).astype(BF16)
        small_in[0:1, :] = total
        held.done("leave", "small_in")

    steps = dict(forward=forward, output=output, mlp=mlp, attend=attend)
    mine = section[0] == who
    common = Held(bufs, {name: sources[name] for name in shared}, stores, spots[-2])

    @pl.when(mine)
    def _():
        held.start()

    common.start()

    @pl.when(mine)
    def _():
        for part in parts:
            steps[part](*[bufs[name] for name in USES[part]])

    if terms:
        made = [name for term in terms for name in TERMS[term] if name not in shared]

        @pl.when(jnp.logical_not(mine))
        def _():
            copies = []
            for n, name in enumerate(made):
                source = stores[name] if name in stores else sources[name]
                copies.append(pltpu.make_async_copy(source, bufs[name], spots[-1].at[n]))
                copies[-1].start()
            for copy in copies:
                copy.wait()

        common.need(*shared)
        low = core[0] == 0
        out_sems = spots[-3]
        leaving = []
        base = 0
        for term in terms:
            left, right = TERMS[term]
            rows, cols = bufs[left].shape[1], bufs[right].shape[1]
            count = lines[left]
            group = TILE // (2 * count)
            tall, wide = rows // TILE, cols // width
            chunks = [
                (n, start, size, bufs[f"send_{term}_{n}"], bufs[f"keep_{term}_{n}"])
                for n, (start, size) in enumerate(chunk_cols(term, cols))
            ]

            def tile(row, col, left=left, right=right, chunks=chunks, group=group, count=count):
                at, to = lanes(row, TILE), lanes(col, width)
                total = dot(bufs[left + "_x"][:, at], bufs[right + "_x"][:, to], 0, 0)
                total += dot(bufs[left][:, at], bufs[right][:, to], 0, 0)
                for _, start, size, send, keep in chunks:
                    first = max(start, col * width)
                    last = min(start + size, (col + 1) * width)
                    if first >= last:
                        continue
                    here = slice(first - col * width, last - col * width)
                    to = slice(first - start, last - start)
                    for g in range(group):
                        even = total[2 * g * count : (2 * g + 1) * count, here]
                        odd = total[(2 * g + 1) * count : (2 * g + 2) * count, here]
                        send[row * group + g, :, to] = jnp.where(low, odd, even).astype(BF16)
                        keep[row * group + g, :, to] = jnp.where(low, even, odd)

            def out_copies(n, at, base, term=term):
                return [
                    pltpu.make_async_copy(
                        bufs[f"{kind}_{term}_{n}"].at[at],
                        stores[f"{kind}_{term}_{n}"].at[at],
                        out_sems.at[base + spot],
                    )
                    for spot, kind in enumerate(("send", "keep"))
                ]

            if tall > 2:
                for part in range(2):

                    def body(n, _, tile=tile, part=part):
                        tile(part * (tall // 2) + n, 0)
                        return _

                    lax.fori_loop(0, tall // 2, body, 0)
                    for n in range(len(chunks)):
                        at = (pl.ds(part * (tall // 2) * group, tall // 2 * group),)
                        copies = out_copies(n, at, base)
                        base += 2
                        leaving += copies
                        for copy in copies:
                            copy.start()
            else:
                for n, start, size, _, _ in chunks:
                    for col in range(start // width, (start + size) // width):
                        for row in range(tall):
                            tile(row, col)
                    copies = out_copies(n, (), base)
                    base += 2
                    leaving += copies
                    for copy in copies:
                        copy.start()
        for copy in leaving:
            copy.wait()

    @pl.when(mine)
    def _():
        held.finish()


def stage(
    name, common, parts, who, slot, loads, stores, carried=None, after=(), terms=(), firsts=None,
    shared=None,
):
    shared = dict(shared or {})
    count = common["count"]
    term_shapes = {}
    for term in terms:
        left, right = TERMS[term]
        shared[left + "_x"] = firsts[left]
        shared[right + "_x"] = firsts[right]
        for n, (_, size) in enumerate(chunk_cols(term, firsts[right].shape[1])):
            block = (count // 2, firsts[left].shape[1] // count, size)
            term_shapes[f"send_{term}_{n}"] = (block, BF16)
            term_shapes[f"keep_{term}_{n}"] = (block, F32)
    loads = dict(loads, **shared)
    carried = carried or {}
    pair = lambda item: item if isinstance(item, tuple) else (item, None)
    width = common["width"]
    span = common["span"]
    hidden = common["hidden"]
    shapes = scratch_shapes_of(span, width, hidden)
    shapes.update({item + "_x": shapes[item] for item in OPERANDS})
    shapes.update(term_shapes)
    stores = dict(stores, **{item: item for item in term_shapes})
    buf_names = []
    for part in parts:
        buf_names += [item for item in USES[part] if item not in buf_names]
    for term in terms:
        named = list(TERMS[term]) + [item + "_x" for item in TERMS[term]]
        named += [item for item in term_shapes if item.split("_", 1)[1].rsplit("_", 1)[0] == term]
        buf_names += [item for item in named if item not in buf_names]
    order = [item for item in buf_names if item in loads]
    sources = [pair(loads[item]) for item in order]
    targets = [(item, *pair(key)) for item, key in stores.items()]
    args = list(common["args"]) + [array for array, _ in sources]
    in_specs = [pl.BlockSpec(memory_space=SMEM)] * 3 + [pl.BlockSpec(memory_space=VMEM)] * 5
    outs, aliases, extra = [], {}, []
    for i, (item, key, row) in enumerate(targets):
        shape, kind = shapes[item]
        if row is not None:
            shape = (common["tokens"],) + shape[1:]
        outs.append(jax.ShapeDtypeStruct(shape, kind))
        if key in carried:
            aliases[len(args) + len(extra)] = i
            extra.append(carried[key])
    extra += list(after)
    args += extra
    in_specs += [pl.BlockSpec(memory_space=ANY)] * (len(args) - len(in_specs))
    plan = (
        order,
        [row for _, row in sources],
        len(extra),
        [item for item, _, _ in targets],
        [row for _, _, row in targets],
        buf_names,
        list(shared),
    )
    lines = {item: shapes[item][0][1] // count for item in OPERANDS}
    results = pl.pallas_call(
        partial(stage_kernel, (span, width, hidden, lines), parts, terms, who, slot, plan),
        out_shape=outs,
        in_specs=in_specs,
        out_specs=[pl.BlockSpec(memory_space=ANY)] * len(outs),
        input_output_aliases=aliases,
        scratch_shapes=[pltpu.VMEM(*shapes[item]) for item in buf_names]
        + [
            pltpu.SemaphoreType.DMA((16,)),
            pltpu.SemaphoreType.DMA((max(len(shared), 1),)),
            pltpu.SemaphoreType.DMA((len(order) + len(targets) + 8,)),
        ],
        cost_estimate=LIGHT,
        compiler_params=pltpu.CompilerParams(vmem_limit_bytes=56 * 1024 * 1024),
        name=name,
    )(*args)
    return {key: value for (_, key, _), value in zip(targets, results)}


def plain_terms(ops, terms, core, count):
    results = {}
    for term in terms:
        left, right = (ops[item] for item in TERMS[term])
        total = dot(left[0], right[0], 0, 0) + dot(left[1], right[1], 0, 0)
        view = total.reshape((count // 2, 2, -1, total.shape[1]))
        own = lax.dynamic_index_in_dim(view, core, 1, keepdims=False)
        other = lax.dynamic_index_in_dim(view, 1 - core, 1, keepdims=False)
        for n, (start, size) in enumerate(chunk_cols(term, total.shape[1])):
            results[f"send_{term}_{n}"] = other[..., start : start + size].astype(BF16)
            results[f"keep_{term}_{n}"] = own[..., start : start + size]
    return results


def bits_of(count):
    bits = count.bit_length() - 1
    assert 1 << bits == count
    return bits


class Chunk:
    def __init__(self, axis, terms):
        self.axis = axis
        self.count = 2 * terms[0].shape[0]
        self.left = list(range(bits_of(self.count) - 1, 0, -1))
        self.terms = []
        for term in terms:
            self.add(term)

    def add(self, term):
        self.terms.append(term.reshape((2,) * len(self.left) + term.shape[-2:]))

    def split(self, bit):
        spot = self.left.index(bit)
        own = (lax.axis_index(self.axis) >> bit) & 1
        cut = lambda item, at: lax.dynamic_index_in_dim(item, at, spot, keepdims=False)
        send = sum(cut(term, 1 - own).astype(F32) for term in self.terms).astype(BF16)
        self.terms = [cut(term, own) for term in self.terms]
        self.left.remove(bit)
        return send

    def total(self):
        return sum(term.astype(F32) for term in self.terms)


def exchange(block, axis, bit):
    count = lax.axis_size(axis)
    return lax.ppermute(block, axis, [(i, i ^ (1 << bit)) for i in range(count)])


def join(*items):
    return lax.optimization_barrier(items)


def angle_table(span):
    half = HEAD // 2
    freqs = np.exp(-math.log(10000.0) * np.arange(half, dtype=np.float32) / half)
    phase = np.arange(span, dtype=np.float32)[:, None] * freqs.astype(np.float32)[None, :]
    cos_part, sin_part = np.cos(phase), np.sin(phase)
    return np.stack(
        [
            np.concatenate([cos_part] * 4, axis=1),
            np.concatenate([-sin_part, sin_part] * 2, axis=1),
        ]
    ).astype(np.float32)


def per_device(
    ends_in,
    lengths,
    times,
    norm_gain,
    attend_in,
    attend_out,
    time_weight,
    time_bias,
    expand_weight,
    expand_bias,
    reduce_weight,
    reduce_bias,
):
    local = ends_in[0]
    micro = lengths.shape[1]
    assert micro == 2
    width = local.shape[1]
    span = local.shape[0] // micro
    hidden = expand_weight.shape[2]
    count = lax.axis_size("rep")
    section = lax.axis_index("section")
    core = lax.axis_index("rep") & 1
    steps = jnp.exp(-math.log(10000.0) * jnp.arange(EMB // 2, dtype=F32) / (EMB // 2))
    turn = times.reshape(micro * SEGS, 1).astype(F32) * steps
    embed = jnp.concatenate([jnp.cos(turn), jnp.sin(turn)], axis=1)
    mods = jnp.dot(
        embed, time_weight[0].astype(F32), precision=lax.Precision.HIGHEST
    ) + time_bias.astype(F32)
    trig = jnp.asarray(angle_table(span))
    common = dict(
        args=(
            lengths[0],
            section.reshape(1),
            core.reshape(1),
            mods,
            trig,
            norm_gain,
            expand_bias,
            reduce_bias,
        ),
        width=width,
        span=span,
        hidden=hidden,
        tokens=local.shape[0],
        count=count,
    )
    weights = dict(zip(BIG, (attend_in[0], attend_out[0], expand_weight[0], reduce_weight[0])))
    rows = [(local, slot * span) for slot in range(micro)]
    back = ("output", "mlp", "attend")
    whole = {key: key for key in OPERANDS + SMALLS}
    run = partial(stage, common=common)
    a = run(
        "first_0",
        parts=("forward",),
        who=0,
        slot=0,
        loads=dict(xv=rows[0], **weights),
        stores=dict(result="result"),
    )
    came_0 = lax.ppermute(a["result"], "section", [(0, 1)])
    b = run(
        "first_1",
        parts=("forward",),
        who=0,
        slot=1,
        loads=dict(xv=rows[1], **weights),
        stores={key: key for key in ("result",) + OPERANDS[:4] + KEPT},
        after=(a["result"],),
    )
    came_1 = lax.ppermute(b["result"], "section", [(0, 1)])
    x = run(
        "second_0",
        parts=("forward",) + back,
        who=1,
        slot=0,
        loads=dict(xv=came_0, dyv=rows[0], **weights),
        stores=dict(result=("ends", 0), leave="leave", **whole),
        after=(b["result"],),
    )
    back_0 = lax.ppermute(x["leave"], "section", [(1, 0)])
    y = run(
        "second_1",
        parts=("forward",) + back,
        who=1,
        slot=1,
        loads=dict(xv=came_1, dyv=rows[1], **weights),
        stores=dict(result=("ends", span), leave="leave", **whole),
        carried=dict(ends=x["ends"], **{key: b[key] for key in OPERANDS[:4]}),
        after=(x["leave"],),
    )
    back_1 = lax.ppermute(y["leave"], "section", [(1, 0)])
    x = run(
        "back_0",
        parts=("forward",) + back,
        who=0,
        slot=0,
        loads=dict(xv=rows[0], dyv=back_0, **weights),
        stores=dict(leave=("ends", 0), **whole),
        carried=dict(ends=y["ends"], **{key: x[key] for key in OPERANDS + SMALLS}),
        after=(y["leave"],),
    )
    fused = width // count % 16 == 0 and TILE % (2 * hidden // count) == 0

    def last(name, part, loads, stores, terms, shared, ends=None, after=()):
        carried = dict(y) if ends is None else dict(y, ends=ends)
        made = run(
            name,
            parts=(part,),
            who=0,
            slot=1,
            loads=loads,
            stores=stores,
            carried=carried,
            after=after,
            terms=terms if fused else (),
            firsts=x,
            shared=shared if fused else None,
        )
        y.update(made)
        if not fused:
            used = [item for term in terms for item in TERMS[term]]
            y.update(plain_terms({item: (x[item], y[item]) for item in used}, terms, core, count))

    last(
        "back_1_out",
        "output",
        dict(dyv=back_1, branch=b["branch"]),
        dict(bgrad="bgrad", small_out="small_out"),
        ("reduce",),
        dict(active=y["active"]),
    )
    half = width // 2
    came_1 = exchange(y["send_reduce_0"], "rep", 0)
    came_2 = exchange(y["send_reduce_1"], "rep", 0)
    r1 = Chunk("rep", [y["keep_reduce_0"], came_1])
    r2 = Chunk("rep", [y["keep_reduce_1"], came_2])
    send_1, send_2 = r1.split(1), r2.split(2)
    came_1, came_2 = exchange(send_1, "rep", 1), exchange(send_2, "rep", 2)
    last(
        "back_1_mlp",
        "mlp",
        dict(
            wre=weights["wre"],
            bgrad=y["bgrad"],
            slope=b["slope"],
            wex=weights["wex"],
            middle=b["middle"],
            dyv=back_1,
        ),
        dict(pgrad="pgrad", agrad="agrad", middle_grad="middle_grad", small_mlp="small_mlp"),
        ("expand",),
        dict(modded=y["modded"]),
        after=(send_1, send_2),
    )
    came_1, came_2, *sent = join(
        came_1, came_2, *[y[f"send_expand_{n}"] for n in range(3)]
    )
    came = [exchange(item, "rep", 0) for item in sent]
    r1.add(came_1)
    r2.add(came_2)
    send_1, send_2 = r1.split(2), r2.split(1)
    came_r1, came_r2 = exchange(send_1, "rep", 2), exchange(send_2, "rep", 1)
    *came, _, _ = join(*came, send_1, send_2)
    e1, e2, e3 = (Chunk("rep", [y[f"keep_expand_{n}"], came[n]]) for n in range(3))
    send_1, send_2, send_3 = e1.split(1), e2.split(1), e3.split(2)
    came_e1, came_e3 = exchange(send_1, "rep", 1), exchange(send_3, "rep", 2)
    last(
        "back_1_attend",
        "attend",
        dict(
            wout=weights["wout"],
            agrad=y["agrad"],
            probs=b["probs"],
            qkv=b["qkv"],
            win=weights["win"],
            xv=rows[1],
            middle_grad=y["middle_grad"],
        ),
        dict(jgrad="jgrad", leave=("ends", span), small_in="small_in"),
        ("attend_in", "attend_out"),
        dict(normed=y["normed"], mixed=y["mixed"]),
        ends=x["ends"],
        after=(send_1, send_2, send_3),
    )
    ends = y["ends"]
    seqs = []
    for item in (x, y):
        seqs.append(
            jnp.concatenate(
                [item["small_mlp"][SEGS:, : 2 * width], item["small_out"][SEGS:]], axis=1
            )
        )
    seq = jnp.concatenate(seqs)
    grad_t = lax.dot_general(
        embed, seq, (((0,), (0,)), ((), ())), precision=lax.Precision.HIGHEST
    )
    pieces = [
        x["small_in"][0] + y["small_in"][0],
        jnp.sum(seq, axis=0),
        x["small_mlp"][0] + y["small_mlp"][0],
        x["small_out"][0] + y["small_out"][0],
    ]
    line = jnp.concatenate([piece.reshape(count, -1) for piece in pieces], 1)
    cuts = [piece.shape[0] // count for piece in pieces]
    deep = EMB // count
    line = jnp.pad(line, ((0, 0), (0, width - line.shape[1])))
    flat = jnp.pad(line[:, None], ((0, 0), (0, 7), (0, 0)))
    grad_t = grad_t.reshape(count, deep, 3 * width)
    tail = jnp.concatenate(
        [grad_t[..., n * width : (n + 1) * width] for n in range(3)] + [flat], axis=1
    )
    tail = tail.reshape((count // 2, 2) + tail.shape[1:])
    came_r1, came_r2, came_e1, came_e3, send_i, send_o = join(
        came_r1, came_r2, came_e1, came_e3, y["send_attend_in_0"], y["send_attend_out_0"]
    )
    came_i = exchange(send_i, "rep", 0)
    send_2, _ = join(send_2, send_i)
    came_e2 = exchange(send_2, "rep", 1)
    send_o = jnp.concatenate(
        [
            send_o,
            lax.dynamic_index_in_dim(tail, 1 - core, 1, keepdims=False).astype(BF16),
        ],
        axis=1,
    )
    keep_o = jnp.concatenate(
        [y["keep_attend_out_0"], lax.dynamic_index_in_dim(tail, core, 1, keepdims=False)], axis=1
    )
    came_o = exchange(send_o, "rep", 0)
    r1.add(came_r1)
    r2.add(came_r2)
    bits = bits_of(count)

    block_r = jnp.concatenate([r1.split(3), r2.split(3)], axis=-1)
    came_r = exchange(block_r, "rep", 3)
    e1.add(came_e1)
    e3.add(came_e3)
    send_1, send_3 = e1.split(2), e3.split(1)
    came_e1, came_e3 = exchange(send_1, "rep", 2), exchange(send_3, "rep", 1)
    came_i, _, _, _ = join(came_i, block_r, send_1, send_3)
    i1 = Chunk("rep", [y["keep_attend_in_0"], came_i])
    send_i = i1.split(1)
    came_i = exchange(send_i, "rep", 1)
    came_o, _ = join(came_o, send_i)
    o1 = Chunk("rep", [keep_o, came_o])
    send_o = o1.split(2)
    came_o = exchange(send_o, "rep", 2)
    came_e1, came_e2, came_e3, _ = join(came_e1, came_e2, came_e3, send_o)
    e1.add(came_e1)
    e2.add(came_e2)
    e3.add(came_e3)
    send_2 = e2.split(2)
    came_e2 = exchange(send_2, "rep", 2)
    came_r, _ = join(came_r, send_2)
    r1.add(came_r[..., :half])
    r2.add(came_r[..., half:])
    came_e2, _ = join(came_e2, came_r)
    e2.add(came_e2)
    block_e = jnp.concatenate([e1.split(3), e2.split(3), e3.split(3)], axis=-1)
    came_e = exchange(block_e, "rep", 3)
    came_o, _ = join(came_o, block_e)
    o1.add(came_o)
    send_o = o1.split(1)
    came_o = exchange(send_o, "rep", 1)
    came_i, _ = join(came_i, send_o)
    i1.add(came_i)
    send_i = i1.split(2)
    came_i = exchange(send_i, "rep", 2)
    came_e, _ = join(came_e, send_i)
    for chunk, (start, size) in zip((e1, e2, e3), chunk_cols("expand", hidden)):
        chunk.add(came_e[..., start : start + size])
    came_o, came_i = join(came_o, came_i)
    o1.add(came_o)
    i1.add(came_i)
    send_i, send_o = i1.split(3), o1.split(3)
    came_i, came_o = exchange(send_i, "rep", 3), exchange(send_o, "rep", 3)
    i1.add(came_i)
    o1.add(came_o)
    for bit in range(4, bits):
        for chunk in (r1, r2, e1, e2, e3, i1, o1):
            chunk.add(exchange(chunk.split(bit), "rep", bit))
    share_r = jnp.concatenate([r1.total(), r2.total()], axis=1)
    share_e = jnp.concatenate([e1.total(), e2.total(), e3.total()], axis=1)
    share_i = i1.total()
    share_o = o1.total()
    deep_o = width // count
    share_w = jnp.concatenate(
        [share_o[deep_o + n * deep : deep_o + (n + 1) * deep] for n in range(3)], axis=1
    )
    share_s = share_o[deep_o + 3 * deep]
    share_o = share_o[:deep_o]
    spots = [sum(cuts[:n]) for n in range(5)]
    share_gain, share_tb, share_eb, share_rb = (share_s[spots[n] : spots[n + 1]] for n in range(4))
    results = (
        share_gain,
        share_i,
        share_o,
        share_w,
        share_tb,
        share_e,
        share_eb,
        share_r,
        share_rb,
    )
    return (ends[None],) + tuple(piece[None] for piece in results)


def solution(mesh):
    return jax.shard_map(
        per_device,
        mesh=mesh,
        in_specs=(
            P("section", "rep", None),
            P("rep", None, None),
            P("rep", None, None),
            P("section", None),
            P("section", None, None),
            P("section", None, None),
            P("section", None, None),
            P("section", None),
            P("section", None, None),
            P("section", None),
            P("section", None, None),
            P("section", None),
        ),
        out_specs=(
            P("section", "rep", None),
            P("section", "rep"),
            P("section", "rep", None),
            P("section", "rep", None),
            P("section", "rep", None),
            P("section", "rep"),
            P("section", "rep", None),
            P("section", "rep"),
            P("section", "rep", None),
            P("section", "rep"),
        ),
        check_vma=False,
    )
```

```python
from functools import partial
import inspect
import math

import jax
import jax.numpy as jnp
import numpy as np
from jax import lax
from jax.experimental import pallas as pl
from jax.experimental.pallas import tpu as pltpu
from jax.sharding import PartitionSpec as P

HEADS = 12
HEAD = 64
EMB = 128
SEGS = 4
ANY = pl.ANY
VMEM = pltpu.MemorySpace.VMEM
SMEM = pltpu.MemorySpace.SMEM
F32 = jnp.float32
BF16 = jnp.bfloat16
ROOT_HALF = 0.7071067811865476
ROOT_TAU = 0.3989422804014327
TILE = 384
SMALL_ROWS = 24


class Bag(dict):
    __getattr__ = dict.__getitem__


def dot(left, right, left_dim=1, right_dim=0):
    return lax.dot_general(
        left, right, (((left_dim,), (right_dim,)), ((), ())), preferred_element_type=F32
    )


def repeat(count, body):
    for i in range(count):
        body(i)


def steps_of(count, size, body):
    def several(i, _):
        for j in range(size):
            body(size * i + j)
        return _

    lax.fori_loop(0, count // size, several, 0)


def lanes(index, size, start=0):
    if isinstance(index, int):
        return slice(start + index * size, start + (index + 1) * size)
    return pl.ds(pl.multiple_of(start + index * size, size), size)


def swap_halves(values, low_half):
    forth = pltpu.roll(values, 128 - HEAD // 2, 1)
    back = pltpu.roll(values, HEAD // 2, 1)
    return jnp.where(low_half, forth, back)


def norm_parts(values):
    center = values - jnp.mean(values, axis=-1, keepdims=True)
    spread = jnp.mean(center * center, axis=-1, keepdims=True)
    factor = lax.rsqrt(spread + 1e-05)
    return center * factor, factor


def norm_back(grad, unit, factor):
    return factor * (
        grad
        - jnp.mean(grad, axis=-1, keepdims=True)
        - unit * jnp.mean(grad * unit, axis=-1, keepdims=True)
    )


class Held:
    def __init__(self, bufs, loads, stores, sems):
        self.bufs = bufs
        self.loads = loads
        self.stores = stores
        self.sems = sems
        self.names = {id(buf): name for name, buf in bufs.items()}
        self.spots = {name: n for n, name in enumerate(loads)}
        self.pending = set(loads)
        self.leaving = {}

    def load(self, name):
        return pltpu.make_async_copy(
            self.loads[name], self.bufs[name], self.sems.at[self.spots[name]]
        )

    def store(self, name):
        return pltpu.make_async_copy(
            self.bufs[name], self.stores[name], self.sems.at[self.leaving[name]]
        )

    def start(self):
        for name in self.loads:
            self.load(name).start()

    def need(self, *bufs):
        for buf in bufs:
            name = self.names[id(buf)]
            if name in self.pending:
                self.pending.remove(name)
                self.load(name).wait()

    def done(self, *bufs):
        for buf in bufs:
            name = self.names[id(buf)]
            if name in self.stores:
                self.leaving[name] = len(self.loads) + len(self.leaving)
                self.store(name).start()

    def finish(self):
        for name in self.leaving:
            self.store(name).wait()


class Layer:
    def __init__(self, sizes, slot, refs):
        self.span, self.width, self.hidden, self.count = sizes
        self.slot = slot
        (
            lengths, section, core, self.mods, self.trig, self.embed, self.gain, self.ebias,
            self.rbias,
        ) = refs
        self.section = section[0]
        self.low = core[0] == 0
        self.single = lengths[slot, 0] == self.span
        self.pairs = self.width // 128
        self.seg = self.span // SEGS
        self.step = 1024
        self.tiles = self.hidden // self.step
        place = lax.broadcasted_iota(jnp.int32, (self.span, 128), 1)
        self.low_half = place % HEAD < HEAD // 2
        self.low_head = place < HEAD
        row = lax.broadcasted_iota(jnp.int32, (1, 128), 1) // HEAD
        self.head_row = [(row == i).astype(F32).astype(BF16) for i in range(2)]
        self.blocks = [(b, slice(b * self.seg, (b + 1) * self.seg)) for b in range(SEGS)]

    def trig_pair(self):
        cos_all, sin_all = self.trig[0], self.trig[1]
        cos_cut = jnp.concatenate([cos_all[: self.seg]] * SEGS, axis=0)
        sin_cut = jnp.concatenate([sin_all[: self.seg]] * SEGS, axis=0)
        return jnp.where(self.single, cos_all, cos_cut), jnp.where(self.single, sin_all, sin_cut)

    def mod_row(self, block, part):
        row = self.slot * SEGS + jnp.where(self.single, 0, block)
        return self.mods[pl.ds(row, 1), part * self.width : (part + 1) * self.width]

    def add_segment(self, small, block, at, sums):
        row = 8 + jnp.where(self.single, 0, block)
        small[pl.ds(row, 1), at * self.width : (at + 1) * self.width] += sums

    def thirds(self, index):
        return [lanes(index, 128, p * self.width) for p in range(3)]


def forward(
    k, xv, win, wout, wex, wre, normed, qkv, probs, mixed, middle, modded, slope, active, branch,
    result, bias,
):
    span, width, held = k.span, k.width, k.held
    held.need(xv)
    unit, _ = norm_parts(xv[...].astype(F32))
    normed[...] = (unit * k.gain[...].astype(F32)).astype(BF16)
    held.done(normed)
    across = lax.broadcasted_iota(jnp.int32, (span, span), 0) // k.seg
    down = lax.broadcasted_iota(jnp.int32, (span, span), 1) // k.seg
    bias[...] = jnp.where((across == down) | k.single, 0.0, -1e30)
    held.need(win)
    cos_part, sin_part = k.trig_pair()
    for tile, factor in ((0, 0.125), (1, 1.0)):
        for i in range(width // 256):
            at = lanes(i, 256, tile * width)
            joint = dot(normed[...], win[:, at])
            outs = []
            for piece in (joint[:, :128], joint[:, 128:]):
                turned = piece * cos_part + swap_halves(piece, k.low_half) * sin_part
                outs.append((turned * factor).astype(BF16))
            qkv[:, at] = jnp.concatenate(outs, axis=1)
    qkv[:, 2 * width :] = dot(normed[...], win[:, 2 * width :]).astype(BF16)
    held.done(qkv)

    def heads(i):
        at = k.thirds(i)
        query, key, value = (qkv[:, a] for a in at)
        outs = []
        for h in range(2):
            scores = dot(key * k.head_row[h], query, 1, 1) + bias[...]
            top = jnp.max(scores, axis=0, keepdims=True)
            raised = jnp.exp(scores - top)
            total = jnp.sum(raised, axis=0, keepdims=True)
            prob = raised * (1.0 / total)
            probs[2 * i + h] = prob
            outs.append(dot(prob.astype(BF16), value, 0, 0))
        mixed[:, at[0]] = jnp.where(k.low_head, outs[0], outs[1]).astype(BF16)

    steps_of(k.pairs, 3, heads)
    held.done(probs, mixed)
    held.need(wout)
    middle[...] = xv[...].astype(F32) + dot(mixed[...], wout[...])
    held.done(middle)
    for b, rows in k.blocks:
        unit, _ = norm_parts(middle[rows])
        modded[rows] = (unit * (1.0 + k.mod_row(b, 0)) + k.mod_row(b, 1)).astype(BF16)
    held.done(modded)
    held.need(wex, wre)
    branch[...] = jnp.broadcast_to(k.rbias[...].astype(F32), (span, width))

    def feed(j):
        at = lanes(j, k.step)
        pre = dot(modded[...], wex[:, at]) + k.ebias[:, at].astype(F32)
        area = 0.5 + 0.5 * lax.erf(pre * ROOT_HALF)
        out = (pre * area).astype(BF16)
        slope[:, at] = area + pre * (jnp.exp(pre * pre * -0.5) * ROOT_TAU)
        active[:, at] = out
        branch[...] += dot(out, wre[at, :])

    repeat(k.tiles, feed)
    held.done(slope, active, branch)
    for b, rows in k.blocks:
        result[rows] = (middle[rows] + k.mod_row(b, 2) * branch[rows]).astype(BF16)
    held.done(result)


def output(k, dyv, bgrad):
    k.held.need(dyv)
    for b, rows in k.blocks:
        bgrad[rows] = (dyv[rows].astype(F32) * k.mod_row(b, 2)).astype(BF16)
    k.held.done(bgrad)


def mlp(k, wre, wex, bgrad, slope, middle, branch, dyv, pgrad, agrad, middle_grad, small_m, acc):
    width, held = k.width, k.held
    small_m[...] = jnp.zeros(small_m.shape, F32)
    acc[...] = jnp.zeros(acc.shape, F32)
    held.need(bgrad, wre, slope, wex)

    def feed(j):
        at = lanes(j, k.step)
        grad = dot(bgrad[...], wre[at, :], 1, 1).astype(BF16).astype(F32)
        pre_grad = (slope[:, at] * grad).astype(BF16)
        pgrad[:, at] = pre_grad
        small_m[0:1, at] = jnp.sum(pre_grad.astype(F32), axis=0, keepdims=True)
        acc[...] += dot(pre_grad, wex[:, at], 1, 1)

    repeat(k.tiles, feed)
    held.done(pgrad)
    held.need(middle, dyv, branch)
    total = jnp.zeros((1, width), F32)
    for b, rows in k.blocks:
        cotan = dyv[rows].astype(F32)
        total += jnp.sum(bgrad[rows].astype(F32), axis=0, keepdims=True)
        grad = acc[rows].astype(BF16).astype(F32)
        unit, factor = norm_parts(middle[rows])
        k.add_segment(small_m, b, 0, jnp.sum(grad * unit, axis=0, keepdims=True))
        k.add_segment(small_m, b, 1, jnp.sum(grad, axis=0, keepdims=True))
        k.add_segment(small_m, b, 2, jnp.sum(cotan * branch[rows], axis=0, keepdims=True))
        back = norm_back(grad * (1.0 + k.mod_row(b, 0)), unit, factor)
        full = cotan + back
        middle_grad[rows] = full
        agrad[rows] = full.astype(BF16)
    small_m[1:2, :width] = total
    held.done(agrad, middle_grad, small_m)


def attend(
    k, wout, win, agrad, probs, qkv, xv, middle_grad, jgrad, leave, small_a, mixed_grad, acc
):
    held = k.held
    held.need(agrad, wout)
    mixed_grad[...] = dot(agrad[...], wout[...], 1, 1).astype(BF16)
    held.need(probs, qkv)
    cos_part, sin_part = k.trig_pair()

    def heads(i):
        at = k.thirds(i)
        query, key, value = (qkv[:, a] for a in at)
        out_grad = mixed_grad[:, at[0]]
        parts = []
        for h in range(2):
            prob = probs[2 * i + h]
            pull = dot(value * k.head_row[h], out_grad, 1, 1).astype(BF16).astype(F32)
            shared = jnp.sum(prob * pull, axis=0, keepdims=True)
            score_grad = (prob * (pull - shared)).astype(BF16)
            parts.append(
                (
                    dot(score_grad, key, 0, 0),
                    dot(score_grad, query),
                    dot(prob.astype(BF16), out_grad),
                )
            )
        for p in range(3):
            grad = jnp.where(k.low_head, parts[0][p], parts[1][p])
            if p < 2:
                grad = grad.astype(BF16).astype(F32)
                grad = grad * cos_part - swap_halves(grad, k.low_half) * sin_part
                if p == 0:
                    grad = grad * 0.125
            jgrad[:, at[p]] = grad.astype(BF16)

    steps_of(k.pairs, 3, heads)
    held.done(jgrad)
    held.need(win, xv, middle_grad)
    acc[...] = dot(jgrad[...], win[...], 1, 1)
    small_a[...] = jnp.zeros(small_a.shape, F32)
    total = jnp.zeros((1, k.width), F32)
    for b, rows in k.blocks:
        grad = acc[rows].astype(BF16).astype(F32)
        unit, factor = norm_parts(xv[rows].astype(F32))
        total += jnp.sum(grad * unit, axis=0, keepdims=True)
        back = norm_back(grad * k.gain[...].astype(F32), unit, factor)
        leave[rows] = (middle_grad[rows] + back).astype(BF16)
    small_a[0:1, :] = total
    held.done(leave, small_a)


def term_tile(k, left, right, row, col):
    at, to = lanes(row, TILE), lanes(col, k.width)
    return sum(dot(a[:, at], b[:, to], 0, 0) for a, b in zip(left, right))


def put_pairs(k, total, lines, send, keep, first, at):
    for g in range(total.shape[0] // (2 * lines)):
        even = total[2 * g * lines : (2 * g + 1) * lines]
        odd = total[(2 * g + 1) * lines : (2 * g + 2) * lines]
        send[first + g, at] = jnp.where(k.low, odd, even).astype(BF16)
        keep[first + g, at] = jnp.where(k.low, even, odd)


def term_reduce(k, active_x, bgrad_x, active, bgrad, send_r, keep_r):
    lines = k.hidden // k.count
    group = TILE // (2 * lines)

    def row(i):
        total = term_tile(k, (active_x, active), (bgrad_x, bgrad), i, 0)
        put_pairs(k, total, lines, send_r, keep_r, i * group, slice(None))

    steps_of(k.hidden // TILE, 2, row)
    k.held.done(send_r, keep_r)


def term_expand(k, modded_x, pgrad_x, modded, pgrad, send_e, keep_e):
    lines = k.width // k.count
    group = TILE // (2 * lines)
    for col in range(k.hidden // k.width):
        at = slice(col * lines, (col + 1) * lines)
        for row in range(k.width // TILE):
            total = term_tile(k, (modded_x, modded), (pgrad_x, pgrad), row, col)
            put_pairs(k, total, lines, send_e, keep_e, row * group, at)
    k.held.done(send_e, keep_e)


def term_attend(
    k, normed_x, jgrad_x, mixed_x, agrad_x, small_m_x, small_a_x, normed, mixed, agrad, jgrad,
    small_m, small_a, send_a, keep_a, lines_v,
):
    width = k.width
    lines = width // k.count
    group = TILE // (2 * lines)
    pairs = [((normed_x, normed), (jgrad_x, jgrad), col) for col in range(3)]
    pairs.append(((mixed_x, mixed), (agrad_x, agrad), 0))
    for part, (left, right, col) in enumerate(pairs):
        at = slice(part * lines, (part + 1) * lines)
        for row in range(width // TILE):
            total = term_tile(k, left, right, row, col)
            put_pairs(k, total, lines, send_a, keep_a, row * group, at)
    seqs = [item[8 : 8 + SEGS, : 3 * width] for item in (small_m_x, small_m)]
    times = sum(
        k.embed[:, n * SEGS + s : n * SEGS + s + 1] * seqs[n][s : s + 1]
        for n in range(2)
        for s in range(SEGS)
    )
    lines_v[...] = jnp.zeros(lines_v.shape, F32)
    lines_v[0:1] = small_a_x[0:1] + small_a[0:1]
    lines_v[1:2] = small_m_x[1:2, :width] + small_m[1:2, :width]
    bias_sum = jnp.sum(seqs[0] + seqs[1], axis=0, keepdims=True)
    for n in range(3):
        lines_v[2 + n : 3 + n] = bias_sum[:, n * width : (n + 1) * width]
    hidden_sum = small_m_x[0:1] + small_m[0:1]
    for n in range(k.hidden // width):
        lines_v[5 + n : 6 + n] = hidden_sum[:, n * width : (n + 1) * width]
    deep = EMB // k.count
    at = slice(4 * lines, 4 * lines + 3 * deep + SMALL_ROWS)
    for g in range(k.count // 2):
        even, odd = (
            jnp.concatenate(
                [
                    times[(2 * g + n) * deep : (2 * g + n + 1) * deep, p * width : (p + 1) * width]
                    for p in range(3)
                ]
                + [lines_v[...]],
                axis=0,
            )
            for n in range(2)
        )
        send_a[g, at] = jnp.where(k.low, odd, even).astype(BF16)
        keep_a[g, at] = jnp.where(k.low, even, odd)
    k.held.done(send_a, keep_a)


def plain_pieces(ops, count):
    def blocks(left, right):
        total = sum(dot(a, b, 0, 0) for a, b in zip(left, right))
        width = ops.bgrad[0].shape[1]
        parts = [total[:, i : i + width] for i in range(0, total.shape[1], width)]
        return [part.reshape(count, -1, width) for part in parts]

    reduce = blocks(ops.active, ops.bgrad)
    expand = blocks(ops.modded, ops.pgrad)
    both = blocks(ops.normed, ops.jgrad) + blocks(ops.mixed, ops.agrad)
    width = ops.bgrad[0].shape[1]
    seqs = jnp.concatenate([item[8 : 8 + SEGS, : 3 * width] for item in ops.small_m])
    times = jnp.dot(ops.embed, seqs, precision=lax.Precision.HIGHEST)
    both += [times[:, i * width : (i + 1) * width].reshape(count, -1, width) for i in range(3)]
    lines = jnp.concatenate(
        [
            sum(item[0:1] for item in ops.small_a),
            sum(item[1:2, :width] for item in ops.small_m),
            jnp.sum(seqs, axis=0).reshape(-1, width),
            sum(item[0] for item in ops.small_m).reshape(-1, width),
        ]
    )
    lines = jnp.pad(lines, ((0, SMALL_ROWS - lines.shape[0]), (0, 0)))
    both.append(jnp.broadcast_to(lines, (count,) + lines.shape))
    return [jnp.concatenate(item, axis=1) for item in (reduce, expand, both)]


def shapes_of(span, width, hidden, count):
    tok = lambda cols, kind=BF16: ((span, cols), kind)
    shapes = dict(
        xv=tok(width),
        dyv=tok(width),
        win=((width, 3 * width), BF16),
        wout=((width, width), BF16),
        wex=((width, hidden), BF16),
        wre=((hidden, width), BF16),
        normed=tok(width),
        qkv=tok(3 * width),
        probs=((HEADS, span, span), F32),
        mixed=tok(width),
        middle=tok(width, F32),
        modded=tok(width),
        slope=tok(hidden, F32),
        active=tok(hidden),
        branch=tok(width, F32),
        result=tok(width),
        bgrad=tok(width),
        pgrad=tok(hidden),
        agrad=tok(width),
        jgrad=tok(3 * width),
        mixed_grad=tok(width),
        middle_grad=tok(width, F32),
        leave=tok(width),
        acc=tok(width, F32),
        bias=tok(span, F32),
        small_m=((16, hidden), F32),
        small_a=((8, width), F32),
        lines_v=((SMALL_ROWS, width), F32),
    )
    shapes.update({item + "_x": shape for item, shape in shapes.items()})
    rows = dict(
        r=hidden // count,
        e=hidden // count,
        a=4 * (width // count) + 3 * (EMB // count) + SMALL_ROWS,
    )
    for item, lines in rows.items():
        shapes["send_" + item] = ((count // 2, lines, width), BF16)
        shapes["keep_" + item] = ((count // 2, lines, width), F32)
    return shapes


def uses(part):
    return list(inspect.signature(part).parameters)[1:]


def stage_kernel(sizes, parts, term, who, slot, plan, *refs):
    refs = list(refs)
    layer = Layer(sizes, slot, refs[:9])
    span = layer.span
    pos = 9
    cut = lambda ref, row: ref if row is None else ref.at[pl.ds(row, span)]
    sources = {}
    for name, row in plan.sources:
        sources[name] = cut(refs[pos], row)
        pos += 1
    pos += plan.extra
    stores = {}
    for name, row in plan.targets:
        stores[name] = cut(refs[pos], row)
        pos += 1
    bufs = {name: sources.pop(name) for name in plan.direct}
    for name in plan.bufs:
        bufs[name] = refs[pos]
        pos += 1
    mine_sems, both_sems, other_sems = refs[pos:]
    mine = layer.section == who
    loads = {name: ref for name, ref in sources.items() if name not in plan.shared}
    held = Held(bufs, loads, stores, mine_sems)
    common = Held(bufs, {name: sources[name] for name in plan.shared}, stores, both_sems)

    @pl.when(mine)
    def _():
        held.start()

    common.start()

    @pl.when(mine)
    def _():
        layer.held = held
        for part in parts:
            part(layer, *[bufs[name] for name in uses(part)])

    if term is not None:
        made = [name for name in uses(term) if name in plan.made]
        there = {name: stores.get(name, sources.get(name)) for name in made}
        other = Held(bufs, there, {}, other_sems)

        @pl.when(jnp.logical_not(mine))
        def _():
            other.start()
            other.need(*[bufs[name] for name in made])

        common.need(*[bufs[name] for name in plan.shared])
        layer.held = common
        term(layer, *[bufs[name] for name in uses(term)])
        common.finish()

    @pl.when(mine)
    def _():
        held.finish()


def stage(
    name, common, parts, who, slot, loads, stores, carried=None, after=(), term=None, firsts=None,
    shared=None,
):
    carried = carried or {}
    shared = dict(shared or {})
    span, width, hidden, count = common.sizes
    shapes = shapes_of(span, width, hidden, count)
    stores = dict(stores)
    if term is not None:
        for item in uses(term):
            if item.endswith("_x"):
                shared[item] = firsts[item[:-2]]
            if item.startswith(("send_", "keep_")):
                stores[item] = item
    loads = dict(loads, **shared)
    bufs = []
    for part in parts + ((term,) if term is not None else ()):
        bufs += [item for item in uses(part) if item not in bufs]
    direct = [item for item in bufs if isinstance(loads.get(item), list)]
    pair = lambda item: item if isinstance(item, tuple) else (item, None)
    args = list(common.args)
    in_specs = [pl.BlockSpec(memory_space=SMEM)] * 3 + [pl.BlockSpec(memory_space=VMEM)] * 6
    plan = Bag(sources=[], targets=[], direct=direct, shared=[], made=[])
    order = [item for item in loads if item in bufs]
    for item in order:
        if item in direct:
            array, row = loads[item][0], None
        else:
            array, row = pair(loads[item])
        args.append(array)
        in_specs.append(pl.BlockSpec(memory_space=VMEM if item in direct else ANY))
        plan.sources.append((item, row))
        if item in shared:
            plan.shared.append(item)
    outs, aliases, extra = [], {}, []
    targets = [(item, *pair(key)) for item, key in stores.items()]
    for i, (item, key, row) in enumerate(targets):
        shape, kind = shapes[item]
        if row is not None:
            shape = (common.tokens,) + shape[1:]
        outs.append(jax.ShapeDtypeStruct(shape, kind))
        plan.targets.append((item, row))
        if key in carried:
            aliases[len(args) + len(extra)] = i
            extra.append(carried[key])
    extra += list(after)
    args += extra
    in_specs += [pl.BlockSpec(memory_space=ANY)] * len(extra)
    plan.update(
        extra=len(extra),
        bufs=[item for item in bufs if item not in direct],
        made=[item for part in parts for item in uses(part)],
    )
    plan["made"] = [item for item in plan.made if item not in shared and item not in direct]
    results = pl.pallas_call(
        partial(stage_kernel, common.sizes, parts, term, who, slot, plan),
        out_shape=outs,
        in_specs=in_specs,
        out_specs=[pl.BlockSpec(memory_space=ANY)] * len(outs),
        input_output_aliases=aliases,
        scratch_shapes=[pltpu.VMEM(*shapes[item]) for item in plan.bufs]
        + [pltpu.SemaphoreType.DMA((n,)) for n in (32, 24, 8)],
        compiler_params=pltpu.CompilerParams(vmem_limit_bytes=56 * 1024 * 1024),
        name=name,
    )(*args)
    return Bag({key: value for (_, key, _), value in zip(targets, results)})


def bits_of(count):
    bits = count.bit_length() - 1
    assert 1 << bits == count
    return bits


class Chunk:
    def __init__(self, axis, terms, rows):
        self.axis = axis
        self.start, self.size = rows
        self.bits = list(range(bits_of(2 * terms[0].shape[0]) - 1, 0, -1))
        self.settled = []
        self.terms = []
        for term in terms:
            self.add(term, self.start)

    def add(self, term, start=0):
        left = [bit for bit in self.bits if bit not in self.settled]
        self.terms.append((term.reshape((2,) * len(left) + term.shape[-2:]), left, start))

    def take(self, term, start, left, flip):
        me = lax.axis_index(self.axis)
        side = lambda bit: 1 - ((me >> bit) & 1) if bit == flip else (me >> bit) & 1
        starts = [side(bit) if bit in self.settled else 0 for bit in left]
        sizes = [1 if bit in self.settled else 2 for bit in left]
        cols = term.shape[-1]
        piece = lax.dynamic_slice(term, starts + [start, 0], sizes + [self.size, cols])
        open_bits = [2] * (len(self.bits) - len(self.settled))
        return piece.reshape(open_bits + [self.size, cols]).astype(F32)

    def split(self, bit):
        self.settled.append(bit)
        return sum(self.take(term, start, left, bit) for term, left, start in self.terms).astype(
            BF16
        )

    def total(self):
        return sum(self.take(term, start, left, None) for term, left, start in self.terms)


def exchange(block, axis, bit):
    count = lax.axis_size(axis)
    return lax.ppermute(block, axis, [(i, i ^ (1 << bit)) for i in range(count)])


def join(*items):
    return lax.optimization_barrier(items)


def angle_table(span):
    half = HEAD // 2
    freqs = np.exp(-math.log(10000.0) * np.arange(half, dtype=np.float32) / half)
    phase = np.arange(span, dtype=np.float32)[:, None] * freqs.astype(np.float32)[None, :]
    cos_part, sin_part = np.cos(phase), np.sin(phase)
    return np.stack(
        [
            np.concatenate([cos_part] * 4, axis=1),
            np.concatenate([-sin_part, sin_part] * 2, axis=1),
        ]
    ).astype(np.float32)


def per_device(
    ends_in,
    lengths,
    times,
    norm_gain,
    attend_in,
    attend_out,
    time_weight,
    time_bias,
    expand_weight,
    expand_bias,
    reduce_weight,
    reduce_bias,
):
    local = ends_in[0]
    micro = lengths.shape[1]
    assert micro == 2
    width = local.shape[1]
    span = local.shape[0] // micro
    hidden = expand_weight.shape[2]
    count = lax.axis_size("rep")
    section = lax.axis_index("section")
    rank = lax.axis_index("rep")
    core = rank & 1
    steps = jnp.exp(-math.log(10000.0) * jnp.arange(EMB // 2, dtype=F32) / (EMB // 2))
    turn = times.reshape(micro * SEGS, 1).astype(F32) * steps
    embed = jnp.concatenate([jnp.cos(turn), jnp.sin(turn)], axis=1)
    mods = jnp.dot(
        embed, time_weight[0].astype(F32), precision=lax.Precision.HIGHEST
    ) + time_bias.astype(F32)
    common = Bag(
        args=(
            lengths[0],
            section.reshape(1),
            core.reshape(1),
            mods,
            jnp.asarray(angle_table(span)),
            embed.T,
            norm_gain,
            expand_bias,
            reduce_bias,
        ),
        sizes=(span, width, hidden, count),
        tokens=local.shape[0],
    )
    weights = Bag(
        win=attend_in[0], wout=attend_out[0], wex=expand_weight[0], wre=reduce_weight[0]
    )
    rows = [(local, slot * span) for slot in range(micro)]
    same = lambda *names: {name: name for name in names}
    whole = {
        name: name
        for part in (term_reduce, term_expand, term_attend)
        for name in uses(part)
        if name + "_x" in uses(part)
    }
    run = partial(stage, common=common)
    both = (forward, output, mlp, attend)
    over = lambda block, route: lax.ppermute(block, "section", route)
    a = run(
        "first_0",
        parts=(forward,),
        who=0,
        slot=0,
        loads=dict(xv=rows[0], **weights),
        stores=dict(result="leave"),
    )
    came_0 = over(a.leave, [(0, 1)])
    held = [item for item in uses(forward) if item not in weights]
    b = run(
        "first_1",
        parts=(forward,),
        who=0,
        slot=1,
        loads=dict(xv=rows[1], **weights),
        stores={item: item for item in held if item not in ("xv", "bias")},
        after=(a.leave,),
    )
    came_1 = over(b.result, [(0, 1)])
    x = run(
        "second_0",
        parts=both,
        who=1,
        slot=0,
        loads=dict(xv=[came_0], dyv=rows[0], **weights),
        stores=dict(whole, result=("ends", 0), leave="leave"),
        after=(b.result,),
    )
    back_0 = over(x.leave, [(1, 0)])
    y = run(
        "second_1",
        parts=both,
        who=1,
        slot=1,
        loads=dict(xv=[came_1], dyv=rows[1], **weights),
        stores=dict(whole, result=("ends", span), leave="leave"),
        carried=dict(b, ends=x.ends),
        after=(x.leave,),
    )
    back_1 = over(y.leave, [(1, 0)])
    x = run(
        "back_0",
        parts=both,
        who=0,
        slot=0,
        loads=dict(xv=rows[0], dyv=[back_0], **weights),
        stores=dict(whole, leave=("ends", 0)),
        carried=dict(x, ends=y.ends),
        after=(y.leave,),
    )
    fused = width // count % 16 == 0 and TILE % (2 * hidden // count) == 0

    def last(name, part, loads, stores, term, shared, after=()):
        y.update(
            run(
                name,
                parts=(part,),
                who=0,
                slot=1,
                loads=loads,
                stores=stores,
                carried=dict(y, ends=x.ends),
                after=after,
                term=term if fused else None,
                firsts=x,
                shared=shared if fused else None,
            )
        )

    last("back_1_out", output, dict(dyv=[back_1]), same("bgrad"), term_reduce, dict(active=y.active))
    last_mlp = partial(
        last,
        "back_1_mlp",
        mlp,
        dict(
            wre=weights.wre,
            bgrad=y.bgrad,
            slope=b.slope,
            wex=weights.wex,
            middle=b.middle,
            branch=b.branch,
            dyv=[back_1],
        ),
        same("pgrad", "agrad", "middle_grad", "small_m"),
        term_expand,
        dict(modded=y.modded),
    )

    def last_attend(after):
        last(
            "back_1_attend",
            attend,
            dict(
                wout=weights.wout,
                agrad=y.agrad,
                probs=b.probs,
                qkv=b.qkv,
                win=weights.win,
                xv=rows[1],
                middle_grad=y.middle_grad,
            ),
            dict(same("jgrad", "small_a"), leave=("ends", span)),
            term_attend,
            dict(normed=y.normed, mixed=y.mixed, small_m=y.small_m),
            after=after,
        )

    if not fused:
        last_mlp()
        last_attend(())
        ops = Bag({item: (x[item], y[item]) for item in whole}, embed=embed.T)
        for item, total in zip("rea", plain_pieces(ops, count)):
            view = total.reshape((count // 2, 2) + total.shape[1:])
            side = lambda at: lax.dynamic_index_in_dim(view, at, 1, keepdims=False)
            y["send_" + item] = side(1 - core).astype(BF16)
            y["keep_" + item] = side(core)
    swap = lambda block, bit: exchange(block, "rep", bit)
    bits = bits_of(count)

    def halves(came, keep, share):
        lines = keep.shape[1]
        cut = lines * share // 100 // 16 * 16
        terms = [keep, came]
        return Chunk("rep", terms, (0, cut)), Chunk("rep", terms, (cut, lines - cut))

    r1, r2 = halves(swap(y.send_r, 0), y.keep_r, 50)
    send_1, send_2 = r1.split(1), r2.split(2)
    came_r1, came_r2 = swap(send_1, 1), swap(send_2, 2)
    if fused:
        last_mlp(after=(send_1, send_2))
    came_r1, came_r2, send_e = join(came_r1, came_r2, y.send_e)
    came_e = swap(send_e, 0)
    r1.add(came_r1)
    r2.add(came_r2)
    send_1, send_2 = r1.split(2), r2.split(1)
    came_r1, came_r2 = swap(send_1, 2), swap(send_2, 1)
    came_e, _, _ = join(came_e, send_1, send_2)
    e1, e2 = halves(came_e, y.keep_e, 50)
    send_1, send_2 = e1.split(1), e2.split(2)
    came_e1, came_e2 = swap(send_1, 1), swap(send_2, 2)
    if fused:
        last_attend((send_1, send_2))
    ends = y.ends
    came_r1, came_r2, came_e1, came_e2, send_a = join(
        came_r1, came_r2, came_e1, came_e2, y.send_a
    )
    came_a = swap(send_a, 0)
    r1.add(came_r1)
    r2.add(came_r2)
    e1.add(came_e1)
    e2.add(came_e2)
    block_r = jnp.concatenate([r1.split(3), r2.split(3)], axis=-2)
    came_r = swap(block_r, 3)
    send_1, send_2 = e1.split(2), e2.split(1)
    came_e1, came_e2 = swap(send_1, 2), swap(send_2, 1)
    came_a, _, _, _ = join(came_a, block_r, send_1, send_2)
    a1, a2 = halves(came_a, y.keep_a, 60)
    send_1, send_2 = a1.split(1), a2.split(2)
    came_a1, came_a2 = swap(send_1, 1), swap(send_2, 2)
    came_e1, came_e2, _, _ = join(came_e1, came_e2, send_1, send_2)
    e1.add(came_e1)
    e2.add(came_e2)
    block_e = jnp.concatenate([e1.split(3), e2.split(3)], axis=-2)
    came_e = swap(block_e, 3)
    came_r, _ = join(came_r, block_e)
    r1.add(came_r[..., : r1.size, :])
    r2.add(came_r[..., r1.size :, :])
    came_a1, came_a2, _ = join(came_a1, came_a2, came_r)
    a1.add(came_a1)
    a2.add(came_a2)
    send_1, send_2 = a1.split(2), a2.split(1)
    came_a1, came_a2 = swap(send_1, 2), swap(send_2, 1)
    came_e, _, _ = join(came_e, send_1, send_2)
    e1.add(came_e[..., : e1.size, :])
    e2.add(came_e[..., e1.size :, :])
    came_a1, came_a2, _ = join(came_a1, came_a2, came_e)
    a1.add(came_a1)
    a2.add(came_a2)
    block_a = jnp.concatenate([a1.split(3), a2.split(3)], axis=-2)
    came_a = swap(block_a, 3)
    a1.add(came_a[..., : a1.size, :])
    a2.add(came_a[..., a1.size :, :])
    for bit in range(4, bits):
        for chunk in (r1, r2, e1, e2, a1, a2):
            chunk.add(swap(chunk.split(bit), bit))
    share_r, share_e, share_a = (
        jnp.concatenate([one.total(), two.total()]) for one, two in ((r1, r2), (e1, e2), (a1, a2))
    )
    lines = width // count
    deep = EMB // count
    side = lambda item, n, size: jnp.concatenate(
        [item[i * size : (i + 1) * size] for i in range(n)], axis=1
    )
    small = share_a[4 * lines + 3 * deep :]
    flat = lambda first, n: lax.dynamic_slice_in_dim(
        small[first : first + n].reshape(-1), rank * (n * width // count), n * width // count
    )
    results = (
        flat(0, 1),
        side(share_a, 3, lines),
        share_a[3 * lines : 4 * lines],
        side(share_a[4 * lines :], 3, deep),
        flat(2, 3),
        side(share_e, hidden // width, lines),
        flat(5, hidden // width),
        share_r,
        flat(1, 1),
    )
    return (ends[None],) + tuple(piece[None] for piece in results)


def solution(mesh):
    return jax.shard_map(
        per_device,
        mesh=mesh,
        in_specs=(
            P("section", "rep", None),
            P("rep", None, None),
            P("rep", None, None),
            P("section", None),
            P("section", None, None),
            P("section", None, None),
            P("section", None, None),
            P("section", None),
            P("section", None, None),
            P("section", None),
            P("section", None, None),
            P("section", None),
        ),
        out_specs=(
            P("section", "rep", None),
            P("section", "rep"),
            P("section", "rep", None),
            P("section", "rep", None),
            P("section", "rep", None),
            P("section", "rep"),
            P("section", "rep", None),
            P("section", "rep"),
            P("section", "rep", None),
            P("section", "rep"),
        ),
        check_vma=False,
    )
```

```python
from functools import partial
import inspect
import math

import jax
import jax.numpy as jnp
import numpy as np
from jax import lax
from jax.experimental import pallas as pl
from jax.experimental.pallas import tpu as pltpu
from jax.sharding import PartitionSpec as P

HEADS = 12
HEAD = 64
EMB = 128
SEGS = 4
ANY = pl.ANY
VMEM = pltpu.MemorySpace.VMEM
SMEM = pltpu.MemorySpace.SMEM
F32 = jnp.float32
BF16 = jnp.bfloat16
ROOT_HALF = 0.7071067811865476
ROOT_TAU = 0.3989422804014327
TILE = 384
SMALL_ROWS = 8
GAIN_ROWS = 16


class Bag(dict):
    __getattr__ = dict.__getitem__


def dot(left, right, left_dim=1, right_dim=0):
    return lax.dot_general(
        left, right, (((left_dim,), (right_dim,)), ((), ())), preferred_element_type=F32
    )


def repeat(count, body):
    for i in range(count):
        body(i)


def steps_of(count, size, body):
    def several(i, _):
        for j in range(size):
            body(size * i + j)
        return _

    lax.fori_loop(0, count // size, several, 0)


def lanes(index, size, start=0):
    if isinstance(index, int):
        return slice(start + index * size, start + (index + 1) * size)
    return pl.ds(pl.multiple_of(start + index * size, size), size)


def swap_halves(values, low_half):
    forth = pltpu.roll(values, 128 - HEAD // 2, 1)
    back = pltpu.roll(values, HEAD // 2, 1)
    return jnp.where(low_half, forth, back)


def norm_parts(values):
    center = values - jnp.mean(values, axis=-1, keepdims=True)
    spread = jnp.mean(center * center, axis=-1, keepdims=True)
    factor = lax.rsqrt(spread + 1e-05)
    return center * factor, factor


def norm_back(grad, unit, factor):
    return factor * (
        grad
        - jnp.mean(grad, axis=-1, keepdims=True)
        - unit * jnp.mean(grad * unit, axis=-1, keepdims=True)
    )


class Held:
    def __init__(self, bufs, loads, stores, sems):
        self.bufs = bufs
        self.loads = loads
        self.stores = stores
        self.sems = sems
        self.names = {id(buf): name for name, buf in bufs.items()}
        self.spots = {name: n for n, name in enumerate(loads)}
        self.pending = set(loads)
        self.waiting = set(loads)
        self.leaving = {}

    def load(self, name):
        return pltpu.make_async_copy(
            self.loads[name], self.bufs[name], self.sems.at[self.spots[name]]
        )

    def store(self, name, at):
        number, _ = self.leaving[(name, at)]
        source, target = self.bufs[name], self.stores[name]
        if at is not None:
            spot = tuple(pl.ds(*item) for item in at)
            source, target = source.at[spot], target.at[spot]
        return pltpu.make_async_copy(source, target, self.sems.at[number])

    def begin(self, *bufs):
        for buf in bufs:
            name = self.names[id(buf)]
            if name in self.waiting:
                self.waiting.remove(name)
                self.load(name).start()

    def begin_all(self):
        self.begin(*[self.bufs[name] for name in self.loads])

    def need(self, *bufs):
        self.begin(*bufs)
        for buf in bufs:
            name = self.names[id(buf)]
            if name in self.pending:
                self.pending.remove(name)
                self.load(name).wait()

    def done(self, *bufs, at=None):
        for buf in bufs:
            name = self.names[id(buf)]
            if name in self.stores:
                self.leaving[(name, at)] = (len(self.loads) + len(self.leaving), at)
                self.store(name, at).start()

    def finish(self):
        for name, at in self.leaving:
            self.store(name, at).wait()


class Layer:
    def __init__(self, sizes, slot, refs):
        self.span, self.width, self.hidden, self.count = sizes
        self.slot = slot
        (
            lengths, section, core, self.mods, self.trig, self.embed, self.gain, self.ebias,
            self.rbias,
        ) = refs
        self.section = section[0]
        self.low = core[0] == 0
        self.single = lengths[slot, 0] == self.span
        self.pairs = self.width // 128
        self.seg = self.span // SEGS
        self.step = 1024
        self.tiles = self.hidden // self.step
        place = lax.broadcasted_iota(jnp.int32, (self.span, 128), 1)
        self.low_half = place % HEAD < HEAD // 2
        self.low_head = place < HEAD
        row = lax.broadcasted_iota(jnp.int32, (1, 128), 1) // HEAD
        self.head_row = [(row == i).astype(F32).astype(BF16) for i in range(2)]
        self.blocks = [(b, slice(b * self.seg, (b + 1) * self.seg)) for b in range(SEGS)]

    def trig_pair(self):
        cos_all, sin_all = self.trig[0], self.trig[1]
        cos_cut = jnp.concatenate([cos_all[: self.seg]] * SEGS, axis=0)
        sin_cut = jnp.concatenate([sin_all[: self.seg]] * SEGS, axis=0)
        return jnp.where(self.single, cos_all, cos_cut), jnp.where(self.single, sin_all, sin_cut)

    def mod_row(self, block, part):
        row = self.slot * SEGS + jnp.where(self.single, 0, block)
        return self.mods[pl.ds(row, 1), part * self.width : (part + 1) * self.width]

    def add_segment(self, small, block, at, sums):
        row = 8 + jnp.where(self.single, 0, block)
        small[pl.ds(row, 1), at * self.width : (at + 1) * self.width] += sums

    def thirds(self, index):
        return [lanes(index, 128, p * self.width) for p in range(3)]


def forward(
    k, xv, win, wout, wex, wre, normed, qkv, probs, mixed, middle, modded, slope, active, branch,
    result, bias,
):
    span, width, held = k.span, k.width, k.held
    held.begin(xv, win)
    held.need(xv)
    unit, _ = norm_parts(xv[...].astype(F32))
    normed[...] = (unit * k.gain[...].astype(F32)).astype(BF16)
    held.done(normed)
    across = lax.broadcasted_iota(jnp.int32, (span, span), 0) // k.seg
    down = lax.broadcasted_iota(jnp.int32, (span, span), 1) // k.seg
    bias[...] = jnp.where((across == down) | k.single, 0.0, -1e30)
    held.need(win)
    held.begin(wout, wex, wre)
    cos_part, sin_part = k.trig_pair()
    for tile, factor in ((0, 0.125), (1, 1.0)):
        for i in range(width // 256):
            at = lanes(i, 256, tile * width)
            joint = dot(normed[...], win[:, at])
            outs = []
            for piece in (joint[:, :128], joint[:, 128:]):
                turned = piece * cos_part + swap_halves(piece, k.low_half) * sin_part
                outs.append((turned * factor).astype(BF16))
            qkv[:, at] = jnp.concatenate(outs, axis=1)
    qkv[:, 2 * width :] = dot(normed[...], win[:, 2 * width :]).astype(BF16)
    held.done(qkv)

    def heads(i):
        at = k.thirds(i)
        query, key, value = (qkv[:, a] for a in at)
        outs = []
        for h in range(2):
            scores = dot(key * k.head_row[h], query, 1, 1) + bias[...]
            top = jnp.max(scores, axis=0, keepdims=True)
            raised = jnp.exp(scores - top)
            total = jnp.sum(raised, axis=0, keepdims=True)
            prob = raised * (1.0 / total)
            probs[2 * i + h] = prob
            outs.append(dot(prob.astype(BF16), value, 0, 0))
        mixed[:, at[0]] = jnp.where(k.low_head, outs[0], outs[1]).astype(BF16)

    steps_of(k.pairs, 3, heads)
    held.done(probs, mixed)
    held.need(wout)
    middle[...] = xv[...].astype(F32) + dot(mixed[...], wout[...])
    held.done(middle)
    for b, rows in k.blocks:
        unit, _ = norm_parts(middle[rows])
        modded[rows] = (unit * (1.0 + k.mod_row(b, 0)) + k.mod_row(b, 1)).astype(BF16)
    held.done(modded)
    held.need(wex, wre)
    branch[...] = jnp.broadcast_to(k.rbias[...].astype(F32), (span, width))

    def feed(j):
        at = lanes(j, k.step)
        pre = dot(modded[...], wex[:, at]) + k.ebias[:, at].astype(F32)
        area = 0.5 + 0.5 * lax.erf(pre * ROOT_HALF)
        out = (pre * area).astype(BF16)
        if k.sloped:
            slope[:, at] = area + pre * (jnp.exp(pre * pre * -0.5) * ROOT_TAU)
        active[:, at] = out
        branch[...] += dot(out, wre[at, :])

    repeat(k.tiles, feed)
    held.done(slope, active, branch)
    for b, rows in k.blocks:
        result[rows] = (middle[rows] + k.mod_row(b, 2) * branch[rows]).astype(BF16)
    held.done(result)


def output(k, dyv, bgrad):
    k.later()
    k.held.need(dyv)
    for b, rows in k.blocks:
        bgrad[rows] = (dyv[rows].astype(F32) * k.mod_row(b, 2)).astype(BF16)
    k.held.done(bgrad)


def mlp(k, wre, wex, bgrad, slope, middle, branch, dyv, pgrad, agrad, middle_grad, small_m, acc):
    width, held = k.width, k.held
    small_m[...] = jnp.zeros(small_m.shape, F32)
    acc[...] = jnp.zeros(acc.shape, F32)
    held.need(bgrad, wre, slope)
    held.begin(wex, middle, dyv, branch)
    k.later()
    held.need(wex)

    def feed(j):
        at = lanes(j, k.step)
        grad = dot(bgrad[...], wre[at, :], 1, 1)
        pre_grad = (slope[:, at] * grad).astype(BF16)
        pgrad[:, at] = pre_grad
        small_m[0:1, at] = jnp.sum(pre_grad.astype(F32), axis=0, keepdims=True)
        acc[...] += dot(pre_grad, wex[:, at], 1, 1)

    repeat(k.tiles, feed)
    held.done(pgrad)
    held.need(middle, dyv, branch)
    total = jnp.zeros((1, width), F32)
    for b, rows in k.blocks:
        cotan = dyv[rows].astype(F32)
        total += jnp.sum(bgrad[rows].astype(F32), axis=0, keepdims=True)
        grad = acc[rows]
        unit, factor = norm_parts(middle[rows])
        k.add_segment(small_m, b, 0, jnp.sum(grad * unit, axis=0, keepdims=True))
        k.add_segment(small_m, b, 1, jnp.sum(grad, axis=0, keepdims=True))
        k.add_segment(small_m, b, 2, jnp.sum(cotan * branch[rows], axis=0, keepdims=True))
        back = norm_back(grad * (1.0 + k.mod_row(b, 0)), unit, factor)
        full = cotan + back
        middle_grad[rows] = full
        agrad[rows] = full.astype(BF16)
    small_m[1:2, :width] = total
    held.done(agrad, middle_grad, small_m)


def attend(
    k, wout, win, agrad, probs, qkv, xv, middle_grad, jgrad, leave, small_a, mixed_grad, acc
):
    held = k.held
    held.need(agrad, wout)
    held.begin(probs, qkv)
    mixed_grad[...] = dot(agrad[...], wout[...], 1, 1).astype(BF16)
    held.need(probs, qkv)
    held.begin(win, xv, middle_grad)
    k.later()
    cos_part, sin_part = k.trig_pair()

    def heads(i):
        at = k.thirds(i)
        query, key, value = (qkv[:, a] for a in at)
        out_grad = mixed_grad[:, at[0]]
        parts = []
        for h in range(2):
            prob = probs[2 * i + h]
            pull = dot(value * k.head_row[h], out_grad, 1, 1)
            shared = jnp.sum(prob * pull, axis=0, keepdims=True)
            score_grad = (prob * (pull - shared)).astype(BF16)
            parts.append(
                (
                    dot(score_grad, key, 0, 0),
                    dot(score_grad, query),
                    dot(prob.astype(BF16), out_grad),
                )
            )
        for p in range(3):
            grad = jnp.where(k.low_head, parts[0][p], parts[1][p])
            if p < 2:
                grad = grad * cos_part - swap_halves(grad, k.low_half) * sin_part
                if p == 0:
                    grad = grad * 0.125
            jgrad[:, at[p]] = grad.astype(BF16)

    steps_of(k.pairs, 3, heads)
    held.done(jgrad)
    held.need(win, xv, middle_grad)
    acc[...] = dot(jgrad[...], win[...], 1, 1)
    small_a[...] = jnp.zeros(small_a.shape, F32)
    total = jnp.zeros((1, k.width), F32)
    for b, rows in k.blocks:
        grad = acc[rows]
        unit, factor = norm_parts(xv[rows].astype(F32))
        total += jnp.sum(grad * unit, axis=0, keepdims=True)
        back = norm_back(grad * k.gain[...].astype(F32), unit, factor)
        leave[rows] = (middle_grad[rows] + back).astype(BF16)
    small_a[0:1, :] = total
    held.done(leave, small_a)


def term_tile(k, left, right, row, col):
    at, to = lanes(row, TILE), lanes(col, k.width)
    return sum(dot(a[:, at], b[:, to], 0, 0) for a, b in zip(left, right))


def put_pairs(k, total, lines, send, keep, first, at):
    for g in range(total.shape[0] // (2 * lines)):
        even = total[2 * g * lines : (2 * g + 1) * lines]
        odd = total[(2 * g + 1) * lines : (2 * g + 2) * lines]
        send[first + g, at] = jnp.where(k.low, odd, even).astype(BF16)
        keep[first + g, at] = jnp.where(k.low, even, odd)


def term_reduce(k, active_x, bgrad_x, active, bgrad, send_r, keep_r):
    lines = k.hidden // k.count
    group = TILE // (2 * lines)
    for row in range(k.hidden // TILE):
        total = term_tile(k, (active_x, active), (bgrad_x, bgrad), row, 0)
        put_pairs(k, total, lines, send_r, keep_r, row * group, slice(None))
        if row % 2:
            k.held.done(send_r, keep_r, at=(((row - 1) * group, 2 * group),))


def square_terms(k, left, right, send, keep, parts):
    lines = k.width // k.count
    group = TILE // (2 * lines)
    for col, part in enumerate(parts):
        for row in range(k.width // TILE):
            total = term_tile(k, left, right, row, col)
            at = slice(part * lines, (part + 1) * lines)
            put_pairs(k, total, lines, send, keep, row * group, at)
        k.held.done(send, keep, at=((0, k.count // 2), (part * lines, lines)))


def term_expand(
    k, modded_x, pgrad_x, mixed_x, agrad_x, small_m_x, modded, pgrad, mixed, agrad, small_m,
    send_e, keep_e, lines_v,
):
    width = k.width
    tall = k.hidden // width
    lines = width // k.count
    square_terms(k, (modded_x, modded), (pgrad_x, pgrad), send_e, keep_e, range(tall))
    square_terms(k, (mixed_x, mixed), (agrad_x, agrad), send_e, keep_e, (tall,))
    seqs = [item[8 : 8 + SEGS, : 3 * width] for item in (small_m_x, small_m)]
    times = sum(
        k.embed[:, n * SEGS + s : n * SEGS + s + 1] * seqs[n][s : s + 1]
        for n in range(2)
        for s in range(SEGS)
    )
    lines_v[0:1] = small_m_x[1:2, :width] + small_m[1:2, :width]
    bias_sum = jnp.sum(seqs[0] + seqs[1], axis=0, keepdims=True)
    for n in range(3):
        lines_v[1 + n : 2 + n] = bias_sum[:, n * width : (n + 1) * width]
    hidden_sum = small_m_x[0:1] + small_m[0:1]
    for n in range(tall):
        lines_v[4 + n : 5 + n] = hidden_sum[:, n * width : (n + 1) * width]
    deep = EMB // k.count
    first = (tall + 1) * lines
    size = 3 * deep + SMALL_ROWS
    for g in range(k.count // 2):
        even, odd = (
            jnp.concatenate(
                [
                    times[(2 * g + n) * deep : (2 * g + n + 1) * deep, p * width : (p + 1) * width]
                    for p in range(3)
                ]
                + [lines_v[...]],
                axis=0,
            )
            for n in range(2)
        )
        send_e[g, first : first + size] = jnp.where(k.low, odd, even).astype(BF16)
        keep_e[g, first : first + size] = jnp.where(k.low, even, odd)
    k.held.done(send_e, keep_e, at=((0, k.count // 2), (first, size)))


def term_attend(k, normed_x, jgrad_x, small_a_x, normed, jgrad, small_a, send_a, keep_a):
    lines = k.width // k.count
    square_terms(k, (normed_x, normed), (jgrad_x, jgrad), send_a, keep_a, range(3))
    total = small_a_x[0:1] + small_a[0:1]
    block = jnp.concatenate([total, jnp.zeros((GAIN_ROWS - 1, k.width), F32)], axis=0)
    at = slice(3 * lines, 3 * lines + GAIN_ROWS)
    for g in range(k.count // 2):
        send_a[g, at] = block.astype(BF16)
        keep_a[g, at] = block
    k.held.done(send_a, keep_a, at=((0, k.count // 2), (3 * lines, GAIN_ROWS)))


def plain_pieces(ops, count):
    def blocks(left, right):
        total = sum(dot(a, b, 0, 0) for a, b in zip(left, right))
        width = ops.bgrad[0].shape[1]
        parts = [total[:, i : i + width] for i in range(0, total.shape[1], width)]
        return [part.reshape(count, -1, width) for part in parts]

    reduce = blocks(ops.active, ops.bgrad)
    expand = blocks(ops.modded, ops.pgrad)
    last = blocks(ops.normed, ops.jgrad)
    expand += blocks(ops.mixed, ops.agrad)
    width = ops.bgrad[0].shape[1]
    seqs = jnp.concatenate([item[8 : 8 + SEGS, : 3 * width] for item in ops.small_m])
    times = jnp.dot(ops.embed, seqs, precision=lax.Precision.HIGHEST)
    expand += [times[:, i * width : (i + 1) * width].reshape(count, -1, width) for i in range(3)]
    lines = jnp.concatenate(
        [
            sum(item[1:2, :width] for item in ops.small_m),
            jnp.sum(seqs, axis=0).reshape(-1, width),
            sum(item[0] for item in ops.small_m).reshape(-1, width),
        ]
    )
    gain = jnp.pad(sum(item[0:1] for item in ops.small_a), ((0, GAIN_ROWS - 1), (0, 0)))
    expand.append(jnp.broadcast_to(lines, (count,) + lines.shape))
    last.append(jnp.broadcast_to(gain, (count,) + gain.shape))
    return [jnp.concatenate(item, axis=1) for item in (reduce, expand, last)]


def shapes_of(span, width, hidden, count):
    tok = lambda cols, kind=BF16: ((span, cols), kind)
    shapes = dict(
        xv=tok(width),
        dyv=tok(width),
        win=((width, 3 * width), BF16),
        wout=((width, width), BF16),
        wex=((width, hidden), BF16),
        wre=((hidden, width), BF16),
        normed=tok(width),
        qkv=tok(3 * width),
        probs=((HEADS, span, span), F32),
        mixed=tok(width),
        middle=tok(width, F32),
        modded=tok(width),
        slope=tok(hidden, F32),
        active=tok(hidden),
        branch=tok(width, F32),
        result=tok(width),
        bgrad=tok(width),
        pgrad=tok(hidden),
        agrad=tok(width),
        jgrad=tok(3 * width),
        mixed_grad=tok(width),
        middle_grad=tok(width, F32),
        leave=tok(width),
        acc=tok(width, F32),
        bias=tok(span, F32),
        small_m=((16, hidden), F32),
        small_a=((8, width), F32),
        lines_v=((SMALL_ROWS, width), F32),
    )
    shapes.update({item + "_x": shape for item, shape in shapes.items()})
    rows = dict(
        r=hidden // count,
        e=(hidden + width + 3 * EMB) // count + SMALL_ROWS,
        a=3 * width // count + GAIN_ROWS,
    )
    for item, lines in rows.items():
        shapes["send_" + item] = ((count // 2, lines, width), BF16)
        shapes["keep_" + item] = ((count // 2, lines, width), F32)
    return shapes


def uses(part):
    return list(inspect.signature(part).parameters)[1:]


def stage_kernel(sizes, parts, term, who, slot, plan, *refs):
    refs = list(refs)
    layer = Layer(sizes, slot, refs[:9])
    span = layer.span
    pos = 9
    cut = lambda ref, row: ref if row is None else ref.at[pl.ds(row, span)]
    sources = {}
    for name, row in plan.sources:
        sources[name] = cut(refs[pos], row)
        pos += 1
    pos += plan.extra
    stores = {}
    for name, row in plan.targets:
        stores[name] = cut(refs[pos], row)
        pos += 1
    bufs = {name: sources.pop(name) for name in plan.direct}
    for name in plan.bufs:
        bufs[name] = refs[pos]
        pos += 1
    mine_sems, both_sems, other_sems = refs[pos:]
    mine = layer.section == who
    loads = {name: ref for name, ref in sources.items() if name not in plan.shared}
    held = Held(bufs, loads, stores, mine_sems)
    common = Held(bufs, {name: sources[name] for name in plan.shared}, stores, both_sems)

    layer.sloped = "slope" in stores or mlp in parts
    layer.later = common.begin_all

    @pl.when(mine)
    def _():
        layer.held = held
        for part in parts:
            part(layer, *[bufs[name] for name in uses(part)])

    if term is not None:
        made = [name for name in uses(term) if name in plan.made]
        there = {name: stores.get(name, sources.get(name)) for name in made}
        other = Held(bufs, there, {}, other_sems)

        @pl.when(jnp.logical_not(mine))
        def _():
            common.waiting = set(common.loads)
            common.begin_all()
            other.need(*[bufs[name] for name in made])

        common.need(*[bufs[name] for name in plan.shared])
        layer.held = common
        term(layer, *[bufs[name] for name in uses(term)])
        common.finish()

    @pl.when(mine)
    def _():
        held.finish()


def stage(
    name, common, parts, who, slot, loads, stores, carried=None, after=(), term=None, firsts=None,
    shared=None,
):
    carried = carried or {}
    shared = dict(shared or {})
    span, width, hidden, count = common.sizes
    shapes = shapes_of(span, width, hidden, count)
    stores = dict(stores)
    if term is not None:
        for item in uses(term):
            if item.endswith("_x"):
                shared[item] = firsts[item[:-2]]
            if item.startswith(("send_", "keep_")):
                stores[item] = item
    loads = dict(loads, **shared)
    bufs = []
    for part in parts + ((term,) if term is not None else ()):
        bufs += [item for item in uses(part) if item not in bufs]
    direct = [item for item in bufs if isinstance(loads.get(item), list)]
    pair = lambda item: item if isinstance(item, tuple) else (item, None)
    args = list(common.args)
    in_specs = [pl.BlockSpec(memory_space=SMEM)] * 3 + [pl.BlockSpec(memory_space=VMEM)] * 6
    plan = Bag(sources=[], targets=[], direct=direct, shared=[], made=[])
    order = [item for item in loads if item in bufs]
    for item in order:
        if item in direct:
            array, row = loads[item][0], None
        else:
            array, row = pair(loads[item])
        args.append(array)
        in_specs.append(pl.BlockSpec(memory_space=VMEM if item in direct else ANY))
        plan.sources.append((item, row))
        if item in shared:
            plan.shared.append(item)
    outs, aliases, extra = [], {}, []
    targets = [(item, *pair(key)) for item, key in stores.items()]
    for i, (item, key, row) in enumerate(targets):
        shape, kind = shapes[item]
        if row is not None:
            shape = (common.tokens,) + shape[1:]
        outs.append(jax.ShapeDtypeStruct(shape, kind))
        plan.targets.append((item, row))
        if key in carried:
            aliases[len(args) + len(extra)] = i
            extra.append(carried[key])
    extra += list(after)
    args += extra
    in_specs += [pl.BlockSpec(memory_space=ANY)] * len(extra)
    plan.update(
        extra=len(extra),
        bufs=[item for item in bufs if item not in direct],
        made=[item for part in parts for item in uses(part)],
    )
    plan["made"] = [item for item in plan.made if item not in shared and item not in direct]
    results = pl.pallas_call(
        partial(stage_kernel, common.sizes, parts, term, who, slot, plan),
        out_shape=outs,
        in_specs=in_specs,
        out_specs=[pl.BlockSpec(memory_space=ANY)] * len(outs),
        input_output_aliases=aliases,
        scratch_shapes=[pltpu.VMEM(*shapes[item]) for item in plan.bufs]
        + [pltpu.SemaphoreType.DMA((n,)) for n in (32, 48, 8)],
        compiler_params=pltpu.CompilerParams(vmem_limit_bytes=56 * 1024 * 1024),
        name=name,
    )(*args)
    return Bag({key: value for (_, key, _), value in zip(targets, results)})


def bits_of(count):
    bits = count.bit_length() - 1
    assert 1 << bits == count
    return bits


class Chunk:
    def __init__(self, axis, terms, rows):
        self.axis = axis
        self.start, self.size = rows
        self.bits = list(range(bits_of(2 * terms[0].shape[0]) - 1, 0, -1))
        self.settled = []
        self.terms = []
        for term in terms:
            self.add(term, self.start)

    def add(self, term, start=0):
        left = [bit for bit in self.bits if bit not in self.settled]
        self.terms.append((term.reshape((2,) * len(left) + term.shape[-2:]), left, start))

    def take(self, term, start, left, flip):
        me = lax.axis_index(self.axis)
        side = lambda bit: 1 - ((me >> bit) & 1) if bit == flip else (me >> bit) & 1
        starts = [side(bit) if bit in self.settled else 0 for bit in left]
        sizes = [1 if bit in self.settled else 2 for bit in left]
        cols = term.shape[-1]
        piece = lax.dynamic_slice(term, starts + [start, 0], sizes + [self.size, cols])
        open_bits = [2] * (len(self.bits) - len(self.settled))
        return piece.reshape(open_bits + [self.size, cols]).astype(F32)

    def split(self, bit):
        self.settled.append(bit)
        return sum(self.take(term, start, left, bit) for term, left, start in self.terms).astype(
            BF16
        )

    def total(self):
        return sum(self.take(term, start, left, None) for term, left, start in self.terms)


def exchange(block, axis, bit):
    count = lax.axis_size(axis)
    return lax.ppermute(block, axis, [(i, i ^ (1 << bit)) for i in range(count)])


def join(*items):
    return lax.optimization_barrier(items)


def angle_table(span):
    half = HEAD // 2
    freqs = np.exp(-math.log(10000.0) * np.arange(half, dtype=np.float32) / half)
    phase = np.arange(span, dtype=np.float32)[:, None] * freqs.astype(np.float32)[None, :]
    cos_part, sin_part = np.cos(phase), np.sin(phase)
    return np.stack(
        [
            np.concatenate([cos_part] * 4, axis=1),
            np.concatenate([-sin_part, sin_part] * 2, axis=1),
        ]
    ).astype(np.float32)


def per_device(
    ends_in,
    lengths,
    times,
    norm_gain,
    attend_in,
    attend_out,
    time_weight,
    time_bias,
    expand_weight,
    expand_bias,
    reduce_weight,
    reduce_bias,
):
    local = ends_in[0]
    micro = lengths.shape[1]
    assert micro == 2
    width = local.shape[1]
    span = local.shape[0] // micro
    hidden = expand_weight.shape[2]
    count = lax.axis_size("rep")
    section = lax.axis_index("section")
    rank = lax.axis_index("rep")
    core = rank & 1
    steps = jnp.exp(-math.log(10000.0) * jnp.arange(EMB // 2, dtype=F32) / (EMB // 2))
    turn = times.reshape(micro * SEGS, 1).astype(F32) * steps
    embed = jnp.concatenate([jnp.cos(turn), jnp.sin(turn)], axis=1)
    mods = jnp.dot(
        embed, time_weight[0].astype(F32), precision=lax.Precision.HIGHEST
    ) + time_bias.astype(F32)
    common = Bag(
        args=(
            lengths[0],
            section.reshape(1),
            core.reshape(1),
            mods,
            jnp.asarray(angle_table(span)),
            embed.T,
            norm_gain,
            expand_bias,
            reduce_bias,
        ),
        sizes=(span, width, hidden, count),
        tokens=local.shape[0],
    )
    weights = Bag(
        win=attend_in[0], wout=attend_out[0], wex=expand_weight[0], wre=reduce_weight[0]
    )
    rows = [(local, slot * span) for slot in range(micro)]
    same = lambda *names: {name: name for name in names}
    whole = {
        name: name
        for part in (term_reduce, term_expand, term_attend)
        for name in uses(part)
        if name + "_x" in uses(part)
    }
    run = partial(stage, common=common)
    both = (forward, output, mlp, attend)
    over = lambda block, route: lax.ppermute(block, "section", route)
    a = run(
        "first_0",
        parts=(forward,),
        who=0,
        slot=0,
        loads=dict(xv=rows[0], **weights),
        stores=dict(result="leave"),
    )
    came_0 = over(a.leave, [(0, 1)])
    held = [item for item in uses(forward) if item not in weights]
    b = run(
        "first_1",
        parts=(forward,),
        who=0,
        slot=1,
        loads=dict(xv=rows[1], **weights),
        stores={item: item for item in held if item not in ("xv", "bias")},
        after=(a.leave,),
    )
    came_1 = over(b.result, [(0, 1)])
    x = run(
        "second_0",
        parts=both,
        who=1,
        slot=0,
        loads=dict(xv=[came_0], dyv=rows[0], **weights),
        stores=dict(whole, result=("ends", 0), leave="leave"),
        after=(b.result,),
    )
    back_0 = over(x.leave, [(1, 0)])
    y = run(
        "second_1",
        parts=both,
        who=1,
        slot=1,
        loads=dict(xv=[came_1], dyv=rows[1], **weights),
        stores=dict(whole, result=("ends", span), leave="leave"),
        carried=dict(b, ends=x.ends),
        after=(x.leave,),
    )
    back_1 = over(y.leave, [(1, 0)])
    x = run(
        "back_0",
        parts=both,
        who=0,
        slot=0,
        loads=dict(xv=rows[0], dyv=[back_0], **weights),
        stores=dict(whole, leave=("ends", 0)),
        carried=dict(x, ends=y.ends),
        after=(y.leave,),
    )
    fused = width // count % 16 == 0 and TILE % (2 * hidden // count) == 0

    def last(name, part, loads, stores, term, shared, after=()):
        y.update(
            run(
                name,
                parts=(part,),
                who=0,
                slot=1,
                loads=loads,
                stores=stores,
                carried=dict(y, ends=x.ends),
                after=after,
                term=term if fused else None,
                firsts=x,
                shared=shared if fused else None,
            )
        )

    last("back_1_out", output, dict(dyv=[back_1]), same("bgrad"), term_reduce, dict(active=y.active))
    last_mlp = partial(
        last,
        "back_1_mlp",
        mlp,
        dict(
            wre=weights.wre,
            bgrad=y.bgrad,
            slope=b.slope,
            wex=weights.wex,
            middle=b.middle,
            branch=b.branch,
            dyv=[back_1],
        ),
        same("pgrad", "agrad", "middle_grad", "small_m"),
        term_expand,
        dict(modded=y.modded, mixed=y.mixed),
    )

    def last_attend(after):
        last(
            "back_1_attend",
            attend,
            dict(
                wout=weights.wout,
                agrad=y.agrad,
                probs=b.probs,
                qkv=b.qkv,
                win=weights.win,
                xv=rows[1],
                middle_grad=y.middle_grad,
            ),
            dict(same("jgrad", "small_a"), leave=("ends", span)),
            term_attend,
            dict(normed=y.normed),
            after=after,
        )

    if not fused:
        last_mlp()
        last_attend(())
        ops = Bag({item: (x[item], y[item]) for item in whole}, embed=embed.T)
        for item, total in zip("rea", plain_pieces(ops, count)):
            view = total.reshape((count // 2, 2) + total.shape[1:])
            side = lambda at: lax.dynamic_index_in_dim(view, at, 1, keepdims=False)
            y["send_" + item] = side(1 - core).astype(BF16)
            y["keep_" + item] = side(core)
    swap = lambda block, bit: exchange(block, "rep", bit)
    bits = bits_of(count)

    def halves(came, keep, share):
        lines = keep.shape[1]
        cut = lines * share // 100 // 16 * 16
        terms = [keep, came]
        return Chunk("rep", terms, (0, cut)), Chunk("rep", terms, (cut, lines - cut))

    r1, r2 = halves(swap(y.send_r, 0), y.keep_r, 50)
    send_1, send_2 = r1.split(1), r2.split(2)
    came_r1, came_r2 = swap(send_1, 1), swap(send_2, 2)
    if fused:
        last_mlp(after=(send_1, send_2))
    came_r1, came_r2, send_e = join(came_r1, came_r2, y.send_e)
    came_e = swap(send_e, 0)
    r1.add(came_r1)
    r2.add(came_r2)
    send_1, send_2 = r1.split(2), r2.split(1)
    came_r1, came_r2 = swap(send_1, 2), swap(send_2, 1)
    came_e, _, _ = join(came_e, send_1, send_2)
    e1, e2 = halves(came_e, y.keep_e, 50)
    send_1, send_2 = e1.split(1), e2.split(2)
    came_e1, came_e2 = swap(send_1, 1), swap(send_2, 2)
    if fused:
        last_attend((send_1, send_2))
    ends = y.ends
    came_r1, came_r2, came_e1, came_e2, send_a = join(
        came_r1, came_r2, came_e1, came_e2, y.send_a
    )
    came_a = swap(send_a, 0)
    e1.add(came_e1)
    e2.add(came_e2)
    send_1, send_2 = e1.split(2), e2.split(1)
    came_e1, came_e2 = swap(send_1, 2), swap(send_2, 1)
    came_r1, came_r2, _, _ = join(came_r1, came_r2, send_1, send_2)
    r1.add(came_r1)
    r2.add(came_r2)
    block_r = jnp.concatenate([r1.split(3), r2.split(3)], axis=-2)
    came_r = swap(block_r, 3)
    came_a, came_e1, came_e2, _ = join(came_a, came_e1, came_e2, block_r)
    a1, a2 = halves(came_a, y.keep_a, 60)
    send_1, send_2 = a1.split(1), a2.split(2)
    came_a1, came_a2 = swap(send_1, 1), swap(send_2, 2)
    came_e1, came_e2, _, _ = join(came_e1, came_e2, send_1, send_2)
    e1.add(came_e1)
    e2.add(came_e2)
    block_e = jnp.concatenate([e1.split(3), e2.split(3)], axis=-2)
    came_e = swap(block_e, 3)
    came_r, _ = join(came_r, block_e)
    r1.add(came_r[..., : r1.size, :])
    r2.add(came_r[..., r1.size :, :])
    came_a1, came_a2, _ = join(came_a1, came_a2, came_r)
    a1.add(came_a1)
    a2.add(came_a2)
    send_1, send_2 = a1.split(2), a2.split(1)
    came_a1, came_a2 = swap(send_1, 2), swap(send_2, 1)
    a1.add(came_a1)
    a2.add(came_a2)
    block_a = jnp.concatenate([a1.split(3), a2.split(3)], axis=-2)
    came_a = swap(block_a, 3)
    came_e, _ = join(came_e, block_a)
    e1.add(came_e[..., : e1.size, :])
    e2.add(came_e[..., e1.size :, :])
    a1.add(came_a[..., : a1.size, :])
    a2.add(came_a[..., a1.size :, :])
    for bit in range(4, bits):
        for chunk in (r1, r2, e1, e2, a1, a2):
            chunk.add(swap(chunk.split(bit), bit))
    share_r, share_e, share_a = (
        jnp.concatenate([one.total(), two.total()]) for one, two in ((r1, r2), (e1, e2), (a1, a2))
    )
    lines = width // count
    deep = EMB // count
    tall = hidden // width
    side = lambda item, n, size: jnp.concatenate(
        [item[i * size : (i + 1) * size] for i in range(n)], axis=1
    )
    at_o = tall * lines
    at_t = at_o + lines
    small = share_e[at_t + 3 * deep :]
    flat = lambda item, first, n: lax.dynamic_slice_in_dim(
        item[first : first + n].reshape(-1), rank * (n * width // count), n * width // count
    )
    results = (
        flat(share_a, 3 * lines, 1),
        side(share_a, 3, lines),
        share_e[at_o:at_t],
        side(share_e[at_t:], 3, deep),
        flat(small, 1, 3),
        side(share_e, tall, lines),
        flat(small, 4, tall),
        share_r,
        flat(small, 0, 1),
    )
    return (ends[None],) + tuple(piece[None] for piece in results)


def solution(mesh):
    return jax.shard_map(
        per_device,
        mesh=mesh,
        in_specs=(
            P("section", "rep", None),
            P("rep", None, None),
            P("rep", None, None),
            P("section", None),
            P("section", None, None),
            P("section", None, None),
            P("section", None, None),
            P("section", None),
            P("section", None, None),
            P("section", None),
            P("section", None, None),
            P("section", None),
        ),
        out_specs=(
            P("section", "rep", None),
            P("section", "rep"),
            P("section", "rep", None),
            P("section", "rep", None),
            P("section", "rep", None),
            P("section", "rep"),
            P("section", "rep", None),
            P("section", "rep"),
            P("section", "rep", None),
            P("section", "rep"),
        ),
        check_vma=False,
    )
```

```python
from functools import partial
import inspect
import math

import jax
import jax.numpy as jnp
import numpy as np
from jax import lax
from jax.experimental import pallas as pl
from jax.experimental.pallas import tpu as pltpu
from jax.sharding import PartitionSpec as P

HEADS = 12
HEAD = 64
EMB = 128
SEGS = 4
ANY = pl.ANY
VMEM = pltpu.MemorySpace.VMEM
SMEM = pltpu.MemorySpace.SMEM
F32 = jnp.float32
BF16 = jnp.bfloat16
ROOT_HALF = 0.7071067811865476
ROOT_TAU = 0.3989422804014327
TILE = 384
TAIL_ROWS = 24
GAIN_ROWS = 16
EXTRA = 16


class Bag(dict):
    __getattr__ = dict.__getitem__


def dot(left, right, left_dim=1, right_dim=0):
    return lax.dot_general(
        left, right, (((left_dim,), (right_dim,)), ((), ())), preferred_element_type=F32
    )


def repeat(count, body):
    for i in range(count):
        body(i)


def steps_of(count, size, body):
    def several(i, _):
        for j in range(size):
            body(size * i + j)
        return _

    lax.fori_loop(0, count // size, several, 0)


def lanes(index, size, start=0):
    if isinstance(index, int):
        return slice(start + index * size, start + (index + 1) * size)
    return pl.ds(pl.multiple_of(start + index * size, size), size)


def swap_halves(values, low_half):
    forth = pltpu.roll(values, 128 - HEAD // 2, 1)
    back = pltpu.roll(values, HEAD // 2, 1)
    return jnp.where(low_half, forth, back)


def norm_parts(values):
    center = values - jnp.mean(values, axis=-1, keepdims=True)
    spread = jnp.mean(center * center, axis=-1, keepdims=True)
    factor = lax.rsqrt(spread + 1e-05)
    return center * factor, factor


def norm_back(grad, unit, factor):
    return factor * (
        grad
        - jnp.mean(grad, axis=-1, keepdims=True)
        - unit * jnp.mean(grad * unit, axis=-1, keepdims=True)
    )


class Held:
    def __init__(self, bufs, loads, stores, sems):
        self.bufs = bufs
        self.loads = loads
        self.stores = stores
        self.sems = sems
        self.names = {id(buf): name for name, buf in bufs.items()}
        self.spots = {name: n for n, name in enumerate(loads)}
        self.pending = set(loads)
        self.waiting = set(loads)
        self.leaving = {}

    def load(self, name):
        return pltpu.make_async_copy(
            self.loads[name], self.bufs[name], self.sems.at[self.spots[name]]
        )

    def store(self, name, at):
        number, _ = self.leaving[(name, at)]
        source, target = self.bufs[name], self.stores[name]
        if at is not None:
            spot = tuple(pl.ds(*item) for item in at)
            source, target = source.at[spot], target.at[spot]
        return pltpu.make_async_copy(source, target, self.sems.at[number])

    def begin(self, *bufs):
        for buf in bufs:
            name = self.names[id(buf)]
            if name in self.waiting:
                self.waiting.remove(name)
                self.load(name).start()

    def begin_all(self):
        self.begin(*[self.bufs[name] for name in self.loads])

    def need(self, *bufs):
        self.begin(*bufs)
        for buf in bufs:
            name = self.names[id(buf)]
            if name in self.pending:
                self.pending.remove(name)
                self.load(name).wait()

    def done(self, *bufs, at=None):
        for buf in bufs:
            name = self.names[id(buf)]
            if name in self.stores:
                self.leaving[(name, at)] = (len(self.loads) + len(self.leaving), at)
                self.store(name, at).start()

    def finish(self):
        for name, at in self.leaving:
            self.store(name, at).wait()


class Layer:
    def __init__(self, sizes, slot, refs):
        self.span, self.width, self.hidden, self.count = sizes
        self.slot = slot
        lengths, section, self.mods, self.trig, self.gain, self.ebias, self.rbias = refs
        self.section = section[0]
        self.single = lengths[slot, 0] == self.span
        self.pairs = self.width // 128
        self.seg = self.span // SEGS
        self.step = self.width
        self.tiles = self.hidden // self.step
        place = lax.broadcasted_iota(jnp.int32, (self.span, 128), 1)
        self.low_half = place % HEAD < HEAD // 2
        self.low_head = place < HEAD
        row = lax.broadcasted_iota(jnp.int32, (1, 128), 1) // HEAD
        self.head_row = [(row == i).astype(F32).astype(BF16) for i in range(2)]
        self.blocks = [(b, slice(b * self.seg, (b + 1) * self.seg)) for b in range(SEGS)]

    def trig_pair(self):
        cos_all, sin_all = self.trig[0], self.trig[1]
        cos_cut = jnp.concatenate([cos_all[: self.seg]] * SEGS, axis=0)
        sin_cut = jnp.concatenate([sin_all[: self.seg]] * SEGS, axis=0)
        return jnp.where(self.single, cos_all, cos_cut), jnp.where(self.single, sin_all, sin_cut)

    def mod_row(self, block, part):
        row = self.slot * SEGS + jnp.where(self.single, 0, block)
        return self.mods[pl.ds(row, 1), part * self.width : (part + 1) * self.width]

    def add_segment(self, small, block, at, sums):
        row = 2 + jnp.where(self.single, 0, block)
        small[pl.ds(row, 1), at * self.width : (at + 1) * self.width] += sums

    def put_left(self, left, base, first, values):
        turned = values.T
        lines = (self.hidden if base == 0 else self.width) // self.count
        if left.shape[0] == 1:
            left[0, 2 * base + first : 2 * base + first + turned.shape[0]] = turned
            return
        for block in range(first // lines, (first + turned.shape[0]) // lines):
            at = block * lines - first
            to = base + block // 2 * lines
            left[block % 2, to : to + lines] = turned[at : at + lines]

    def thirds(self, index):
        return [lanes(index, 128, p * self.width) for p in range(3)]


def left_bases(width, hidden):
    return 0, hidden // 2, (hidden + width) // 2, (hidden + 2 * width) // 2


def forward(
    k, xv, win, wout, wex, wre, left, qkv, probs, middle, slope, branch, result, bias, normed,
    mixed, modded,
):
    span, width, held = k.span, k.width, k.held
    at_active, at_modded, at_mixed, at_normed = left_bases(width, k.hidden)
    held.begin(xv, win)
    held.need(xv)
    unit, _ = norm_parts(xv[...].astype(F32))
    normed[...] = (unit * k.gain[...].astype(F32)).astype(BF16)
    across = lax.broadcasted_iota(jnp.int32, (span, span), 0) // k.seg
    down = lax.broadcasted_iota(jnp.int32, (span, span), 1) // k.seg
    bias[...] = jnp.where((across == down) | k.single, 0.0, -1e30)
    held.need(win)
    held.begin(wout, wex, wre)
    cos_part, sin_part = k.trig_pair()
    for tile, factor in ((0, 0.125), (1, 1.0)):
        for i in range(width // 256):
            at = lanes(i, 256, tile * width)
            joint = dot(normed[...], win[:, at])
            outs = []
            for piece in (joint[:, :128], joint[:, 128:]):
                turned = piece * cos_part + swap_halves(piece, k.low_half) * sin_part
                outs.append((turned * factor).astype(BF16))
            qkv[:, at] = jnp.concatenate(outs, axis=1)
    qkv[:, 2 * width :] = dot(normed[...], win[:, 2 * width :]).astype(BF16)
    held.done(qkv)
    if k.kept:
        k.put_left(left, at_normed, 0, normed[...])

    def heads(i):
        at = k.thirds(i)
        query, key, value = (qkv[:, a] for a in at)
        outs = []
        for h in range(2):
            scores = dot(key * k.head_row[h], query, 1, 1) + bias[...]
            top = jnp.max(scores, axis=0, keepdims=True)
            raised = jnp.exp(scores - top)
            total = jnp.sum(raised, axis=0, keepdims=True)
            prob = raised * (1.0 / total)
            if k.kept:
                probs[2 * i + h] = prob
            outs.append(dot(prob.astype(BF16), value, 0, 0))
        mixed[:, at[0]] = jnp.where(k.low_head, outs[0], outs[1]).astype(BF16)

    steps_of(k.pairs, k.heads_step, heads)
    held.done(probs)
    held.need(wout)
    middle[...] = xv[...].astype(F32) + dot(mixed[...], wout[...])
    held.done(middle)
    if k.kept:
        k.put_left(left, at_mixed, 0, mixed[...])
    for b, rows in k.blocks:
        unit, _ = norm_parts(middle[rows])
        modded[rows] = (unit * (1.0 + k.mod_row(b, 0)) + k.mod_row(b, 1)).astype(BF16)
    if k.kept:
        k.put_left(left, at_modded, 0, modded[...])
    held.need(wex, wre)
    branch[...] = jnp.broadcast_to(k.rbias[...].astype(F32), (span, width))

    def feed(j):
        at = lanes(j, k.step)
        pre = dot(modded[...], wex[:, at]) + k.ebias[:, at].astype(F32)
        area = 0.5 + 0.5 * lax.erf(pre * ROOT_HALF)
        out = (pre * area).astype(BF16)
        if k.kept:
            slope[:, at] = area + pre * (jnp.exp(pre * pre * -0.5) * ROOT_TAU)
            k.put_left(left, at_active, j * k.step, out)
        branch[...] += dot(out, wre[at, :])

    repeat(k.tiles, feed)
    held.done(slope, left, branch)
    for b, rows in k.blocks:
        result[rows] = (middle[rows] + k.mod_row(b, 2) * branch[rows]).astype(BF16)
    held.done(result)


def output(k, dyv, bg):
    k.held.need(dyv)
    for b, rows in k.blocks:
        bg[rows] = (dyv[rows].astype(F32) * k.mod_row(b, 2)).astype(BF16)
    k.held.done(bg)


def mlp(k, wre, wex, bg, slope, middle, branch, dyv, pa, middle_grad, small, acc):
    span, width, hidden, held = k.span, k.width, k.hidden, k.held
    small[...] = jnp.zeros(small.shape, F32)
    acc[...] = jnp.zeros(acc.shape, F32)
    held.need(bg, wre, slope)
    held.begin(wex, middle, dyv, branch)
    held.need(wex)

    def feed(j):
        at = lanes(j, k.step)
        grad = dot(bg[...], wre[at, :], 1, 1)
        pre_grad = (slope[:, at] * grad).astype(BF16)
        pa[:span, at] = pre_grad
        small[0:1, at] = jnp.sum(pre_grad.astype(F32), axis=0, keepdims=True)
        acc[...] += dot(pre_grad, wex[:, at], 1, 1)

    repeat(k.tiles, feed)
    held.need(middle, dyv, branch)
    total = jnp.zeros((1, width), F32)
    for b, rows in k.blocks:
        cotan = dyv[rows].astype(F32)
        total += jnp.sum(bg[rows].astype(F32), axis=0, keepdims=True)
        grad = acc[rows]
        unit, factor = norm_parts(middle[rows])
        k.add_segment(small, b, 0, jnp.sum(grad * unit, axis=0, keepdims=True))
        k.add_segment(small, b, 1, jnp.sum(grad, axis=0, keepdims=True))
        k.add_segment(small, b, 2, jnp.sum(cotan * branch[rows], axis=0, keepdims=True))
        back = norm_back(grad * (1.0 + k.mod_row(b, 0)), unit, factor)
        full = cotan + back
        middle_grad[rows] = full
        pa[rows, hidden:] = full.astype(BF16)
    small[1:2, :width] = total
    pa[span:, :] = small[...].astype(BF16)
    held.done(pa, middle_grad)


def attend(
    k, wout, win, agrad, probs, qkv, xv, middle_grad, jg, leave, mixed_grad, acc
):
    span, held = k.span, k.held
    held.need(agrad, wout)
    held.begin(probs, qkv)
    mixed_grad[...] = dot(agrad[...], wout[...], 1, 1).astype(BF16)
    held.need(probs, qkv)
    held.begin(win, xv, middle_grad)
    cos_part, sin_part = k.trig_pair()

    def heads(i):
        at = k.thirds(i)
        query, key, value = (qkv[:, a] for a in at)
        out_grad = mixed_grad[:, at[0]]
        parts = []
        for h in range(2):
            prob = probs[2 * i + h]
            pull = dot(value * k.head_row[h], out_grad, 1, 1)
            shared = jnp.sum(prob * pull, axis=0, keepdims=True)
            score_grad = (prob * (pull - shared)).astype(BF16)
            parts.append(
                (
                    dot(score_grad, key, 0, 0),
                    dot(score_grad, query),
                    dot(prob.astype(BF16), out_grad),
                )
            )
        for p in range(3):
            grad = jnp.where(k.low_head, parts[0][p], parts[1][p])
            if p < 2:
                grad = grad * cos_part - swap_halves(grad, k.low_half) * sin_part
                if p == 0:
                    grad = grad * 0.125
            jg[:span, at[p]] = grad.astype(BF16)

    steps_of(k.pairs, k.heads_step, heads)
    held.need(win, xv, middle_grad)
    acc[...] = dot(jg[:span, :], win[...], 1, 1)
    total = jnp.zeros((1, k.width), F32)
    for b, rows in k.blocks:
        grad = acc[rows]
        unit, factor = norm_parts(xv[rows].astype(F32))
        total += jnp.sum(grad * unit, axis=0, keepdims=True)
        back = norm_back(grad * k.gain[...].astype(F32), unit, factor)
        leave[rows] = (middle_grad[rows] + back).astype(BF16)
    below = jnp.concatenate([total, jnp.zeros((EXTRA - 1, k.width), F32)], axis=0)
    jg[span:, : k.width] = below.astype(BF16)
    jg[span:, k.width :] = jnp.zeros((EXTRA, 2 * k.width), BF16)
    held.done(jg, leave)


def copy_agrad(k, pa, agrad):
    agrad[...] = pa[: k.span, k.hidden :]


class Sums:
    def __init__(self, ranks, full, outs, sems):
        self.full = full
        self.own = [((ranks[0] >> bit) & 1) == 0 for bit in (1, 2)]
        self.bufs = outs[:4]
        self.targets = outs[4:]
        self.sems = sems
        self.half = full.shape[1] // 2
        self.copies = []

    def put(self, block, at, values):
        self.full[block, at] = values

    def settle(self, which, groups):
        send, keep = self.bufs[2 * which : 2 * which + 2]
        at = slice(which * self.half, (which + 1) * self.half)
        apart = 1 + which
        for group in groups:
            for n in range(2):
                first = 4 * group + (2 * n if which == 0 else n)
                even, odd = self.full[first, at], self.full[first + apart, at]
                send[2 * group + n] = jnp.where(self.own[which], odd, even).astype(BF16)
                keep[2 * group + n] = jnp.where(self.own[which], even, odd)
            spot = pl.ds(2 * group, 2)
            for n in range(2 * which, 2 * which + 2):
                copy = pltpu.make_async_copy(
                    self.bufs[n].at[spot], self.targets[n].at[spot], self.sems.at[len(self.copies)]
                )
                copy.start()
                self.copies.append(copy)

    def finish(self):
        for copy in self.copies:
            copy.wait()


def term_reduce(k, sums, left, right):
    lines = k.hidden // k.count
    per = TILE // lines
    for tile in range(k.hidden // 2 // TILE):
        total = dot(left[tile * TILE : (tile + 1) * TILE], right[...])
        for n in range(per):
            sums.put(tile * per + n, slice(0, lines), total[n * lines : (n + 1) * lines])
        if (tile + 1) * per % 4 == 0:
            group = ((tile + 1) * per // 4 - 1,)
            sums.settle(0, group)
            sums.settle(1, group)


def square_terms(k, sums, left, right, cols, part):
    lines = k.width // k.count
    total = dot(left, right[: 4 * k.span, cols])
    for n in range(k.count // 2):
        sums.put(n, slice(part * lines, (part + 1) * lines), total[n * lines : (n + 1) * lines])


def term_expand(k, sums, left, right):
    width, hidden, span = k.width, k.hidden, k.span
    groups = range(k.count // 8)
    tall = hidden // width
    lines = width // k.count
    rows = width // 2
    half = sums.half
    settled = False
    for col in range(tall + 1):
        part = left[:rows] if col < tall else left[rows:]
        square_terms(k, sums, part, right, slice(col * width, (col + 1) * width), col)
        if (col + 1) * lines >= half and not settled:
            sums.settle(0, groups)
            settled = True
    smalls = [k.small[n].astype(F32) for n in range(4)]
    times = sum(
        k.embeds[n // 2][:, n % 2 * SEGS + s : n % 2 * SEGS + s + 1]
        * smalls[n][2 + s : 3 + s, : 3 * width]
        for n in range(4)
        for s in range(SEGS)
    )
    both = sum(smalls)
    seq_sum = jnp.sum(both[2 : 2 + SEGS, : 3 * width], axis=0, keepdims=True)
    lines_v = k.lines
    lines_v[...] = jnp.zeros(lines_v.shape, F32)
    lines_v[0:1] = both[1:2, :width]
    for n in range(3):
        lines_v[1 + n : 2 + n] = seq_sum[:, n * width : (n + 1) * width]
    for n in range(tall):
        lines_v[4 + n : 5 + n] = both[0:1, n * width : (n + 1) * width]
    deep = EMB // k.count
    first = (tall + 1) * lines
    for g in range(k.count // 2):
        for side in range(2):

            @pl.when(k.core == side)
            def _(at=(2 * g + side) * deep, g=g):
                for p in range(3):
                    to = first + p * deep
                    piece = times[at : at + deep, p * width : (p + 1) * width]
                    sums.put(g, slice(to, to + deep), piece)

        sums.put(g, slice(first + 3 * deep, 2 * half), lines_v[...])
    sums.settle(1, groups)


def term_attend(k, sums, left, right):
    width = k.width
    groups = range(k.count // 8)
    lines = width // k.count
    settled = False
    for col in range(3):
        square_terms(k, sums, left[...], right, slice(col * width, (col + 1) * width), col)
        if (col + 1) * lines >= sums.half and not settled:
            sums.settle(0, groups)
            settled = True
    gain = sum(k.small[n].astype(F32) for n in range(4))[:, :width]
    for g in range(k.count // 2):
        sums.put(g, slice(3 * lines, 3 * lines + GAIN_ROWS), gain)
    sums.settle(1, groups)


def load_terms(k, refs, bufs, base, sems):
    left_v, right_v, small_v = bufs
    copies = []
    rows = left_v.shape[0]
    for n, (left, right) in enumerate(zip(refs[:4], refs[4:8])):
        source = left.at[k.core] if n < 2 else left
        tokens = pl.ds(n * k.span, k.span)
        copies.append((source.at[pl.ds(base, rows)], left_v.at[:, tokens]))
        copies.append((right.at[pl.ds(0, k.span)], right_v.at[tokens]))
        if small_v is not None:
            copies.append((right.at[pl.ds(k.span, EXTRA)], small_v.at[n]))
    made = [pltpu.make_async_copy(*pair, sems.at[n]) for n, pair in enumerate(copies)]
    for copy in made:
        copy.start()
    return made


class Terms:
    def __init__(self, sizes, core):
        self.span, self.width, self.hidden, self.count = sizes
        self.core = core[0]


def term_kernel(sizes, body, base, extra, *refs):
    refs = list(refs)
    core, rank = refs[:2]
    k = Terms(sizes, core)
    pos = 2
    if body is term_expand:
        k.embeds = refs[pos : pos + 2]
        pos += 2
    sources = refs[pos : pos + 8]
    pos += 8 + extra
    targets = refs[pos : pos + 4]
    pos += 4
    left_v, right_v, full, *outs = refs[pos : pos + 7]
    pos += 7
    k.small = None
    if body is not term_reduce:
        k.small, k.lines = refs[pos : pos + 2]
        pos += 2
    sems, out_sems = refs[pos:]
    copies = load_terms(k, sources, (left_v, right_v, k.small), base, sems)
    sums = Sums(rank, full, outs + targets, out_sems)
    for copy in copies:
        copy.wait()
    body(k, sums, left_v, right_v)
    sums.finish()


def term_call(name, body, sizes, lines, base, rows, core, rank, lefts, rights, embeds=(), after=()):
    span, width, hidden, count = sizes
    blocks = count // 2
    cols = rights[0].shape[1]
    half = lines // 2
    outs = [((blocks // 2, half, width), kind) for kind in (BF16, F32)] * 2
    scratch = [
        ((rows, 4 * span), BF16),
        ((4 * span, cols), BF16),
        ((blocks, lines, width), F32),
        *outs,
    ]
    if body is not term_reduce:
        scratch += [((4, EXTRA, cols), BF16), ((TAIL_ROWS, width), F32)]
    args = [core.reshape(1), rank.reshape(1), *embeds, *lefts, *rights, *after]
    in_specs = [pl.BlockSpec(memory_space=SMEM)] * 2
    in_specs += [pl.BlockSpec(memory_space=VMEM)] * len(embeds)
    in_specs += [pl.BlockSpec(memory_space=ANY)] * (8 + len(after))
    return pl.pallas_call(
        partial(term_kernel, sizes, body, base, len(after)),
        out_shape=[jax.ShapeDtypeStruct(*item) for item in outs],
        in_specs=in_specs,
        out_specs=[pl.BlockSpec(memory_space=ANY)] * 4,
        scratch_shapes=[pltpu.VMEM(*item) for item in scratch]
        + [pltpu.SemaphoreType.DMA((12,)), pltpu.SemaphoreType.DMA((8,))],
        compiler_params=pltpu.CompilerParams(vmem_limit_bytes=56 * 1024 * 1024),
        name=name,
    )(*args)


def plain_pieces(lefts, rights, embed, sizes):
    span, width, hidden, count = sizes
    bg, pa, jg = rights
    bases = [2 * base for base in left_bases(width, hidden)]

    def blocks(base, rows, right):
        total = sum(dot(a[0, base : base + rows], b) for a, b in zip(lefts, right))
        parts = [total[:, i : i + width] for i in range(0, total.shape[1], width)]
        return [part.reshape(count, -1, width) for part in parts]

    take = lambda items, cols: [item[:span, cols] for item in items]
    reduce = blocks(bases[0], hidden, bg)
    expand = blocks(bases[1], width, take(pa, slice(0, hidden)))
    expand += blocks(bases[2], width, take(pa, slice(hidden, hidden + width)))
    last = blocks(bases[3], width, take(jg, slice(None)))
    small = [item[span:].astype(F32) for item in pa]
    seqs = jnp.concatenate([item[2 : 2 + SEGS, : 3 * width] for item in small])
    times = jnp.dot(embed, seqs, precision=lax.Precision.HIGHEST)
    expand += [times[:, i * width : (i + 1) * width].reshape(count, -1, width) for i in range(3)]
    lines = jnp.concatenate(
        [
            sum(item[1:2, :width] for item in small),
            jnp.sum(seqs, axis=0).reshape(-1, width),
            sum(item[0, :hidden] for item in small).reshape(-1, width),
        ]
    )
    lines = jnp.pad(lines, ((0, TAIL_ROWS - lines.shape[0]), (0, 0)))
    gain = sum(item[span:, :width].astype(F32) for item in jg)
    expand.append(jnp.broadcast_to(lines, (count,) + lines.shape))
    last.append(jnp.broadcast_to(gain, (count,) + gain.shape))
    return [jnp.concatenate(item, axis=1) for item in (reduce, expand, last)]


def shapes_of(span, width, hidden, cores):
    tok = lambda cols, kind=BF16: ((span, cols), kind)
    below = lambda cols: ((span + EXTRA, cols), BF16)
    return dict(
        xv=tok(width),
        dyv=tok(width),
        win=((width, 3 * width), BF16),
        wout=((width, width), BF16),
        wex=((width, hidden), BF16),
        wre=((hidden, width), BF16),
        left=((cores, (hidden + 3 * width) // cores, span), BF16),
        normed=tok(width),
        qkv=tok(3 * width),
        probs=((HEADS, span, span), F32),
        mixed=tok(width),
        middle=tok(width, F32),
        modded=tok(width),
        slope=tok(hidden, F32),
        branch=tok(width, F32),
        result=tok(width),
        bg=tok(width),
        pa=below(hidden + width),
        jg=below(3 * width),
        agrad=tok(width),
        mixed_grad=tok(width),
        middle_grad=tok(width, F32),
        leave=tok(width),
        acc=tok(width, F32),
        bias=tok(span, F32),
        small=((EXTRA, hidden + width), F32),
    )


def uses(part):
    return list(inspect.signature(part).parameters)[1:]


def stage_kernel(sizes, parts, who, slot, plan, *refs):
    refs = list(refs)
    layer = Layer(sizes, slot, refs[:7])
    span = layer.span
    pos = 7
    loads = {}
    for name, row, cols in plan.sources:
        ref = refs[pos]
        if cols is not None:
            ref = ref.at[pl.ds(0, span), pl.ds(*cols)]
        elif row is not None:
            ref = ref.at[pl.ds(row, span)]
        loads[name] = ref
        pos += 1
    pos += plan.extra
    stores = {}
    for name, row in plan.targets:
        stores[name] = refs[pos] if row is None else refs[pos].at[pl.ds(row, span)]
        pos += 1
    bufs = {}
    for name in plan.bufs:
        bufs[name] = refs[pos]
        pos += 1
    layer.held = Held(bufs, loads, stores, refs[pos])
    layer.kept = plan.kept
    layer.heads_step = plan.heads_step

    @pl.when(layer.section == who)
    def _():
        for part in parts:
            part(layer, *[bufs[name] for name in uses(part)])
        layer.held.finish()


def stage(
    name, common, parts, who, slot, loads, stores, carried=None, after=(), kept=True, heads_step=3
):
    carried = carried or {}
    span, width, hidden, count = common.sizes
    shapes = shapes_of(span, width, hidden, common.cores)
    bufs = []
    for part in parts:
        bufs += [item for item in uses(part) if item not in bufs]
    pair = lambda item: item if isinstance(item, tuple) else (item, None)
    args = list(common.args)
    in_specs = [pl.BlockSpec(memory_space=SMEM)] * 2 + [pl.BlockSpec(memory_space=VMEM)] * 5
    plan = Bag(sources=[], targets=[], bufs=bufs, kept=kept, heads_step=heads_step)
    for item in loads:
        if item in bufs:
            array, row, *cols = pair(loads[item])
            args.append(array)
            plan.sources.append((item, row, cols[0] if cols else None))
    outs, aliases, extra = [], {}, []
    targets = [(item, *pair(key)) for item, key in stores.items()]
    for i, (item, key, row) in enumerate(targets):
        shape, kind = shapes[item]
        if row is not None:
            shape = (common.tokens,) + shape[1:]
        outs.append(jax.ShapeDtypeStruct(shape, kind))
        plan.targets.append((item, row))
        if key in carried:
            aliases[len(args) + len(extra)] = i
            extra.append(carried[key])
    extra += list(after)
    args += extra
    plan["extra"] = len(extra)
    in_specs += [pl.BlockSpec(memory_space=ANY)] * (len(args) - len(in_specs))
    results = pl.pallas_call(
        partial(stage_kernel, common.sizes, parts, who, slot, plan),
        out_shape=outs,
        in_specs=in_specs,
        out_specs=[pl.BlockSpec(memory_space=ANY)] * len(outs),
        input_output_aliases=aliases,
        scratch_shapes=[pltpu.VMEM(*shapes[item]) for item in bufs]
        + [pltpu.SemaphoreType.DMA((32,))],
        compiler_params=pltpu.CompilerParams(vmem_limit_bytes=56 * 1024 * 1024),
        name=name,
    )(*args)
    return Bag({key: value for (_, key, _), value in zip(targets, results)})


def bits_of(count):
    bits = count.bit_length() - 1
    assert 1 << bits == count
    return bits


class Chunk:
    def __init__(self, axis, bits, size, settled=()):
        self.axis = axis
        self.bits = list(range(bits - 1, 0, -1))
        self.size = size
        self.settled = list(settled)
        self.terms = []

    def add(self, term, start=0):
        left = [bit for bit in self.bits if bit not in self.settled]
        self.terms.append((term.reshape((2,) * len(left) + term.shape[-2:]), left, start))

    def take(self, term, start, left, flip):
        me = lax.axis_index(self.axis)
        side = lambda bit: 1 - ((me >> bit) & 1) if bit == flip else (me >> bit) & 1
        starts = [side(bit) if bit in self.settled else 0 for bit in left]
        sizes = [1 if bit in self.settled else 2 for bit in left]
        cols = term.shape[-1]
        piece = lax.dynamic_slice(term, starts + [start, 0], sizes + [self.size, cols])
        open_bits = [2] * (len(self.bits) - len(self.settled))
        return piece.reshape(open_bits + [self.size, cols]).astype(F32)

    def split(self, bit):
        self.settled.append(bit)
        return sum(self.take(term, start, left, bit) for term, left, start in self.terms).astype(
            BF16
        )

    def total(self):
        return sum(self.take(term, start, left, None) for term, left, start in self.terms)


def exchange(block, axis, bit):
    count = lax.axis_size(axis)
    return lax.ppermute(block, axis, [(i, i ^ (1 << bit)) for i in range(count)])


def join(*items):
    return lax.optimization_barrier(items)


def angle_table(span):
    half = HEAD // 2
    freqs = np.exp(-math.log(10000.0) * np.arange(half, dtype=np.float32) / half)
    phase = np.arange(span, dtype=np.float32)[:, None] * freqs.astype(np.float32)[None, :]
    cos_part, sin_part = np.cos(phase), np.sin(phase)
    return np.stack(
        [
            np.concatenate([cos_part] * 4, axis=1),
            np.concatenate([-sin_part, sin_part] * 2, axis=1),
        ]
    ).astype(np.float32)


def per_device(
    ends_in,
    lengths,
    times,
    norm_gain,
    attend_in,
    attend_out,
    time_weight,
    time_bias,
    expand_weight,
    expand_bias,
    reduce_weight,
    reduce_bias,
):
    local = ends_in[0]
    micro = lengths.shape[1]
    assert micro == 2
    width = local.shape[1]
    span = local.shape[0] // micro
    hidden = expand_weight.shape[2]
    count = lax.axis_size("rep")
    section = lax.axis_index("section")
    rank = lax.axis_index("rep")
    core = rank & 1
    steps = jnp.exp(-math.log(10000.0) * jnp.arange(EMB // 2, dtype=F32) / (EMB // 2))
    turn = times.reshape(micro * SEGS, 1).astype(F32) * steps
    embed = jnp.concatenate([jnp.cos(turn), jnp.sin(turn)], axis=1)
    mods = jnp.dot(
        embed, time_weight[0].astype(F32), precision=lax.Precision.HIGHEST
    ) + time_bias.astype(F32)
    fused = width // count % 16 == 0 and TILE % (hidden // count) == 0 and count >= 16
    common = Bag(
        args=(
            lengths[0],
            section.reshape(1),
            mods,
            jnp.asarray(angle_table(span)),
            norm_gain,
            expand_bias,
            reduce_bias,
        ),
        sizes=(span, width, hidden, count),
        tokens=local.shape[0],
        cores=2 if fused else 1,
    )
    weights = Bag(
        win=attend_in[0], wout=attend_out[0], wex=expand_weight[0], wre=reduce_weight[0]
    )
    rows = [(local, slot * span) for slot in range(micro)]
    same = lambda *names: {name: name for name in names}
    whole = same("left", "bg", "pa", "jg")
    run = partial(stage, common=common)
    both = (forward, output, mlp, copy_agrad, attend)
    over = lambda block, route: lax.ppermute(block, "section", route)
    swap = lambda block, bit: exchange(block, "rep", bit)
    a = run(
        "first_0",
        parts=(forward,),
        who=0,
        slot=0,
        loads=dict(xv=rows[0], **weights),
        stores=dict(result="leave"),
        kept=False,
    )
    came_0 = over(a.leave, [(0, 1)])
    b = run(
        "first_1",
        parts=(forward,),
        who=0,
        slot=1,
        loads=dict(xv=rows[1], **weights),
        stores=same("result", "left", "qkv", "probs", "middle", "slope", "branch"),
        after=(a.leave,),
        heads_step=1,
    )
    came_1 = over(b.result, [(0, 1)])
    x = run(
        "second_0",
        parts=both,
        who=1,
        slot=0,
        loads=dict(xv=came_0, dyv=rows[0], **weights),
        stores=dict(whole, result=("ends", 0), leave="leave"),
        after=(b.result,),
    )
    back_0 = over(x.leave, [(1, 0)])
    y = run(
        "second_1",
        parts=both,
        who=1,
        slot=1,
        loads=dict(xv=came_1, dyv=rows[1], **weights),
        stores=dict(whole, result=("ends", span), leave="leave"),
        carried=dict(b, ends=x.ends),
        after=(x.leave,),
    )
    back_1 = over(y.leave, [(1, 0)])
    x = run(
        "back_0",
        parts=both,
        who=0,
        slot=0,
        loads=dict(xv=rows[0], dyv=back_0, **weights),
        stores=dict(whole, leave=("ends", 0)),
        carried=dict(x, ends=y.ends),
        after=(y.leave,),
    )
    if fused:
        side = lambda item: lax.dynamic_index_in_dim(item, 1 - core, 0, keepdims=False)
        lefts = [x.left, y.left, swap(side(x.left), 0), swap(side(y.left), 0)]
        others = [swap(item, 0) for item in (x.bg, x.pa, x.jg)]
        embeds = (embed.T, swap(embed.T, 0))
    gates = mods[SEGS : 2 * SEGS, 2 * width :]
    gates = jnp.where(lengths[0, 1, 0] == span, gates[:1], gates)
    cotan = back_1.astype(F32).reshape(SEGS, -1, width)
    made = (cotan * gates[:, None]).reshape(span, width).astype(BF16)
    bg_1 = jnp.where(section == 0, made, y.bg)
    if fused:
        bg_1_other = swap(bg_1, 0)
    part = run(
        "back_1_mlp",
        parts=(mlp,),
        who=0,
        slot=1,
        loads=dict(
            bg=bg_1,
            wre=weights.wre,
            slope=b.slope,
            wex=weights.wex,
            middle=b.middle,
            dyv=back_1,
            branch=b.branch,
        ),
        stores=same("pa", "middle_grad"),
        carried=y,
    )
    pa_1 = part.pa
    bits = bits_of(count)
    term = partial(term_call, sizes=common.sizes, core=core, rank=rank)
    lines = width // count
    deep = EMB // count
    sizes = (hidden // count, hidden // count + lines + 3 * deep + TAIL_ROWS, 3 * lines + GAIN_ROWS)
    bases = left_bases(width, hidden)

    def last_attend(after):
        return run(
            "back_1_attend",
            parts=(attend,),
            who=0,
            slot=1,
            loads=dict(
                agrad=(pa_1, None, (hidden, width)),
                wout=weights.wout,
                probs=b.probs,
                qkv=b.qkv,
                win=weights.win,
                xv=rows[1],
                middle_grad=part.middle_grad,
            ),
            stores=dict(jg="jg", leave=("ends", span)),
            carried=dict(y, ends=x.ends),
            after=after,
        )

    def pair_of(size, first):
        cut = size // 2 if fused else size // 32 * 16
        one = Chunk("rep", bits, cut, (1,) if fused else ())
        two = Chunk("rep", bits, size - cut, (2,) if fused else ())
        if fused:
            send_1, keep_1, send_2, keep_2 = first
            one.add(keep_1)
            two.add(keep_2)
            return one, two, send_1, send_2
        view = first.reshape((count // 2, 2) + first.shape[1:])
        cut = lambda at: lax.dynamic_index_in_dim(view, at, 1, keepdims=False)
        came = swap(cut(1 - core).astype(BF16), 0)
        for item in (cut(core), came):
            one.add(item)
            two.add(item, one.size)
        return one, two, one.split(1), two.split(2)

    if fused:
        pa_other = swap(pa_1, 0)
        sent = term(
            "term_reduce",
            term_reduce,
            lines=sizes[0],
            base=bases[0],
            rows=hidden // 2,
            lefts=lefts,
            rights=[x.bg, bg_1, others[0], bg_1_other],
            after=(pa_1,),
        )
        r1, r2, send_1, send_2 = pair_of(sizes[0], sent)
        came_r1, came_r2 = swap(send_1, 1), swap(send_2, 2)
        sent = term(
            "term_expand",
            term_expand,
            lines=sizes[1],
            base=bases[1],
            rows=width,
            lefts=lefts,
            rights=[x.pa, pa_1, others[1], pa_other],
            embeds=embeds,
            after=(send_1, send_2),
        )
        last = last_attend((sent[0],))
        came_r1, came_r2, jg_1, *sent = join(came_r1, came_r2, last.jg, *sent)
        jg_other = swap(jg_1, 0)
        e1, e2, send_1, send_2 = pair_of(sizes[1], sent)
        came_e1, came_e2 = swap(send_1, 1), swap(send_2, 2)
        r1.add(came_r1)
        r2.add(came_r2)
        send_1, send_2 = r1.split(2), r2.split(1)
        came_r1, came_r2 = swap(send_1, 2), swap(send_2, 1)
        sent = term(
            "term_attend",
            term_attend,
            lines=sizes[2],
            base=bases[3],
            rows=width // 2,
            lefts=lefts,
            rights=[x.jg, jg_1, others[2], jg_other],
            after=(send_1, send_2),
        )
        came_e1, came_e2, came_r1, came_r2, *sent = join(
            came_e1, came_e2, came_r1, came_r2, *sent
        )
        a1, a2, send_1, send_2 = pair_of(sizes[2], sent)
    else:
        last = last_attend(())
        rights = [(x.bg, bg_1), (x.pa, pa_1), (x.jg, last.jg)]
        totals = plain_pieces((x.left, y.left), rights, embed.T, common.sizes)
        r1, r2, send_1, send_2 = pair_of(sizes[0], totals[0])
        r1.add(swap(send_1, 1))
        r2.add(swap(send_2, 2))
        came_r1, came_r2 = swap(r1.split(2), 2), swap(r2.split(1), 1)
        e1, e2, send_1, send_2 = pair_of(sizes[1], totals[1])
        came_e1, came_e2 = swap(send_1, 1), swap(send_2, 2)
        a1, a2, send_1, send_2 = pair_of(sizes[2], totals[2])
    ends = last.ends
    came_a1, came_a2 = swap(send_1, 1), swap(send_2, 2)
    r1.add(came_r1)
    r2.add(came_r2)
    block_r = jnp.concatenate([r1.split(3), r2.split(3)], axis=-2)
    came_r = swap(block_r, 3)
    e1.add(came_e1)
    e2.add(came_e2)
    send_1, send_2 = e1.split(2), e2.split(1)
    came_e1, came_e2 = swap(send_1, 2), swap(send_2, 1)
    came_a1, came_a2, _, _, _ = join(came_a1, came_a2, send_1, send_2, block_r)
    a1.add(came_a1)
    a2.add(came_a2)
    send_1, send_2 = a1.split(2), a2.split(1)
    came_a1, came_a2 = swap(send_1, 2), swap(send_2, 1)
    came_e1, came_e2, _, _ = join(came_e1, came_e2, send_1, send_2)
    e1.add(came_e1)
    e2.add(came_e2)
    block_e = jnp.concatenate([e1.split(3), e2.split(3)], axis=-2)
    came_e = swap(block_e, 3)
    came_r, _ = join(came_r, block_e)
    r1.add(came_r[..., : r1.size, :])
    r2.add(came_r[..., r1.size :, :])
    came_a1, came_a2, _ = join(came_a1, came_a2, came_r)
    a1.add(came_a1)
    a2.add(came_a2)
    block_a = jnp.concatenate([a1.split(3), a2.split(3)], axis=-2)
    came_a = swap(block_a, 3)
    came_e, _ = join(came_e, block_a)
    e1.add(came_e[..., : e1.size, :])
    e2.add(came_e[..., e1.size :, :])
    a1.add(came_a[..., : a1.size, :])
    a2.add(came_a[..., a1.size :, :])
    for bit in range(4, bits):
        for chunk in (r1, r2, e1, e2, a1, a2):
            chunk.add(swap(chunk.split(bit), bit))
    share_r, share_e, share_a = (
        jnp.concatenate([one.total(), two.total()]) for one, two in ((r1, r2), (e1, e2), (a1, a2))
    )
    tall = hidden // width
    side = lambda item, n, size: jnp.concatenate(
        [item[i * size : (i + 1) * size] for i in range(n)], axis=1
    )
    at_o = tall * lines
    at_t = at_o + lines
    small = share_e[at_t + 3 * deep :]
    flat = lambda item, first, n: lax.dynamic_slice_in_dim(
        item[first : first + n].reshape(-1), rank * (n * width // count), n * width // count
    )
    results = (
        flat(share_a, 3 * lines, 1),
        side(share_a, 3, lines),
        share_e[at_o:at_t],
        side(share_e[at_t:], 3, deep),
        flat(small, 1, 3),
        side(share_e, tall, lines),
        flat(small, 4, tall),
        share_r,
        flat(small, 0, 1),
    )
    return (ends[None],) + tuple(piece[None] for piece in results)


def solution(mesh):
    return jax.shard_map(
        per_device,
        mesh=mesh,
        in_specs=(
            P("section", "rep", None),
            P("rep", None, None),
            P("rep", None, None),
            P("section", None),
            P("section", None, None),
            P("section", None, None),
            P("section", None, None),
            P("section", None),
            P("section", None, None),
            P("section", None),
            P("section", None, None),
            P("section", None),
        ),
        out_specs=(
            P("section", "rep", None),
            P("section", "rep"),
            P("section", "rep", None),
            P("section", "rep", None),
            P("section", "rep", None),
            P("section", "rep"),
            P("section", "rep", None),
            P("section", "rep"),
            P("section", "rep", None),
            P("section", "rep"),
        ),
        check_vma=False,
    )
```

```python
from functools import partial
import inspect
import math

import jax
import jax.numpy as jnp
import numpy as np
from jax import lax
from jax.experimental import pallas as pl
from jax.experimental.pallas import tpu as pltpu
from jax.sharding import PartitionSpec as P

HEADS = 12
HEAD = 64
EMB = 128
SEGS = 4
ANY = pl.ANY
VMEM = pltpu.MemorySpace.VMEM
SMEM = pltpu.MemorySpace.SMEM
F32 = jnp.float32
BF16 = jnp.bfloat16
ROOT_HALF = 0.7071067811865476
ROOT_TAU = 0.3989422804014327
TILE = 384
TAIL_ROWS = 24
GAIN_ROWS = 16
EXTRA = 16


class Bag(dict):
    __getattr__ = dict.__getitem__


def dot(left, right, left_dim=1, right_dim=0):
    return lax.dot_general(
        left, right, (((left_dim,), (right_dim,)), ((), ())), preferred_element_type=F32
    )


def repeat(count, body):
    for i in range(count):
        body(i)


def steps_of(count, size, body):
    def several(i, _):
        for j in range(size):
            body(size * i + j)
        return _

    lax.fori_loop(0, count // size, several, 0)


def lanes(index, size, start=0):
    if isinstance(index, int):
        return slice(start + index * size, start + (index + 1) * size)
    return pl.ds(pl.multiple_of(start + index * size, size), size)


def swap_halves(values, low_half):
    forth = pltpu.roll(values, 128 - HEAD // 2, 1)
    back = pltpu.roll(values, HEAD // 2, 1)
    return jnp.where(low_half, forth, back)


def norm_parts(values):
    center = values - jnp.mean(values, axis=-1, keepdims=True)
    spread = jnp.mean(center * center, axis=-1, keepdims=True)
    factor = lax.rsqrt(spread + 1e-05)
    return center * factor, factor


def norm_back(grad, unit, factor):
    return factor * (
        grad
        - jnp.mean(grad, axis=-1, keepdims=True)
        - unit * jnp.mean(grad * unit, axis=-1, keepdims=True)
    )


class Held:
    def __init__(self, bufs, loads, stores, sems, pieces):
        self.bufs = bufs
        self.loads = loads
        self.stores = stores
        self.sems = sems
        self.pieces = pieces
        self.names = {id(buf): name for name, buf in bufs.items()}
        keys = [(name, j) for name in loads for j in range(self.parts_of(name))]
        self.spots = {key: n for n, key in enumerate(keys)}
        self.waiting = set(keys)
        self.pending = set(keys)
        self.leaving = {}

    def parts_of(self, name):
        return self.pieces[name][1] if name in self.pieces else 1

    def load(self, name, j):
        source, target = self.loads[name], self.bufs[name]
        if name in self.pieces:
            axis, count = self.pieces[name]
            size = target.shape[axis] // count
            at = (slice(None),) * axis + (pl.ds(j * size, size),)
            source, target = source.at[at], target.at[at]
        return pltpu.make_async_copy(source, target, self.sems.at[self.spots[(name, j)]])

    def store(self, name):
        return pltpu.make_async_copy(
            self.bufs[name], self.stores[name], self.sems.at[self.leaving[name]]
        )

    def keys(self, bufs, part):
        for buf in bufs:
            name = self.names[id(buf)]
            for j in range(self.parts_of(name)):
                if part in (None, j):
                    yield name, j

    def begin(self, *bufs, part=None):
        for key in self.keys(bufs, part):
            if key in self.waiting:
                self.waiting.remove(key)
                self.load(*key).start()

    def need(self, *bufs, part=None):
        self.begin(*bufs, part=part)
        for key in self.keys(bufs, part):
            if key in self.pending:
                self.pending.remove(key)
                self.load(*key).wait()

    def done(self, *bufs):
        for buf in bufs:
            name = self.names[id(buf)]
            if name in self.stores:
                self.leaving[name] = len(self.spots) + len(self.leaving)
                self.store(name).start()

    def finish(self):
        for name in self.leaving:
            self.store(name).wait()


class Layer:
    def __init__(self, sizes, slot, refs):
        self.span, self.width, self.hidden, self.count = sizes
        self.slot = slot
        lengths, section, self.mods, self.trig, self.gain, self.ebias, self.rbias = refs
        self.section = section[0]
        self.single = lengths[slot, 0] == self.span
        self.pairs = self.width // 128
        self.seg = self.span // SEGS
        self.step = self.width
        self.tiles = self.hidden // self.step
        place = lax.broadcasted_iota(jnp.int32, (self.span, 128), 1)
        self.low_half = place % HEAD < HEAD // 2
        self.low_head = place < HEAD
        row = lax.broadcasted_iota(jnp.int32, (1, 128), 1) // HEAD
        self.head_row = [(row == i).astype(F32).astype(BF16) for i in range(2)]
        self.blocks = [(b, slice(b * self.seg, (b + 1) * self.seg)) for b in range(SEGS)]

    def trig_pair(self):
        cos_all, sin_all = self.trig[0], self.trig[1]
        cos_cut = jnp.concatenate([cos_all[: self.seg]] * SEGS, axis=0)
        sin_cut = jnp.concatenate([sin_all[: self.seg]] * SEGS, axis=0)
        return jnp.where(self.single, cos_all, cos_cut), jnp.where(self.single, sin_all, sin_cut)

    def mod_row(self, block, part):
        row = self.slot * SEGS + jnp.where(self.single, 0, block)
        return self.mods[pl.ds(row, 1), part * self.width : (part + 1) * self.width]

    def add_segment(self, small, block, at, sums):
        row = 2 + jnp.where(self.single, 0, block)
        small[pl.ds(row, 1), at * self.width : (at + 1) * self.width] += sums

    def put_left(self, left, base, first, values):
        turned = values.T
        lines = (self.hidden if base == 0 else self.width) // self.count
        if left.shape[0] == 1:
            left[0, 2 * base + first : 2 * base + first + turned.shape[0]] = turned
            return
        for block in range(first // lines, (first + turned.shape[0]) // lines):
            at = block * lines - first
            to = base + block // 2 * lines
            left[block % 2, to : to + lines] = turned[at : at + lines]

    def put_active(self, left, j, values):
        turned = values.T
        if left.shape[0] == 1:
            left[0, lanes(j, self.step)] = turned
            return
        lines = self.hidden // self.count
        per = self.step // lines
        for n in range(per):
            to = lanes(j, lines * (per // 2), n // 2 * lines)
            to = slice(to.start, to.start + lines) if isinstance(j, int) else pl.ds(to.start, lines)
            left[n % 2, to] = turned[n * lines : (n + 1) * lines]

    def thirds(self, index):
        return [lanes(index, 128, p * self.width) for p in range(3)]


def left_bases(width, hidden):
    return 0, hidden // 2, (hidden + width) // 2, (hidden + 2 * width) // 2


def forward(
    k, xv, win, wout, wex, wre, left, qkv, probs, middle, slope, branch, result, bias, normed,
    mixed, modded,
):
    span, width, held = k.span, k.width, k.held
    _, at_modded, at_mixed, at_normed = left_bases(width, k.hidden)
    held.begin(xv, win)
    held.need(xv)
    unit, _ = norm_parts(xv[...].astype(F32))
    normed[...] = (unit * k.gain[...].astype(F32)).astype(BF16)
    across = lax.broadcasted_iota(jnp.int32, (span, span), 0) // k.seg
    down = lax.broadcasted_iota(jnp.int32, (span, span), 1) // k.seg
    bias[...] = jnp.where((across == down) | k.single, 0.0, -1e30)
    held.need(win)
    held.begin(wout, wex, wre)
    cos_part, sin_part = k.trig_pair()
    for tile, factor in ((0, 0.125), (1, 1.0)):
        for i in range(width // 256):
            at = lanes(i, 256, tile * width)
            joint = dot(normed[...], win[:, at])
            outs = []
            for piece in (joint[:, :128], joint[:, 128:]):
                turned = piece * cos_part + swap_halves(piece, k.low_half) * sin_part
                outs.append((turned * factor).astype(BF16))
            qkv[:, at] = jnp.concatenate(outs, axis=1)
    qkv[:, 2 * width :] = dot(normed[...], win[:, 2 * width :]).astype(BF16)
    held.done(qkv)
    if k.kept:
        k.put_left(left, at_normed, 0, normed[...])

    def heads(i):
        at = k.thirds(i)
        query, key, value = (qkv[:, a] for a in at)
        outs = []
        for h in range(2):
            scores = dot(key * k.head_row[h], query, 1, 1) + bias[...]
            top = jnp.max(scores, axis=0, keepdims=True)
            raised = jnp.exp(scores - top)
            total = jnp.sum(raised, axis=0, keepdims=True)
            prob = raised * (1.0 / total)
            if k.kept:
                probs[2 * i + h] = prob
            outs.append(dot(prob.astype(BF16), value, 0, 0))
        mixed[:, at[0]] = jnp.where(k.low_head, outs[0], outs[1]).astype(BF16)

    steps_of(k.pairs, k.heads_step, heads)
    held.done(probs)
    held.need(wout)
    middle[...] = xv[...].astype(F32) + dot(mixed[...], wout[...])
    held.done(middle)
    if k.kept:
        k.put_left(left, at_mixed, 0, mixed[...])
    for b, rows in k.blocks:
        unit, _ = norm_parts(middle[rows])
        modded[rows] = (unit * (1.0 + k.mod_row(b, 0)) + k.mod_row(b, 1)).astype(BF16)
    if k.kept:
        k.put_left(left, at_modded, 0, modded[...])
    held.need(wex, wre)
    branch[...] = jnp.broadcast_to(k.rbias[...].astype(F32), (span, width))

    def feed(j):
        at = lanes(j, k.step)
        pre = dot(modded[...], wex[:, at]) + k.ebias[:, at].astype(F32)
        area = 0.5 + 0.5 * lax.erf(pre * ROOT_HALF)
        out = (pre * area).astype(BF16)
        if k.kept:
            slope[:, at] = area + pre * (jnp.exp(pre * pre * -0.5) * ROOT_TAU)
            k.put_active(left, j, out)
        branch[...] += dot(out, wre[at, :])

    if k.heads_step == 1:
        steps_of(k.tiles, 1, feed)
    else:
        repeat(k.tiles, feed)
    held.done(slope, left, branch)
    for b, rows in k.blocks:
        result[rows] = (middle[rows] + k.mod_row(b, 2) * branch[rows]).astype(BF16)
    held.done(result)


def output(k, dyv, bg):
    k.held.need(dyv)
    for b, rows in k.blocks:
        bg[rows] = (dyv[rows].astype(F32) * k.mod_row(b, 2)).astype(BF16)
    k.held.done(bg)


def mlp(k, wre, wex, bg, slope, middle, branch, dyv, pa, middle_grad, small, acc):
    span, width, hidden, held = k.span, k.width, k.hidden, k.held
    small[...] = jnp.zeros(small.shape, F32)
    acc[...] = jnp.zeros(acc.shape, F32)
    held.begin(bg)
    for j in range(k.tiles):
        held.begin(wre, slope, wex, part=j)
    held.begin(middle, dyv, branch)
    held.need(bg)

    def feed(j):
        at = lanes(j, k.step)
        held.need(wre, slope, wex, part=j)
        grad = dot(bg[...], wre[at, :], 1, 1)
        pre_grad = (slope[:, at] * grad).astype(BF16)
        pa[:span, at] = pre_grad
        small[0:1, at] = jnp.sum(pre_grad.astype(F32), axis=0, keepdims=True)
        acc[...] += dot(pre_grad, wex[:, at], 1, 1)

    repeat(k.tiles, feed)
    held.need(middle, dyv, branch)
    total = jnp.zeros((1, width), F32)
    for b, rows in k.blocks:
        cotan = dyv[rows].astype(F32)
        total += jnp.sum(bg[rows].astype(F32), axis=0, keepdims=True)
        grad = acc[rows]
        unit, factor = norm_parts(middle[rows])
        k.add_segment(small, b, 0, jnp.sum(grad * unit, axis=0, keepdims=True))
        k.add_segment(small, b, 1, jnp.sum(grad, axis=0, keepdims=True))
        k.add_segment(small, b, 2, jnp.sum(cotan * branch[rows], axis=0, keepdims=True))
        back = norm_back(grad * (1.0 + k.mod_row(b, 0)), unit, factor)
        full = cotan + back
        middle_grad[rows] = full
        pa[rows, hidden:] = full.astype(BF16)
    small[1:2, :width] = total
    pa[span:, :] = small[...].astype(BF16)
    held.done(pa, middle_grad)


def attend(
    k, wout, win, agrad, probs, qkv, xv, middle_grad, jg, leave, mixed_grad, acc
):
    span, held = k.span, k.held
    held.need(agrad, wout)
    held.begin(probs, qkv)
    mixed_grad[...] = dot(agrad[...], wout[...], 1, 1).astype(BF16)
    held.need(probs, qkv)
    held.begin(win, xv, middle_grad)
    cos_part, sin_part = k.trig_pair()

    def heads(i):
        at = k.thirds(i)
        query, key, value = (qkv[:, a] for a in at)
        out_grad = mixed_grad[:, at[0]]
        parts = []
        for h in range(2):
            prob = probs[2 * i + h]
            pull = dot(value * k.head_row[h], out_grad, 1, 1)
            shared = jnp.sum(prob * pull, axis=0, keepdims=True)
            score_grad = (prob * (pull - shared)).astype(BF16)
            parts.append(
                (
                    dot(score_grad, key, 0, 0),
                    dot(score_grad, query),
                    dot(prob.astype(BF16), out_grad),
                )
            )
        for p in range(3):
            grad = jnp.where(k.low_head, parts[0][p], parts[1][p])
            if p < 2:
                grad = grad * cos_part - swap_halves(grad, k.low_half) * sin_part
                if p == 0:
                    grad = grad * 0.125
            jg[:span, at[p]] = grad.astype(BF16)

    steps_of(k.pairs, k.heads_step, heads)
    held.need(win, xv, middle_grad)
    acc[...] = dot(jg[:span, :], win[...], 1, 1)
    total = jnp.zeros((1, k.width), F32)
    for b, rows in k.blocks:
        grad = acc[rows]
        unit, factor = norm_parts(xv[rows].astype(F32))
        total += jnp.sum(grad * unit, axis=0, keepdims=True)
        back = norm_back(grad * k.gain[...].astype(F32), unit, factor)
        leave[rows] = (middle_grad[rows] + back).astype(BF16)
    below = jnp.concatenate([total, jnp.zeros((EXTRA - 1, k.width), F32)], axis=0)
    jg[span:, : k.width] = below.astype(BF16)
    jg[span:, k.width :] = jnp.zeros((EXTRA, 2 * k.width), BF16)
    held.done(jg, leave)


def copy_agrad(k, pa, agrad):
    agrad[...] = pa[: k.span, k.hidden :]


class Sums:
    def __init__(self, ranks, full, outs, sems):
        self.full = full
        self.own = [((ranks[0] >> bit) & 1) == 0 for bit in (1, 2)]
        self.bufs = outs[:4]
        self.targets = outs[4:]
        self.sems = sems
        self.half = full.shape[1] // 2
        self.copies = []

    def put(self, block, at, values):
        self.full[block, at] = values

    def settle(self, which, groups):
        send, keep = self.bufs[2 * which : 2 * which + 2]
        at = slice(which * self.half, (which + 1) * self.half)
        apart = 1 + which
        for group in groups:
            for n in range(2):
                first = 4 * group + (2 * n if which == 0 else n)
                even, odd = self.full[first, at], self.full[first + apart, at]
                send[2 * group + n] = jnp.where(self.own[which], odd, even).astype(BF16)
                keep[2 * group + n] = jnp.where(self.own[which], even, odd)
            spot = pl.ds(2 * group, 2)
            for n in range(2 * which, 2 * which + 2):
                copy = pltpu.make_async_copy(
                    self.bufs[n].at[spot], self.targets[n].at[spot], self.sems.at[len(self.copies)]
                )
                copy.start()
                self.copies.append(copy)

    def finish(self):
        for copy in self.copies:
            copy.wait()


def term_reduce(k, sums, left, right):
    lines = k.hidden // k.count
    per = TILE // lines
    for tile in range(k.hidden // 2 // TILE):
        k.arrive(tile)
        total = dot(left[tile * TILE : (tile + 1) * TILE], right[...])
        for n in range(per):
            sums.put(tile * per + n, slice(0, lines), total[n * lines : (n + 1) * lines])
        if (tile + 1) * per % 4 == 0:
            group = ((tile + 1) * per // 4 - 1,)
            sums.settle(0, group)
            sums.settle(1, group)


def square_terms(k, sums, left, right, cols, part):
    lines = k.width // k.count
    total = dot(left, right[: 4 * k.span, cols])
    for n in range(k.count // 2):
        sums.put(n, slice(part * lines, (part + 1) * lines), total[n * lines : (n + 1) * lines])


def term_expand(k, sums, left, right):
    width, hidden, span = k.width, k.hidden, k.span
    groups = range(k.count // 8)
    tall = hidden // width
    lines = width // k.count
    rows = width // 2
    half = sums.half
    settled = False
    for col in range(tall + 1):
        k.arrive(col)
        part = left[:rows] if col < tall else left[rows:]
        square_terms(k, sums, part, right, slice(col * width, (col + 1) * width), col)
        if (col + 1) * lines >= half and not settled:
            sums.settle(0, groups)
            settled = True
    smalls = [k.small[n].astype(F32) for n in range(4)]
    times = sum(
        k.embeds[n // 2][:, n % 2 * SEGS + s : n % 2 * SEGS + s + 1]
        * smalls[n][2 + s : 3 + s, : 3 * width]
        for n in range(4)
        for s in range(SEGS)
    )
    both = sum(smalls)
    seq_sum = jnp.sum(both[2 : 2 + SEGS, : 3 * width], axis=0, keepdims=True)
    lines_v = k.lines
    lines_v[...] = jnp.zeros(lines_v.shape, F32)
    lines_v[0:1] = both[1:2, :width]
    for n in range(3):
        lines_v[1 + n : 2 + n] = seq_sum[:, n * width : (n + 1) * width]
    for n in range(tall):
        lines_v[4 + n : 5 + n] = both[0:1, n * width : (n + 1) * width]
    deep = EMB // k.count
    first = (tall + 1) * lines
    for g in range(k.count // 2):
        for side in range(2):

            @pl.when(k.core == side)
            def _(at=(2 * g + side) * deep, g=g):
                for p in range(3):
                    to = first + p * deep
                    piece = times[at : at + deep, p * width : (p + 1) * width]
                    sums.put(g, slice(to, to + deep), piece)

        sums.put(g, slice(first + 3 * deep, 2 * half), lines_v[...])
    sums.settle(1, groups)


def term_attend(k, sums, left, right):
    width = k.width
    groups = range(k.count // 8)
    lines = width // k.count
    settled = False
    for col in range(3):
        k.arrive(col)
        square_terms(k, sums, left[...], right, slice(col * width, (col + 1) * width), col)
        if (col + 1) * lines >= sums.half and not settled:
            sums.settle(0, groups)
            settled = True
    gain = sum(k.small[n].astype(F32) for n in range(4))[:, :width]
    for g in range(k.count // 2):
        sums.put(g, slice(3 * lines, 3 * lines + GAIN_ROWS), gain)
    sums.settle(1, groups)


def load_terms(k, refs, bufs, base, sems):
    left_v, right_v, small_v = bufs
    rows, cols = left_v.shape[0], right_v.shape[1]
    tall = rows // TILE if small_v is None else 1
    wide = cols // k.width
    groups = []
    for i in range(tall):
        for j in range(wide):
            copies = []
            for n, (left, right) in enumerate(zip(refs[:4], refs[4:8])):
                source = left.at[k.core] if n < 2 else left
                tokens = pl.ds(n * k.span, k.span)
                part = pl.ds(i * (rows // tall), rows // tall)
                from_part = pl.ds(base + i * (rows // tall), rows // tall)
                at = pl.ds(j * k.width, k.width)
                if j == 0:
                    copies.append((source.at[from_part], left_v.at[part, tokens]))
                if i == 0:
                    copies.append((right.at[pl.ds(0, k.span), at], right_v.at[tokens, at]))
                if small_v is not None and j == wide - 1:
                    copies.append((right.at[pl.ds(k.span, EXTRA)], small_v.at[n]))
            groups.append(copies)
    made, count = [], 0
    for copies in groups:
        made.append([])
        for pair in copies:
            made[-1].append(pltpu.make_async_copy(*pair, sems.at[count]))
            made[-1][-1].start()
            count += 1
    return made


class Terms:
    def __init__(self, sizes, core):
        self.span, self.width, self.hidden, self.count = sizes
        self.core = core[0]

    def arrive(self, group):
        for copy in self.groups[group]:
            copy.wait()


def term_kernel(sizes, body, base, extra, *refs):
    refs = list(refs)
    core, rank = refs[:2]
    k = Terms(sizes, core)
    pos = 2
    if body is term_expand:
        k.embeds = refs[pos : pos + 2]
        pos += 2
    sources = refs[pos : pos + 8]
    pos += 8 + extra
    targets = refs[pos : pos + 4]
    pos += 4
    left_v, right_v, full, *outs = refs[pos : pos + 7]
    pos += 7
    k.small = None
    if body is not term_reduce:
        k.small, k.lines = refs[pos : pos + 2]
        pos += 2
    sems, out_sems = refs[pos:]
    k.groups = load_terms(k, sources, (left_v, right_v, k.small), base, sems)
    sums = Sums(rank, full, outs + targets, out_sems)
    body(k, sums, left_v, right_v)
    sums.finish()


def term_call(name, body, sizes, lines, base, rows, core, rank, lefts, rights, embeds=(), after=()):
    span, width, hidden, count = sizes
    blocks = count // 2
    cols = rights[0].shape[1]
    half = lines // 2
    outs = [((blocks // 2, half, width), kind) for kind in (BF16, F32)] * 2
    scratch = [
        ((rows, 4 * span), BF16),
        ((4 * span, cols), BF16),
        ((blocks, lines, width), F32),
        *outs,
    ]
    if body is not term_reduce:
        scratch += [((4, EXTRA, cols), BF16), ((TAIL_ROWS, width), F32)]
    args = [core.reshape(1), rank.reshape(1), *embeds, *lefts, *rights, *after]
    in_specs = [pl.BlockSpec(memory_space=SMEM)] * 2
    in_specs += [pl.BlockSpec(memory_space=VMEM)] * len(embeds)
    in_specs += [pl.BlockSpec(memory_space=ANY)] * (8 + len(after))
    return pl.pallas_call(
        partial(term_kernel, sizes, body, base, len(after)),
        out_shape=[jax.ShapeDtypeStruct(*item) for item in outs],
        in_specs=in_specs,
        out_specs=[pl.BlockSpec(memory_space=ANY)] * 4,
        scratch_shapes=[pltpu.VMEM(*item) for item in scratch]
        + [pltpu.SemaphoreType.DMA((32,)), pltpu.SemaphoreType.DMA((8,))],
        compiler_params=pltpu.CompilerParams(vmem_limit_bytes=56 * 1024 * 1024),
        name=name,
    )(*args)


def plain_pieces(lefts, rights, embed, sizes):
    span, width, hidden, count = sizes
    bg, pa, jg = rights
    bases = [2 * base for base in left_bases(width, hidden)]

    def blocks(base, rows, right):
        total = sum(dot(a[0, base : base + rows], b) for a, b in zip(lefts, right))
        parts = [total[:, i : i + width] for i in range(0, total.shape[1], width)]
        return [part.reshape(count, -1, width) for part in parts]

    take = lambda items, cols: [item[:span, cols] for item in items]
    reduce = blocks(bases[0], hidden, bg)
    expand = blocks(bases[1], width, take(pa, slice(0, hidden)))
    expand += blocks(bases[2], width, take(pa, slice(hidden, hidden + width)))
    last = blocks(bases[3], width, take(jg, slice(None)))
    small = [item[span:].astype(F32) for item in pa]
    seqs = jnp.concatenate([item[2 : 2 + SEGS, : 3 * width] for item in small])
    times = jnp.dot(embed, seqs, precision=lax.Precision.HIGHEST)
    expand += [times[:, i * width : (i + 1) * width].reshape(count, -1, width) for i in range(3)]
    lines = jnp.concatenate(
        [
            sum(item[1:2, :width] for item in small),
            jnp.sum(seqs, axis=0).reshape(-1, width),
            sum(item[0, :hidden] for item in small).reshape(-1, width),
        ]
    )
    lines = jnp.pad(lines, ((0, TAIL_ROWS - lines.shape[0]), (0, 0)))
    gain = sum(item[span:, :width].astype(F32) for item in jg)
    expand.append(jnp.broadcast_to(lines, (count,) + lines.shape))
    last.append(jnp.broadcast_to(gain, (count,) + gain.shape))
    return [jnp.concatenate(item, axis=1) for item in (reduce, expand, last)]


def shapes_of(span, width, hidden, cores):
    tok = lambda cols, kind=BF16: ((span, cols), kind)
    below = lambda cols: ((span + EXTRA, cols), BF16)
    return dict(
        xv=tok(width),
        dyv=tok(width),
        win=((width, 3 * width), BF16),
        wout=((width, width), BF16),
        wex=((width, hidden), BF16),
        wre=((hidden, width), BF16),
        left=((cores, (hidden + 3 * width) // cores, span), BF16),
        normed=tok(width),
        qkv=tok(3 * width),
        probs=((HEADS, span, span), F32),
        mixed=tok(width),
        middle=tok(width, F32),
        modded=tok(width),
        slope=tok(hidden, F32),
        branch=tok(width, F32),
        result=tok(width),
        bg=tok(width),
        pa=below(hidden + width),
        jg=below(3 * width),
        agrad=tok(width),
        mixed_grad=tok(width),
        middle_grad=tok(width, F32),
        leave=tok(width),
        acc=tok(width, F32),
        bias=tok(span, F32),
        small=((EXTRA, hidden + width), F32),
    )


def uses(part):
    return list(inspect.signature(part).parameters)[1:]


def stage_kernel(sizes, parts, who, slot, plan, *refs):
    refs = list(refs)
    layer = Layer(sizes, slot, refs[:7])
    span = layer.span
    pos = 7
    loads = {}
    for name, row, cols in plan.sources:
        ref = refs[pos]
        if cols is not None:
            ref = ref.at[pl.ds(0, span), pl.ds(*cols)]
        elif row is not None:
            ref = ref.at[pl.ds(row, span)]
        loads[name] = ref
        pos += 1
    pos += plan.extra
    stores = {}
    for name, row in plan.targets:
        stores[name] = refs[pos] if row is None else refs[pos].at[pl.ds(row, span)]
        pos += 1
    bufs = {}
    for name in plan.bufs:
        bufs[name] = refs[pos]
        pos += 1
    layer.held = Held(bufs, loads, stores, refs[pos], plan.pieces)
    layer.kept = plan.kept
    layer.heads_step = plan.heads_step

    @pl.when(layer.section == who)
    def _():
        for part in parts:
            part(layer, *[bufs[name] for name in uses(part)])
        layer.held.finish()


def stage(
    name, common, parts, who, slot, loads, stores, carried=None, after=(), kept=True, heads_step=3,
    pieces=None,
):
    carried = carried or {}
    span, width, hidden, count = common.sizes
    shapes = shapes_of(span, width, hidden, common.cores)
    bufs = []
    for part in parts:
        bufs += [item for item in uses(part) if item not in bufs]
    pair = lambda item: item if isinstance(item, tuple) else (item, None)
    args = list(common.args)
    in_specs = [pl.BlockSpec(memory_space=SMEM)] * 2 + [pl.BlockSpec(memory_space=VMEM)] * 5
    plan = Bag(sources=[], targets=[], bufs=bufs, kept=kept, heads_step=heads_step)
    plan["pieces"] = pieces or {}
    for item in loads:
        if item in bufs:
            array, row, *cols = pair(loads[item])
            args.append(array)
            plan.sources.append((item, row, cols[0] if cols else None))
    outs, aliases, extra = [], {}, []
    targets = [(item, *pair(key)) for item, key in stores.items()]
    for i, (item, key, row) in enumerate(targets):
        shape, kind = shapes[item]
        if row is not None:
            shape = (common.tokens,) + shape[1:]
        outs.append(jax.ShapeDtypeStruct(shape, kind))
        plan.targets.append((item, row))
        if key in carried:
            aliases[len(args) + len(extra)] = i
            extra.append(carried[key])
    extra += list(after)
    args += extra
    plan["extra"] = len(extra)
    in_specs += [pl.BlockSpec(memory_space=ANY)] * (len(args) - len(in_specs))
    results = pl.pallas_call(
        partial(stage_kernel, common.sizes, parts, who, slot, plan),
        out_shape=outs,
        in_specs=in_specs,
        out_specs=[pl.BlockSpec(memory_space=ANY)] * len(outs),
        input_output_aliases=aliases,
        scratch_shapes=[pltpu.VMEM(*shapes[item]) for item in bufs]
        + [pltpu.SemaphoreType.DMA((32,))],
        compiler_params=pltpu.CompilerParams(vmem_limit_bytes=56 * 1024 * 1024),
        name=name,
    )(*args)
    return Bag({key: value for (_, key, _), value in zip(targets, results)})


def bits_of(count):
    bits = count.bit_length() - 1
    assert 1 << bits == count
    return bits


class Chunk:
    def __init__(self, axis, bits, size, settled=()):
        self.axis = axis
        self.bits = list(range(bits - 1, 0, -1))
        self.size = size
        self.settled = list(settled)
        self.terms = []

    def add(self, term, start=0):
        left = [bit for bit in self.bits if bit not in self.settled]
        self.terms.append((term.reshape((2,) * len(left) + term.shape[-2:]), left, start))

    def take(self, term, start, left, flip):
        me = lax.axis_index(self.axis)
        side = lambda bit: 1 - ((me >> bit) & 1) if bit == flip else (me >> bit) & 1
        starts = [side(bit) if bit in self.settled else 0 for bit in left]
        sizes = [1 if bit in self.settled else 2 for bit in left]
        cols = term.shape[-1]
        piece = lax.dynamic_slice(term, starts + [start, 0], sizes + [self.size, cols])
        open_bits = [2] * (len(self.bits) - len(self.settled))
        return piece.reshape(open_bits + [self.size, cols]).astype(F32)

    def split(self, bit):
        self.settled.append(bit)
        return sum(self.take(term, start, left, bit) for term, left, start in self.terms).astype(
            BF16
        )

    def total(self):
        return sum(self.take(term, start, left, None) for term, left, start in self.terms)


def exchange(block, axis, bit):
    count = lax.axis_size(axis)
    return lax.ppermute(block, axis, [(i, i ^ (1 << bit)) for i in range(count)])


def join(*items):
    return lax.optimization_barrier(items)


def angle_table(span):
    half = HEAD // 2
    freqs = np.exp(-math.log(10000.0) * np.arange(half, dtype=np.float32) / half)
    phase = np.arange(span, dtype=np.float32)[:, None] * freqs.astype(np.float32)[None, :]
    cos_part, sin_part = np.cos(phase), np.sin(phase)
    return np.stack(
        [
            np.concatenate([cos_part] * 4, axis=1),
            np.concatenate([-sin_part, sin_part] * 2, axis=1),
        ]
    ).astype(np.float32)


def per_device(
    ends_in,
    lengths,
    times,
    norm_gain,
    attend_in,
    attend_out,
    time_weight,
    time_bias,
    expand_weight,
    expand_bias,
    reduce_weight,
    reduce_bias,
):
    local = ends_in[0]
    micro = lengths.shape[1]
    assert micro == 2
    width = local.shape[1]
    span = local.shape[0] // micro
    hidden = expand_weight.shape[2]
    count = lax.axis_size("rep")
    section = lax.axis_index("section")
    rank = lax.axis_index("rep")
    core = rank & 1
    steps = jnp.exp(-math.log(10000.0) * jnp.arange(EMB // 2, dtype=F32) / (EMB // 2))
    turn = times.reshape(micro * SEGS, 1).astype(F32) * steps
    embed = jnp.concatenate([jnp.cos(turn), jnp.sin(turn)], axis=1)
    mods = jnp.dot(
        embed, time_weight[0].astype(F32), precision=lax.Precision.HIGHEST
    ) + time_bias.astype(F32)
    fused = width // count % 16 == 0 and TILE % (hidden // count) == 0 and count >= 16
    common = Bag(
        args=(
            lengths[0],
            section.reshape(1),
            mods,
            jnp.asarray(angle_table(span)),
            norm_gain,
            expand_bias,
            reduce_bias,
        ),
        sizes=(span, width, hidden, count),
        tokens=local.shape[0],
        cores=2 if fused else 1,
    )
    weights = Bag(
        win=attend_in[0], wout=attend_out[0], wex=expand_weight[0], wre=reduce_weight[0]
    )
    rows = [(local, slot * span) for slot in range(micro)]
    same = lambda *names: {name: name for name in names}
    whole = same("left", "bg", "pa", "jg")
    run = partial(stage, common=common)
    both = (forward, output, mlp, copy_agrad, attend)
    over = lambda block, route: lax.ppermute(block, "section", route)
    swap = lambda block, bit: exchange(block, "rep", bit)
    a = run(
        "first_0",
        parts=(forward,),
        who=0,
        slot=0,
        loads=dict(xv=rows[0], **weights),
        stores=dict(result="leave"),
        kept=False,
    )
    came_0 = over(a.leave, [(0, 1)])
    after = (a.leave,)
    if fused:
        embeds = (embed.T, swap(embed.T, 0))
        after += (embeds[1],)
    b = run(
        "first_1",
        parts=(forward,),
        who=0,
        slot=1,
        loads=dict(xv=rows[1], **weights),
        stores=same("result", "left", "qkv", "probs", "middle", "slope", "branch"),
        after=after,
        heads_step=1,
    )
    came_1 = over(b.result, [(0, 1)])
    x = run(
        "second_0",
        parts=both,
        who=1,
        slot=0,
        loads=dict(xv=came_0, dyv=rows[0], **weights),
        stores=dict(whole, result=("ends", 0), leave="leave"),
        after=(b.result,),
    )
    back_0 = over(x.leave, [(1, 0)])
    y = run(
        "second_1",
        parts=both,
        who=1,
        slot=1,
        loads=dict(xv=came_1, dyv=rows[1], **weights),
        stores=dict(whole, result=("ends", span), leave="leave"),
        carried=dict(b, ends=x.ends),
        after=(x.leave,),
    )
    back_1 = over(y.leave, [(1, 0)])
    x = run(
        "back_0",
        parts=both,
        who=0,
        slot=0,
        loads=dict(xv=rows[0], dyv=back_0, **weights),
        stores=dict(whole, leave=("ends", 0)),
        carried=dict(x, ends=y.ends),
        after=(y.leave,),
    )
    if fused:
        side = lambda item: lax.dynamic_index_in_dim(item, 1 - core, 0, keepdims=False)
        lefts = [x.left, y.left, swap(side(x.left), 0), swap(side(y.left), 0)]
        others = [swap(item, 0) for item in (x.bg, x.pa, x.jg)]
    gates = mods[SEGS : 2 * SEGS, 2 * width :]
    gates = jnp.where(lengths[0, 1, 0] == span, gates[:1], gates)
    cotan = back_1.astype(F32).reshape(SEGS, -1, width)
    made = (cotan * gates[:, None]).reshape(span, width).astype(BF16)
    bg_1 = jnp.where(section == 0, made, y.bg)
    after = ()
    if fused:
        bg_1_other = swap(bg_1, 0)
        after = (bg_1_other, others[0], lefts[2], lefts[3])
    part = run(
        "back_1_mlp",
        parts=(mlp,),
        who=0,
        slot=1,
        loads=dict(
            bg=bg_1,
            wre=weights.wre,
            slope=b.slope,
            wex=weights.wex,
            middle=b.middle,
            dyv=back_1,
            branch=b.branch,
        ),
        stores=same("pa", "middle_grad"),
        carried=y,
        after=after,
        pieces=dict(wre=(0, hidden // width), slope=(1, hidden // width), wex=(1, hidden // width)),
    )
    pa_1 = part.pa
    bits = bits_of(count)
    term = partial(term_call, sizes=common.sizes, core=core, rank=rank)
    lines = width // count
    deep = EMB // count
    sizes = (hidden // count, hidden // count + lines + 3 * deep + TAIL_ROWS, 3 * lines + GAIN_ROWS)
    bases = left_bases(width, hidden)

    def last_attend(after):
        return run(
            "back_1_attend",
            parts=(attend,),
            who=0,
            slot=1,
            loads=dict(
                agrad=(pa_1, None, (hidden, width)),
                wout=weights.wout,
                probs=b.probs,
                qkv=b.qkv,
                win=weights.win,
                xv=rows[1],
                middle_grad=part.middle_grad,
            ),
            stores=dict(jg="jg", leave=("ends", span)),
            carried=dict(y, ends=x.ends),
            after=after,
        )

    def pair_of(size, first):
        cut = size // 2 if fused else size // 32 * 16
        one = Chunk("rep", bits, cut, (1,) if fused else ())
        two = Chunk("rep", bits, size - cut, (2,) if fused else ())
        if fused:
            send_1, keep_1, send_2, keep_2 = first
            one.add(keep_1)
            two.add(keep_2)
            return one, two, send_1, send_2
        view = first.reshape((count // 2, 2) + first.shape[1:])
        cut = lambda at: lax.dynamic_index_in_dim(view, at, 1, keepdims=False)
        came = swap(cut(1 - core).astype(BF16), 0)
        for item in (cut(core), came):
            one.add(item)
            two.add(item, one.size)
        return one, two, one.split(1), two.split(2)

    if fused:
        pa_other = swap(pa_1, 0)
        sent = term(
            "term_reduce",
            term_reduce,
            lines=sizes[0],
            base=bases[0],
            rows=hidden // 2,
            lefts=lefts,
            rights=[x.bg, bg_1, others[0], bg_1_other],
            after=(pa_1,),
        )
        r1, r2, send_1, send_2 = pair_of(sizes[0], sent)
        came_r1, came_r2 = swap(send_1, 1), swap(send_2, 2)
        sent = term(
            "term_expand",
            term_expand,
            lines=sizes[1],
            base=bases[1],
            rows=width,
            lefts=lefts,
            rights=[x.pa, pa_1, others[1], pa_other],
            embeds=embeds,
            after=(send_1, send_2),
        )
        came_r1, came_r2, *sent = join(came_r1, came_r2, *sent)
        e1, e2, send_1, send_2 = pair_of(sizes[1], sent)
        came_e1, came_e2 = swap(send_1, 1), swap(send_2, 2)
        last = last_attend((send_1, send_2))
        came_e1, came_e2, jg_1 = join(came_e1, came_e2, last.jg)
        jg_other = swap(jg_1, 0)
        r1.add(came_r1)
        r2.add(came_r2)
        send_1, send_2 = r1.split(2), r2.split(1)
        came_r1, came_r2 = swap(send_1, 2), swap(send_2, 1)
        came_e1, came_e2, _, _ = join(came_e1, came_e2, send_1, send_2)
        e1.add(came_e1)
        e2.add(came_e2)
        send_3, send_4 = e1.split(2), e2.split(1)
        came_e1, came_e2 = swap(send_3, 2), swap(send_4, 1)
        sent = term(
            "term_attend",
            term_attend,
            lines=sizes[2],
            base=bases[3],
            rows=width // 2,
            lefts=lefts,
            rights=[x.jg, jg_1, others[2], jg_other],
            after=(send_1, send_2, send_3, send_4),
        )
        came_e1, came_e2, came_r1, came_r2, *sent = join(
            came_e1, came_e2, came_r1, came_r2, *sent
        )
        a1, a2, send_1, send_2 = pair_of(sizes[2], sent)
    else:
        last = last_attend(())
        rights = [(x.bg, bg_1), (x.pa, pa_1), (x.jg, last.jg)]
        totals = plain_pieces((x.left, y.left), rights, embed.T, common.sizes)
        r1, r2, send_1, send_2 = pair_of(sizes[0], totals[0])
        r1.add(swap(send_1, 1))
        r2.add(swap(send_2, 2))
        came_r1, came_r2 = swap(r1.split(2), 2), swap(r2.split(1), 1)
        e1, e2, send_1, send_2 = pair_of(sizes[1], totals[1])
        e1.add(swap(send_1, 1))
        e2.add(swap(send_2, 2))
        came_e1, came_e2 = swap(e1.split(2), 2), swap(e2.split(1), 1)
        a1, a2, send_1, send_2 = pair_of(sizes[2], totals[2])
    ends = last.ends
    came_a1, came_a2 = swap(send_1, 1), swap(send_2, 2)
    for chunk, came in ((r1, came_r1), (r2, came_r2), (e1, came_e1), (e2, came_e2)):
        chunk.add(came)
    parts = (r1, r2, e1, e2)
    block = jnp.concatenate([chunk.split(3) for chunk in parts], axis=-2)
    came_re = swap(block, 3)
    came_a1, came_a2, _ = join(came_a1, came_a2, block)
    a1.add(came_a1)
    a2.add(came_a2)
    send_1, send_2 = a1.split(2), a2.split(1)
    came_a1, came_a2 = swap(send_1, 2), swap(send_2, 1)
    a1.add(came_a1)
    a2.add(came_a2)
    block_a = jnp.concatenate([a1.split(3), a2.split(3)], axis=-2)
    came_a = swap(block_a, 3)
    came_re, _ = join(came_re, block_a)
    spot = 0
    for chunk in parts:
        chunk.add(came_re[..., spot : spot + chunk.size, :])
        spot += chunk.size
    a1.add(came_a[..., : a1.size, :])
    a2.add(came_a[..., a1.size :, :])
    for bit in range(4, bits):
        for chunk in (r1, r2, e1, e2, a1, a2):
            chunk.add(swap(chunk.split(bit), bit))
    share_r, share_e, share_a = (
        jnp.concatenate([one.total(), two.total()]) for one, two in ((r1, r2), (e1, e2), (a1, a2))
    )
    tall = hidden // width
    side = lambda item, n, size: jnp.concatenate(
        [item[i * size : (i + 1) * size] for i in range(n)], axis=1
    )
    at_o = tall * lines
    at_t = at_o + lines
    small = share_e[at_t + 3 * deep :]
    flat = lambda item, first, n: lax.dynamic_slice_in_dim(
        item[first : first + n].reshape(-1), rank * (n * width // count), n * width // count
    )
    results = (
        flat(share_a, 3 * lines, 1),
        side(share_a, 3, lines),
        share_e[at_o:at_t],
        side(share_e[at_t:], 3, deep),
        flat(small, 1, 3),
        side(share_e, tall, lines),
        flat(small, 4, tall),
        share_r,
        flat(small, 0, 1),
    )
    return (ends[None],) + tuple(piece[None] for piece in results)


def solution(mesh):
    return jax.shard_map(
        per_device,
        mesh=mesh,
        in_specs=(
            P("section", "rep", None),
            P("rep", None, None),
            P("rep", None, None),
            P("section", None),
            P("section", None, None),
            P("section", None, None),
            P("section", None, None),
            P("section", None),
            P("section", None, None),
            P("section", None),
            P("section", None, None),
            P("section", None),
        ),
        out_specs=(
            P("section", "rep", None),
            P("section", "rep"),
            P("section", "rep", None),
            P("section", "rep", None),
            P("section", "rep", None),
            P("section", "rep"),
            P("section", "rep", None),
            P("section", "rep"),
            P("section", "rep", None),
            P("section", "rep"),
        ),
        check_vma=False,
    )
```

```python
from functools import partial
import inspect
import math

import jax
import jax.numpy as jnp
import numpy as np
from jax import lax
from jax.experimental import pallas as pl
from jax.experimental.pallas import tpu as pltpu
from jax.sharding import PartitionSpec as P

HEADS = 12
HEAD = 64
EMB = 128
SEGS = 4
ANY = pl.ANY
VMEM = pltpu.MemorySpace.VMEM
SMEM = pltpu.MemorySpace.SMEM
F32 = jnp.float32
BF16 = jnp.bfloat16
ROOT_HALF = 0.7071067811865476
ROOT_TAU = 0.3989422804014327
TILE = 384
TAIL_ROWS = 24
GAIN_ROWS = 16
EXTRA = 16


class Bag(dict):
    __getattr__ = dict.__getitem__


def dot(left, right, left_dim=1, right_dim=0):
    return lax.dot_general(
        left, right, (((left_dim,), (right_dim,)), ((), ())), preferred_element_type=F32
    )


def repeat(count, body):
    for i in range(count):
        body(i)


def steps_of(count, size, body):
    def several(i, _):
        for j in range(size):
            body(size * i + j)
        return _

    lax.fori_loop(0, count // size, several, 0)


def lanes(index, size, start=0):
    if isinstance(index, int):
        return slice(start + index * size, start + (index + 1) * size)
    return pl.ds(pl.multiple_of(start + index * size, size), size)


def swap_halves(values, low_half):
    forth = pltpu.roll(values, 128 - HEAD // 2, 1)
    back = pltpu.roll(values, HEAD // 2, 1)
    return jnp.where(low_half, forth, back)


def norm_parts(values):
    center = values - jnp.mean(values, axis=-1, keepdims=True)
    spread = jnp.mean(center * center, axis=-1, keepdims=True)
    factor = lax.rsqrt(spread + 1e-05)
    return center * factor, factor


def norm_back(grad, unit, factor):
    return factor * (
        grad
        - jnp.mean(grad, axis=-1, keepdims=True)
        - unit * jnp.mean(grad * unit, axis=-1, keepdims=True)
    )


class Held:
    def __init__(self, bufs, loads, stores, sems, pieces):
        self.bufs = bufs
        self.loads = loads
        self.stores = stores
        self.sems = sems
        self.pieces = pieces
        self.names = {id(buf): name for name, buf in bufs.items()}
        keys = [(name, j) for name in loads for j in range(self.parts_of(name))]
        self.spots = {key: n for n, key in enumerate(keys)}
        self.waiting = set(keys)
        self.pending = set(keys)
        self.leaving = {}

    def parts_of(self, name):
        return self.pieces[name][1] if name in self.pieces else 1

    def load(self, name, j):
        source, target = self.loads[name], self.bufs[name]
        if name in self.pieces:
            axis, count = self.pieces[name]
            size = target.shape[axis] // count
            at = (slice(None),) * axis + (pl.ds(j * size, size),)
            source, target = source.at[at], target.at[at]
        return pltpu.make_async_copy(source, target, self.sems.at[self.spots[(name, j)]])

    def store(self, name, n):
        at, target = self.stores[name][n]
        source = self.bufs[name] if at is None else self.bufs[name].at[at]
        return pltpu.make_async_copy(source, target, self.sems.at[self.leaving[(name, n)]])

    def keys(self, bufs, part):
        for buf in bufs:
            name = self.names[id(buf)]
            for j in range(self.parts_of(name)):
                if part in (None, j):
                    yield name, j

    def begin(self, *bufs, part=None):
        for key in self.keys(bufs, part):
            if key in self.waiting:
                self.waiting.remove(key)
                self.load(*key).start()

    def need(self, *bufs, part=None):
        self.begin(*bufs, part=part)
        for key in self.keys(bufs, part):
            if key in self.pending:
                self.pending.remove(key)
                self.load(*key).wait()

    def done(self, *bufs):
        for buf in bufs:
            name = self.names[id(buf)]
            for n in range(len(self.stores.get(name, ()))):
                self.leaving[(name, n)] = len(self.spots) + len(self.leaving)
                self.store(name, n).start()

    def finish(self):
        for name, n in self.leaving:
            self.store(name, n).wait()


class Layer:
    def __init__(self, sizes, slot, refs):
        self.span, self.width, self.hidden, self.count = sizes
        self.slot = slot
        lengths, place, self.mods, self.trig, self.gain, self.ebias, self.rbias = refs
        self.section = place[0]
        self.core = place[1]
        self.single = lengths[slot, 0] == self.span
        self.pairs = self.width // 128
        self.seg = self.span // SEGS
        self.step = self.width
        self.tiles = self.hidden // self.step
        place = lax.broadcasted_iota(jnp.int32, (self.span, 128), 1)
        self.low_half = place % HEAD < HEAD // 2
        self.low_head = place < HEAD
        row = lax.broadcasted_iota(jnp.int32, (1, 128), 1) // HEAD
        self.head_row = [(row == i).astype(F32).astype(BF16) for i in range(2)]
        self.blocks = [(b, slice(b * self.seg, (b + 1) * self.seg)) for b in range(SEGS)]

    def trig_pair(self):
        cos_all, sin_all = self.trig[0], self.trig[1]
        cos_cut = jnp.concatenate([cos_all[: self.seg]] * SEGS, axis=0)
        sin_cut = jnp.concatenate([sin_all[: self.seg]] * SEGS, axis=0)
        return jnp.where(self.single, cos_all, cos_cut), jnp.where(self.single, sin_all, sin_cut)

    def mod_row(self, block, part):
        row = self.slot * SEGS + jnp.where(self.single, 0, block)
        return self.mods[pl.ds(row, 1), part * self.width : (part + 1) * self.width]

    def add_segment(self, small, block, at, sums):
        row = 2 + jnp.where(self.single, 0, block)
        small[pl.ds(row, 1), at * self.width : (at + 1) * self.width] += sums

    def side(self, block):
        return self.core if block % 2 == 0 else 1 - self.core

    def put_left(self, left, base, values):
        turned = values.T
        if left.shape[0] == 1:
            left[0, 2 * base : 2 * base + self.width] = turned
            return
        lines = self.width // self.count
        for block in range(self.count):
            to = base + block // 2 * lines
            left[self.side(block), to : to + lines] = turned[block * lines : (block + 1) * lines]

    def put_active(self, left, j, values):
        turned = values.T
        if left.shape[0] == 1:
            left[0, lanes(j, self.step)] = turned
            return
        lines = self.hidden // self.count
        per = self.step // lines
        for n in range(per):
            to = lanes(j, lines * (per // 2), n // 2 * lines)
            to = slice(to.start, to.start + lines) if isinstance(j, int) else pl.ds(to.start, lines)
            left[self.side(n), to] = turned[n * lines : (n + 1) * lines]

    def thirds(self, index):
        return [lanes(index, 128, p * self.width) for p in range(3)]


def left_bases(width, hidden):
    return 0, hidden // 2, (hidden + width) // 2, (hidden + 2 * width) // 2


def forward(
    k, xv, win, wout, wex, wre, left, qkv, probs, middle, slope, branch, result, bias, normed,
    mixed, modded,
):
    span, width, held = k.span, k.width, k.held
    _, at_modded, at_mixed, at_normed = left_bases(width, k.hidden)
    held.begin(xv, win)
    held.need(xv)
    unit, _ = norm_parts(xv[...].astype(F32))
    normed[...] = (unit * k.gain[...].astype(F32)).astype(BF16)
    across = lax.broadcasted_iota(jnp.int32, (span, span), 0) // k.seg
    down = lax.broadcasted_iota(jnp.int32, (span, span), 1) // k.seg
    bias[...] = jnp.where((across == down) | k.single, 0.0, -1e30)
    held.need(win)
    held.begin(wout, wex, wre)
    cos_part, sin_part = k.trig_pair()
    for tile, factor in ((0, 0.125), (1, 1.0)):
        for i in range(width // 256):
            at = lanes(i, 256, tile * width)
            joint = dot(normed[...], win[:, at])
            outs = []
            for piece in (joint[:, :128], joint[:, 128:]):
                turned = piece * cos_part + swap_halves(piece, k.low_half) * sin_part
                outs.append((turned * factor).astype(BF16))
            qkv[:, at] = jnp.concatenate(outs, axis=1)
    qkv[:, 2 * width :] = dot(normed[...], win[:, 2 * width :]).astype(BF16)
    held.done(qkv)
    if k.kept:
        k.put_left(left, at_normed, normed[...])

    def heads(i):
        at = k.thirds(i)
        query, key, value = (qkv[:, a] for a in at)
        outs = []
        for h in range(2):
            scores = dot(key * k.head_row[h], query, 1, 1) + bias[...]
            top = jnp.max(scores, axis=0, keepdims=True)
            raised = jnp.exp(scores - top)
            total = jnp.sum(raised, axis=0, keepdims=True)
            prob = raised * (1.0 / total)
            if k.kept:
                probs[2 * i + h] = prob
            outs.append(dot(prob.astype(BF16), value, 0, 0))
        mixed[:, at[0]] = jnp.where(k.low_head, outs[0], outs[1]).astype(BF16)

    steps_of(k.pairs, k.heads_step, heads)
    held.done(probs)
    held.need(wout)
    middle[...] = xv[...].astype(F32) + dot(mixed[...], wout[...])
    held.done(middle)
    if k.kept:
        k.put_left(left, at_mixed, mixed[...])
    for b, rows in k.blocks:
        unit, _ = norm_parts(middle[rows])
        modded[rows] = (unit * (1.0 + k.mod_row(b, 0)) + k.mod_row(b, 1)).astype(BF16)
    if k.kept:
        k.put_left(left, at_modded, modded[...])
    held.need(wex, wre)
    branch[...] = jnp.broadcast_to(k.rbias[...].astype(F32), (span, width))

    def feed(j):
        at = lanes(j, k.step)
        pre = dot(modded[...], wex[:, at]) + k.ebias[:, at].astype(F32)
        area = 0.5 + 0.5 * lax.erf(pre * ROOT_HALF)
        out = (pre * area).astype(BF16)
        if k.kept:
            slope[:, at] = area + pre * (jnp.exp(pre * pre * -0.5) * ROOT_TAU)
            k.put_active(left, j, out)
        branch[...] += dot(out, wre[at, :])

    if k.heads_step == 1:
        steps_of(k.tiles, 1, feed)
    else:
        repeat(k.tiles, feed)
    held.done(slope, left, branch)
    for b, rows in k.blocks:
        result[rows] = (middle[rows] + k.mod_row(b, 2) * branch[rows]).astype(BF16)
    held.done(result)


def output(k, dyv, bg):
    k.held.need(dyv)
    for b, rows in k.blocks:
        bg[rows] = (dyv[rows].astype(F32) * k.mod_row(b, 2)).astype(BF16)
    k.held.done(bg)


def mlp(k, wre, wex, bg, slope, middle, branch, dyv, pa, middle_grad, small, acc):
    span, width, hidden, held = k.span, k.width, k.hidden, k.held
    small[...] = jnp.zeros(small.shape, F32)
    acc[...] = jnp.zeros(acc.shape, F32)
    held.begin(bg)
    for j in range(k.tiles):
        held.begin(wre, slope, wex, part=j)
    held.begin(middle, dyv, branch)
    held.need(bg)

    def feed(j):
        at = lanes(j, k.step)
        held.need(wre, slope, wex, part=j)
        grad = dot(bg[...], wre[at, :], 1, 1)
        pre_grad = (slope[:, at] * grad).astype(BF16)
        pa[:span, at] = pre_grad
        small[0:1, at] = jnp.sum(pre_grad.astype(F32), axis=0, keepdims=True)
        acc[...] += dot(pre_grad, wex[:, at], 1, 1)

    repeat(k.tiles, feed)
    held.need(middle, dyv, branch)
    total = jnp.zeros((1, width), F32)
    for b, rows in k.blocks:
        cotan = dyv[rows].astype(F32)
        total += jnp.sum(bg[rows].astype(F32), axis=0, keepdims=True)
        grad = acc[rows]
        unit, factor = norm_parts(middle[rows])
        k.add_segment(small, b, 0, jnp.sum(grad * unit, axis=0, keepdims=True))
        k.add_segment(small, b, 1, jnp.sum(grad, axis=0, keepdims=True))
        k.add_segment(small, b, 2, jnp.sum(cotan * branch[rows], axis=0, keepdims=True))
        back = norm_back(grad * (1.0 + k.mod_row(b, 0)), unit, factor)
        full = cotan + back
        middle_grad[rows] = full
        pa[rows, hidden:] = full.astype(BF16)
    small[1:2, :width] = total
    pa[span:, :] = small[...].astype(BF16)
    held.done(pa, middle_grad)


def attend(
    k, wout, win, agrad, probs, qkv, xv, middle_grad, jg, leave, mixed_grad, acc
):
    span, held = k.span, k.held
    held.need(agrad, wout)
    held.begin(probs, qkv)
    mixed_grad[...] = dot(agrad[...], wout[...], 1, 1).astype(BF16)
    held.need(probs, qkv)
    held.begin(win, xv, middle_grad)
    cos_part, sin_part = k.trig_pair()

    def heads(i):
        at = k.thirds(i)
        query, key, value = (qkv[:, a] for a in at)
        out_grad = mixed_grad[:, at[0]]
        parts = []
        for h in range(2):
            prob = probs[2 * i + h]
            pull = dot(value * k.head_row[h], out_grad, 1, 1)
            shared = jnp.sum(prob * pull, axis=0, keepdims=True)
            score_grad = (prob * (pull - shared)).astype(BF16)
            parts.append(
                (
                    dot(score_grad, key, 0, 0),
                    dot(score_grad, query),
                    dot(prob.astype(BF16), out_grad),
                )
            )
        for p in range(3):
            grad = jnp.where(k.low_head, parts[0][p], parts[1][p])
            if p < 2:
                grad = grad * cos_part - swap_halves(grad, k.low_half) * sin_part
                if p == 0:
                    grad = grad * 0.125
            jg[:span, at[p]] = grad.astype(BF16)

    steps_of(k.pairs, k.heads_step, heads)
    held.need(win, xv, middle_grad)
    acc[...] = dot(jg[:span, :], win[...], 1, 1)
    total = jnp.zeros((1, k.width), F32)
    for b, rows in k.blocks:
        grad = acc[rows]
        unit, factor = norm_parts(xv[rows].astype(F32))
        total += jnp.sum(grad * unit, axis=0, keepdims=True)
        back = norm_back(grad * k.gain[...].astype(F32), unit, factor)
        leave[rows] = (middle_grad[rows] + back).astype(BF16)
    below = jnp.concatenate([total, jnp.zeros((EXTRA - 1, k.width), F32)], axis=0)
    jg[span:, : k.width] = below.astype(BF16)
    jg[span:, k.width :] = jnp.zeros((EXTRA, 2 * k.width), BF16)
    held.done(jg, leave)


def copy_agrad(k, pa, agrad):
    agrad[...] = pa[: k.span, k.hidden :]


class Sums:
    def __init__(self, ranks, full, outs, sems):
        self.full = full
        self.own = [((ranks[0] >> bit) & 1) == 0 for bit in (1, 2)]
        self.bufs = outs[:4]
        self.targets = outs[4:]
        self.sems = sems
        self.half = full.shape[1] // 2
        self.copies = []

    def put(self, block, at, values):
        self.full[block, at] = values

    def settle(self, which, groups):
        send, keep = self.bufs[2 * which : 2 * which + 2]
        at = slice(which * self.half, (which + 1) * self.half)
        apart = 1 + which
        for group in groups:
            for n in range(2):
                first = 4 * group + (2 * n if which == 0 else n)
                even, odd = self.full[first, at], self.full[first + apart, at]
                send[2 * group + n] = jnp.where(self.own[which], odd, even).astype(BF16)
                keep[2 * group + n] = jnp.where(self.own[which], even, odd)
            spot = pl.ds(2 * group, 2)
            for n in range(2 * which, 2 * which + 2):
                copy = pltpu.make_async_copy(
                    self.bufs[n].at[spot], self.targets[n].at[spot], self.sems.at[len(self.copies)]
                )
                copy.start()
                self.copies.append(copy)

    def finish(self):
        for copy in self.copies:
            copy.wait()


def term_reduce(k, sums, left, right):
    lines = k.hidden // k.count
    per = TILE // lines
    for tile in range(k.hidden // 2 // TILE):
        k.arrive(tile)
        total = dot(left[tile * TILE : (tile + 1) * TILE], right[...])
        for n in range(per):
            sums.put(tile * per + n, slice(0, lines), total[n * lines : (n + 1) * lines])
        if (tile + 1) * per % 4 == 0:
            group = ((tile + 1) * per // 4 - 1,)
            sums.settle(0, group)
            sums.settle(1, group)


def square_terms(k, sums, left, right, cols, part):
    lines = k.width // k.count
    total = dot(left, right[: 4 * k.span, cols])
    for n in range(k.count // 2):
        sums.put(n, slice(part * lines, (part + 1) * lines), total[n * lines : (n + 1) * lines])


def term_expand(k, sums, left, right):
    width, hidden, span = k.width, k.hidden, k.span
    groups = range(k.count // 8)
    tall = hidden // width
    lines = width // k.count
    rows = width // 2
    half = sums.half
    settled = False
    for col in range(tall + 1):
        k.arrive(col)
        part = left[:rows] if col < tall else left[rows:]
        square_terms(k, sums, part, right, slice(col * width, (col + 1) * width), col)
        if (col + 1) * lines >= half and not settled:
            sums.settle(0, groups)
            settled = True
    smalls = [k.small[n].astype(F32) for n in range(4)]
    times = sum(
        k.embeds[n // 2][:, n % 2 * SEGS + s : n % 2 * SEGS + s + 1]
        * smalls[n][2 + s : 3 + s, : 3 * width]
        for n in range(4)
        for s in range(SEGS)
    )
    both = sum(smalls)
    seq_sum = jnp.sum(both[2 : 2 + SEGS, : 3 * width], axis=0, keepdims=True)
    lines_v = k.lines
    lines_v[...] = jnp.zeros(lines_v.shape, F32)
    lines_v[0:1] = both[1:2, :width]
    for n in range(3):
        lines_v[1 + n : 2 + n] = seq_sum[:, n * width : (n + 1) * width]
    for n in range(tall):
        lines_v[4 + n : 5 + n] = both[0:1, n * width : (n + 1) * width]
    deep = EMB // k.count
    first = (tall + 1) * lines
    for g in range(k.count // 2):
        for side in range(2):

            @pl.when(k.core == side)
            def _(at=(2 * g + side) * deep, g=g):
                for p in range(3):
                    to = first + p * deep
                    piece = times[at : at + deep, p * width : (p + 1) * width]
                    sums.put(g, slice(to, to + deep), piece)

        sums.put(g, slice(first + 3 * deep, 2 * half), lines_v[...])
    sums.settle(1, groups)


def term_attend(k, sums, left, right):
    width = k.width
    groups = range(k.count // 8)
    lines = width // k.count
    settled = False
    for col in range(3):
        k.arrive(col)
        square_terms(k, sums, left[...], right, slice(col * width, (col + 1) * width), col)
        if (col + 1) * lines >= sums.half and not settled:
            sums.settle(0, groups)
            settled = True
    gain = sum(k.small[n].astype(F32) for n in range(4))[:, :width]
    for g in range(k.count // 2):
        sums.put(g, slice(3 * lines, 3 * lines + GAIN_ROWS), gain)
    sums.settle(1, groups)


def load_terms(k, refs, bufs, base, sems):
    left_v, right_v, small_v = bufs
    rows, cols = left_v.shape[0], right_v.shape[1]
    tall = rows // TILE if small_v is None else 1
    wide = cols // k.width
    groups = []
    for i in range(tall):
        for j in range(wide):
            copies = []
            for n, (left, right) in enumerate(zip(refs[:4], refs[4:8])):
                tokens = pl.ds(n * k.span, k.span)
                part = pl.ds(i * (rows // tall), rows // tall)
                from_part = pl.ds(base + i * (rows // tall), rows // tall)
                at = pl.ds(j * k.width, k.width)
                if j == 0:
                    copies.append((left.at[from_part], left_v.at[part, tokens]))
                if i == 0:
                    copies.append((right.at[pl.ds(0, k.span), at], right_v.at[tokens, at]))
                if small_v is not None and j == wide - 1:
                    copies.append((right.at[pl.ds(k.span, EXTRA)], small_v.at[n]))
            groups.append(copies)
    made, count = [], 0
    for copies in groups:
        made.append([])
        for pair in copies:
            made[-1].append(pltpu.make_async_copy(*pair, sems.at[count]))
            made[-1][-1].start()
            count += 1
    return made


class Terms:
    def __init__(self, sizes, core):
        self.span, self.width, self.hidden, self.count = sizes
        self.core = core[0]

    def arrive(self, group):
        for copy in self.groups[group]:
            copy.wait()


def term_kernel(sizes, body, base, extra, *refs):
    refs = list(refs)
    core, rank = refs[:2]
    k = Terms(sizes, core)
    pos = 2
    if body is term_expand:
        k.embeds = refs[pos : pos + 2]
        pos += 2
    sources = refs[pos : pos + 8]
    pos += 8 + extra
    targets = refs[pos : pos + 4]
    pos += 4
    left_v, right_v, full, *outs = refs[pos : pos + 7]
    pos += 7
    k.small = None
    if body is not term_reduce:
        k.small, k.lines = refs[pos : pos + 2]
        pos += 2
    sems, out_sems = refs[pos:]
    k.groups = load_terms(k, sources, (left_v, right_v, k.small), base, sems)
    sums = Sums(rank, full, outs + targets, out_sems)
    body(k, sums, left_v, right_v)
    sums.finish()


def term_call(name, body, sizes, lines, base, rows, core, rank, lefts, rights, embeds=(), after=()):
    span, width, hidden, count = sizes
    blocks = count // 2
    cols = rights[0].shape[1]
    half = lines // 2
    outs = [((blocks // 2, half, width), kind) for kind in (BF16, F32)] * 2
    scratch = [
        ((rows, 4 * span), BF16),
        ((4 * span, cols), BF16),
        ((blocks, lines, width), F32),
        *outs,
    ]
    if body is not term_reduce:
        scratch += [((4, EXTRA, cols), BF16), ((TAIL_ROWS, width), F32)]
    args = [core.reshape(1), rank.reshape(1), *embeds, *lefts, *rights, *after]
    in_specs = [pl.BlockSpec(memory_space=SMEM)] * 2
    in_specs += [pl.BlockSpec(memory_space=VMEM)] * len(embeds)
    in_specs += [pl.BlockSpec(memory_space=ANY)] * (8 + len(after))
    return pl.pallas_call(
        partial(term_kernel, sizes, body, base, len(after)),
        out_shape=[jax.ShapeDtypeStruct(*item) for item in outs],
        in_specs=in_specs,
        out_specs=[pl.BlockSpec(memory_space=ANY)] * 4,
        scratch_shapes=[pltpu.VMEM(*item) for item in scratch]
        + [pltpu.SemaphoreType.DMA((32,)), pltpu.SemaphoreType.DMA((8,))],
        compiler_params=pltpu.CompilerParams(vmem_limit_bytes=56 * 1024 * 1024),
        name=name,
    )(*args)


def plain_pieces(lefts, rights, embed, sizes):
    span, width, hidden, count = sizes
    bg, pa, jg = rights
    bases = [2 * base for base in left_bases(width, hidden)]

    def blocks(base, rows, right):
        total = sum(dot(a[base : base + rows], b) for a, b in zip(lefts, right))
        parts = [total[:, i : i + width] for i in range(0, total.shape[1], width)]
        return [part.reshape(count, -1, width) for part in parts]

    take = lambda items, cols: [item[:span, cols] for item in items]
    reduce = blocks(bases[0], hidden, bg)
    expand = blocks(bases[1], width, take(pa, slice(0, hidden)))
    expand += blocks(bases[2], width, take(pa, slice(hidden, hidden + width)))
    last = blocks(bases[3], width, take(jg, slice(None)))
    small = [item[span:].astype(F32) for item in pa]
    seqs = jnp.concatenate([item[2 : 2 + SEGS, : 3 * width] for item in small])
    times = jnp.dot(embed, seqs, precision=lax.Precision.HIGHEST)
    expand += [times[:, i * width : (i + 1) * width].reshape(count, -1, width) for i in range(3)]
    lines = jnp.concatenate(
        [
            sum(item[1:2, :width] for item in small),
            jnp.sum(seqs, axis=0).reshape(-1, width),
            sum(item[0, :hidden] for item in small).reshape(-1, width),
        ]
    )
    lines = jnp.pad(lines, ((0, TAIL_ROWS - lines.shape[0]), (0, 0)))
    gain = sum(item[span:, :width].astype(F32) for item in jg)
    expand.append(jnp.broadcast_to(lines, (count,) + lines.shape))
    last.append(jnp.broadcast_to(gain, (count,) + gain.shape))
    return [jnp.concatenate(item, axis=1) for item in (reduce, expand, last)]


def shapes_of(span, width, hidden, cores):
    tok = lambda cols, kind=BF16: ((span, cols), kind)
    below = lambda cols: ((span + EXTRA, cols), BF16)
    return dict(
        xv=tok(width),
        dyv=tok(width),
        win=((width, 3 * width), BF16),
        wout=((width, width), BF16),
        wex=((width, hidden), BF16),
        wre=((hidden, width), BF16),
        left=((cores, (hidden + 3 * width) // cores, span), BF16),
        normed=tok(width),
        qkv=tok(3 * width),
        probs=((HEADS, span, span), F32),
        mixed=tok(width),
        middle=tok(width, F32),
        modded=tok(width),
        slope=tok(hidden, F32),
        branch=tok(width, F32),
        result=tok(width),
        bg=tok(width),
        pa=below(hidden + width),
        jg=below(3 * width),
        agrad=tok(width),
        mixed_grad=tok(width),
        middle_grad=tok(width, F32),
        leave=tok(width),
        acc=tok(width, F32),
        bias=tok(span, F32),
        small=((EXTRA, hidden + width), F32),
    )


def uses(part):
    return list(inspect.signature(part).parameters)[1:]


def stage_kernel(sizes, parts, who, slot, plan, *refs):
    refs = list(refs)
    layer = Layer(sizes, slot, refs[:7])
    span = layer.span
    pos = 7
    loads = {}
    for name, row, cols in plan.sources:
        ref = refs[pos]
        if cols is not None:
            ref = ref.at[pl.ds(0, span), pl.ds(*cols)]
        elif row is not None:
            ref = ref.at[pl.ds(row, span)]
        loads[name] = ref
        pos += 1
    pos += plan.extra
    stores = {}
    for name, row, at in plan.targets:
        target = refs[pos] if row is None else refs[pos].at[pl.ds(row, span)]
        stores.setdefault(name, []).append((at, target))
        pos += 1
    bufs = {}
    for name in plan.bufs:
        bufs[name] = refs[pos]
        pos += 1
    layer.held = Held(bufs, loads, stores, refs[pos], plan.pieces)
    layer.kept = plan.kept
    layer.heads_step = plan.heads_step

    @pl.when(layer.section == who)
    def _():
        for part in parts:
            part(layer, *[bufs[name] for name in uses(part)])
        layer.held.finish()


def stage(
    name, common, parts, who, slot, loads, stores, carried=None, after=(), kept=True, heads_step=3,
    pieces=None,
):
    carried = carried or {}
    span, width, hidden, count = common.sizes
    shapes = shapes_of(span, width, hidden, common.cores)
    bufs = []
    for part in parts:
        bufs += [item for item in uses(part) if item not in bufs]
    pair = lambda item: item if isinstance(item, tuple) else (item, None)
    args = list(common.args)
    in_specs = [pl.BlockSpec(memory_space=SMEM)] * 2 + [pl.BlockSpec(memory_space=VMEM)] * 5
    plan = Bag(sources=[], targets=[], bufs=bufs, kept=kept, heads_step=heads_step)
    plan["pieces"] = pieces or {}
    for item in loads:
        if item in bufs:
            array, row, *cols = pair(loads[item])
            args.append(array)
            plan.sources.append((item, row, cols[0] if cols else None))
    outs, aliases, extra = [], {}, []
    targets = []
    for item, key in stores.items():
        if item == "left":
            targets += [(item, key + "_send" * n, None, n) for n in range(common.cores)]
        else:
            targets.append((item, *pair(key), None))
    for i, (item, key, row, at) in enumerate(targets):
        shape, kind = shapes[item]
        if row is not None:
            shape = (common.tokens,) + shape[1:]
        if at is not None:
            shape = shape[1:]
        outs.append(jax.ShapeDtypeStruct(shape, kind))
        plan.targets.append((item, row, at))
        if key in carried:
            aliases[len(args) + len(extra)] = i
            extra.append(carried[key])
    extra += list(after)
    args += extra
    plan["extra"] = len(extra)
    in_specs += [pl.BlockSpec(memory_space=ANY)] * (len(args) - len(in_specs))
    results = pl.pallas_call(
        partial(stage_kernel, common.sizes, parts, who, slot, plan),
        out_shape=outs,
        in_specs=in_specs,
        out_specs=[pl.BlockSpec(memory_space=ANY)] * len(outs),
        input_output_aliases=aliases,
        scratch_shapes=[pltpu.VMEM(*shapes[item]) for item in bufs]
        + [pltpu.SemaphoreType.DMA((32,))],
        compiler_params=pltpu.CompilerParams(vmem_limit_bytes=56 * 1024 * 1024),
        name=name,
    )(*args)
    return Bag({key: value for (_, key, _, _), value in zip(targets, results)})


def bits_of(count):
    bits = count.bit_length() - 1
    assert 1 << bits == count
    return bits


class Chunk:
    def __init__(self, axis, bits, size, settled=()):
        self.axis = axis
        self.bits = list(range(bits - 1, 0, -1))
        self.size = size
        self.settled = list(settled)
        self.terms = []

    def add(self, term, start=0):
        left = [bit for bit in self.bits if bit not in self.settled]
        self.terms.append((term.reshape((2,) * len(left) + term.shape[-2:]), left, start))

    def take(self, term, start, left, flip):
        me = lax.axis_index(self.axis)
        side = lambda bit: 1 - ((me >> bit) & 1) if bit == flip else (me >> bit) & 1
        starts = [side(bit) if bit in self.settled else 0 for bit in left]
        sizes = [1 if bit in self.settled else 2 for bit in left]
        cols = term.shape[-1]
        piece = lax.dynamic_slice(term, starts + [start, 0], sizes + [self.size, cols])
        open_bits = [2] * (len(self.bits) - len(self.settled))
        return piece.reshape(open_bits + [self.size, cols]).astype(F32)

    def split(self, bit):
        self.settled.append(bit)
        return sum(self.take(term, start, left, bit) for term, left, start in self.terms).astype(
            BF16
        )

    def total(self):
        return sum(self.take(term, start, left, None) for term, left, start in self.terms)


def exchange(block, axis, bit):
    count = lax.axis_size(axis)
    return lax.ppermute(block, axis, [(i, i ^ (1 << bit)) for i in range(count)])


def join(*items):
    return lax.optimization_barrier(items)


def angle_table(span):
    half = HEAD // 2
    freqs = np.exp(-math.log(10000.0) * np.arange(half, dtype=np.float32) / half)
    phase = np.arange(span, dtype=np.float32)[:, None] * freqs.astype(np.float32)[None, :]
    cos_part, sin_part = np.cos(phase), np.sin(phase)
    return np.stack(
        [
            np.concatenate([cos_part] * 4, axis=1),
            np.concatenate([-sin_part, sin_part] * 2, axis=1),
        ]
    ).astype(np.float32)


def per_device(
    ends_in,
    lengths,
    times,
    norm_gain,
    attend_in,
    attend_out,
    time_weight,
    time_bias,
    expand_weight,
    expand_bias,
    reduce_weight,
    reduce_bias,
):
    local = ends_in[0]
    micro = lengths.shape[1]
    assert micro == 2
    width = local.shape[1]
    span = local.shape[0] // micro
    hidden = expand_weight.shape[2]
    count = lax.axis_size("rep")
    section = lax.axis_index("section")
    rank = lax.axis_index("rep")
    core = rank & 1
    steps = jnp.exp(-math.log(10000.0) * jnp.arange(EMB // 2, dtype=F32) / (EMB // 2))
    turn = times.reshape(micro * SEGS, 1).astype(F32) * steps
    embed = jnp.concatenate([jnp.cos(turn), jnp.sin(turn)], axis=1)
    mods = jnp.dot(
        embed, time_weight[0].astype(F32), precision=lax.Precision.HIGHEST
    ) + time_bias.astype(F32)
    fused = width // count % 16 == 0 and TILE % (hidden // count) == 0 and count >= 16
    common = Bag(
        args=(
            lengths[0],
            jnp.stack([section, core]),
            mods,
            jnp.asarray(angle_table(span)),
            norm_gain,
            expand_bias,
            reduce_bias,
        ),
        sizes=(span, width, hidden, count),
        tokens=local.shape[0],
        cores=2 if fused else 1,
    )
    weights = Bag(
        win=attend_in[0], wout=attend_out[0], wex=expand_weight[0], wre=reduce_weight[0]
    )
    rows = [(local, slot * span) for slot in range(micro)]
    same = lambda *names: {name: name for name in names}
    whole = same("left", "bg", "pa", "jg")
    run = partial(stage, common=common)
    both = (forward, output, mlp, copy_agrad, attend)
    over = lambda block, route: lax.ppermute(block, "section", route)
    swap = lambda block, bit: exchange(block, "rep", bit)
    a = run(
        "first_0",
        parts=(forward,),
        who=0,
        slot=0,
        loads=dict(xv=rows[0], **weights),
        stores=dict(result="leave"),
        kept=False,
    )
    came_0 = over(a.leave, [(0, 1)])
    after = (a.leave,)
    if fused:
        embeds = (embed.T, swap(embed.T, 0))
        after += (embeds[1],)
    b = run(
        "first_1",
        parts=(forward,),
        who=0,
        slot=1,
        loads=dict(xv=rows[1], **weights),
        stores=same("result", "left", "qkv", "probs", "middle", "slope", "branch"),
        after=after,
        heads_step=1,
    )
    came_1 = over(b.result, [(0, 1)])
    x = run(
        "second_0",
        parts=both,
        who=1,
        slot=0,
        loads=dict(xv=came_0, dyv=rows[0], **weights),
        stores=dict(whole, result=("ends", 0), leave="leave"),
        after=(b.result,),
    )
    back_0 = over(x.leave, [(1, 0)])
    y = run(
        "second_1",
        parts=both,
        who=1,
        slot=1,
        loads=dict(xv=came_1, dyv=rows[1], **weights),
        stores=dict(whole, result=("ends", span), leave="leave"),
        carried=dict(b, ends=x.ends),
        after=(x.leave,),
    )
    back_1 = over(y.leave, [(1, 0)])
    x = run(
        "back_0",
        parts=both,
        who=0,
        slot=0,
        loads=dict(xv=rows[0], dyv=back_0, **weights),
        stores=dict(whole, leave=("ends", 0)),
        carried=dict(x, ends=y.ends),
        after=(y.leave,),
    )
    if fused:
        y_left = swap(y.left_send, 0)
        back_1, x_send, x_bg = join(back_1, x.left_send, x.bg)
        lefts = [x.left, y.left, swap(x_send, 0), y_left]
        others = [swap(item, 0) for item in (x_bg, x.pa, x.jg)]
    gates = mods[SEGS : 2 * SEGS, 2 * width :]
    gates = jnp.where(lengths[0, 1, 0] == span, gates[:1], gates)
    cotan = back_1.astype(F32).reshape(SEGS, -1, width)
    made = (cotan * gates[:, None]).reshape(span, width).astype(BF16)
    bg_1 = jnp.where(section == 0, made, y.bg)
    after = ()
    if fused:
        bg_1_other = swap(bg_1, 0)
        after = (bg_1_other, others[0], lefts[2], lefts[3])
    part = run(
        "back_1_mlp",
        parts=(mlp,),
        who=0,
        slot=1,
        loads=dict(
            bg=bg_1,
            wre=weights.wre,
            slope=b.slope,
            wex=weights.wex,
            middle=b.middle,
            dyv=back_1,
            branch=b.branch,
        ),
        stores=same("pa", "middle_grad"),
        carried=y,
        after=after,
        pieces=dict(wre=(0, hidden // width), slope=(1, hidden // width), wex=(1, hidden // width)),
    )
    pa_1 = part.pa
    bits = bits_of(count)
    term = partial(term_call, sizes=common.sizes, core=core, rank=rank)
    lines = width // count
    deep = EMB // count
    sizes = (hidden // count, hidden // count + lines + 3 * deep + TAIL_ROWS, 3 * lines + GAIN_ROWS)
    bases = left_bases(width, hidden)

    def last_attend(after):
        return run(
            "back_1_attend",
            parts=(attend,),
            who=0,
            slot=1,
            loads=dict(
                agrad=(pa_1, None, (hidden, width)),
                wout=weights.wout,
                probs=b.probs,
                qkv=b.qkv,
                win=weights.win,
                xv=rows[1],
                middle_grad=part.middle_grad,
            ),
            stores=dict(jg="jg", leave=("ends", span)),
            carried=dict(y, ends=x.ends),
            after=after,
        )

    def pair_of(size, first):
        cut = size // 2 if fused else size // 32 * 16
        one = Chunk("rep", bits, cut, (1,) if fused else ())
        two = Chunk("rep", bits, size - cut, (2,) if fused else ())
        if fused:
            send_1, keep_1, send_2, keep_2 = first
            one.add(keep_1)
            two.add(keep_2)
            return one, two, send_1, send_2
        view = first.reshape((count // 2, 2) + first.shape[1:])
        cut = lambda at: lax.dynamic_index_in_dim(view, at, 1, keepdims=False)
        came = swap(cut(1 - core).astype(BF16), 0)
        for item in (cut(core), came):
            one.add(item)
            two.add(item, one.size)
        return one, two, one.split(1), two.split(2)

    if fused:
        pa_other = swap(pa_1, 0)
        sent = term(
            "term_reduce",
            term_reduce,
            lines=sizes[0],
            base=bases[0],
            rows=hidden // 2,
            lefts=lefts,
            rights=[x.bg, bg_1, others[0], bg_1_other],
            after=(pa_1,),
        )
        r1, r2, send_1, send_2 = pair_of(sizes[0], sent)
        came_r1, came_r2 = swap(send_1, 1), swap(send_2, 2)
        sent = term(
            "term_expand",
            term_expand,
            lines=sizes[1],
            base=bases[1],
            rows=width,
            lefts=lefts,
            rights=[x.pa, pa_1, others[1], pa_other],
            embeds=embeds,
            after=(send_1, send_2),
        )
        came_r1, came_r2, *sent = join(came_r1, came_r2, *sent)
        e1, e2, send_1, send_2 = pair_of(sizes[1], sent)
        came_e1, came_e2 = swap(send_1, 1), swap(send_2, 2)
        came_r1, came_r2, _, _ = join(came_r1, came_r2, send_1, send_2)
        r1.add(came_r1)
        r2.add(came_r2)
        send_1, send_2 = r1.split(2), r2.split(1)
        came_r1, came_r2 = swap(send_1, 2), swap(send_2, 1)
        last = last_attend((send_1, send_2))
        came_e1, came_e2, came_r1, came_r2, jg_1 = join(
            came_e1, came_e2, came_r1, came_r2, last.jg
        )
        jg_other = swap(jg_1, 0)
        e1.add(came_e1)
        e2.add(came_e2)
        send_1, send_2 = e1.split(2), e2.split(1)
        came_e1, came_e2 = swap(send_1, 2), swap(send_2, 1)
        came_r1, came_r2, _, _ = join(came_r1, came_r2, send_1, send_2)
        r1.add(came_r1)
        r2.add(came_r2)
        block_r = jnp.concatenate([r1.split(3), r2.split(3)], axis=-2)
        came_r = swap(block_r, 3)
        sent = term(
            "term_attend",
            term_attend,
            lines=sizes[2],
            base=bases[3],
            rows=width // 2,
            lefts=lefts,
            rights=[x.jg, jg_1, others[2], jg_other],
            after=(send_1, send_2, block_r),
        )
        came_e1, came_e2, *sent = join(came_e1, came_e2, *sent)
        a1, a2, send_1, send_2 = pair_of(sizes[2], sent)
    else:
        last = last_attend(())
        rights = [(x.bg, bg_1), (x.pa, pa_1), (x.jg, last.jg)]
        totals = plain_pieces((x.left, y.left), rights, embed.T, common.sizes)
        r1, r2, send_1, send_2 = pair_of(sizes[0], totals[0])
        r1.add(swap(send_1, 1))
        r2.add(swap(send_2, 2))
        r1.add(swap(r1.split(2), 2))
        r2.add(swap(r2.split(1), 1))
        block_r = jnp.concatenate([r1.split(3), r2.split(3)], axis=-2)
        came_r = swap(block_r, 3)
        e1, e2, send_1, send_2 = pair_of(sizes[1], totals[1])
        e1.add(swap(send_1, 1))
        e2.add(swap(send_2, 2))
        came_e1, came_e2 = swap(e1.split(2), 2), swap(e2.split(1), 1)
        a1, a2, send_1, send_2 = pair_of(sizes[2], totals[2])
    ends = last.ends
    came_a1, came_a2 = swap(send_1, 1), swap(send_2, 2)
    e1.add(came_e1)
    e2.add(came_e2)
    block_e = jnp.concatenate([e1.split(3), e2.split(3)], axis=-2)
    came_e = swap(block_e, 3)
    came_r, _ = join(came_r, block_e)
    r1.add(came_r[..., : r1.size, :])
    r2.add(came_r[..., r1.size :, :])
    came_a1, came_a2, _ = join(came_a1, came_a2, block_e)
    a1.add(came_a1)
    a2.add(came_a2)
    send_1, send_2 = a1.split(2), a2.split(1)
    came_a1, came_a2 = swap(send_1, 2), swap(send_2, 1)
    a1.add(came_a1)
    a2.add(came_a2)
    block_a = jnp.concatenate([a1.split(3), a2.split(3)], axis=-2)
    came_a = swap(block_a, 3)
    came_e, _ = join(came_e, block_a)
    e1.add(came_e[..., : e1.size, :])
    e2.add(came_e[..., e1.size :, :])
    a1.add(came_a[..., : a1.size, :])
    a2.add(came_a[..., a1.size :, :])
    for bit in range(4, bits):
        for chunk in (r1, r2, e1, e2, a1, a2):
            chunk.add(swap(chunk.split(bit), bit))
    share_r, share_e, share_a = (
        jnp.concatenate([one.total(), two.total()]) for one, two in ((r1, r2), (e1, e2), (a1, a2))
    )
    tall = hidden // width
    side = lambda item, n, size: jnp.concatenate(
        [item[i * size : (i + 1) * size] for i in range(n)], axis=1
    )
    at_o = tall * lines
    at_t = at_o + lines
    small = share_e[at_t + 3 * deep :]
    flat = lambda item, first, n: lax.dynamic_slice_in_dim(
        item[first : first + n].reshape(-1), rank * (n * width // count), n * width // count
    )
    results = (
        flat(share_a, 3 * lines, 1),
        side(share_a, 3, lines),
        share_e[at_o:at_t],
        side(share_e[at_t:], 3, deep),
        flat(small, 1, 3),
        side(share_e, tall, lines),
        flat(small, 4, tall),
        share_r,
        flat(small, 0, 1),
    )
    return (ends[None],) + tuple(piece[None] for piece in results)


def solution(mesh):
    return jax.shard_map(
        per_device,
        mesh=mesh,
        in_specs=(
            P("section", "rep", None),
            P("rep", None, None),
            P("rep", None, None),
            P("section", None),
            P("section", None, None),
            P("section", None, None),
            P("section", None, None),
            P("section", None),
            P("section", None, None),
            P("section", None),
            P("section", None, None),
            P("section", None),
        ),
        out_specs=(
            P("section", "rep", None),
            P("section", "rep"),
            P("section", "rep", None),
            P("section", "rep", None),
            P("section", "rep", None),
            P("section", "rep"),
            P("section", "rep", None),
            P("section", "rep"),
            P("section", "rep", None),
            P("section", "rep"),
        ),
        check_vma=False,
    )
```

```python
from functools import partial
import inspect
import math

import jax
import jax.numpy as jnp
import numpy as np
from jax import lax
from jax.experimental import pallas as pl
from jax.experimental.pallas import tpu as pltpu
from jax.sharding import PartitionSpec as P

HEADS = 12
HEAD = 64
EMB = 128
SEGS = 4
ANY = pl.ANY
VMEM = pltpu.MemorySpace.VMEM
SMEM = pltpu.MemorySpace.SMEM
F32 = jnp.float32
BF16 = jnp.bfloat16
ROOT_HALF = 0.7071067811865476
ROOT_TAU = 0.3989422804014327
TILE = 384
TAIL_ROWS = 24
GAIN_ROWS = 16
EXTRA = 16


class Bag(dict):
    __getattr__ = dict.__getitem__


def dot(left, right, left_dim=1, right_dim=0):
    return lax.dot_general(
        left, right, (((left_dim,), (right_dim,)), ((), ())), preferred_element_type=F32
    )


def repeat(count, body):
    for i in range(count):
        body(i)


def steps_of(count, size, body):
    def several(i, _):
        for j in range(size):
            body(size * i + j)
        return _

    lax.fori_loop(0, count // size, several, 0)


def lanes(index, size, start=0):
    if isinstance(index, int):
        return slice(start + index * size, start + (index + 1) * size)
    return pl.ds(pl.multiple_of(start + index * size, size), size)


def swap_halves(values, low_half):
    forth = pltpu.roll(values, 128 - HEAD // 2, 1)
    back = pltpu.roll(values, HEAD // 2, 1)
    return jnp.where(low_half, forth, back)


def norm_parts(values):
    center = values - jnp.mean(values, axis=-1, keepdims=True)
    spread = jnp.mean(center * center, axis=-1, keepdims=True)
    factor = lax.rsqrt(spread + 1e-05)
    return center * factor, factor


def norm_back(grad, unit, factor):
    return factor * (
        grad
        - jnp.mean(grad, axis=-1, keepdims=True)
        - unit * jnp.mean(grad * unit, axis=-1, keepdims=True)
    )


class Held:
    def __init__(self, bufs, loads, stores, sems, pieces):
        self.bufs = bufs
        self.loads = loads
        self.stores = stores
        self.sems = sems
        self.pieces = pieces
        self.names = {id(buf): name for name, buf in bufs.items()}
        keys = [(name, j) for name in loads for j in range(self.parts_of(name))]
        self.spots = {key: n for n, key in enumerate(keys)}
        self.waiting = set(keys)
        self.pending = set(keys)
        self.leaving = {}

    def parts_of(self, name):
        return self.pieces[name][1] if name in self.pieces else 1

    def load(self, name, j):
        source, target = self.loads[name], self.bufs[name]
        if name in self.pieces:
            axis, count = self.pieces[name]
            size = target.shape[axis] // count
            at = (slice(None),) * axis + (pl.ds(j * size, size),)
            source, target = source.at[at], target.at[at]
        return pltpu.make_async_copy(source, target, self.sems.at[self.spots[(name, j)]])

    def store(self, name, n):
        at, target = self.stores[name][n]
        source = self.bufs[name] if at is None else self.bufs[name].at[at]
        return pltpu.make_async_copy(source, target, self.sems.at[self.leaving[(name, n)]])

    def keys(self, bufs, part):
        for buf in bufs:
            name = self.names[id(buf)]
            for j in range(self.parts_of(name)):
                if part in (None, j):
                    yield name, j

    def begin(self, *bufs, part=None):
        for key in self.keys(bufs, part):
            if key in self.waiting:
                self.waiting.remove(key)
                self.load(*key).start()

    def need(self, *bufs, part=None):
        self.begin(*bufs, part=part)
        for key in self.keys(bufs, part):
            if key in self.pending:
                self.pending.remove(key)
                self.load(*key).wait()

    def done(self, *bufs):
        for buf in bufs:
            name = self.names[id(buf)]
            for n in range(len(self.stores.get(name, ()))):
                self.leaving[(name, n)] = len(self.spots) + len(self.leaving)
                self.store(name, n).start()

    def finish(self):
        for name, n in self.leaving:
            self.store(name, n).wait()


class Layer:
    def __init__(self, sizes, slot, refs):
        self.span, self.width, self.hidden, self.count = sizes
        self.slot = slot
        lengths, place, self.mods, self.trig, self.gain, self.ebias, self.rbias = refs
        self.section = place[0]
        self.core = place[1]
        self.single = lengths[slot, 0] == self.span
        self.pairs = self.width // 128
        self.seg = self.span // SEGS
        self.step = self.width
        self.tiles = self.hidden // self.step
        place = lax.broadcasted_iota(jnp.int32, (self.span, 128), 1)
        self.low_half = place % HEAD < HEAD // 2
        self.low_head = place < HEAD
        row = lax.broadcasted_iota(jnp.int32, (1, 128), 1) // HEAD
        self.head_row = [(row == i).astype(F32).astype(BF16) for i in range(2)]
        self.blocks = [(b, slice(b * self.seg, (b + 1) * self.seg)) for b in range(SEGS)]

    def trig_pair(self):
        cos_all, sin_all = self.trig[0], self.trig[1]
        cos_cut = jnp.concatenate([cos_all[: self.seg]] * SEGS, axis=0)
        sin_cut = jnp.concatenate([sin_all[: self.seg]] * SEGS, axis=0)
        return jnp.where(self.single, cos_all, cos_cut), jnp.where(self.single, sin_all, sin_cut)

    def mod_row(self, block, part):
        row = self.slot * SEGS + jnp.where(self.single, 0, block)
        return self.mods[pl.ds(row, 1), part * self.width : (part + 1) * self.width]

    def add_segment(self, small, block, at, sums):
        row = 2 + jnp.where(self.single, 0, block)
        small[pl.ds(row, 1), at * self.width : (at + 1) * self.width] += sums

    def side(self, block):
        return self.core if block % 2 == 0 else 1 - self.core

    def put_left(self, left, base, values):
        turned = values.T
        if left.shape[0] == 1:
            left[0, 2 * base : 2 * base + self.width] = turned
            return
        lines = self.width // self.count
        for block in range(self.count):
            to = base + block // 2 * lines
            left[self.side(block), to : to + lines] = turned[block * lines : (block + 1) * lines]

    def put_active(self, left, j, values):
        turned = values.T
        if left.shape[0] == 1:
            left[0, lanes(j, self.step)] = turned
            return
        lines = self.hidden // self.count
        per = self.step // lines
        for n in range(per):
            to = lanes(j, lines * (per // 2), n // 2 * lines)
            to = slice(to.start, to.start + lines) if isinstance(j, int) else pl.ds(to.start, lines)
            left[self.side(n), to] = turned[n * lines : (n + 1) * lines]

    def thirds(self, index):
        return [lanes(index, 128, p * self.width) for p in range(3)]


def left_bases(width, hidden):
    return 0, hidden // 2, (hidden + width) // 2, (hidden + 2 * width) // 2


def forward(
    k, xv, win, wout, wex, wre, left, qkv, probs, middle, slope, branch, result, bias, normed,
    mixed, modded,
):
    span, width, held = k.span, k.width, k.held
    _, at_modded, at_mixed, at_normed = left_bases(width, k.hidden)
    held.begin(xv, win)
    held.need(xv)
    unit, _ = norm_parts(xv[...].astype(F32))
    normed[...] = (unit * k.gain[...].astype(F32)).astype(BF16)
    across = lax.broadcasted_iota(jnp.int32, (span, span), 0) // k.seg
    down = lax.broadcasted_iota(jnp.int32, (span, span), 1) // k.seg
    bias[...] = jnp.where((across == down) | k.single, 0.0, -1e30)
    held.need(win)
    held.begin(wout, wex, wre)
    cos_part, sin_part = k.trig_pair()
    for tile, factor in ((0, 0.125), (1, 1.0)):
        for i in range(width // 256):
            at = lanes(i, 256, tile * width)
            joint = dot(normed[...], win[:, at])
            outs = []
            for piece in (joint[:, :128], joint[:, 128:]):
                turned = piece * cos_part + swap_halves(piece, k.low_half) * sin_part
                outs.append((turned * factor).astype(BF16))
            qkv[:, at] = jnp.concatenate(outs, axis=1)
    qkv[:, 2 * width :] = dot(normed[...], win[:, 2 * width :]).astype(BF16)
    held.done(qkv)
    if k.kept:
        k.put_left(left, at_normed, normed[...])

    def heads(i):
        at = k.thirds(i)
        query, key, value = (qkv[:, a] for a in at)
        outs = []
        for h in range(2):
            scores = dot(key * k.head_row[h], query, 1, 1) + bias[...]
            top = jnp.max(scores, axis=0, keepdims=True)
            raised = jnp.exp(scores - top)
            total = jnp.sum(raised, axis=0, keepdims=True)
            prob = raised * (1.0 / total)
            if k.kept:
                probs[2 * i + h] = prob
            outs.append(dot(prob.astype(BF16), value, 0, 0))
        mixed[:, at[0]] = jnp.where(k.low_head, outs[0], outs[1]).astype(BF16)

    steps_of(k.pairs, k.heads_step, heads)
    held.done(probs)
    held.need(wout)
    middle[...] = xv[...].astype(F32) + dot(mixed[...], wout[...])
    held.done(middle)
    if k.kept:
        k.put_left(left, at_mixed, mixed[...])
    for b, rows in k.blocks:
        unit, _ = norm_parts(middle[rows])
        modded[rows] = (unit * (1.0 + k.mod_row(b, 0)) + k.mod_row(b, 1)).astype(BF16)
    if k.kept:
        k.put_left(left, at_modded, modded[...])
    held.need(wex, wre)
    branch[...] = jnp.broadcast_to(k.rbias[...].astype(F32), (span, width))

    def feed(j):
        at = lanes(j, k.step)
        pre = dot(modded[...], wex[:, at]) + k.ebias[:, at].astype(F32)
        area = 0.5 + 0.5 * lax.erf(pre * ROOT_HALF)
        out = (pre * area).astype(BF16)
        if k.kept:
            slope[:, at] = area + pre * (jnp.exp(pre * pre * -0.5) * ROOT_TAU)
            k.put_active(left, j, out)
        branch[...] += dot(out, wre[at, :])

    if k.heads_step == 1:
        steps_of(k.tiles, 1, feed)
    else:
        repeat(k.tiles, feed)
    held.done(slope, left, branch)
    for b, rows in k.blocks:
        result[rows] = (middle[rows] + k.mod_row(b, 2) * branch[rows]).astype(BF16)
    held.done(result)


def output(k, dyv, bg):
    k.held.need(dyv)
    for b, rows in k.blocks:
        bg[rows] = (dyv[rows].astype(F32) * k.mod_row(b, 2)).astype(BF16)
    k.held.done(bg)


def mlp(k, wre, wex, bg, slope, middle, branch, dyv, pa, middle_grad, small, acc):
    span, width, hidden, held = k.span, k.width, k.hidden, k.held
    small[...] = jnp.zeros(small.shape, F32)
    acc[...] = jnp.zeros(acc.shape, F32)
    held.begin(bg)
    for j in range(k.tiles):
        held.begin(wre, slope, wex, part=j)
    held.begin(middle, dyv, branch)
    held.need(bg)

    def feed(j):
        at = lanes(j, k.step)
        held.need(wre, slope, wex, part=j)
        grad = dot(bg[...], wre[at, :], 1, 1)
        pre_grad = (slope[:, at] * grad).astype(BF16)
        pa[:span, at] = pre_grad
        small[0:1, at] = jnp.sum(pre_grad.astype(F32), axis=0, keepdims=True)
        acc[...] += dot(pre_grad, wex[:, at], 1, 1)

    repeat(k.tiles, feed)
    held.need(middle, dyv, branch)
    total = jnp.zeros((1, width), F32)
    for b, rows in k.blocks:
        cotan = dyv[rows].astype(F32)
        total += jnp.sum(bg[rows].astype(F32), axis=0, keepdims=True)
        grad = acc[rows]
        unit, factor = norm_parts(middle[rows])
        k.add_segment(small, b, 0, jnp.sum(grad * unit, axis=0, keepdims=True))
        k.add_segment(small, b, 1, jnp.sum(grad, axis=0, keepdims=True))
        k.add_segment(small, b, 2, jnp.sum(cotan * branch[rows], axis=0, keepdims=True))
        back = norm_back(grad * (1.0 + k.mod_row(b, 0)), unit, factor)
        full = cotan + back
        middle_grad[rows] = full
        pa[rows, hidden:] = full.astype(BF16)
    small[1:2, :width] = total
    pa[span:, :] = small[...].astype(BF16)
    held.done(pa, middle_grad)


def attend(
    k, wout, win, agrad, probs, qkv, xv, middle_grad, jg, leave, mixed_grad, acc
):
    span, held = k.span, k.held
    held.need(agrad, wout)
    held.begin(probs, qkv)
    mixed_grad[...] = dot(agrad[...], wout[...], 1, 1).astype(BF16)
    held.need(probs, qkv)
    held.begin(win, xv, middle_grad)
    cos_part, sin_part = k.trig_pair()

    def heads(i):
        at = k.thirds(i)
        query, key, value = (qkv[:, a] for a in at)
        out_grad = mixed_grad[:, at[0]]
        parts = []
        for h in range(2):
            prob = probs[2 * i + h]
            pull = dot(value * k.head_row[h], out_grad, 1, 1)
            shared = jnp.sum(prob * pull, axis=0, keepdims=True)
            score_grad = (prob * (pull - shared)).astype(BF16)
            parts.append(
                (
                    dot(score_grad, key, 0, 0),
                    dot(score_grad, query),
                    dot(prob.astype(BF16), out_grad),
                )
            )
        for p in range(3):
            grad = jnp.where(k.low_head, parts[0][p], parts[1][p])
            if p < 2:
                grad = grad * cos_part - swap_halves(grad, k.low_half) * sin_part
                if p == 0:
                    grad = grad * 0.125
            jg[:span, at[p]] = grad.astype(BF16)

    steps_of(k.pairs, k.heads_step, heads)
    held.need(win, xv, middle_grad)
    acc[...] = dot(jg[:span, :], win[...], 1, 1)
    total = jnp.zeros((1, k.width), F32)
    for b, rows in k.blocks:
        grad = acc[rows]
        unit, factor = norm_parts(xv[rows].astype(F32))
        total += jnp.sum(grad * unit, axis=0, keepdims=True)
        back = norm_back(grad * k.gain[...].astype(F32), unit, factor)
        leave[rows] = (middle_grad[rows] + back).astype(BF16)
    below = jnp.concatenate([total, jnp.zeros((EXTRA - 1, k.width), F32)], axis=0)
    jg[span:, : k.width] = below.astype(BF16)
    jg[span:, k.width :] = jnp.zeros((EXTRA, 2 * k.width), BF16)
    held.done(jg, leave)


def copy_agrad(k, pa, agrad):
    agrad[...] = pa[: k.span, k.hidden :]


class Sums:
    def __init__(self, ranks, full, outs, sems):
        self.full = full
        self.own = [((ranks[0] >> bit) & 1) == 0 for bit in (1, 2)]
        self.bufs = outs[:4]
        self.targets = outs[4:]
        self.sems = sems
        self.half = full.shape[1] // 2
        self.copies = []

    def put(self, block, at, values):
        self.full[block, at] = values

    def settle(self, which, groups):
        send, keep = self.bufs[2 * which : 2 * which + 2]
        at = slice(which * self.half, (which + 1) * self.half)
        apart = 1 + which
        for group in groups:
            for n in range(2):
                first = 4 * group + (2 * n if which == 0 else n)
                even, odd = self.full[first, at], self.full[first + apart, at]
                send[2 * group + n] = jnp.where(self.own[which], odd, even).astype(BF16)
                keep[2 * group + n] = jnp.where(self.own[which], even, odd)
            spot = pl.ds(2 * group, 2)
            for n in range(2 * which, 2 * which + 2):
                copy = pltpu.make_async_copy(
                    self.bufs[n].at[spot], self.targets[n].at[spot], self.sems.at[len(self.copies)]
                )
                copy.start()
                self.copies.append(copy)

    def finish(self):
        for copy in self.copies:
            copy.wait()


def term_reduce(k, sums, left, right):
    lines = k.hidden // k.count
    per = TILE // lines
    for tile in range(k.hidden // 2 // TILE):
        k.arrive(tile)
        total = dot(left[tile * TILE : (tile + 1) * TILE], right[...])
        for n in range(per):
            sums.put(tile * per + n, slice(0, lines), total[n * lines : (n + 1) * lines])
        if (tile + 1) * per % 4 == 0:
            group = ((tile + 1) * per // 4 - 1,)
            sums.settle(0, group)
            sums.settle(1, group)


def square_terms(k, sums, left, right, cols, part):
    lines = k.width // k.count
    total = dot(left, right[: 4 * k.span, cols])
    for n in range(k.count // 2):
        sums.put(n, slice(part * lines, (part + 1) * lines), total[n * lines : (n + 1) * lines])


def term_expand(k, sums, left, right):
    width, hidden, span = k.width, k.hidden, k.span
    groups = range(k.count // 8)
    tall = hidden // width
    lines = width // k.count
    rows = width // 2
    half = sums.half
    settled = False
    for col in range(tall + 1):
        k.arrive(col)
        part = left[:rows] if col < tall else left[rows:]
        square_terms(k, sums, part, right, slice(col * width, (col + 1) * width), col)
        if (col + 1) * lines >= half and not settled:
            sums.settle(0, groups)
            settled = True
    smalls = [k.small[n].astype(F32) for n in range(4)]
    angles = jnp.concatenate([embed[...] for embed in k.embeds], axis=1)
    pieces = []
    for _ in range(3):
        pieces.append(angles.astype(BF16))
        angles = angles - pieces[-1].astype(F32)
    seqs = jnp.concatenate([small[2 : 2 + SEGS, : 3 * width] for small in smalls]).astype(BF16)
    times = sum(dot(piece, seqs) for piece in pieces)
    both = sum(smalls)
    seq_sum = jnp.sum(both[2 : 2 + SEGS, : 3 * width], axis=0, keepdims=True)
    lines_v = k.lines
    lines_v[...] = jnp.zeros(lines_v.shape, F32)
    lines_v[0:1] = both[1:2, :width]
    for n in range(3):
        lines_v[1 + n : 2 + n] = seq_sum[:, n * width : (n + 1) * width]
    for n in range(tall):
        lines_v[4 + n : 5 + n] = both[0:1, n * width : (n + 1) * width]
    deep = EMB // k.count
    first = (tall + 1) * lines
    low = k.core == 0
    for g in range(k.count // 2):
        for p in range(3):
            at = slice(p * width, (p + 1) * width)
            even = times[2 * g * deep : (2 * g + 1) * deep, at]
            odd = times[(2 * g + 1) * deep : (2 * g + 2) * deep, at]
            to = first + p * deep
            sums.put(g, slice(to, to + deep), jnp.where(low, even, odd))
        sums.put(g, slice(first + 3 * deep, 2 * half), lines_v[...])
    sums.settle(1, groups)


def term_attend(k, sums, left, right):
    width = k.width
    groups = range(k.count // 8)
    lines = width // k.count
    settled = False
    for col in range(3):
        k.arrive(col)
        square_terms(k, sums, left[...], right, slice(col * width, (col + 1) * width), col)
        if (col + 1) * lines >= sums.half and not settled:
            sums.settle(0, groups)
            settled = True
    gain = sum(k.small[n].astype(F32) for n in range(4))[:, :width]
    for g in range(k.count // 2):
        sums.put(g, slice(3 * lines, 3 * lines + GAIN_ROWS), gain)
    sums.settle(1, groups)


def load_terms(k, refs, bufs, base, sems):
    left_v, right_v, small_v = bufs
    rows, cols = left_v.shape[0], right_v.shape[1]
    tall = rows // TILE if small_v is None else 1
    wide = cols // k.width
    groups = []
    for i in range(tall):
        for j in range(wide):
            copies = []
            for n, (left, right) in enumerate(zip(refs[:4], refs[4:8])):
                tokens = pl.ds(n * k.span, k.span)
                part = pl.ds(i * (rows // tall), rows // tall)
                from_part = pl.ds(base + i * (rows // tall), rows // tall)
                at = pl.ds(j * k.width, k.width)
                if j == 0:
                    copies.append((left.at[from_part], left_v.at[part, tokens]))
                if i == 0:
                    copies.append((right.at[pl.ds(0, k.span), at], right_v.at[tokens, at]))
                if small_v is not None and j == wide - 1:
                    copies.append((right.at[pl.ds(k.span, EXTRA)], small_v.at[n]))
            groups.append(copies)
    made, count = [], 0
    for copies in groups:
        made.append([])
        for pair in copies:
            made[-1].append(pltpu.make_async_copy(*pair, sems.at[count]))
            made[-1][-1].start()
            count += 1
    return made


class Terms:
    def __init__(self, sizes, core):
        self.span, self.width, self.hidden, self.count = sizes
        self.core = core[0]

    def arrive(self, group):
        for copy in self.groups[group]:
            copy.wait()


def term_kernel(sizes, body, base, extra, *refs):
    refs = list(refs)
    core, rank = refs[:2]
    k = Terms(sizes, core)
    pos = 2
    if body is term_expand:
        k.embeds = refs[pos : pos + 2]
        pos += 2
    sources = refs[pos : pos + 8]
    pos += 8 + extra
    targets = refs[pos : pos + 4]
    pos += 4
    left_v, right_v, full, *outs = refs[pos : pos + 7]
    pos += 7
    k.small = None
    if body is not term_reduce:
        k.small, k.lines = refs[pos : pos + 2]
        pos += 2
    sems, out_sems = refs[pos:]
    k.groups = load_terms(k, sources, (left_v, right_v, k.small), base, sems)
    sums = Sums(rank, full, outs + targets, out_sems)
    body(k, sums, left_v, right_v)
    sums.finish()


def term_call(name, body, sizes, lines, base, rows, core, rank, lefts, rights, embeds=(), after=()):
    span, width, hidden, count = sizes
    blocks = count // 2
    cols = rights[0].shape[1]
    half = lines // 2
    outs = [((blocks // 2, half, width), kind) for kind in (BF16, F32)] * 2
    scratch = [
        ((rows, 4 * span), BF16),
        ((4 * span, cols), BF16),
        ((blocks, lines, width), F32),
        *outs,
    ]
    if body is not term_reduce:
        scratch += [((4, EXTRA, cols), BF16), ((TAIL_ROWS, width), F32)]
    args = [core.reshape(1), rank.reshape(1), *embeds, *lefts, *rights, *after]
    in_specs = [pl.BlockSpec(memory_space=SMEM)] * 2
    in_specs += [pl.BlockSpec(memory_space=VMEM)] * len(embeds)
    in_specs += [pl.BlockSpec(memory_space=ANY)] * (8 + len(after))
    return pl.pallas_call(
        partial(term_kernel, sizes, body, base, len(after)),
        out_shape=[jax.ShapeDtypeStruct(*item) for item in outs],
        in_specs=in_specs,
        out_specs=[pl.BlockSpec(memory_space=ANY)] * 4,
        scratch_shapes=[pltpu.VMEM(*item) for item in scratch]
        + [pltpu.SemaphoreType.DMA((32,)), pltpu.SemaphoreType.DMA((8,))],
        compiler_params=pltpu.CompilerParams(vmem_limit_bytes=62 * 1024 * 1024),
        name=name,
    )(*args)


def plain_pieces(lefts, rights, embed, sizes):
    span, width, hidden, count = sizes
    bg, pa, jg = rights
    bases = [2 * base for base in left_bases(width, hidden)]

    def blocks(base, rows, right):
        total = sum(dot(a[base : base + rows], b) for a, b in zip(lefts, right))
        parts = [total[:, i : i + width] for i in range(0, total.shape[1], width)]
        return [part.reshape(count, -1, width) for part in parts]

    take = lambda items, cols: [item[:span, cols] for item in items]
    reduce = blocks(bases[0], hidden, bg)
    expand = blocks(bases[1], width, take(pa, slice(0, hidden)))
    expand += blocks(bases[2], width, take(pa, slice(hidden, hidden + width)))
    last = blocks(bases[3], width, take(jg, slice(None)))
    small = [item[span:].astype(F32) for item in pa]
    seqs = jnp.concatenate([item[2 : 2 + SEGS, : 3 * width] for item in small])
    times = jnp.dot(embed, seqs, precision=lax.Precision.HIGHEST)
    expand += [times[:, i * width : (i + 1) * width].reshape(count, -1, width) for i in range(3)]
    lines = jnp.concatenate(
        [
            sum(item[1:2, :width] for item in small),
            jnp.sum(seqs, axis=0).reshape(-1, width),
            sum(item[0, :hidden] for item in small).reshape(-1, width),
        ]
    )
    lines = jnp.pad(lines, ((0, TAIL_ROWS - lines.shape[0]), (0, 0)))
    gain = sum(item[span:, :width].astype(F32) for item in jg)
    expand.append(jnp.broadcast_to(lines, (count,) + lines.shape))
    last.append(jnp.broadcast_to(gain, (count,) + gain.shape))
    return [jnp.concatenate(item, axis=1) for item in (reduce, expand, last)]


def shapes_of(span, width, hidden, cores):
    tok = lambda cols, kind=BF16: ((span, cols), kind)
    below = lambda cols: ((span + EXTRA, cols), BF16)
    return dict(
        xv=tok(width),
        dyv=tok(width),
        win=((width, 3 * width), BF16),
        wout=((width, width), BF16),
        wex=((width, hidden), BF16),
        wre=((hidden, width), BF16),
        left=((cores, (hidden + 3 * width) // cores, span), BF16),
        normed=tok(width),
        qkv=tok(3 * width),
        probs=((HEADS, span, span), F32),
        mixed=tok(width),
        middle=tok(width, F32),
        modded=tok(width),
        slope=tok(hidden, F32),
        branch=tok(width, F32),
        result=tok(width),
        bg=tok(width),
        pa=below(hidden + width),
        jg=below(3 * width),
        agrad=tok(width),
        mixed_grad=tok(width),
        middle_grad=tok(width, F32),
        leave=tok(width),
        acc=tok(width, F32),
        bias=tok(span, F32),
        small=((EXTRA, hidden + width), F32),
    )


def uses(part):
    return list(inspect.signature(part).parameters)[1:]


def stage_kernel(sizes, parts, who, slot, plan, *refs):
    refs = list(refs)
    layer = Layer(sizes, slot, refs[:7])
    span = layer.span
    pos = 7
    loads = {}
    for name, row, cols in plan.sources:
        ref = refs[pos]
        if cols is not None:
            ref = ref.at[pl.ds(0, span), pl.ds(*cols)]
        elif row is not None:
            ref = ref.at[pl.ds(row, span)]
        loads[name] = ref
        pos += 1
    pos += plan.extra
    stores = {}
    for name, row, at in plan.targets:
        target = refs[pos] if row is None else refs[pos].at[pl.ds(row, span)]
        stores.setdefault(name, []).append((at, target))
        pos += 1
    bufs = {}
    for name in plan.bufs:
        bufs[name] = refs[pos]
        pos += 1
    layer.held = Held(bufs, loads, stores, refs[pos], plan.pieces)
    layer.kept = plan.kept
    layer.heads_step = plan.heads_step

    @pl.when(layer.section == who)
    def _():
        for part in parts:
            part(layer, *[bufs[name] for name in uses(part)])
        layer.held.finish()


def stage(
    name, common, parts, who, slot, loads, stores, carried=None, after=(), kept=True, heads_step=3,
    pieces=None,
):
    carried = carried or {}
    span, width, hidden, count = common.sizes
    shapes = shapes_of(span, width, hidden, common.cores)
    bufs = []
    for part in parts:
        bufs += [item for item in uses(part) if item not in bufs]
    pair = lambda item: item if isinstance(item, tuple) else (item, None)
    args = list(common.args)
    in_specs = [pl.BlockSpec(memory_space=SMEM)] * 2 + [pl.BlockSpec(memory_space=VMEM)] * 5
    plan = Bag(sources=[], targets=[], bufs=bufs, kept=kept, heads_step=heads_step)
    plan["pieces"] = pieces or {}
    for item in loads:
        if item in bufs:
            array, row, *cols = pair(loads[item])
            args.append(array)
            plan.sources.append((item, row, cols[0] if cols else None))
    outs, aliases, extra = [], {}, []
    targets = []
    for item, key in stores.items():
        if item == "left":
            targets += [(item, key + "_send" * n, None, n) for n in range(common.cores)]
        else:
            targets.append((item, *pair(key), None))
    for i, (item, key, row, at) in enumerate(targets):
        shape, kind = shapes[item]
        if row is not None:
            shape = (common.tokens,) + shape[1:]
        if at is not None:
            shape = shape[1:]
        outs.append(jax.ShapeDtypeStruct(shape, kind))
        plan.targets.append((item, row, at))
        if key in carried:
            aliases[len(args) + len(extra)] = i
            extra.append(carried[key])
    extra += list(after)
    args += extra
    plan["extra"] = len(extra)
    in_specs += [pl.BlockSpec(memory_space=ANY)] * (len(args) - len(in_specs))
    results = pl.pallas_call(
        partial(stage_kernel, common.sizes, parts, who, slot, plan),
        out_shape=outs,
        in_specs=in_specs,
        out_specs=[pl.BlockSpec(memory_space=ANY)] * len(outs),
        input_output_aliases=aliases,
        scratch_shapes=[pltpu.VMEM(*shapes[item]) for item in bufs]
        + [pltpu.SemaphoreType.DMA((32,))],
        compiler_params=pltpu.CompilerParams(vmem_limit_bytes=62 * 1024 * 1024),
        name=name,
    )(*args)
    return Bag({key: value for (_, key, _, _), value in zip(targets, results)})


def bits_of(count):
    bits = count.bit_length() - 1
    assert 1 << bits == count
    return bits


class Chunk:
    def __init__(self, axis, bits, size, settled=()):
        self.axis = axis
        self.bits = list(range(bits - 1, 0, -1))
        self.size = size
        self.settled = list(settled)
        self.terms = []

    def add(self, term, start=0):
        left = [bit for bit in self.bits if bit not in self.settled]
        self.terms.append((term.reshape((2,) * len(left) + term.shape[-2:]), left, start))

    def take(self, term, start, left, flip):
        me = lax.axis_index(self.axis)
        side = lambda bit: 1 - ((me >> bit) & 1) if bit == flip else (me >> bit) & 1
        starts = [side(bit) if bit in self.settled else 0 for bit in left]
        sizes = [1 if bit in self.settled else 2 for bit in left]
        cols = term.shape[-1]
        piece = lax.dynamic_slice(term, starts + [start, 0], sizes + [self.size, cols])
        open_bits = [2] * (len(self.bits) - len(self.settled))
        return piece.reshape(open_bits + [self.size, cols]).astype(F32)

    def split(self, bit):
        self.settled.append(bit)
        return sum(self.take(term, start, left, bit) for term, left, start in self.terms).astype(
            BF16
        )

    def total(self):
        return sum(self.take(term, start, left, None) for term, left, start in self.terms)


def exchange(block, axis, bit):
    count = lax.axis_size(axis)
    return lax.ppermute(block, axis, [(i, i ^ (1 << bit)) for i in range(count)])


def join(*items):
    return lax.optimization_barrier(items)


def angle_table(span):
    half = HEAD // 2
    freqs = np.exp(-math.log(10000.0) * np.arange(half, dtype=np.float32) / half)
    phase = np.arange(span, dtype=np.float32)[:, None] * freqs.astype(np.float32)[None, :]
    cos_part, sin_part = np.cos(phase), np.sin(phase)
    return np.stack(
        [
            np.concatenate([cos_part] * 4, axis=1),
            np.concatenate([-sin_part, sin_part] * 2, axis=1),
        ]
    ).astype(np.float32)


def per_device(
    ends_in,
    lengths,
    times,
    norm_gain,
    attend_in,
    attend_out,
    time_weight,
    time_bias,
    expand_weight,
    expand_bias,
    reduce_weight,
    reduce_bias,
):
    local = ends_in[0]
    micro = lengths.shape[1]
    assert micro == 2
    width = local.shape[1]
    span = local.shape[0] // micro
    hidden = expand_weight.shape[2]
    count = lax.axis_size("rep")
    section = lax.axis_index("section")
    rank = lax.axis_index("rep")
    core = rank & 1
    steps = jnp.exp(-math.log(10000.0) * jnp.arange(EMB // 2, dtype=F32) / (EMB // 2))
    turn = times.reshape(micro * SEGS, 1).astype(F32) * steps
    embed = jnp.concatenate([jnp.cos(turn), jnp.sin(turn)], axis=1)
    mods = jnp.dot(
        embed, time_weight[0].astype(F32), precision=lax.Precision.HIGHEST
    ) + time_bias.astype(F32)
    fused = width // count % 16 == 0 and TILE % (hidden // count) == 0 and count >= 16
    common = Bag(
        args=(
            lengths[0],
            jnp.stack([section, core]),
            mods,
            jnp.asarray(angle_table(span)),
            norm_gain,
            expand_bias,
            reduce_bias,
        ),
        sizes=(span, width, hidden, count),
        tokens=local.shape[0],
        cores=2 if fused else 1,
    )
    weights = Bag(
        win=attend_in[0], wout=attend_out[0], wex=expand_weight[0], wre=reduce_weight[0]
    )
    rows = [(local, slot * span) for slot in range(micro)]
    same = lambda *names: {name: name for name in names}
    whole = same("left", "bg", "pa", "jg")
    run = partial(stage, common=common)
    both = (forward, output, mlp, copy_agrad, attend)
    over = lambda block, route: lax.ppermute(block, "section", route)
    swap = lambda block, bit: exchange(block, "rep", bit)
    a = run(
        "first_0",
        parts=(forward,),
        who=0,
        slot=0,
        loads=dict(xv=rows[0], **weights),
        stores=dict(result="leave"),
        kept=False,
    )
    came_0 = over(a.leave, [(0, 1)])
    after = (a.leave,)
    if fused:
        embeds = (embed.T, swap(embed.T, 0))
        after += (embeds[1],)
    b = run(
        "first_1",
        parts=(forward,),
        who=0,
        slot=1,
        loads=dict(xv=rows[1], **weights),
        stores=same("result", "left", "qkv", "probs", "middle", "slope", "branch"),
        after=after,
        heads_step=1,
    )
    came_1 = over(b.result, [(0, 1)])
    gates = mods[SEGS : 2 * SEGS, 2 * width :]
    gates = jnp.where(lengths[0, 1, 0] == span, gates[:1], gates)
    x = run(
        "second_0",
        parts=both,
        who=1,
        slot=0,
        loads=dict(xv=came_0, dyv=rows[0], **weights),
        stores=dict(whole, result=("ends", 0), leave="leave"),
        after=(b.result, gates),
    )
    back_0 = over(x.leave, [(1, 0)])
    y = run(
        "second_1",
        parts=both,
        who=1,
        slot=1,
        loads=dict(xv=came_1, dyv=rows[1], **weights),
        stores=dict(whole, result=("ends", span), leave="leave"),
        carried=dict(b, ends=x.ends),
        after=(x.leave,),
    )
    back_1 = over(y.leave, [(1, 0)])
    x = run(
        "back_0",
        parts=both,
        who=0,
        slot=0,
        loads=dict(xv=rows[0], dyv=back_0, **weights),
        stores=dict(whole, leave=("ends", 0)),
        carried=dict(x, ends=y.ends),
        after=(y.leave,),
    )
    if fused:
        y_left = swap(y.left_send, 0)
        back_1, x_send, x_bg = join(back_1, x.left_send, x.bg)
        lefts = [x.left, y.left, swap(x_send, 0), y_left]
        others = [swap(item, 0) for item in (x_bg, x.pa, x.jg)]
    cotan = back_1.astype(F32).reshape(SEGS, -1, width)
    made = (cotan * gates[:, None]).reshape(span, width).astype(BF16)
    bg_1 = jnp.where(section == 0, made, y.bg)
    after = ()
    if fused:
        bg_1_other = swap(bg_1, 0)
        after = (bg_1_other, others[0], lefts[2], lefts[3])
    part = run(
        "back_1_mlp",
        parts=(mlp,),
        who=0,
        slot=1,
        loads=dict(
            bg=bg_1,
            wre=weights.wre,
            slope=b.slope,
            wex=weights.wex,
            middle=b.middle,
            dyv=back_1,
            branch=b.branch,
        ),
        stores=same("pa", "middle_grad"),
        carried=y,
        after=after,
        pieces=dict(wre=(0, hidden // width), slope=(1, hidden // width), wex=(1, hidden // width)),
    )
    pa_1 = part.pa
    bits = bits_of(count)
    term = partial(term_call, sizes=common.sizes, core=core, rank=rank)
    lines = width // count
    deep = EMB // count
    sizes = (hidden // count, hidden // count + lines + 3 * deep + TAIL_ROWS, 3 * lines + GAIN_ROWS)
    bases = left_bases(width, hidden)

    def last_attend(after):
        return run(
            "back_1_attend",
            parts=(attend,),
            who=0,
            slot=1,
            loads=dict(
                agrad=(pa_1, None, (hidden, width)),
                wout=weights.wout,
                probs=b.probs,
                qkv=b.qkv,
                win=weights.win,
                xv=rows[1],
                middle_grad=part.middle_grad,
            ),
            stores=dict(jg="jg", leave=("ends", span)),
            carried=dict(y, ends=x.ends),
            after=after,
        )

    def pair_of(size, first):
        cut = size // 2 if fused else size // 32 * 16
        one = Chunk("rep", bits, cut, (1,) if fused else ())
        two = Chunk("rep", bits, size - cut, (2,) if fused else ())
        if fused:
            send_1, keep_1, send_2, keep_2 = first
            one.add(keep_1)
            two.add(keep_2)
            return one, two, send_1, send_2
        view = first.reshape((count // 2, 2) + first.shape[1:])
        cut = lambda at: lax.dynamic_index_in_dim(view, at, 1, keepdims=False)
        came = swap(cut(1 - core).astype(BF16), 0)
        for item in (cut(core), came):
            one.add(item)
            two.add(item, one.size)
        return one, two, one.split(1), two.split(2)

    if fused:
        pa_other = swap(pa_1, 0)
        sent = term(
            "term_reduce",
            term_reduce,
            lines=sizes[0],
            base=bases[0],
            rows=hidden // 2,
            lefts=lefts,
            rights=[x.bg, bg_1, others[0], bg_1_other],
            after=(pa_1,),
        )
        r1, r2, send_1, send_2 = pair_of(sizes[0], sent)
        came_r1, came_r2 = swap(send_1, 1), swap(send_2, 2)
        sent = term(
            "term_expand",
            term_expand,
            lines=sizes[1],
            base=bases[1],
            rows=width,
            lefts=lefts,
            rights=[x.pa, pa_1, others[1], pa_other],
            embeds=embeds,
            after=(send_1, send_2),
        )
        came_r1, came_r2, *sent = join(came_r1, came_r2, *sent)
        e1, e2, send_1, send_2 = pair_of(sizes[1], sent)
        came_e1, came_e2 = swap(send_1, 1), swap(send_2, 2)
        came_r1, came_r2, _, _ = join(came_r1, came_r2, send_1, send_2)
        r1.add(came_r1)
        r2.add(came_r2)
        send_1, send_2 = r1.split(3), r2.split(3)
        came_r1, came_r2 = swap(send_1, 3), swap(send_2, 3)
        last = last_attend((send_1, send_2))
        came_e1, came_e2, came_r1, came_r2, jg_1 = join(
            came_e1, came_e2, came_r1, came_r2, last.jg
        )
        jg_other = swap(jg_1, 0)
        e1.add(came_e1)
        e2.add(came_e2)
        send_1, send_2 = e1.split(2), e2.split(1)
        came_e1, came_e2 = swap(send_1, 2), swap(send_2, 1)
        came_r1, came_r2, _, _ = join(came_r1, came_r2, send_1, send_2)
        r1.add(came_r1)
        r2.add(came_r2)
        send_3, send_4 = r1.split(2), r2.split(1)
        came_r1, came_r2 = swap(send_3, 2), swap(send_4, 1)
        sent = term(
            "term_attend",
            term_attend,
            lines=sizes[2],
            base=bases[3],
            rows=width // 2,
            lefts=lefts,
            rights=[x.jg, jg_1, others[2], jg_other],
            after=(send_1, send_2, send_3, send_4),
        )
        came_e1, came_e2, came_r1, came_r2, *sent = join(
            came_e1, came_e2, came_r1, came_r2, *sent
        )
        a1, a2, send_1, send_2 = pair_of(sizes[2], sent)
    else:
        last = last_attend(())
        rights = [(x.bg, bg_1), (x.pa, pa_1), (x.jg, last.jg)]
        totals = plain_pieces((x.left, y.left), rights, embed.T, common.sizes)
        r1, r2, send_1, send_2 = pair_of(sizes[0], totals[0])
        r1.add(swap(send_1, 1))
        r2.add(swap(send_2, 2))
        r1.add(swap(r1.split(3), 3))
        r2.add(swap(r2.split(3), 3))
        came_r1, came_r2 = swap(r1.split(2), 2), swap(r2.split(1), 1)
        e1, e2, send_1, send_2 = pair_of(sizes[1], totals[1])
        e1.add(swap(send_1, 1))
        e2.add(swap(send_2, 2))
        came_e1, came_e2 = swap(e1.split(2), 2), swap(e2.split(1), 1)
        a1, a2, send_1, send_2 = pair_of(sizes[2], totals[2])
    ends = last.ends
    came_a1, came_a2 = swap(send_1, 1), swap(send_2, 2)
    e1.add(came_e1)
    e2.add(came_e2)
    block_e = jnp.concatenate([e1.split(3), e2.split(3)], axis=-2)
    came_e = swap(block_e, 3)
    came_r1, came_r2, _ = join(came_r1, came_r2, block_e)
    r1.add(came_r1)
    r2.add(came_r2)
    came_a1, came_a2, _ = join(came_a1, came_a2, block_e)
    a1.add(came_a1)
    a2.add(came_a2)
    send_1, send_2 = a1.split(2), a2.split(1)
    came_a1, came_a2 = swap(send_1, 2), swap(send_2, 1)
    a1.add(came_a1)
    a2.add(came_a2)
    block_a = jnp.concatenate([a1.split(3), a2.split(3)], axis=-2)
    came_a = swap(block_a, 3)
    came_e, _ = join(came_e, block_a)
    e1.add(came_e[..., : e1.size, :])
    e2.add(came_e[..., e1.size :, :])
    a1.add(came_a[..., : a1.size, :])
    a2.add(came_a[..., a1.size :, :])
    for bit in range(4, bits):
        for chunk in (r1, r2, e1, e2, a1, a2):
            chunk.add(swap(chunk.split(bit), bit))
    share_r, share_e, share_a = (
        jnp.concatenate([one.total(), two.total()]) for one, two in ((r1, r2), (e1, e2), (a1, a2))
    )
    tall = hidden // width
    side = lambda item, n, size: jnp.concatenate(
        [item[i * size : (i + 1) * size] for i in range(n)], axis=1
    )
    at_o = tall * lines
    at_t = at_o + lines
    small = share_e[at_t + 3 * deep :]
    flat = lambda item, first, n: lax.dynamic_slice_in_dim(
        item[first : first + n].reshape(-1), rank * (n * width // count), n * width // count
    )
    results = (
        flat(share_a, 3 * lines, 1),
        side(share_a, 3, lines),
        share_e[at_o:at_t],
        side(share_e[at_t:], 3, deep),
        flat(small, 1, 3),
        side(share_e, tall, lines),
        flat(small, 4, tall),
        share_r,
        flat(small, 0, 1),
    )
    return (ends[None],) + tuple(piece[None] for piece in results)


def solution(mesh):
    return jax.shard_map(
        per_device,
        mesh=mesh,
        in_specs=(
            P("section", "rep", None),
            P("rep", None, None),
            P("rep", None, None),
            P("section", None),
            P("section", None, None),
            P("section", None, None),
            P("section", None, None),
            P("section", None),
            P("section", None, None),
            P("section", None),
            P("section", None, None),
            P("section", None),
        ),
        out_specs=(
            P("section", "rep", None),
            P("section", "rep"),
            P("section", "rep", None),
            P("section", "rep", None),
            P("section", "rep", None),
            P("section", "rep"),
            P("section", "rep", None),
            P("section", "rep"),
            P("section", "rep", None),
            P("section", "rep"),
        ),
        check_vma=False,
    )
```

```python
from functools import partial
import inspect
import math

import jax
import jax.numpy as jnp
import numpy as np
from jax import lax
from jax.experimental import pallas as pl
from jax.experimental.pallas import tpu as pltpu
from jax.sharding import PartitionSpec as P

HEADS = 12
HEAD = 64
EMB = 128
SEGS = 4
ANY = pl.ANY
VMEM = pltpu.MemorySpace.VMEM
SMEM = pltpu.MemorySpace.SMEM
F32 = jnp.float32
BF16 = jnp.bfloat16
ROOT_HALF = 0.7071067811865476
ROOT_TAU = 0.3989422804014327
TILE = 384
TAIL_ROWS = 24
GAIN_ROWS = 16
EXTRA = 16


class Bag(dict):
    __getattr__ = dict.__getitem__


def dot(left, right, left_dim=1, right_dim=0):
    return lax.dot_general(
        left, right, (((left_dim,), (right_dim,)), ((), ())), preferred_element_type=F32
    )


def repeat(count, body):
    for i in range(count):
        body(i)


def steps_of(count, size, body):
    def several(i, _):
        for j in range(size):
            body(size * i + j)
        return _

    lax.fori_loop(0, count // size, several, 0)


def lanes(index, size, start=0):
    if isinstance(index, int):
        return slice(start + index * size, start + (index + 1) * size)
    return pl.ds(pl.multiple_of(start + index * size, size), size)


def swap_halves(values, low_half):
    forth = pltpu.roll(values, 128 - HEAD // 2, 1)
    back = pltpu.roll(values, HEAD // 2, 1)
    return jnp.where(low_half, forth, back)


def norm_parts(values):
    center = values - jnp.mean(values, axis=-1, keepdims=True)
    spread = jnp.mean(center * center, axis=-1, keepdims=True)
    factor = lax.rsqrt(spread + 1e-05)
    return center * factor, factor


def norm_back(grad, unit, factor):
    return factor * (
        grad
        - jnp.mean(grad, axis=-1, keepdims=True)
        - unit * jnp.mean(grad * unit, axis=-1, keepdims=True)
    )


class Held:
    def __init__(self, bufs, loads, stores, sems, pieces):
        self.bufs = bufs
        self.loads = loads
        self.stores = stores
        self.sems = sems
        self.pieces = pieces
        self.names = {id(buf): name for name, buf in bufs.items()}
        keys = [(name, j) for name in loads for j in range(self.parts_of(name))]
        self.spots = {key: n for n, key in enumerate(keys)}
        self.waiting = set(keys)
        self.pending = set(keys)
        self.leaving = {}

    def parts_of(self, name):
        return self.pieces[name][1] if name in self.pieces else 1

    def load(self, name, j):
        source, target = self.loads[name], self.bufs[name]
        if name in self.pieces:
            axis, count = self.pieces[name]
            size = target.shape[axis] // count
            at = (slice(None),) * axis + (pl.ds(j * size, size),)
            source, target = source.at[at], target.at[at]
        return pltpu.make_async_copy(source, target, self.sems.at[self.spots[(name, j)]])

    def store(self, name, n):
        at, target = self.stores[name][n]
        source = self.bufs[name] if at is None else self.bufs[name].at[at]
        return pltpu.make_async_copy(source, target, self.sems.at[self.leaving[(name, n)]])

    def keys(self, bufs, part):
        for buf in bufs:
            name = self.names[id(buf)]
            for j in range(self.parts_of(name)):
                if part in (None, j):
                    yield name, j

    def begin(self, *bufs, part=None):
        for key in self.keys(bufs, part):
            if key in self.waiting:
                self.waiting.remove(key)
                self.load(*key).start()

    def need(self, *bufs, part=None):
        self.begin(*bufs, part=part)
        for key in self.keys(bufs, part):
            if key in self.pending:
                self.pending.remove(key)
                self.load(*key).wait()

    def done(self, *bufs):
        for buf in bufs:
            name = self.names[id(buf)]
            for n in range(len(self.stores.get(name, ()))):
                self.leaving[(name, n)] = len(self.spots) + len(self.leaving)
                self.store(name, n).start()

    def finish(self):
        for name, n in self.leaving:
            self.store(name, n).wait()


class Layer:
    def __init__(self, sizes, slot, refs):
        self.span, self.width, self.hidden, self.count = sizes
        self.slot = slot
        lengths, place, self.mods, self.trig, self.gain, self.ebias, self.rbias = refs
        self.section = place[0]
        self.core = place[1]
        self.single = lengths[slot, 0] == self.span
        self.pairs = self.width // 128
        self.seg = self.span // SEGS
        self.step = self.width
        self.tiles = self.hidden // self.step
        place = lax.broadcasted_iota(jnp.int32, (self.span, 128), 1)
        self.low_half = place % HEAD < HEAD // 2
        self.low_head = place < HEAD
        row = lax.broadcasted_iota(jnp.int32, (1, 128), 1) // HEAD
        self.head_row = [(row == i).astype(F32).astype(BF16) for i in range(2)]
        self.blocks = [(b, slice(b * self.seg, (b + 1) * self.seg)) for b in range(SEGS)]

    def trig_pair(self):
        cos_all, sin_all = self.trig[0], self.trig[1]
        cos_cut = jnp.concatenate([cos_all[: self.seg]] * SEGS, axis=0)
        sin_cut = jnp.concatenate([sin_all[: self.seg]] * SEGS, axis=0)
        return jnp.where(self.single, cos_all, cos_cut), jnp.where(self.single, sin_all, sin_cut)

    def mod_row(self, block, part):
        row = self.slot * SEGS + jnp.where(self.single, 0, block)
        return self.mods[pl.ds(row, 1), part * self.width : (part + 1) * self.width]

    def add_segment(self, small, block, at, sums):
        row = 2 + jnp.where(self.single, 0, block)
        small[pl.ds(row, 1), at * self.width : (at + 1) * self.width] += sums

    def side(self, block):
        return self.core if block % 2 == 0 else 1 - self.core

    def put_left(self, left, base, values):
        turned = values.T
        if left.shape[0] == 1:
            left[0, 2 * base : 2 * base + self.width] = turned
            return
        lines = self.width // self.count
        for block in range(self.count):
            to = base + block // 2 * lines
            left[self.side(block), to : to + lines] = turned[block * lines : (block + 1) * lines]

    def put_active(self, left, j, values):
        turned = values.T
        if left.shape[0] == 1:
            left[0, lanes(j, self.step)] = turned
            return
        lines = self.hidden // self.count
        per = self.step // lines
        for n in range(per):
            to = lanes(j, lines * (per // 2), n // 2 * lines)
            to = slice(to.start, to.start + lines) if isinstance(j, int) else pl.ds(to.start, lines)
            left[self.side(n), to] = turned[n * lines : (n + 1) * lines]

    def thirds(self, index):
        return [lanes(index, 128, p * self.width) for p in range(3)]


def left_bases(width, hidden):
    return 0, hidden // 2, (hidden + width) // 2, (hidden + 2 * width) // 2


def forward(
    k, xv, win, wout, wex, wre, left, qkv, probs, middle, slope, branch, result, bias, normed,
    mixed, modded,
):
    span, width, held = k.span, k.width, k.held
    _, at_modded, at_mixed, at_normed = left_bases(width, k.hidden)
    held.begin(xv, win)
    held.need(xv)
    unit, _ = norm_parts(xv[...].astype(F32))
    normed[...] = (unit * k.gain[...].astype(F32)).astype(BF16)
    across = lax.broadcasted_iota(jnp.int32, (span, span), 0) // k.seg
    down = lax.broadcasted_iota(jnp.int32, (span, span), 1) // k.seg
    bias[...] = jnp.where((across == down) | k.single, 0.0, -1e30)
    held.need(win)
    held.begin(wout, wex, wre)
    cos_part, sin_part = k.trig_pair()
    for tile, factor in ((0, 0.125), (1, 1.0)):
        for i in range(width // 256):
            at = lanes(i, 256, tile * width)
            joint = dot(normed[...], win[:, at])
            outs = []
            for piece in (joint[:, :128], joint[:, 128:]):
                turned = piece * cos_part + swap_halves(piece, k.low_half) * sin_part
                outs.append((turned * factor).astype(BF16))
            qkv[:, at] = jnp.concatenate(outs, axis=1)
    qkv[:, 2 * width :] = dot(normed[...], win[:, 2 * width :]).astype(BF16)
    held.done(qkv)
    if k.kept:
        k.put_left(left, at_normed, normed[...])

    def heads(i):
        at = k.thirds(i)
        query, key, value = (qkv[:, a] for a in at)
        outs = []
        for h in range(2):
            scores = dot(key * k.head_row[h], query, 1, 1) + bias[...]
            top = jnp.max(scores, axis=0, keepdims=True)
            raised = jnp.exp(scores - top)
            total = jnp.sum(raised, axis=0, keepdims=True)
            prob = raised * (1.0 / total)
            if k.kept:
                probs[2 * i + h] = prob
            outs.append(dot(prob.astype(BF16), value, 0, 0))
        mixed[:, at[0]] = jnp.where(k.low_head, outs[0], outs[1]).astype(BF16)

    steps_of(k.pairs, k.heads_step, heads)
    held.done(probs)
    held.need(wout)
    middle[...] = xv[...].astype(F32) + dot(mixed[...], wout[...])
    held.done(middle)
    if k.kept:
        k.put_left(left, at_mixed, mixed[...])
    for b, rows in k.blocks:
        unit, _ = norm_parts(middle[rows])
        modded[rows] = (unit * (1.0 + k.mod_row(b, 0)) + k.mod_row(b, 1)).astype(BF16)
    if k.kept:
        k.put_left(left, at_modded, modded[...])
    held.need(wex, wre)
    branch[...] = jnp.broadcast_to(k.rbias[...].astype(F32), (span, width))

    def feed(j):
        at = lanes(j, k.step)
        pre = dot(modded[...], wex[:, at]) + k.ebias[:, at].astype(F32)
        area = 0.5 + 0.5 * lax.erf(pre * ROOT_HALF)
        out = (pre * area).astype(BF16)
        if k.kept:
            slope[:, at] = area + pre * (jnp.exp(pre * pre * -0.5) * ROOT_TAU)
            k.put_active(left, j, out)
        branch[...] += dot(out, wre[at, :])

    if k.heads_step == 1:
        steps_of(k.tiles, 1, feed)
    else:
        repeat(k.tiles, feed)
    held.done(slope, left, branch)
    for b, rows in k.blocks:
        result[rows] = (middle[rows] + k.mod_row(b, 2) * branch[rows]).astype(BF16)
    held.done(result)


def output(k, dyv, bg):
    k.held.need(dyv)
    for b, rows in k.blocks:
        bg[rows] = (dyv[rows].astype(F32) * k.mod_row(b, 2)).astype(BF16)
    k.held.done(bg)


def mlp(k, wre, wex, bg, slope, middle, branch, dyv, pa, middle_grad, small, acc):
    span, width, hidden, held = k.span, k.width, k.hidden, k.held
    small[...] = jnp.zeros(small.shape, F32)
    acc[...] = jnp.zeros(acc.shape, F32)
    held.begin(bg)
    for j in range(k.tiles):
        held.begin(wre, slope, wex, part=j)
    held.begin(middle, dyv, branch)
    held.need(bg)

    def feed(j):
        at = lanes(j, k.step)
        held.need(wre, slope, wex, part=j)
        grad = dot(bg[...], wre[at, :], 1, 1)
        pre_grad = (slope[:, at] * grad).astype(BF16)
        pa[:span, at] = pre_grad
        small[0:1, at] = jnp.sum(pre_grad.astype(F32), axis=0, keepdims=True)
        acc[...] += dot(pre_grad, wex[:, at], 1, 1)

    repeat(k.tiles, feed)
    held.need(middle, dyv, branch)
    total = jnp.zeros((1, width), F32)
    for b, rows in k.blocks:
        cotan = dyv[rows].astype(F32)
        total += jnp.sum(bg[rows].astype(F32), axis=0, keepdims=True)
        grad = acc[rows]
        unit, factor = norm_parts(middle[rows])
        k.add_segment(small, b, 0, jnp.sum(grad * unit, axis=0, keepdims=True))
        k.add_segment(small, b, 1, jnp.sum(grad, axis=0, keepdims=True))
        k.add_segment(small, b, 2, jnp.sum(cotan * branch[rows], axis=0, keepdims=True))
        back = norm_back(grad * (1.0 + k.mod_row(b, 0)), unit, factor)
        full = cotan + back
        middle_grad[rows] = full
        pa[rows, hidden:] = full.astype(BF16)
    small[1:2, :width] = total
    pa[span:, :] = small[...].astype(BF16)
    held.done(pa, middle_grad)


def attend(
    k, wout, win, agrad, probs, qkv, xv, middle_grad, jg, leave, mixed_grad, acc
):
    span, held = k.span, k.held
    held.need(agrad, wout)
    held.begin(probs, qkv)
    mixed_grad[...] = dot(agrad[...], wout[...], 1, 1).astype(BF16)
    held.need(probs, qkv)
    held.begin(win, xv, middle_grad)
    cos_part, sin_part = k.trig_pair()

    def heads(i):
        at = k.thirds(i)
        query, key, value = (qkv[:, a] for a in at)
        out_grad = mixed_grad[:, at[0]]
        parts = []
        for h in range(2):
            prob = probs[2 * i + h]
            pull = dot(value * k.head_row[h], out_grad, 1, 1)
            shared = jnp.sum(prob * pull, axis=0, keepdims=True)
            score_grad = (prob * (pull - shared)).astype(BF16)
            parts.append(
                (
                    dot(score_grad, key, 0, 0),
                    dot(score_grad, query),
                    dot(prob.astype(BF16), out_grad),
                )
            )
        for p in range(3):
            grad = jnp.where(k.low_head, parts[0][p], parts[1][p])
            if p < 2:
                grad = grad * cos_part - swap_halves(grad, k.low_half) * sin_part
                if p == 0:
                    grad = grad * 0.125
            jg[:span, at[p]] = grad.astype(BF16)

    steps_of(k.pairs, k.heads_step, heads)
    held.need(win, xv, middle_grad)
    acc[...] = dot(jg[:span, :], win[...], 1, 1)
    total = jnp.zeros((1, k.width), F32)
    for b, rows in k.blocks:
        grad = acc[rows]
        unit, factor = norm_parts(xv[rows].astype(F32))
        total += jnp.sum(grad * unit, axis=0, keepdims=True)
        back = norm_back(grad * k.gain[...].astype(F32), unit, factor)
        leave[rows] = (middle_grad[rows] + back).astype(BF16)
    below = jnp.concatenate([total, jnp.zeros((EXTRA - 1, k.width), F32)], axis=0)
    jg[span:, : k.width] = below.astype(BF16)
    jg[span:, k.width :] = jnp.zeros((EXTRA, 2 * k.width), BF16)
    held.done(jg, leave)


def copy_agrad(k, pa, agrad):
    agrad[...] = pa[: k.span, k.hidden :]


class Sums:
    def __init__(self, ranks, full, outs, sems):
        self.full = full
        self.own = [((ranks[0] >> bit) & 1) == 0 for bit in (1, 2)]
        self.bufs = outs[:4]
        self.targets = outs[4:]
        self.sems = sems
        self.half = full.shape[1] // 2
        self.copies = []

    def put(self, block, at, values):
        self.full[block, at] = values

    def settle(self, which, groups):
        send, keep = self.bufs[2 * which : 2 * which + 2]
        at = slice(which * self.half, (which + 1) * self.half)
        apart = 1 + which
        for group in groups:
            for n in range(2):
                first = 4 * group + (2 * n if which == 0 else n)
                even, odd = self.full[first, at], self.full[first + apart, at]
                send[2 * group + n] = jnp.where(self.own[which], odd, even).astype(BF16)
                keep[2 * group + n] = jnp.where(self.own[which], even, odd)
            spot = pl.ds(2 * group, 2)
            for n in range(2 * which, 2 * which + 2):
                copy = pltpu.make_async_copy(
                    self.bufs[n].at[spot], self.targets[n].at[spot], self.sems.at[len(self.copies)]
                )
                copy.start()
                self.copies.append(copy)

    def finish(self):
        for copy in self.copies:
            copy.wait()


def term_reduce(k, sums, left, right):
    lines = k.hidden // k.count
    per = TILE // lines
    for tile in range(k.hidden // 2 // TILE):
        k.arrive(tile)
        total = dot(left[tile * TILE : (tile + 1) * TILE], right[...])
        for n in range(per):
            sums.put(tile * per + n, slice(0, lines), total[n * lines : (n + 1) * lines])
        if (tile + 1) * per % 4 == 0:
            group = ((tile + 1) * per // 4 - 1,)
            sums.settle(0, group)
            sums.settle(1, group)


def square_terms(k, sums, left, right, cols, part):
    lines = k.width // k.count
    total = dot(left, right[: 4 * k.span, cols])
    for n in range(k.count // 2):
        sums.put(n, slice(part * lines, (part + 1) * lines), total[n * lines : (n + 1) * lines])


def term_expand(k, sums, left, right):
    width, hidden, span = k.width, k.hidden, k.span
    groups = range(k.count // 8)
    tall = hidden // width
    lines = width // k.count
    rows = width // 2
    half = sums.half
    settled = False
    for col in range(tall + 1):
        k.arrive(col)
        part = left[:rows] if col < tall else left[rows:]
        square_terms(k, sums, part, right, slice(col * width, (col + 1) * width), col)
        if (col + 1) * lines >= half and not settled:
            sums.settle(0, groups)
            settled = True
    smalls = [k.small[n].astype(F32) for n in range(4)]
    angles = jnp.concatenate([embed[...] for embed in k.embeds], axis=1)
    pieces = []
    for _ in range(3):
        pieces.append(angles.astype(BF16))
        angles = angles - pieces[-1].astype(F32)
    seqs = jnp.concatenate([small[2 : 2 + SEGS, : 3 * width] for small in smalls]).astype(BF16)
    times = sum(dot(piece, seqs) for piece in pieces)
    both = sum(smalls)
    seq_sum = jnp.sum(both[2 : 2 + SEGS, : 3 * width], axis=0, keepdims=True)
    lines_v = k.lines
    lines_v[...] = jnp.zeros(lines_v.shape, F32)
    lines_v[0:1] = both[1:2, :width]
    for n in range(3):
        lines_v[1 + n : 2 + n] = seq_sum[:, n * width : (n + 1) * width]
    for n in range(tall):
        lines_v[4 + n : 5 + n] = both[0:1, n * width : (n + 1) * width]
    deep = EMB // k.count
    first = (tall + 1) * lines
    low = k.core == 0
    for g in range(k.count // 2):
        for p in range(3):
            at = slice(p * width, (p + 1) * width)
            even = times[2 * g * deep : (2 * g + 1) * deep, at]
            odd = times[(2 * g + 1) * deep : (2 * g + 2) * deep, at]
            to = first + p * deep
            sums.put(g, slice(to, to + deep), jnp.where(low, even, odd))
        sums.put(g, slice(first + 3 * deep, 2 * half), lines_v[...])
    sums.settle(1, groups)


def term_attend(k, sums, left, right):
    width = k.width
    groups = range(k.count // 8)
    lines = width // k.count
    settled = False
    for col in range(3):
        k.arrive(col)
        square_terms(k, sums, left[...], right, slice(col * width, (col + 1) * width), col)
        if (col + 1) * lines >= sums.half and not settled:
            sums.settle(0, groups)
            settled = True
    gain = sum(k.small[n].astype(F32) for n in range(4))[:, :width]
    for g in range(k.count // 2):
        sums.put(g, slice(3 * lines, 3 * lines + GAIN_ROWS), gain)
    sums.settle(1, groups)


def load_terms(k, refs, bufs, base, sems):
    left_v, right_v, small_v = bufs
    rows, cols = left_v.shape[0], right_v.shape[1]
    tall = rows // TILE if small_v is None else 1
    wide = cols // k.width
    groups = []
    for i in range(tall):
        for j in range(wide):
            copies = []
            for n, (left, right) in enumerate(zip(refs[:4], refs[4:8])):
                tokens = pl.ds(n * k.span, k.span)
                part = pl.ds(i * (rows // tall), rows // tall)
                from_part = pl.ds(base + i * (rows // tall), rows // tall)
                at = pl.ds(j * k.width, k.width)
                if j == 0:
                    copies.append((left.at[from_part], left_v.at[part, tokens]))
                if i == 0:
                    copies.append((right.at[pl.ds(0, k.span), at], right_v.at[tokens, at]))
                if small_v is not None and j == wide - 1:
                    copies.append((right.at[pl.ds(k.span, EXTRA)], small_v.at[n]))
            groups.append(copies)
    made, count = [], 0
    for copies in groups:
        made.append([])
        for pair in copies:
            made[-1].append(pltpu.make_async_copy(*pair, sems.at[count]))
            made[-1][-1].start()
            count += 1
    return made


class Terms:
    def __init__(self, sizes, core):
        self.span, self.width, self.hidden, self.count = sizes
        self.core = core[0]

    def arrive(self, group):
        for copy in self.groups[group]:
            copy.wait()


def term_kernel(sizes, body, base, extra, *refs):
    refs = list(refs)
    core, rank = refs[:2]
    k = Terms(sizes, core)
    pos = 2
    if body is term_expand:
        k.embeds = refs[pos : pos + 2]
        pos += 2
    sources = refs[pos : pos + 8]
    pos += 8 + extra
    targets = refs[pos : pos + 4]
    pos += 4
    left_v, right_v, full, *outs = refs[pos : pos + 7]
    pos += 7
    k.small = None
    if body is not term_reduce:
        k.small, k.lines = refs[pos : pos + 2]
        pos += 2
    sems, out_sems = refs[pos:]
    k.groups = load_terms(k, sources, (left_v, right_v, k.small), base, sems)
    sums = Sums(rank, full, outs + targets, out_sems)
    body(k, sums, left_v, right_v)
    sums.finish()


def term_call(name, body, sizes, lines, base, rows, core, rank, lefts, rights, embeds=(), after=()):
    span, width, hidden, count = sizes
    blocks = count // 2
    cols = rights[0].shape[1]
    half = lines // 2
    outs = [((blocks // 2, half, width), kind) for kind in (BF16, F32)] * 2
    scratch = [
        ((rows, 4 * span), BF16),
        ((4 * span, cols), BF16),
        ((blocks, lines, width), F32),
        *outs,
    ]
    if body is not term_reduce:
        scratch += [((4, EXTRA, cols), BF16), ((TAIL_ROWS, width), F32)]
    args = [core.reshape(1), rank.reshape(1), *embeds, *lefts, *rights, *after]
    in_specs = [pl.BlockSpec(memory_space=SMEM)] * 2
    in_specs += [pl.BlockSpec(memory_space=VMEM)] * len(embeds)
    in_specs += [pl.BlockSpec(memory_space=ANY)] * (8 + len(after))
    return pl.pallas_call(
        partial(term_kernel, sizes, body, base, len(after)),
        out_shape=[jax.ShapeDtypeStruct(*item) for item in outs],
        in_specs=in_specs,
        out_specs=[pl.BlockSpec(memory_space=ANY)] * 4,
        scratch_shapes=[pltpu.VMEM(*item) for item in scratch]
        + [pltpu.SemaphoreType.DMA((32,)), pltpu.SemaphoreType.DMA((8,))],
        compiler_params=pltpu.CompilerParams(vmem_limit_bytes=62 * 1024 * 1024),
        name=name,
    )(*args)


def plain_pieces(lefts, rights, embed, sizes):
    span, width, hidden, count = sizes
    bg, pa, jg = rights
    bases = [2 * base for base in left_bases(width, hidden)]

    def blocks(base, rows, right):
        total = sum(dot(a[base : base + rows], b) for a, b in zip(lefts, right))
        parts = [total[:, i : i + width] for i in range(0, total.shape[1], width)]
        return [part.reshape(count, -1, width) for part in parts]

    take = lambda items, cols: [item[:span, cols] for item in items]
    reduce = blocks(bases[0], hidden, bg)
    expand = blocks(bases[1], width, take(pa, slice(0, hidden)))
    expand += blocks(bases[2], width, take(pa, slice(hidden, hidden + width)))
    last = blocks(bases[3], width, take(jg, slice(None)))
    small = [item[span:].astype(F32) for item in pa]
    seqs = jnp.concatenate([item[2 : 2 + SEGS, : 3 * width] for item in small])
    times = jnp.dot(embed, seqs, precision=lax.Precision.HIGHEST)
    expand += [times[:, i * width : (i + 1) * width].reshape(count, -1, width) for i in range(3)]
    lines = jnp.concatenate(
        [
            sum(item[1:2, :width] for item in small),
            jnp.sum(seqs, axis=0).reshape(-1, width),
            sum(item[0, :hidden] for item in small).reshape(-1, width),
        ]
    )
    lines = jnp.pad(lines, ((0, TAIL_ROWS - lines.shape[0]), (0, 0)))
    gain = sum(item[span:, :width].astype(F32) for item in jg)
    expand.append(jnp.broadcast_to(lines, (count,) + lines.shape))
    last.append(jnp.broadcast_to(gain, (count,) + gain.shape))
    return [jnp.concatenate(item, axis=1) for item in (reduce, expand, last)]


def shapes_of(span, width, hidden, cores):
    tok = lambda cols, kind=BF16: ((span, cols), kind)
    below = lambda cols: ((span + EXTRA, cols), BF16)
    return dict(
        xv=tok(width),
        dyv=tok(width),
        win=((width, 3 * width), BF16),
        wout=((width, width), BF16),
        wex=((width, hidden), BF16),
        wre=((hidden, width), BF16),
        left=((cores, (hidden + 3 * width) // cores, span), BF16),
        normed=tok(width),
        qkv=tok(3 * width),
        probs=((HEADS, span, span), F32),
        mixed=tok(width),
        middle=tok(width, F32),
        modded=tok(width),
        slope=tok(hidden, F32),
        branch=tok(width, F32),
        result=tok(width),
        bg=tok(width),
        pa=below(hidden + width),
        jg=below(3 * width),
        agrad=tok(width),
        mixed_grad=tok(width),
        middle_grad=tok(width, F32),
        leave=tok(width),
        acc=tok(width, F32),
        bias=tok(span, F32),
        small=((EXTRA, hidden + width), F32),
    )


def uses(part):
    return list(inspect.signature(part).parameters)[1:]


def stage_kernel(sizes, parts, who, slot, plan, *refs):
    refs = list(refs)
    layer = Layer(sizes, slot, refs[:7])
    span = layer.span
    pos = 7
    loads = {}
    for name, row, cols in plan.sources:
        ref = refs[pos]
        if cols is not None:
            ref = ref.at[pl.ds(0, span), pl.ds(*cols)]
        elif row is not None:
            ref = ref.at[pl.ds(row, span)]
        loads[name] = ref
        pos += 1
    pos += plan.extra
    stores = {}
    for name, row, at in plan.targets:
        target = refs[pos] if row is None else refs[pos].at[pl.ds(row, span)]
        stores.setdefault(name, []).append((at, target))
        pos += 1
    bufs = {}
    for name in plan.bufs:
        bufs[name] = refs[pos]
        pos += 1
    layer.held = Held(bufs, loads, stores, refs[pos], plan.pieces)
    layer.kept = plan.kept
    layer.heads_step = plan.heads_step

    @pl.when(layer.section == who)
    def _():
        for part in parts:
            part(layer, *[bufs[name] for name in uses(part)])
        layer.held.finish()


def stage(
    name, common, parts, who, slot, loads, stores, carried=None, after=(), kept=True, heads_step=3,
    pieces=None,
):
    carried = carried or {}
    span, width, hidden, count = common.sizes
    shapes = shapes_of(span, width, hidden, common.cores)
    bufs = []
    for part in parts:
        bufs += [item for item in uses(part) if item not in bufs]
    pair = lambda item: item if isinstance(item, tuple) else (item, None)
    args = list(common.args)
    in_specs = [pl.BlockSpec(memory_space=SMEM)] * 2 + [pl.BlockSpec(memory_space=VMEM)] * 5
    plan = Bag(sources=[], targets=[], bufs=bufs, kept=kept, heads_step=heads_step)
    plan["pieces"] = pieces or {}
    for item in loads:
        if item in bufs:
            array, row, *cols = pair(loads[item])
            args.append(array)
            plan.sources.append((item, row, cols[0] if cols else None))
    outs, aliases, extra = [], {}, []
    targets = []
    for item, key in stores.items():
        if item == "left":
            targets += [(item, key + "_send" * n, None, n) for n in range(common.cores)]
        else:
            targets.append((item, *pair(key), None))
    for i, (item, key, row, at) in enumerate(targets):
        shape, kind = shapes[item]
        if row is not None:
            shape = (common.tokens,) + shape[1:]
        if at is not None:
            shape = shape[1:]
        outs.append(jax.ShapeDtypeStruct(shape, kind))
        plan.targets.append((item, row, at))
        if key in carried:
            aliases[len(args) + len(extra)] = i
            extra.append(carried[key])
    extra += list(after)
    args += extra
    plan["extra"] = len(extra)
    in_specs += [pl.BlockSpec(memory_space=ANY)] * (len(args) - len(in_specs))
    results = pl.pallas_call(
        partial(stage_kernel, common.sizes, parts, who, slot, plan),
        out_shape=outs,
        in_specs=in_specs,
        out_specs=[pl.BlockSpec(memory_space=ANY)] * len(outs),
        input_output_aliases=aliases,
        scratch_shapes=[pltpu.VMEM(*shapes[item]) for item in bufs]
        + [pltpu.SemaphoreType.DMA((32,))],
        compiler_params=pltpu.CompilerParams(vmem_limit_bytes=62 * 1024 * 1024),
        name=name,
    )(*args)
    return Bag({key: value for (_, key, _, _), value in zip(targets, results)})


def bits_of(count):
    bits = count.bit_length() - 1
    assert 1 << bits == count
    return bits


class Chunk:
    def __init__(self, axis, bits, size, settled=()):
        self.axis = axis
        self.bits = list(range(bits - 1, 0, -1))
        self.size = size
        self.settled = list(settled)
        self.terms = []

    def add(self, term, start=0):
        left = [bit for bit in self.bits if bit not in self.settled]
        self.terms.append((term.reshape((2,) * len(left) + term.shape[-2:]), left, start))

    def take(self, term, start, left, flip):
        me = lax.axis_index(self.axis)
        side = lambda bit: 1 - ((me >> bit) & 1) if bit == flip else (me >> bit) & 1
        starts = [side(bit) if bit in self.settled else 0 for bit in left]
        sizes = [1 if bit in self.settled else 2 for bit in left]
        cols = term.shape[-1]
        piece = lax.dynamic_slice(term, starts + [start, 0], sizes + [self.size, cols])
        open_bits = [2] * (len(self.bits) - len(self.settled))
        return piece.reshape(open_bits + [self.size, cols]).astype(F32)

    def split(self, bit):
        self.settled.append(bit)
        return sum(self.take(term, start, left, bit) for term, left, start in self.terms).astype(
            BF16
        )

    def total(self):
        return sum(self.take(term, start, left, None) for term, left, start in self.terms)


def exchange(block, axis, bit):
    count = lax.axis_size(axis)
    return lax.ppermute(block, axis, [(i, i ^ (1 << bit)) for i in range(count)])


def join(*items):
    return lax.optimization_barrier(items)


def angle_table(span):
    half = HEAD // 2
    freqs = np.exp(-math.log(10000.0) * np.arange(half, dtype=np.float32) / half)
    phase = np.arange(span, dtype=np.float32)[:, None] * freqs.astype(np.float32)[None, :]
    cos_part, sin_part = np.cos(phase), np.sin(phase)
    return np.stack(
        [
            np.concatenate([cos_part] * 4, axis=1),
            np.concatenate([-sin_part, sin_part] * 2, axis=1),
        ]
    ).astype(np.float32)


def per_device(
    ends_in,
    lengths,
    times,
    norm_gain,
    attend_in,
    attend_out,
    time_weight,
    time_bias,
    expand_weight,
    expand_bias,
    reduce_weight,
    reduce_bias,
):
    local = ends_in[0]
    micro = lengths.shape[1]
    assert micro == 2
    width = local.shape[1]
    span = local.shape[0] // micro
    hidden = expand_weight.shape[2]
    count = lax.axis_size("rep")
    section = lax.axis_index("section")
    rank = lax.axis_index("rep")
    core = rank & 1
    steps = jnp.exp(-math.log(10000.0) * jnp.arange(EMB // 2, dtype=F32) / (EMB // 2))
    turn = times.reshape(micro * SEGS, 1).astype(F32) * steps
    embed = jnp.concatenate([jnp.cos(turn), jnp.sin(turn)], axis=1)
    mods = jnp.dot(
        embed, time_weight[0].astype(F32), precision=lax.Precision.HIGHEST
    ) + time_bias.astype(F32)
    fused = width // count % 16 == 0 and TILE % (hidden // count) == 0 and count >= 16
    common = Bag(
        args=(
            lengths[0],
            jnp.stack([section, core]),
            mods,
            jnp.asarray(angle_table(span)),
            norm_gain,
            expand_bias,
            reduce_bias,
        ),
        sizes=(span, width, hidden, count),
        tokens=local.shape[0],
        cores=2 if fused else 1,
    )
    weights = Bag(
        win=attend_in[0], wout=attend_out[0], wex=expand_weight[0], wre=reduce_weight[0]
    )
    rows = [(local, slot * span) for slot in range(micro)]
    same = lambda *names: {name: name for name in names}
    whole = same("left", "bg", "pa", "jg")
    run = partial(stage, common=common)
    both = (forward, output, mlp, copy_agrad, attend)
    over = lambda block, route: lax.ppermute(block, "section", route)
    swap = lambda block, bit: exchange(block, "rep", bit)
    a = run(
        "first_0",
        parts=(forward,),
        who=0,
        slot=0,
        loads=dict(xv=rows[0], **weights),
        stores=dict(result="leave"),
        kept=False,
    )
    came_0 = over(a.leave, [(0, 1)])
    after = (a.leave,)
    if fused:
        embeds = (embed.T, swap(embed.T, 0))
        after += (embeds[1],)
    b = run(
        "first_1",
        parts=(forward,),
        who=0,
        slot=1,
        loads=dict(xv=rows[1], **weights),
        stores=same("result", "left", "qkv", "probs", "middle", "slope", "branch"),
        after=after,
        heads_step=1,
    )
    came_1 = over(b.result, [(0, 1)])
    gates = mods[SEGS : 2 * SEGS, 2 * width :]
    gates = jnp.where(lengths[0, 1, 0] == span, gates[:1], gates)
    x = run(
        "second_0",
        parts=both,
        who=1,
        slot=0,
        loads=dict(xv=came_0, dyv=rows[0], **weights),
        stores=dict(whole, result=("ends", 0), leave="leave"),
        after=(b.result, gates),
    )
    back_0 = over(x.leave, [(1, 0)])
    y = run(
        "second_1",
        parts=both,
        who=1,
        slot=1,
        loads=dict(xv=came_1, dyv=rows[1], **weights),
        stores=dict(whole, result=("ends", span), leave="leave"),
        carried=dict(b, ends=x.ends),
        after=(x.leave,),
    )
    back_1 = over(y.leave, [(1, 0)])
    x = run(
        "back_0",
        parts=both,
        who=0,
        slot=0,
        loads=dict(xv=rows[0], dyv=back_0, **weights),
        stores=dict(whole, leave=("ends", 0)),
        carried=dict(x, ends=y.ends),
        after=(y.leave,),
    )
    if fused:
        y_left = swap(y.left_send, 0)
        back_1, x_send, x_bg = join(back_1, x.left_send, x.bg)
        lefts = [x.left, y.left, swap(x_send, 0), y_left]
        others = [swap(item, 0) for item in (x_bg, x.pa, x.jg)]
    cotan = back_1.astype(F32).reshape(SEGS, -1, width)
    made = (cotan * gates[:, None]).reshape(span, width).astype(BF16)
    bg_1 = jnp.where(section == 0, made, y.bg)
    after = ()
    if fused:
        bg_1_other = swap(bg_1, 0)
        after = (bg_1_other, others[0], lefts[2], lefts[3])
    part = run(
        "back_1_mlp",
        parts=(mlp,),
        who=0,
        slot=1,
        loads=dict(
            bg=bg_1,
            wre=weights.wre,
            slope=b.slope,
            wex=weights.wex,
            middle=b.middle,
            dyv=back_1,
            branch=b.branch,
        ),
        stores=same("pa", "middle_grad"),
        carried=y,
        after=after,
        pieces=dict(wre=(0, hidden // width), slope=(1, hidden // width), wex=(1, hidden // width)),
    )
    pa_1 = part.pa
    bits = bits_of(count)
    term = partial(term_call, sizes=common.sizes, core=core, rank=rank)
    lines = width // count
    deep = EMB // count
    sizes = (hidden // count, hidden // count + lines + 3 * deep + TAIL_ROWS, 3 * lines + GAIN_ROWS)
    bases = left_bases(width, hidden)

    def last_attend(after):
        return run(
            "back_1_attend",
            parts=(attend,),
            who=0,
            slot=1,
            loads=dict(
                agrad=(pa_1, None, (hidden, width)),
                wout=weights.wout,
                probs=b.probs,
                qkv=b.qkv,
                win=weights.win,
                xv=rows[1],
                middle_grad=part.middle_grad,
            ),
            stores=dict(jg="jg", leave=("ends", span)),
            carried=dict(y, ends=x.ends),
            after=after,
        )

    def pair_of(size, first):
        cut = size // 2 if fused else size // 32 * 16
        one = Chunk("rep", bits, cut, (1,) if fused else ())
        two = Chunk("rep", bits, size - cut, (2,) if fused else ())
        if fused:
            send_1, keep_1, send_2, keep_2 = first
            one.add(keep_1)
            two.add(keep_2)
            return one, two, send_1, send_2
        view = first.reshape((count // 2, 2) + first.shape[1:])
        cut = lambda at: lax.dynamic_index_in_dim(view, at, 1, keepdims=False)
        came = swap(cut(1 - core).astype(BF16), 0)
        for item in (cut(core), came):
            one.add(item)
            two.add(item, one.size)
        return one, two, one.split(1), two.split(2)

    if fused:
        pa_other = swap(pa_1, 0)
        sent = term(
            "term_reduce",
            term_reduce,
            lines=sizes[0],
            base=bases[0],
            rows=hidden // 2,
            lefts=lefts,
            rights=[x.bg, bg_1, others[0], bg_1_other],
            after=(pa_1,),
        )
        r1, r2, send_1, send_2 = pair_of(sizes[0], sent)
        came_r1, came_r2 = swap(send_1, 1), swap(send_2, 2)
        sent = term(
            "term_expand",
            term_expand,
            lines=sizes[1],
            base=bases[1],
            rows=width,
            lefts=lefts,
            rights=[x.pa, pa_1, others[1], pa_other],
            embeds=embeds,
            after=(send_1, send_2),
        )
        came_r1, came_r2, *sent = join(came_r1, came_r2, *sent)
        e1, e2, send_1, send_2 = pair_of(sizes[1], sent)
        came_e1, came_e2 = swap(send_1, 1), swap(send_2, 2)
        last = last_attend((send_1, send_2))
        jg_1 = last.jg
        jg_other = swap(jg_1, 0)
        came_r1, came_r2, _ = join(came_r1, came_r2, jg_1)
        r1.add(came_r1)
        r2.add(came_r2)
        send_3, send_4 = r1.split(2), r2.split(1)
        came_r1, came_r2 = swap(send_3, 2), swap(send_4, 1)
        came_e1, came_e2, _, _ = join(came_e1, came_e2, send_3, send_4)
        e1.add(came_e1)
        e2.add(came_e2)
        send_1, send_2 = e1.split(2), e2.split(1)
        came_e1, came_e2 = swap(send_1, 2), swap(send_2, 1)
        sent = term(
            "term_attend",
            term_attend,
            lines=sizes[2],
            base=bases[3],
            rows=width // 2,
            lefts=lefts,
            rights=[x.jg, jg_1, others[2], jg_other],
            after=(send_1, send_2, send_3, send_4),
        )
        came_r1, came_r2, *sent = join(came_r1, came_r2, *sent)
        a1, a2, send_1, send_2 = pair_of(sizes[2], sent)
    else:
        last = last_attend(())
        rights = [(x.bg, bg_1), (x.pa, pa_1), (x.jg, last.jg)]
        totals = plain_pieces((x.left, y.left), rights, embed.T, common.sizes)
        r1, r2, send_1, send_2 = pair_of(sizes[0], totals[0])
        r1.add(swap(send_1, 1))
        r2.add(swap(send_2, 2))
        came_r1, came_r2 = swap(r1.split(2), 2), swap(r2.split(1), 1)
        e1, e2, send_1, send_2 = pair_of(sizes[1], totals[1])
        e1.add(swap(send_1, 1))
        e2.add(swap(send_2, 2))
        came_e1, came_e2 = swap(e1.split(2), 2), swap(e2.split(1), 1)
        a1, a2, send_1, send_2 = pair_of(sizes[2], totals[2])
    ends = last.ends
    came_a1, came_a2 = swap(send_1, 1), swap(send_2, 2)
    r1.add(came_r1)
    r2.add(came_r2)
    block_r = jnp.concatenate([r1.split(3), r2.split(3)], axis=-2)
    came_r = swap(block_r, 3)
    came_e1, came_e2, _ = join(came_e1, came_e2, block_r)
    e1.add(came_e1)
    e2.add(came_e2)
    block_e = jnp.concatenate([e1.split(3), e2.split(3)], axis=-2)
    came_e = swap(block_e, 3)
    came_a1, came_a2, _ = join(came_a1, came_a2, block_e)
    a1.add(came_a1)
    a2.add(came_a2)
    send_1, send_2 = a1.split(2), a2.split(1)
    came_a1, came_a2 = swap(send_1, 2), swap(send_2, 1)
    a1.add(came_a1)
    a2.add(came_a2)
    block_a = jnp.concatenate([a1.split(3), a2.split(3)], axis=-2)
    came_a = swap(block_a, 3)
    came_r, _ = join(came_r, send_1)
    r1.add(came_r[..., : r1.size, :])
    r2.add(came_r[..., r1.size :, :])
    came_e, _ = join(came_e, block_a)
    e1.add(came_e[..., : e1.size, :])
    e2.add(came_e[..., e1.size :, :])
    a1.add(came_a[..., : a1.size, :])
    a2.add(came_a[..., a1.size :, :])
    for bit in range(4, bits):
        for chunk in (r1, r2, e1, e2, a1, a2):
            chunk.add(swap(chunk.split(bit), bit))
    share_r, share_e, share_a = (
        jnp.concatenate([one.total(), two.total()]) for one, two in ((r1, r2), (e1, e2), (a1, a2))
    )
    tall = hidden // width
    side = lambda item, n, size: jnp.concatenate(
        [item[i * size : (i + 1) * size] for i in range(n)], axis=1
    )
    at_o = tall * lines
    at_t = at_o + lines
    small = share_e[at_t + 3 * deep :]
    flat = lambda item, first, n: lax.dynamic_slice_in_dim(
        item[first : first + n].reshape(-1), rank * (n * width // count), n * width // count
    )
    results = (
        flat(share_a, 3 * lines, 1),
        side(share_a, 3, lines),
        share_e[at_o:at_t],
        side(share_e[at_t:], 3, deep),
        flat(small, 1, 3),
        side(share_e, tall, lines),
        flat(small, 4, tall),
        share_r,
        flat(small, 0, 1),
    )
    return (ends[None],) + tuple(piece[None] for piece in results)


def solution(mesh):
    return jax.shard_map(
        per_device,
        mesh=mesh,
        in_specs=(
            P("section", "rep", None),
            P("rep", None, None),
            P("rep", None, None),
            P("section", None),
            P("section", None, None),
            P("section", None, None),
            P("section", None, None),
            P("section", None),
            P("section", None, None),
            P("section", None),
            P("section", None, None),
            P("section", None),
        ),
        out_specs=(
            P("section", "rep", None),
            P("section", "rep"),
            P("section", "rep", None),
            P("section", "rep", None),
            P("section", "rep", None),
            P("section", "rep"),
            P("section", "rep", None),
            P("section", "rep"),
            P("section", "rep", None),
            P("section", "rep"),
        ),
        check_vma=False,
    )
```

```python
from functools import partial
import inspect
import math

import jax
import jax.numpy as jnp
import numpy as np
from jax import lax
from jax.experimental import pallas as pl
from jax.experimental.pallas import tpu as pltpu
from jax.sharding import PartitionSpec as P

HEADS = 12
HEAD = 64
EMB = 128
SEGS = 4
ANY = pl.ANY
VMEM = pltpu.MemorySpace.VMEM
SMEM = pltpu.MemorySpace.SMEM
F32 = jnp.float32
BF16 = jnp.bfloat16
ROOT_HALF = 0.7071067811865476
ROOT_TAU = 0.3989422804014327
TILE = 384
TAIL_ROWS = 24
GAIN_ROWS = 16
EXTRA = 16


class Bag(dict):
    __getattr__ = dict.__getitem__


def dot(left, right, left_dim=1, right_dim=0):
    return lax.dot_general(
        left, right, (((left_dim,), (right_dim,)), ((), ())), preferred_element_type=F32
    )


def repeat(count, body):
    for i in range(count):
        body(i)


def steps_of(count, size, body):
    def several(i, _):
        for j in range(size):
            body(size * i + j)
        return _

    lax.fori_loop(0, count // size, several, 0)


def lanes(index, size, start=0):
    if isinstance(index, int):
        return slice(start + index * size, start + (index + 1) * size)
    return pl.ds(pl.multiple_of(start + index * size, size), size)


def swap_halves(values, low_half):
    forth = pltpu.roll(values, 128 - HEAD // 2, 1)
    back = pltpu.roll(values, HEAD // 2, 1)
    return jnp.where(low_half, forth, back)


def norm_parts(values):
    center = values - jnp.mean(values, axis=-1, keepdims=True)
    spread = jnp.mean(center * center, axis=-1, keepdims=True)
    factor = lax.rsqrt(spread + 1e-05)
    return center * factor, factor


def norm_back(grad, unit, factor):
    return factor * (
        grad
        - jnp.mean(grad, axis=-1, keepdims=True)
        - unit * jnp.mean(grad * unit, axis=-1, keepdims=True)
    )


class Held:
    def __init__(self, bufs, loads, stores, sems, pieces):
        self.bufs = bufs
        self.loads = loads
        self.stores = stores
        self.sems = sems
        self.pieces = pieces
        self.names = {id(buf): name for name, buf in bufs.items()}
        keys = [(name, j) for name in loads for j in range(self.parts_of(name))]
        self.spots = {key: n for n, key in enumerate(keys)}
        self.waiting = set(keys)
        self.pending = set(keys)
        self.leaving = {}

    def parts_of(self, name):
        return self.pieces[name][1] if name in self.pieces else 1

    def load(self, name, j):
        source, target = self.loads[name], self.bufs[name]
        if name in self.pieces:
            axis, count = self.pieces[name]
            size = target.shape[axis] // count
            at = (slice(None),) * axis + (pl.ds(j * size, size),)
            source, target = source.at[at], target.at[at]
        return pltpu.make_async_copy(source, target, self.sems.at[self.spots[(name, j)]])

    def store(self, name, n):
        at, target = self.stores[name][n]
        source = self.bufs[name] if at is None else self.bufs[name].at[at]
        return pltpu.make_async_copy(source, target, self.sems.at[self.leaving[(name, n)]])

    def keys(self, bufs, part):
        for buf in bufs:
            name = self.names[id(buf)]
            for j in range(self.parts_of(name)):
                if part in (None, j):
                    yield name, j

    def begin(self, *bufs, part=None):
        for key in self.keys(bufs, part):
            if key in self.waiting:
                self.waiting.remove(key)
                self.load(*key).start()

    def need(self, *bufs, part=None):
        self.begin(*bufs, part=part)
        for key in self.keys(bufs, part):
            if key in self.pending:
                self.pending.remove(key)
                self.load(*key).wait()

    def done(self, *bufs):
        for buf in bufs:
            name = self.names[id(buf)]
            for n in range(len(self.stores.get(name, ()))):
                self.leaving[(name, n)] = len(self.spots) + len(self.leaving)
                self.store(name, n).start()

    def finish(self):
        for name, n in self.leaving:
            self.store(name, n).wait()


class Layer:
    def __init__(self, sizes, slot, refs):
        self.span, self.width, self.hidden, self.count = sizes
        self.slot = slot
        lengths, place, self.mods, self.trig, self.gain, self.ebias, self.rbias = refs
        self.section = place[0]
        self.core = place[1]
        self.single = lengths[slot, 0] == self.span
        self.pairs = self.width // 128
        self.seg = self.span // SEGS
        self.step = self.width
        self.tiles = self.hidden // self.step
        place = lax.broadcasted_iota(jnp.int32, (self.span, 128), 1)
        self.low_half = place % HEAD < HEAD // 2
        self.low_head = place < HEAD
        row = lax.broadcasted_iota(jnp.int32, (1, 128), 1) // HEAD
        self.head_row = [(row == i).astype(F32).astype(BF16) for i in range(2)]
        self.blocks = [(b, slice(b * self.seg, (b + 1) * self.seg)) for b in range(SEGS)]

    def trig_pair(self):
        cos_all, sin_all = self.trig[0], self.trig[1]
        cos_cut = jnp.concatenate([cos_all[: self.seg]] * SEGS, axis=0)
        sin_cut = jnp.concatenate([sin_all[: self.seg]] * SEGS, axis=0)
        return jnp.where(self.single, cos_all, cos_cut), jnp.where(self.single, sin_all, sin_cut)

    def mod_row(self, block, part):
        row = self.slot * SEGS + jnp.where(self.single, 0, block)
        return self.mods[pl.ds(row, 1), part * self.width : (part + 1) * self.width]

    def add_segment(self, small, block, at, sums):
        row = 2 + jnp.where(self.single, 0, block)
        small[pl.ds(row, 1), at * self.width : (at + 1) * self.width] += sums

    def side(self, block):
        return self.core if block % 2 == 0 else 1 - self.core

    def put_left(self, left, base, values):
        turned = values.T
        if left.shape[0] == 1:
            left[0, 2 * base : 2 * base + self.width] = turned
            return
        lines = self.width // self.count
        for block in range(self.count):
            to = base + block // 2 * lines
            left[self.side(block), to : to + lines] = turned[block * lines : (block + 1) * lines]

    def put_active(self, left, j, values):
        turned = values.T
        if left.shape[0] == 1:
            left[0, lanes(j, self.step)] = turned
            return
        lines = self.hidden // self.count
        per = self.step // lines
        for n in range(per):
            to = lanes(j, lines * (per // 2), n // 2 * lines)
            to = slice(to.start, to.start + lines) if isinstance(j, int) else pl.ds(to.start, lines)
            left[self.side(n), to] = turned[n * lines : (n + 1) * lines]

    def thirds(self, index):
        return [lanes(index, 128, p * self.width) for p in range(3)]


def left_bases(width, hidden):
    return 0, hidden // 2, (hidden + width) // 2, (hidden + 2 * width) // 2


def forward(
    k, xv, win, wout, wex, wre, left, qkv, probs, middle, slope, branch, result, bias, normed,
    mixed, modded,
):
    span, width, held = k.span, k.width, k.held
    _, at_modded, at_mixed, at_normed = left_bases(width, k.hidden)
    held.begin(xv, win)
    held.need(xv)
    unit, _ = norm_parts(xv[...].astype(F32))
    normed[...] = (unit * k.gain[...].astype(F32)).astype(BF16)
    across = lax.broadcasted_iota(jnp.int32, (span, span), 0) // k.seg
    down = lax.broadcasted_iota(jnp.int32, (span, span), 1) // k.seg
    bias[...] = jnp.where((across == down) | k.single, 0.0, -1e30)
    held.need(win)
    held.begin(wout, wex, wre)
    cos_part, sin_part = k.trig_pair()
    for tile, factor in ((0, 0.125), (1, 1.0)):
        for i in range(width // 256):
            at = lanes(i, 256, tile * width)
            joint = dot(normed[...], win[:, at])
            outs = []
            for piece in (joint[:, :128], joint[:, 128:]):
                turned = piece * cos_part + swap_halves(piece, k.low_half) * sin_part
                outs.append((turned * factor).astype(BF16))
            qkv[:, at] = jnp.concatenate(outs, axis=1)
    qkv[:, 2 * width :] = dot(normed[...], win[:, 2 * width :]).astype(BF16)
    held.done(qkv)
    if k.kept:
        k.put_left(left, at_normed, normed[...])

    def heads(i):
        at = k.thirds(i)
        query, key, value = (qkv[:, a] for a in at)
        outs = []
        for h in range(2):
            scores = dot(key * k.head_row[h], query, 1, 1) + bias[...]
            top = jnp.max(scores, axis=0, keepdims=True)
            raised = jnp.exp(scores - top)
            total = jnp.sum(raised, axis=0, keepdims=True)
            prob = raised * (1.0 / total)
            if k.kept:
                probs[2 * i + h] = prob
            outs.append(dot(prob.astype(BF16), value, 0, 0))
        mixed[:, at[0]] = jnp.where(k.low_head, outs[0], outs[1]).astype(BF16)

    steps_of(k.pairs, k.heads_step, heads)
    held.done(probs)
    held.need(wout)
    middle[...] = xv[...].astype(F32) + dot(mixed[...], wout[...])
    held.done(middle)
    if k.kept:
        k.put_left(left, at_mixed, mixed[...])
    for b, rows in k.blocks:
        unit, _ = norm_parts(middle[rows])
        modded[rows] = (unit * (1.0 + k.mod_row(b, 0)) + k.mod_row(b, 1)).astype(BF16)
    if k.kept:
        k.put_left(left, at_modded, modded[...])
    held.need(wex, wre)
    branch[...] = jnp.broadcast_to(k.rbias[...].astype(F32), (span, width))

    def feed(j):
        at = lanes(j, k.step)
        pre = dot(modded[...], wex[:, at]) + k.ebias[:, at].astype(F32)
        area = 0.5 + 0.5 * lax.erf(pre * ROOT_HALF)
        out = (pre * area).astype(BF16)
        if k.kept:
            slope[:, at] = area + pre * (jnp.exp(pre * pre * -0.5) * ROOT_TAU)
            k.put_active(left, j, out)
        branch[...] += dot(out, wre[at, :])

    if k.heads_step == 1:
        steps_of(k.tiles, 1, feed)
    else:
        repeat(k.tiles, feed)
    held.done(slope, left, branch)
    for b, rows in k.blocks:
        result[rows] = (middle[rows] + k.mod_row(b, 2) * branch[rows]).astype(BF16)
    held.done(result)


def output(k, dyv, bg):
    k.held.need(dyv)
    for b, rows in k.blocks:
        bg[rows] = (dyv[rows].astype(F32) * k.mod_row(b, 2)).astype(BF16)
    k.held.done(bg)


def mlp(k, wre, wex, bg, slope, middle, branch, dyv, pa, middle_grad, small, acc):
    span, width, hidden, held = k.span, k.width, k.hidden, k.held
    small[...] = jnp.zeros(small.shape, F32)
    acc[...] = jnp.zeros(acc.shape, F32)
    held.begin(bg)
    for j in range(k.tiles):
        held.begin(wre, slope, wex, part=j)
    held.begin(middle, dyv, branch)
    held.need(bg)

    def feed(j):
        at = lanes(j, k.step)
        held.need(wre, slope, wex, part=j)
        grad = dot(bg[...], wre[at, :], 1, 1)
        pre_grad = (slope[:, at] * grad).astype(BF16)
        pa[:span, at] = pre_grad
        small[0:1, at] = jnp.sum(pre_grad.astype(F32), axis=0, keepdims=True)
        acc[...] += dot(pre_grad, wex[:, at], 1, 1)

    repeat(k.tiles, feed)
    held.need(middle, dyv, branch)
    total = jnp.zeros((1, width), F32)
    for b, rows in k.blocks:
        cotan = dyv[rows].astype(F32)
        total += jnp.sum(bg[rows].astype(F32), axis=0, keepdims=True)
        grad = acc[rows]
        unit, factor = norm_parts(middle[rows])
        k.add_segment(small, b, 0, jnp.sum(grad * unit, axis=0, keepdims=True))
        k.add_segment(small, b, 1, jnp.sum(grad, axis=0, keepdims=True))
        k.add_segment(small, b, 2, jnp.sum(cotan * branch[rows], axis=0, keepdims=True))
        back = norm_back(grad * (1.0 + k.mod_row(b, 0)), unit, factor)
        full = cotan + back
        middle_grad[rows] = full
        pa[rows, hidden:] = full.astype(BF16)
    small[1:2, :width] = total
    pa[span:, :] = small[...].astype(BF16)
    held.done(pa, middle_grad)


def attend(
    k, wout, win, agrad, probs, qkv, xv, middle_grad, jg, leave, mixed_grad, acc
):
    span, held = k.span, k.held
    held.need(agrad, wout)
    held.begin(probs, qkv)
    mixed_grad[...] = dot(agrad[...], wout[...], 1, 1).astype(BF16)
    held.need(probs, qkv)
    held.begin(win, xv, middle_grad)
    cos_part, sin_part = k.trig_pair()

    def heads(i):
        at = k.thirds(i)
        query, key, value = (qkv[:, a] for a in at)
        out_grad = mixed_grad[:, at[0]]
        parts = []
        for h in range(2):
            prob = probs[2 * i + h]
            pull = dot(value * k.head_row[h], out_grad, 1, 1)
            shared = jnp.sum(prob * pull, axis=0, keepdims=True)
            score_grad = (prob * (pull - shared)).astype(BF16)
            parts.append(
                (
                    dot(score_grad, key, 0, 0),
                    dot(score_grad, query),
                    dot(prob.astype(BF16), out_grad),
                )
            )
        for p in range(3):
            grad = jnp.where(k.low_head, parts[0][p], parts[1][p])
            if p < 2:
                grad = grad * cos_part - swap_halves(grad, k.low_half) * sin_part
                if p == 0:
                    grad = grad * 0.125
            jg[:span, at[p]] = grad.astype(BF16)

    steps_of(k.pairs, k.heads_step, heads)
    held.need(win, xv, middle_grad)
    acc[...] = dot(jg[:span, :], win[...], 1, 1)
    total = jnp.zeros((1, k.width), F32)
    for b, rows in k.blocks:
        grad = acc[rows]
        unit, factor = norm_parts(xv[rows].astype(F32))
        total += jnp.sum(grad * unit, axis=0, keepdims=True)
        back = norm_back(grad * k.gain[...].astype(F32), unit, factor)
        leave[rows] = (middle_grad[rows] + back).astype(BF16)
    below = jnp.concatenate([total, jnp.zeros((EXTRA - 1, k.width), F32)], axis=0)
    jg[span:, : k.width] = below.astype(BF16)
    jg[span:, k.width :] = jnp.zeros((EXTRA, 2 * k.width), BF16)
    held.done(jg, leave)


def copy_agrad(k, pa, agrad):
    agrad[...] = pa[: k.span, k.hidden :]


class Sums:
    def __init__(self, ranks, full, outs, sems):
        self.full = full
        self.own = [((ranks[0] >> bit) & 1) == 0 for bit in (1, 2)]
        self.bufs = outs[:4]
        self.targets = outs[4:]
        self.sems = sems
        self.half = full.shape[1] // 2
        self.copies = []

    def put(self, block, at, values):
        self.full[block, at] = values

    def settle(self, which, groups):
        send, keep = self.bufs[2 * which : 2 * which + 2]
        at = slice(which * self.half, (which + 1) * self.half)
        apart = 1 + which
        for group in groups:
            for n in range(2):
                first = 4 * group + (2 * n if which == 0 else n)
                even, odd = self.full[first, at], self.full[first + apart, at]
                send[2 * group + n] = jnp.where(self.own[which], odd, even).astype(BF16)
                keep[2 * group + n] = jnp.where(self.own[which], even, odd)
            spot = pl.ds(2 * group, 2)
            for n in range(2 * which, 2 * which + 2):
                copy = pltpu.make_async_copy(
                    self.bufs[n].at[spot], self.targets[n].at[spot], self.sems.at[len(self.copies)]
                )
                copy.start()
                self.copies.append(copy)

    def finish(self):
        for copy in self.copies:
            copy.wait()


def term_reduce(k, sums, left, right):
    lines = k.hidden // k.count
    per = TILE // lines
    for tile in range(k.hidden // 2 // TILE):
        k.arrive(tile)
        total = dot(left[tile * TILE : (tile + 1) * TILE], right[...])
        for n in range(per):
            sums.put(tile * per + n, slice(0, lines), total[n * lines : (n + 1) * lines])
        if (tile + 1) * per % 4 == 0:
            group = ((tile + 1) * per // 4 - 1,)
            sums.settle(0, group)
            sums.settle(1, group)


def square_terms(k, sums, left, right, cols, part):
    lines = k.width // k.count
    total = dot(left, right[: 4 * k.span, cols])
    for n in range(k.count // 2):
        sums.put(n, slice(part * lines, (part + 1) * lines), total[n * lines : (n + 1) * lines])


def term_expand(k, sums, left, right):
    width, hidden, span = k.width, k.hidden, k.span
    groups = range(k.count // 8)
    tall = hidden // width
    lines = width // k.count
    rows = width // 2
    half = sums.half
    settled = False
    for col in range(tall + 1):
        k.arrive(col)
        part = left[:rows] if col < tall else left[rows:]
        square_terms(k, sums, part, right, slice(col * width, (col + 1) * width), col)
        if (col + 1) * lines >= half and not settled:
            sums.settle(0, groups)
            settled = True
    smalls = [k.small[n].astype(F32) for n in range(4)]
    angles = jnp.concatenate([embed[...] for embed in k.embeds], axis=1)
    pieces = []
    for _ in range(3):
        pieces.append(angles.astype(BF16))
        angles = angles - pieces[-1].astype(F32)
    seqs = jnp.concatenate([small[2 : 2 + SEGS, : 3 * width] for small in smalls]).astype(BF16)
    times = sum(dot(piece, seqs) for piece in pieces)
    both = sum(smalls)
    seq_sum = jnp.sum(both[2 : 2 + SEGS, : 3 * width], axis=0, keepdims=True)
    lines_v = k.lines
    lines_v[...] = jnp.zeros(lines_v.shape, F32)
    lines_v[0:1] = both[1:2, :width]
    for n in range(3):
        lines_v[1 + n : 2 + n] = seq_sum[:, n * width : (n + 1) * width]
    for n in range(tall):
        lines_v[4 + n : 5 + n] = both[0:1, n * width : (n + 1) * width]
    deep = EMB // k.count
    first = (tall + 1) * lines
    low = k.core == 0
    for g in range(k.count // 2):
        for p in range(3):
            at = slice(p * width, (p + 1) * width)
            even = times[2 * g * deep : (2 * g + 1) * deep, at]
            odd = times[(2 * g + 1) * deep : (2 * g + 2) * deep, at]
            to = first + p * deep
            sums.put(g, slice(to, to + deep), jnp.where(low, even, odd))
        sums.put(g, slice(first + 3 * deep, 2 * half), lines_v[...])
    sums.settle(1, groups)


def term_attend(k, sums, left, right):
    width = k.width
    groups = range(k.count // 8)
    lines = width // k.count
    settled = False
    for col in range(3):
        k.arrive(col)
        square_terms(k, sums, left[...], right, slice(col * width, (col + 1) * width), col)
        if (col + 1) * lines >= sums.half and not settled:
            sums.settle(0, groups)
            settled = True
    gain = sum(k.small[n].astype(F32) for n in range(4))[:, :width]
    for g in range(k.count // 2):
        sums.put(g, slice(3 * lines, 3 * lines + GAIN_ROWS), gain)
    sums.settle(1, groups)


def load_terms(k, refs, bufs, base, sems):
    left_v, right_v, small_v = bufs
    rows, cols = left_v.shape[0], right_v.shape[1]
    tall = rows // TILE if small_v is None else 1
    wide = cols // k.width
    groups = []
    for i in range(tall):
        for j in range(wide):
            copies = []
            for n, (left, right) in enumerate(zip(refs[:4], refs[4:8])):
                tokens = pl.ds(n * k.span, k.span)
                part = pl.ds(i * (rows // tall), rows // tall)
                from_part = pl.ds(base + i * (rows // tall), rows // tall)
                at = pl.ds(j * k.width, k.width)
                if j == 0:
                    copies.append((left.at[from_part], left_v.at[part, tokens]))
                if i == 0:
                    copies.append((right.at[pl.ds(0, k.span), at], right_v.at[tokens, at]))
                if small_v is not None and j == wide - 1:
                    copies.append((right.at[pl.ds(k.span, EXTRA)], small_v.at[n]))
            groups.append(copies)
    made, count = [], 0
    for copies in groups:
        made.append([])
        for pair in copies:
            made[-1].append(pltpu.make_async_copy(*pair, sems.at[count]))
            made[-1][-1].start()
            count += 1
    return made


class Terms:
    def __init__(self, sizes, core):
        self.span, self.width, self.hidden, self.count = sizes
        self.core = core[0]

    def arrive(self, group):
        for copy in self.groups[group]:
            copy.wait()


def term_kernel(sizes, body, base, extra, *refs):
    refs = list(refs)
    core, rank = refs[:2]
    k = Terms(sizes, core)
    pos = 2
    if body is term_expand:
        k.embeds = refs[pos : pos + 2]
        pos += 2
    sources = refs[pos : pos + 8]
    pos += 8 + extra
    targets = refs[pos : pos + 4]
    pos += 4
    left_v, right_v, full, *outs = refs[pos : pos + 7]
    pos += 7
    k.small = None
    if body is not term_reduce:
        k.small, k.lines = refs[pos : pos + 2]
        pos += 2
    sems, out_sems = refs[pos:]
    k.groups = load_terms(k, sources, (left_v, right_v, k.small), base, sems)
    sums = Sums(rank, full, outs + targets, out_sems)
    body(k, sums, left_v, right_v)
    sums.finish()


def term_call(name, body, sizes, lines, base, rows, core, rank, lefts, rights, embeds=(), after=()):
    span, width, hidden, count = sizes
    blocks = count // 2
    cols = rights[0].shape[1]
    half = lines // 2
    outs = [((blocks // 2, half, width), kind) for kind in (BF16, F32)] * 2
    scratch = [
        ((rows, 4 * span), BF16),
        ((4 * span, cols), BF16),
        ((blocks, lines, width), F32),
        *outs,
    ]
    if body is not term_reduce:
        scratch += [((4, EXTRA, cols), BF16), ((TAIL_ROWS, width), F32)]
    args = [core.reshape(1), rank.reshape(1), *embeds, *lefts, *rights, *after]
    in_specs = [pl.BlockSpec(memory_space=SMEM)] * 2
    in_specs += [pl.BlockSpec(memory_space=VMEM)] * len(embeds)
    in_specs += [pl.BlockSpec(memory_space=ANY)] * (8 + len(after))
    return pl.pallas_call(
        partial(term_kernel, sizes, body, base, len(after)),
        out_shape=[jax.ShapeDtypeStruct(*item) for item in outs],
        in_specs=in_specs,
        out_specs=[pl.BlockSpec(memory_space=ANY)] * 4,
        scratch_shapes=[pltpu.VMEM(*item) for item in scratch]
        + [pltpu.SemaphoreType.DMA((32,)), pltpu.SemaphoreType.DMA((8,))],
        compiler_params=pltpu.CompilerParams(vmem_limit_bytes=62 * 1024 * 1024),
        name=name,
    )(*args)


def plain_pieces(lefts, rights, embed, sizes):
    span, width, hidden, count = sizes
    bg, pa, jg = rights
    bases = [2 * base for base in left_bases(width, hidden)]

    def blocks(base, rows, right):
        total = sum(dot(a[base : base + rows], b) for a, b in zip(lefts, right))
        parts = [total[:, i : i + width] for i in range(0, total.shape[1], width)]
        return [part.reshape(count, -1, width) for part in parts]

    take = lambda items, cols: [item[:span, cols] for item in items]
    reduce = blocks(bases[0], hidden, bg)
    expand = blocks(bases[1], width, take(pa, slice(0, hidden)))
    expand += blocks(bases[2], width, take(pa, slice(hidden, hidden + width)))
    last = blocks(bases[3], width, take(jg, slice(None)))
    small = [item[span:].astype(F32) for item in pa]
    seqs = jnp.concatenate([item[2 : 2 + SEGS, : 3 * width] for item in small])
    times = jnp.dot(embed, seqs, precision=lax.Precision.HIGHEST)
    expand += [times[:, i * width : (i + 1) * width].reshape(count, -1, width) for i in range(3)]
    lines = jnp.concatenate(
        [
            sum(item[1:2, :width] for item in small),
            jnp.sum(seqs, axis=0).reshape(-1, width),
            sum(item[0, :hidden] for item in small).reshape(-1, width),
        ]
    )
    lines = jnp.pad(lines, ((0, TAIL_ROWS - lines.shape[0]), (0, 0)))
    gain = sum(item[span:, :width].astype(F32) for item in jg)
    expand.append(jnp.broadcast_to(lines, (count,) + lines.shape))
    last.append(jnp.broadcast_to(gain, (count,) + gain.shape))
    return [jnp.concatenate(item, axis=1) for item in (reduce, expand, last)]


def shapes_of(span, width, hidden, cores):
    tok = lambda cols, kind=BF16: ((span, cols), kind)
    below = lambda cols: ((span + EXTRA, cols), BF16)
    return dict(
        xv=tok(width),
        dyv=tok(width),
        win=((width, 3 * width), BF16),
        wout=((width, width), BF16),
        wex=((width, hidden), BF16),
        wre=((hidden, width), BF16),
        left=((cores, (hidden + 3 * width) // cores, span), BF16),
        normed=tok(width),
        qkv=tok(3 * width),
        probs=((HEADS, span, span), F32),
        mixed=tok(width),
        middle=tok(width, F32),
        modded=tok(width),
        slope=tok(hidden, F32),
        branch=tok(width, F32),
        result=tok(width),
        bg=tok(width),
        pa=below(hidden + width),
        jg=below(3 * width),
        agrad=tok(width),
        mixed_grad=tok(width),
        middle_grad=tok(width, F32),
        leave=tok(width),
        acc=tok(width, F32),
        bias=tok(span, F32),
        small=((EXTRA, hidden + width), F32),
    )


def uses(part):
    return list(inspect.signature(part).parameters)[1:]


def stage_kernel(sizes, parts, who, slot, plan, *refs):
    refs = list(refs)
    layer = Layer(sizes, slot, refs[:7])
    span = layer.span
    pos = 7
    loads = {}
    for name, row, cols in plan.sources:
        ref = refs[pos]
        if cols is not None:
            ref = ref.at[pl.ds(0, span), pl.ds(*cols)]
        elif row is not None:
            ref = ref.at[pl.ds(row, span)]
        loads[name] = ref
        pos += 1
    pos += plan.extra
    stores = {}
    for name, row, at in plan.targets:
        target = refs[pos] if row is None else refs[pos].at[pl.ds(row, span)]
        stores.setdefault(name, []).append((at, target))
        pos += 1
    bufs = {}
    for name in plan.bufs:
        bufs[name] = refs[pos]
        pos += 1
    layer.held = Held(bufs, loads, stores, refs[pos], plan.pieces)
    layer.kept = plan.kept
    layer.heads_step = plan.heads_step

    @pl.when(layer.section == who)
    def _():
        for part in parts:
            part(layer, *[bufs[name] for name in uses(part)])
        layer.held.finish()


def stage(
    name, common, parts, who, slot, loads, stores, carried=None, after=(), kept=True, heads_step=3,
    pieces=None,
):
    carried = carried or {}
    span, width, hidden, count = common.sizes
    shapes = shapes_of(span, width, hidden, common.cores)
    bufs = []
    for part in parts:
        bufs += [item for item in uses(part) if item not in bufs]
    pair = lambda item: item if isinstance(item, tuple) else (item, None)
    args = list(common.args)
    in_specs = [pl.BlockSpec(memory_space=SMEM)] * 2 + [pl.BlockSpec(memory_space=VMEM)] * 5
    plan = Bag(sources=[], targets=[], bufs=bufs, kept=kept, heads_step=heads_step)
    plan["pieces"] = pieces or {}
    for item in loads:
        if item in bufs:
            array, row, *cols = pair(loads[item])
            args.append(array)
            plan.sources.append((item, row, cols[0] if cols else None))
    outs, aliases, extra = [], {}, []
    targets = []
    for item, key in stores.items():
        if item == "left":
            targets += [(item, key + "_send" * n, None, n) for n in range(common.cores)]
        else:
            targets.append((item, *pair(key), None))
    for i, (item, key, row, at) in enumerate(targets):
        shape, kind = shapes[item]
        if row is not None:
            shape = (common.tokens,) + shape[1:]
        if at is not None:
            shape = shape[1:]
        outs.append(jax.ShapeDtypeStruct(shape, kind))
        plan.targets.append((item, row, at))
        if key in carried:
            aliases[len(args) + len(extra)] = i
            extra.append(carried[key])
    extra += list(after)
    args += extra
    plan["extra"] = len(extra)
    in_specs += [pl.BlockSpec(memory_space=ANY)] * (len(args) - len(in_specs))
    results = pl.pallas_call(
        partial(stage_kernel, common.sizes, parts, who, slot, plan),
        out_shape=outs,
        in_specs=in_specs,
        out_specs=[pl.BlockSpec(memory_space=ANY)] * len(outs),
        input_output_aliases=aliases,
        scratch_shapes=[pltpu.VMEM(*shapes[item]) for item in bufs]
        + [pltpu.SemaphoreType.DMA((32,))],
        compiler_params=pltpu.CompilerParams(vmem_limit_bytes=62 * 1024 * 1024),
        name=name,
    )(*args)
    return Bag({key: value for (_, key, _, _), value in zip(targets, results)})


def bits_of(count):
    bits = count.bit_length() - 1
    assert 1 << bits == count
    return bits


class Chunk:
    def __init__(self, axis, bits, size, settled=()):
        self.axis = axis
        self.bits = list(range(bits - 1, 0, -1))
        self.size = size
        self.settled = list(settled)
        self.terms = []

    def add(self, term, start=0):
        left = [bit for bit in self.bits if bit not in self.settled]
        self.terms.append((term.reshape((2,) * len(left) + term.shape[-2:]), left, start))

    def take(self, term, start, left, flip):
        me = lax.axis_index(self.axis)
        side = lambda bit: 1 - ((me >> bit) & 1) if bit == flip else (me >> bit) & 1
        starts = [side(bit) if bit in self.settled else 0 for bit in left]
        sizes = [1 if bit in self.settled else 2 for bit in left]
        cols = term.shape[-1]
        piece = lax.dynamic_slice(term, starts + [start, 0], sizes + [self.size, cols])
        open_bits = [2] * (len(self.bits) - len(self.settled))
        return piece.reshape(open_bits + [self.size, cols]).astype(F32)

    def split(self, bit):
        self.settled.append(bit)
        return sum(self.take(term, start, left, bit) for term, left, start in self.terms).astype(
            BF16
        )

    def total(self):
        return sum(self.take(term, start, left, None) for term, left, start in self.terms)


def exchange(block, axis, bit):
    count = lax.axis_size(axis)
    return lax.ppermute(block, axis, [(i, i ^ (1 << bit)) for i in range(count)])


def join(*items):
    return lax.optimization_barrier(items)


def angle_table(span):
    half = HEAD // 2
    freqs = np.exp(-math.log(10000.0) * np.arange(half, dtype=np.float32) / half)
    phase = np.arange(span, dtype=np.float32)[:, None] * freqs.astype(np.float32)[None, :]
    cos_part, sin_part = np.cos(phase), np.sin(phase)
    return np.stack(
        [
            np.concatenate([cos_part] * 4, axis=1),
            np.concatenate([-sin_part, sin_part] * 2, axis=1),
        ]
    ).astype(np.float32)


def per_device(
    ends_in,
    lengths,
    times,
    norm_gain,
    attend_in,
    attend_out,
    time_weight,
    time_bias,
    expand_weight,
    expand_bias,
    reduce_weight,
    reduce_bias,
):
    local = ends_in[0]
    micro = lengths.shape[1]
    assert micro == 2
    width = local.shape[1]
    span = local.shape[0] // micro
    hidden = expand_weight.shape[2]
    count = lax.axis_size("rep")
    section = lax.axis_index("section")
    rank = lax.axis_index("rep")
    core = rank & 1
    steps = jnp.exp(-math.log(10000.0) * jnp.arange(EMB // 2, dtype=F32) / (EMB // 2))
    turn = times.reshape(micro * SEGS, 1).astype(F32) * steps
    embed = jnp.concatenate([jnp.cos(turn), jnp.sin(turn)], axis=1)
    mods = jnp.dot(
        embed, time_weight[0].astype(F32), precision=lax.Precision.HIGHEST
    ) + time_bias.astype(F32)
    fused = width // count % 16 == 0 and TILE % (hidden // count) == 0 and count >= 16
    common = Bag(
        args=(
            lengths[0],
            jnp.stack([section, core]),
            mods,
            jnp.asarray(angle_table(span)),
            norm_gain,
            expand_bias,
            reduce_bias,
        ),
        sizes=(span, width, hidden, count),
        tokens=local.shape[0],
        cores=2 if fused else 1,
    )
    weights = Bag(
        win=attend_in[0], wout=attend_out[0], wex=expand_weight[0], wre=reduce_weight[0]
    )
    rows = [(local, slot * span) for slot in range(micro)]
    same = lambda *names: {name: name for name in names}
    whole = same("left", "bg", "pa", "jg")
    run = partial(stage, common=common)
    both = (forward, output, mlp, copy_agrad, attend)
    over = lambda block, route: lax.ppermute(block, "section", route)
    swap = lambda block, bit: exchange(block, "rep", bit)
    a = run(
        "first_0",
        parts=(forward,),
        who=0,
        slot=0,
        loads=dict(xv=rows[0], **weights),
        stores=dict(result="leave"),
        kept=False,
    )
    came_0 = over(a.leave, [(0, 1)])
    after = (a.leave,)
    if fused:
        embeds = (embed.T, swap(embed.T, 0))
        after += (embeds[1],)
    b = run(
        "first_1",
        parts=(forward,),
        who=0,
        slot=1,
        loads=dict(xv=rows[1], **weights),
        stores=same("result", "left", "qkv", "probs", "middle", "slope", "branch"),
        after=after,
        heads_step=1,
    )
    came_1 = over(b.result, [(0, 1)])
    x = run(
        "second_0",
        parts=both,
        who=1,
        slot=0,
        loads=dict(xv=came_0, dyv=rows[0], **weights),
        stores=dict(whole, result=("ends", 0), leave="leave"),
        after=(b.result,),
    )
    back_0 = over(x.leave, [(1, 0)])
    y = run(
        "second_1",
        parts=both,
        who=1,
        slot=1,
        loads=dict(xv=came_1, dyv=rows[1], **weights),
        stores=dict(whole, result=("ends", span), leave="leave"),
        carried=dict(b, ends=x.ends),
        after=(x.leave,),
    )
    back_1 = over(y.leave, [(1, 0)])
    gates = mods[SEGS : 2 * SEGS, 2 * width :]
    gates = jnp.where(lengths[0, 1, 0] == span, gates[:1], gates)
    x = run(
        "back_0",
        parts=both,
        who=0,
        slot=0,
        loads=dict(xv=rows[0], dyv=back_0, **weights),
        stores=dict(whole, leave=("ends", 0)),
        carried=dict(x, ends=y.ends),
        after=(y.leave, gates),
    )
    if fused:
        y_left = swap(y.left_send, 0)
        back_1, x_send, x_bg = join(back_1, x.left_send, x.bg)
        lefts = [x.left, y.left, swap(x_send, 0), y_left]
        others = [swap(item, 0) for item in (x_bg, x.pa, x.jg)]
    cotan = back_1.astype(F32).reshape(SEGS, -1, width)
    made = (cotan * gates[:, None]).reshape(span, width).astype(BF16)
    bg_1 = jnp.where(section == 0, made, y.bg)
    def last_mlp(after):
        return run(
            "back_1_mlp",
            parts=(mlp,),
            who=0,
            slot=1,
            loads=dict(
                bg=bg_1,
                wre=weights.wre,
                slope=b.slope,
                wex=weights.wex,
                middle=b.middle,
                dyv=back_1,
                branch=b.branch,
            ),
            stores=same("pa", "middle_grad"),
            carried=y,
            after=after,
            pieces=dict.fromkeys(("slope", "wex"), (1, hidden // width))
            | dict(wre=(0, hidden // width)),
        )

    bits = bits_of(count)
    term = partial(term_call, sizes=common.sizes, core=core, rank=rank)
    lines = width // count
    deep = EMB // count
    sizes = (hidden // count, hidden // count + lines + 3 * deep + TAIL_ROWS, 3 * lines + GAIN_ROWS)
    bases = left_bases(width, hidden)

    def last_attend(part, after):
        return run(
            "back_1_attend",
            parts=(attend,),
            who=0,
            slot=1,
            loads=dict(
                agrad=(part.pa, None, (hidden, width)),
                wout=weights.wout,
                probs=b.probs,
                qkv=b.qkv,
                win=weights.win,
                xv=rows[1],
                middle_grad=part.middle_grad,
            ),
            stores=dict(jg="jg", leave=("ends", span)),
            carried=dict(y, ends=x.ends),
            after=after,
        )

    def pair_of(size, first):
        cut = size // 2 if fused else size // 32 * 16
        one = Chunk("rep", bits, cut, (1,) if fused else ())
        two = Chunk("rep", bits, size - cut, (2,) if fused else ())
        if fused:
            send_1, keep_1, send_2, keep_2 = first
            one.add(keep_1)
            two.add(keep_2)
            return one, two, send_1, send_2
        view = first.reshape((count // 2, 2) + first.shape[1:])
        cut = lambda at: lax.dynamic_index_in_dim(view, at, 1, keepdims=False)
        came = swap(cut(1 - core).astype(BF16), 0)
        for item in (cut(core), came):
            one.add(item)
            two.add(item, one.size)
        return one, two, one.split(1), two.split(2)

    if fused:
        bg_1_other = swap(bg_1, 0)
        sent = term(
            "term_reduce",
            term_reduce,
            lines=sizes[0],
            base=bases[0],
            rows=hidden // 2,
            lefts=lefts,
            rights=[x.bg, bg_1, others[0], bg_1_other],
        )
        r1, r2, send_1, send_2 = pair_of(sizes[0], sent)
        came_r1, came_r2 = swap(send_1, 1), swap(send_2, 2)
        part = last_mlp((send_1, send_2))
        came_r1, came_r2, pa_1 = join(came_r1, came_r2, part.pa)
        pa_other = swap(pa_1, 0)
        r1.add(came_r1)
        r2.add(came_r2)
        send_1, send_2 = r1.split(2), r2.split(1)
        came_r1, came_r2 = swap(send_1, 2), swap(send_2, 1)
        sent = term(
            "term_expand",
            term_expand,
            lines=sizes[1],
            base=bases[1],
            rows=width,
            lefts=lefts,
            rights=[x.pa, pa_1, others[1], pa_other],
            embeds=embeds,
            after=(send_1, send_2),
        )
        came_r1, came_r2, *sent = join(came_r1, came_r2, *sent)
        e1, e2, send_1, send_2 = pair_of(sizes[1], sent)
        came_e1, came_e2 = swap(send_1, 1), swap(send_2, 2)
        last = last_attend(part, (send_1, send_2))
        jg_1 = last.jg
        jg_other = swap(jg_1, 0)
        came_r1, came_r2, _ = join(came_r1, came_r2, jg_1)
        r1.add(came_r1)
        r2.add(came_r2)
        block_r = jnp.concatenate([r1.split(3), r2.split(3)], axis=-2)
        came_r = swap(block_r, 3)
        came_e1, came_e2, _ = join(came_e1, came_e2, block_r)
        e1.add(came_e1)
        e2.add(came_e2)
        send_1, send_2 = e1.split(2), e2.split(1)
        came_e1, came_e2 = swap(send_1, 2), swap(send_2, 1)
        sent = term(
            "term_attend",
            term_attend,
            lines=sizes[2],
            base=bases[3],
            rows=width // 2,
            lefts=lefts,
            rights=[x.jg, jg_1, others[2], jg_other],
            after=(send_1, send_2),
        )
        came_r, *sent = join(came_r, *sent)
        a1, a2, send_1, send_2 = pair_of(sizes[2], sent)
    else:
        part = last_mlp(())
        pa_1 = part.pa
        last = last_attend(part, ())
        rights = [(x.bg, bg_1), (x.pa, pa_1), (x.jg, last.jg)]
        totals = plain_pieces((x.left, y.left), rights, embed.T, common.sizes)
        r1, r2, send_1, send_2 = pair_of(sizes[0], totals[0])
        r1.add(swap(send_1, 1))
        r2.add(swap(send_2, 2))
        r1.add(swap(r1.split(2), 2))
        r2.add(swap(r2.split(1), 1))
        came_r = swap(jnp.concatenate([r1.split(3), r2.split(3)], axis=-2), 3)
        e1, e2, send_1, send_2 = pair_of(sizes[1], totals[1])
        e1.add(swap(send_1, 1))
        e2.add(swap(send_2, 2))
        came_e1, came_e2 = swap(e1.split(2), 2), swap(e2.split(1), 1)
        a1, a2, send_1, send_2 = pair_of(sizes[2], totals[2])
    ends = last.ends
    came_a1, came_a2 = swap(send_1, 1), swap(send_2, 2)
    came_e1, came_e2, _ = join(came_e1, came_e2, send_1)
    e1.add(came_e1)
    e2.add(came_e2)
    block_e = jnp.concatenate([e1.split(3), e2.split(3)], axis=-2)
    came_e = swap(block_e, 3)
    came_a1, came_a2, _ = join(came_a1, came_a2, block_e)
    a1.add(came_a1)
    a2.add(came_a2)
    send_1, send_2 = a1.split(2), a2.split(1)
    came_a1, came_a2 = swap(send_1, 2), swap(send_2, 1)
    a1.add(came_a1)
    a2.add(came_a2)
    block_a = jnp.concatenate([a1.split(3), a2.split(3)], axis=-2)
    came_a = swap(block_a, 3)
    came_r, _ = join(came_r, send_1)
    r1.add(came_r[..., : r1.size, :])
    r2.add(came_r[..., r1.size :, :])
    came_e, _ = join(came_e, block_a)
    e1.add(came_e[..., : e1.size, :])
    e2.add(came_e[..., e1.size :, :])
    a1.add(came_a[..., : a1.size, :])
    a2.add(came_a[..., a1.size :, :])
    for bit in range(4, bits):
        for chunk in (r1, r2, e1, e2, a1, a2):
            chunk.add(swap(chunk.split(bit), bit))
    share_r, share_e, share_a = (
        jnp.concatenate([one.total(), two.total()]) for one, two in ((r1, r2), (e1, e2), (a1, a2))
    )
    tall = hidden // width
    side = lambda item, n, size: jnp.concatenate(
        [item[i * size : (i + 1) * size] for i in range(n)], axis=1
    )
    at_o = tall * lines
    at_t = at_o + lines
    small = share_e[at_t + 3 * deep :]
    flat = lambda item, first, n: lax.dynamic_slice_in_dim(
        item[first : first + n].reshape(-1), rank * (n * width // count), n * width // count
    )
    results = (
        flat(share_a, 3 * lines, 1),
        side(share_a, 3, lines),
        share_e[at_o:at_t],
        side(share_e[at_t:], 3, deep),
        flat(small, 1, 3),
        side(share_e, tall, lines),
        flat(small, 4, tall),
        share_r,
        flat(small, 0, 1),
    )
    return (ends[None],) + tuple(piece[None] for piece in results)


def solution(mesh):
    return jax.shard_map(
        per_device,
        mesh=mesh,
        in_specs=(
            P("section", "rep", None),
            P("rep", None, None),
            P("rep", None, None),
            P("section", None),
            P("section", None, None),
            P("section", None, None),
            P("section", None, None),
            P("section", None),
            P("section", None, None),
            P("section", None),
            P("section", None, None),
            P("section", None),
        ),
        out_specs=(
            P("section", "rep", None),
            P("section", "rep"),
            P("section", "rep", None),
            P("section", "rep", None),
            P("section", "rep", None),
            P("section", "rep"),
            P("section", "rep", None),
            P("section", "rep"),
            P("section", "rep", None),
            P("section", "rep"),
        ),
        check_vma=False,
    )
```

```python
from functools import partial
import inspect
import math

import jax
import jax.numpy as jnp
import numpy as np
from jax import lax
from jax.experimental import pallas as pl
from jax.experimental.pallas import tpu as pltpu
from jax.sharding import PartitionSpec as P

HEADS = 12
HEAD = 64
EMB = 128
SEGS = 4
ANY = pl.ANY
VMEM = pltpu.MemorySpace.VMEM
SMEM = pltpu.MemorySpace.SMEM
F32 = jnp.float32
BF16 = jnp.bfloat16
ROOT_HALF = 0.7071067811865476
ROOT_TAU = 0.3989422804014327
TILE = 384
TAIL_ROWS = 24
GAIN_ROWS = 16
EXTRA = 16


class Bag(dict):
    __getattr__ = dict.__getitem__


def dot(left, right, left_dim=1, right_dim=0):
    return lax.dot_general(
        left, right, (((left_dim,), (right_dim,)), ((), ())), preferred_element_type=F32
    )


def repeat(count, body):
    for i in range(count):
        body(i)


def steps_of(count, size, body):
    def several(i, _):
        for j in range(size):
            body(size * i + j)
        return _

    lax.fori_loop(0, count // size, several, 0)


def lanes(index, size, start=0):
    if isinstance(index, int):
        return slice(start + index * size, start + (index + 1) * size)
    return pl.ds(pl.multiple_of(start + index * size, size), size)


def swap_halves(values, low_half):
    forth = pltpu.roll(values, 128 - HEAD // 2, 1)
    back = pltpu.roll(values, HEAD // 2, 1)
    return jnp.where(low_half, forth, back)


def norm_parts(values):
    center = values - jnp.mean(values, axis=-1, keepdims=True)
    spread = jnp.mean(center * center, axis=-1, keepdims=True)
    factor = lax.rsqrt(spread + 1e-05)
    return center * factor, factor


def norm_back(grad, unit, factor):
    return factor * (
        grad
        - jnp.mean(grad, axis=-1, keepdims=True)
        - unit * jnp.mean(grad * unit, axis=-1, keepdims=True)
    )


class Held:
    def __init__(self, bufs, loads, stores, sems, pieces):
        self.bufs = bufs
        self.loads = loads
        self.stores = stores
        self.sems = sems
        self.pieces = pieces
        self.names = {id(buf): name for name, buf in bufs.items()}
        keys = [(name, j) for name in loads for j in range(self.parts_of(name))]
        self.spots = {key: n for n, key in enumerate(keys)}
        self.waiting = set(keys)
        self.pending = set(keys)
        self.leaving = {}

    def parts_of(self, name):
        return self.pieces[name][1] if name in self.pieces else 1

    def load(self, name, j):
        source, target = self.loads[name], self.bufs[name]
        if name in self.pieces:
            axis, count = self.pieces[name]
            size = target.shape[axis] // count
            at = (slice(None),) * axis + (pl.ds(j * size, size),)
            source, target = source.at[at], target.at[at]
        return pltpu.make_async_copy(source, target, self.sems.at[self.spots[(name, j)]])

    def store(self, name, n):
        at, target = self.stores[name][n]
        source = self.bufs[name] if at is None else self.bufs[name].at[at]
        return pltpu.make_async_copy(source, target, self.sems.at[self.leaving[(name, n)]])

    def keys(self, bufs, part):
        for buf in bufs:
            name = self.names[id(buf)]
            for j in range(self.parts_of(name)):
                if part in (None, j):
                    yield name, j

    def begin(self, *bufs, part=None):
        for key in self.keys(bufs, part):
            if key in self.waiting:
                self.waiting.remove(key)
                self.load(*key).start()

    def need(self, *bufs, part=None):
        self.begin(*bufs, part=part)
        for key in self.keys(bufs, part):
            if key in self.pending:
                self.pending.remove(key)
                self.load(*key).wait()

    def done(self, *bufs):
        for buf in bufs:
            name = self.names[id(buf)]
            for n in range(len(self.stores.get(name, ()))):
                self.leaving[(name, n)] = len(self.spots) + len(self.leaving)
                self.store(name, n).start()

    def finish(self):
        for name, n in self.leaving:
            self.store(name, n).wait()


class Layer:
    def __init__(self, sizes, slot, refs):
        self.span, self.width, self.hidden, self.count = sizes
        self.slot = slot
        lengths, place, self.mods, self.trig, self.gain, self.ebias, self.rbias = refs
        self.section = place[0]
        self.core = place[1]
        self.single = lengths[slot, 0] == self.span
        self.pairs = self.width // 128
        self.seg = self.span // SEGS
        self.step = self.width
        self.tiles = self.hidden // self.step
        place = lax.broadcasted_iota(jnp.int32, (self.span, 128), 1)
        self.low_half = place % HEAD < HEAD // 2
        self.low_head = place < HEAD
        row = lax.broadcasted_iota(jnp.int32, (1, 128), 1) // HEAD
        self.head_row = [(row == i).astype(F32).astype(BF16) for i in range(2)]
        self.blocks = [(b, slice(b * self.seg, (b + 1) * self.seg)) for b in range(SEGS)]

    def trig_pair(self):
        cos_all, sin_all = self.trig[0], self.trig[1]
        cos_cut = jnp.concatenate([cos_all[: self.seg]] * SEGS, axis=0)
        sin_cut = jnp.concatenate([sin_all[: self.seg]] * SEGS, axis=0)
        return jnp.where(self.single, cos_all, cos_cut), jnp.where(self.single, sin_all, sin_cut)

    def mod_row(self, block, part):
        row = self.slot * SEGS + jnp.where(self.single, 0, block)
        return self.mods[pl.ds(row, 1), part * self.width : (part + 1) * self.width]

    def add_segment(self, small, block, at, sums):
        row = 2 + jnp.where(self.single, 0, block)
        small[pl.ds(row, 1), at * self.width : (at + 1) * self.width] += sums

    def side(self, block):
        return self.core if block % 2 == 0 else 1 - self.core

    def put_left(self, left, base, values):
        turned = values.T
        if left.shape[0] == 1:
            left[0, 2 * base : 2 * base + self.width] = turned
            return
        lines = self.width // self.count
        for block in range(self.count):
            to = base + block // 2 * lines
            left[self.side(block), to : to + lines] = turned[block * lines : (block + 1) * lines]

    def put_active(self, left, j, values):
        turned = values.T
        if left.shape[0] == 1:
            left[0, lanes(j, self.step)] = turned
            return
        lines = self.hidden // self.count
        per = self.step // lines
        for n in range(per):
            to = lanes(j, lines * (per // 2), n // 2 * lines)
            to = slice(to.start, to.start + lines) if isinstance(j, int) else pl.ds(to.start, lines)
            left[self.side(n), to] = turned[n * lines : (n + 1) * lines]

    def thirds(self, index):
        return [lanes(index, 128, p * self.width) for p in range(3)]


def left_bases(width, hidden):
    return 0, hidden // 2, (hidden + width) // 2, (hidden + 2 * width) // 2


def forward(
    k, xv, win, wout, wex, wre, left, qkv, probs, middle, slope, branch, result, bias, normed,
    mixed, modded,
):
    span, width, held = k.span, k.width, k.held
    _, at_modded, at_mixed, at_normed = left_bases(width, k.hidden)
    held.begin(xv, win)
    held.need(xv)
    unit, _ = norm_parts(xv[...].astype(F32))
    normed[...] = (unit * k.gain[...].astype(F32)).astype(BF16)
    across = lax.broadcasted_iota(jnp.int32, (span, span), 0) // k.seg
    down = lax.broadcasted_iota(jnp.int32, (span, span), 1) // k.seg
    bias[...] = jnp.where((across == down) | k.single, 0.0, -1e30)
    held.need(win)
    held.begin(wout, wex, wre)
    cos_part, sin_part = k.trig_pair()
    for tile, factor in ((0, 0.125), (1, 1.0)):
        for i in range(width // 256):
            at = lanes(i, 256, tile * width)
            joint = dot(normed[...], win[:, at])
            outs = []
            for piece in (joint[:, :128], joint[:, 128:]):
                turned = piece * cos_part + swap_halves(piece, k.low_half) * sin_part
                outs.append((turned * factor).astype(BF16))
            qkv[:, at] = jnp.concatenate(outs, axis=1)
    qkv[:, 2 * width :] = dot(normed[...], win[:, 2 * width :]).astype(BF16)
    held.done(qkv)
    if k.kept:
        k.put_left(left, at_normed, normed[...])

    def heads(i):
        at = k.thirds(i)
        query, key, value = (qkv[:, a] for a in at)
        outs = []
        for h in range(2):
            scores = dot(key * k.head_row[h], query, 1, 1) + bias[...]
            top = jnp.max(scores, axis=0, keepdims=True)
            raised = jnp.exp(scores - top)
            total = jnp.sum(raised, axis=0, keepdims=True)
            prob = raised * (1.0 / total)
            if k.kept:
                probs[2 * i + h] = prob
            outs.append(dot(prob.astype(BF16), value, 0, 0))
        mixed[:, at[0]] = jnp.where(k.low_head, outs[0], outs[1]).astype(BF16)

    steps_of(k.pairs, k.heads_step, heads)
    held.done(probs)
    held.need(wout)
    middle[...] = xv[...].astype(F32) + dot(mixed[...], wout[...])
    held.done(middle)
    if k.kept:
        k.put_left(left, at_mixed, mixed[...])
    for b, rows in k.blocks:
        unit, _ = norm_parts(middle[rows])
        modded[rows] = (unit * (1.0 + k.mod_row(b, 0)) + k.mod_row(b, 1)).astype(BF16)
    if k.kept:
        k.put_left(left, at_modded, modded[...])
    held.need(wex, wre)
    branch[...] = jnp.broadcast_to(k.rbias[...].astype(F32), (span, width))

    def feed(j):
        at = lanes(j, k.step)
        pre = dot(modded[...], wex[:, at]) + k.ebias[:, at].astype(F32)
        area = 0.5 + 0.5 * lax.erf(pre * ROOT_HALF)
        out = (pre * area).astype(BF16)
        if k.kept:
            slope[:, at] = area + pre * (jnp.exp(pre * pre * -0.5) * ROOT_TAU)
            k.put_active(left, j, out)
        branch[...] += dot(out, wre[at, :])

    if k.heads_step == 1:
        steps_of(k.tiles, 1, feed)
    else:
        repeat(k.tiles, feed)
    held.done(slope, left, branch)
    for b, rows in k.blocks:
        result[rows] = (middle[rows] + k.mod_row(b, 2) * branch[rows]).astype(BF16)
    held.done(result)


def output(k, dyv, bg):
    k.held.need(dyv)
    for b, rows in k.blocks:
        bg[rows] = (dyv[rows].astype(F32) * k.mod_row(b, 2)).astype(BF16)
    k.held.done(bg)


def mlp(k, wre, wex, bg, slope, middle, branch, dyv, pa, middle_grad, small, acc):
    span, width, hidden, held = k.span, k.width, k.hidden, k.held
    small[...] = jnp.zeros(small.shape, F32)
    acc[...] = jnp.zeros(acc.shape, F32)
    held.begin(bg)
    for j in range(k.tiles):
        held.begin(wre, slope, wex, part=j)
    held.begin(middle, dyv, branch)
    held.need(bg)

    def feed(j):
        at = lanes(j, k.step)
        held.need(wre, slope, wex, part=j)
        grad = dot(bg[...], wre[at, :], 1, 1)
        pre_grad = (slope[:, at] * grad).astype(BF16)
        pa[:span, at] = pre_grad
        small[0:1, at] = jnp.sum(pre_grad.astype(F32), axis=0, keepdims=True)
        acc[...] += dot(pre_grad, wex[:, at], 1, 1)

    repeat(k.tiles, feed)
    held.need(middle, dyv, branch)
    total = jnp.zeros((1, width), F32)
    for b, rows in k.blocks:
        cotan = dyv[rows].astype(F32)
        total += jnp.sum(bg[rows].astype(F32), axis=0, keepdims=True)
        grad = acc[rows]
        unit, factor = norm_parts(middle[rows])
        k.add_segment(small, b, 0, jnp.sum(grad * unit, axis=0, keepdims=True))
        k.add_segment(small, b, 1, jnp.sum(grad, axis=0, keepdims=True))
        k.add_segment(small, b, 2, jnp.sum(cotan * branch[rows], axis=0, keepdims=True))
        back = norm_back(grad * (1.0 + k.mod_row(b, 0)), unit, factor)
        full = cotan + back
        middle_grad[rows] = full
        pa[rows, hidden:] = full.astype(BF16)
    small[1:2, :width] = total
    pa[span:, :] = small[...].astype(BF16)
    held.done(pa, middle_grad)


def attend(
    k, wout, win, agrad, probs, qkv, xv, middle_grad, jg, leave, mixed_grad, acc
):
    span, held = k.span, k.held
    held.need(agrad, wout)
    held.begin(probs, qkv)
    mixed_grad[...] = dot(agrad[...], wout[...], 1, 1).astype(BF16)
    held.need(probs, qkv)
    held.begin(win, xv, middle_grad)
    cos_part, sin_part = k.trig_pair()

    def heads(i):
        at = k.thirds(i)
        query, key, value = (qkv[:, a] for a in at)
        out_grad = mixed_grad[:, at[0]]
        parts = []
        for h in range(2):
            prob = probs[2 * i + h]
            pull = dot(value * k.head_row[h], out_grad, 1, 1)
            shared = jnp.sum(prob * pull, axis=0, keepdims=True)
            score_grad = (prob * (pull - shared)).astype(BF16)
            parts.append(
                (
                    dot(score_grad, key, 0, 0),
                    dot(score_grad, query),
                    dot(prob.astype(BF16), out_grad),
                )
            )
        for p in range(3):
            grad = jnp.where(k.low_head, parts[0][p], parts[1][p])
            if p < 2:
                grad = grad * cos_part - swap_halves(grad, k.low_half) * sin_part
                if p == 0:
                    grad = grad * 0.125
            jg[:span, at[p]] = grad.astype(BF16)

    steps_of(k.pairs, k.heads_step, heads)
    held.need(win, xv, middle_grad)
    acc[...] = dot(jg[:span, :], win[...], 1, 1)
    total = jnp.zeros((1, k.width), F32)
    for b, rows in k.blocks:
        grad = acc[rows]
        unit, factor = norm_parts(xv[rows].astype(F32))
        total += jnp.sum(grad * unit, axis=0, keepdims=True)
        back = norm_back(grad * k.gain[...].astype(F32), unit, factor)
        leave[rows] = (middle_grad[rows] + back).astype(BF16)
    below = jnp.concatenate([total, jnp.zeros((EXTRA - 1, k.width), F32)], axis=0)
    jg[span:, : k.width] = below.astype(BF16)
    jg[span:, k.width :] = jnp.zeros((EXTRA, 2 * k.width), BF16)
    held.done(jg, leave)


def copy_agrad(k, pa, agrad):
    agrad[...] = pa[: k.span, k.hidden :]


class Sums:
    def __init__(self, ranks, full, outs, sems):
        self.full = full
        self.own = [((ranks[0] >> bit) & 1) == 0 for bit in (1, 2)]
        self.bufs = outs[:4]
        self.targets = outs[4:]
        self.sems = sems
        self.half = full.shape[1] // 2
        self.copies = []

    def put(self, block, at, values):
        self.full[block, at] = values

    def settle(self, which, groups):
        send, keep = self.bufs[2 * which : 2 * which + 2]
        at = slice(which * self.half, (which + 1) * self.half)
        apart = 1 + which
        for group in groups:
            for n in range(2):
                first = 4 * group + (2 * n if which == 0 else n)
                even, odd = self.full[first, at], self.full[first + apart, at]
                send[2 * group + n] = jnp.where(self.own[which], odd, even).astype(BF16)
                keep[2 * group + n] = jnp.where(self.own[which], even, odd).astype(BF16)
            spot = pl.ds(2 * group, 2)
            for n in range(2 * which, 2 * which + 2):
                copy = pltpu.make_async_copy(
                    self.bufs[n].at[spot], self.targets[n].at[spot], self.sems.at[len(self.copies)]
                )
                copy.start()
                self.copies.append(copy)

    def finish(self):
        for copy in self.copies:
            copy.wait()


def term_reduce(k, sums, left, right):
    lines = k.hidden // k.count
    per = TILE // lines
    for tile in range(k.hidden // 2 // TILE):
        k.arrive(tile)
        total = dot(left[tile * TILE : (tile + 1) * TILE], right[...])
        for n in range(per):
            sums.put(tile * per + n, slice(0, lines), total[n * lines : (n + 1) * lines])
        if (tile + 1) * per % 4 == 0:
            group = ((tile + 1) * per // 4 - 1,)
            sums.settle(0, group)
            sums.settle(1, group)


def square_terms(k, sums, left, right, cols, part):
    lines = k.width // k.count
    total = dot(left, right[: 4 * k.span, cols])
    for n in range(k.count // 2):
        sums.put(n, slice(part * lines, (part + 1) * lines), total[n * lines : (n + 1) * lines])


def term_expand(k, sums, left, right):
    width, hidden, span = k.width, k.hidden, k.span
    groups = range(k.count // 8)
    tall = hidden // width
    lines = width // k.count
    rows = width // 2
    half = sums.half
    settled = False
    for col in range(tall + 1):
        k.arrive(col)
        part = left[:rows] if col < tall else left[rows:]
        square_terms(k, sums, part, right, slice(col * width, (col + 1) * width), col)
        if (col + 1) * lines >= half and not settled:
            sums.settle(0, groups)
            settled = True
    smalls = [k.small[n].astype(F32) for n in range(4)]
    angles = jnp.concatenate([embed[...] for embed in k.embeds], axis=1)
    pieces = []
    for _ in range(3):
        pieces.append(angles.astype(BF16))
        angles = angles - pieces[-1].astype(F32)
    seqs = jnp.concatenate([small[2 : 2 + SEGS, : 3 * width] for small in smalls]).astype(BF16)
    times = sum(dot(piece, seqs) for piece in pieces)
    both = sum(smalls)
    seq_sum = jnp.sum(both[2 : 2 + SEGS, : 3 * width], axis=0, keepdims=True)
    lines_v = k.lines
    lines_v[...] = jnp.zeros(lines_v.shape, F32)
    lines_v[0:1] = both[1:2, :width]
    for n in range(3):
        lines_v[1 + n : 2 + n] = seq_sum[:, n * width : (n + 1) * width]
    for n in range(tall):
        lines_v[4 + n : 5 + n] = both[0:1, n * width : (n + 1) * width]
    deep = EMB // k.count
    first = (tall + 1) * lines
    low = k.core == 0
    for g in range(k.count // 2):
        for p in range(3):
            at = slice(p * width, (p + 1) * width)
            even = times[2 * g * deep : (2 * g + 1) * deep, at]
            odd = times[(2 * g + 1) * deep : (2 * g + 2) * deep, at]
            to = first + p * deep
            sums.put(g, slice(to, to + deep), jnp.where(low, even, odd))
        sums.put(g, slice(first + 3 * deep, 2 * half), lines_v[...])
    sums.settle(1, groups)


def term_attend(k, sums, left, right):
    width = k.width
    groups = range(k.count // 8)
    lines = width // k.count
    settled = False
    for col in range(3):
        k.arrive(col)
        square_terms(k, sums, left[...], right, slice(col * width, (col + 1) * width), col)
        if (col + 1) * lines >= sums.half and not settled:
            sums.settle(0, groups)
            settled = True
    gain = sum(k.small[n].astype(F32) for n in range(4))[:, :width]
    for g in range(k.count // 2):
        sums.put(g, slice(3 * lines, 3 * lines + GAIN_ROWS), gain)
    sums.settle(1, groups)


def load_terms(k, refs, bufs, base, sems):
    left_v, right_v, small_v = bufs
    rows, cols = left_v.shape[0], right_v.shape[1]
    tall = rows // TILE if small_v is None else 1
    wide = cols // k.width
    groups = []
    for i in range(tall):
        for j in range(wide):
            copies = []
            for n, (left, right) in enumerate(zip(refs[:4], refs[4:8])):
                tokens = pl.ds(n * k.span, k.span)
                part = pl.ds(i * (rows // tall), rows // tall)
                from_part = pl.ds(base + i * (rows // tall), rows // tall)
                at = pl.ds(j * k.width, k.width)
                if j == 0:
                    copies.append((left.at[from_part], left_v.at[part, tokens]))
                if i == 0:
                    copies.append((right.at[pl.ds(0, k.span), at], right_v.at[tokens, at]))
                if small_v is not None and j == wide - 1:
                    copies.append((right.at[pl.ds(k.span, EXTRA)], small_v.at[n]))
            groups.append(copies)
    made, count = [], 0
    for copies in groups:
        made.append([])
        for pair in copies:
            made[-1].append(pltpu.make_async_copy(*pair, sems.at[count]))
            made[-1][-1].start()
            count += 1
    return made


class Terms:
    def __init__(self, sizes, core):
        self.span, self.width, self.hidden, self.count = sizes
        self.core = core[0]

    def arrive(self, group):
        for copy in self.groups[group]:
            copy.wait()


def term_kernel(sizes, body, base, extra, *refs):
    refs = list(refs)
    core, rank = refs[:2]
    k = Terms(sizes, core)
    pos = 2
    if body is term_expand:
        k.embeds = refs[pos : pos + 2]
        pos += 2
    sources = refs[pos : pos + 8]
    pos += 8 + extra
    targets = refs[pos : pos + 4]
    pos += 4
    left_v, right_v, full, *outs = refs[pos : pos + 7]
    pos += 7
    k.small = None
    if body is not term_reduce:
        k.small, k.lines = refs[pos : pos + 2]
        pos += 2
    sems, out_sems = refs[pos:]
    k.groups = load_terms(k, sources, (left_v, right_v, k.small), base, sems)
    sums = Sums(rank, full, outs + targets, out_sems)
    body(k, sums, left_v, right_v)
    sums.finish()


def term_call(name, body, sizes, lines, base, rows, core, rank, lefts, rights, embeds=(), after=()):
    span, width, hidden, count = sizes
    blocks = count // 2
    cols = rights[0].shape[1]
    half = lines // 2
    outs = [((blocks // 2, half, width), BF16)] * 4
    scratch = [
        ((rows, 4 * span), BF16),
        ((4 * span, cols), BF16),
        ((blocks, lines, width), F32),
        *outs,
    ]
    if body is not term_reduce:
        scratch += [((4, EXTRA, cols), BF16), ((TAIL_ROWS, width), F32)]
    args = [core.reshape(1), rank.reshape(1), *embeds, *lefts, *rights, *after]
    in_specs = [pl.BlockSpec(memory_space=SMEM)] * 2
    in_specs += [pl.BlockSpec(memory_space=VMEM)] * len(embeds)
    in_specs += [pl.BlockSpec(memory_space=ANY)] * (8 + len(after))
    return pl.pallas_call(
        partial(term_kernel, sizes, body, base, len(after)),
        out_shape=[jax.ShapeDtypeStruct(*item) for item in outs],
        in_specs=in_specs,
        out_specs=[pl.BlockSpec(memory_space=ANY)] * 4,
        scratch_shapes=[pltpu.VMEM(*item) for item in scratch]
        + [pltpu.SemaphoreType.DMA((32,)), pltpu.SemaphoreType.DMA((8,))],
        compiler_params=pltpu.CompilerParams(vmem_limit_bytes=62 * 1024 * 1024),
        name=name,
    )(*args)


def plain_pieces(lefts, rights, embed, sizes):
    span, width, hidden, count = sizes
    bg, pa, jg = rights
    bases = [2 * base for base in left_bases(width, hidden)]

    def blocks(base, rows, right):
        total = sum(dot(a[base : base + rows], b) for a, b in zip(lefts, right))
        parts = [total[:, i : i + width] for i in range(0, total.shape[1], width)]
        return [part.reshape(count, -1, width) for part in parts]

    take = lambda items, cols: [item[:span, cols] for item in items]
    reduce = blocks(bases[0], hidden, bg)
    expand = blocks(bases[1], width, take(pa, slice(0, hidden)))
    expand += blocks(bases[2], width, take(pa, slice(hidden, hidden + width)))
    last = blocks(bases[3], width, take(jg, slice(None)))
    small = [item[span:].astype(F32) for item in pa]
    seqs = jnp.concatenate([item[2 : 2 + SEGS, : 3 * width] for item in small])
    times = jnp.dot(embed, seqs, precision=lax.Precision.HIGHEST)
    expand += [times[:, i * width : (i + 1) * width].reshape(count, -1, width) for i in range(3)]
    lines = jnp.concatenate(
        [
            sum(item[1:2, :width] for item in small),
            jnp.sum(seqs, axis=0).reshape(-1, width),
            sum(item[0, :hidden] for item in small).reshape(-1, width),
        ]
    )
    lines = jnp.pad(lines, ((0, TAIL_ROWS - lines.shape[0]), (0, 0)))
    gain = sum(item[span:, :width].astype(F32) for item in jg)
    expand.append(jnp.broadcast_to(lines, (count,) + lines.shape))
    last.append(jnp.broadcast_to(gain, (count,) + gain.shape))
    return [jnp.concatenate(item, axis=1) for item in (reduce, expand, last)]


def shapes_of(span, width, hidden, cores):
    tok = lambda cols, kind=BF16: ((span, cols), kind)
    below = lambda cols: ((span + EXTRA, cols), BF16)
    return dict(
        xv=tok(width),
        dyv=tok(width),
        win=((width, 3 * width), BF16),
        wout=((width, width), BF16),
        wex=((width, hidden), BF16),
        wre=((hidden, width), BF16),
        left=((cores, (hidden + 3 * width) // cores, span), BF16),
        normed=tok(width),
        qkv=tok(3 * width),
        probs=((HEADS, span, span), F32),
        mixed=tok(width),
        middle=tok(width, F32),
        modded=tok(width),
        slope=tok(hidden, F32),
        branch=tok(width, F32),
        result=tok(width),
        bg=tok(width),
        pa=below(hidden + width),
        jg=below(3 * width),
        agrad=tok(width),
        mixed_grad=tok(width),
        middle_grad=tok(width, F32),
        leave=tok(width),
        acc=tok(width, F32),
        bias=tok(span, F32),
        small=((EXTRA, hidden + width), F32),
    )


def uses(part):
    return list(inspect.signature(part).parameters)[1:]


def stage_kernel(sizes, parts, who, slot, plan, *refs):
    refs = list(refs)
    layer = Layer(sizes, slot, refs[:7])
    span = layer.span
    pos = 7
    loads = {}
    for name, row, cols in plan.sources:
        ref = refs[pos]
        if cols is not None:
            ref = ref.at[pl.ds(0, span), pl.ds(*cols)]
        elif row is not None:
            ref = ref.at[pl.ds(row, span)]
        loads[name] = ref
        pos += 1
    pos += plan.extra
    stores = {}
    for name, row, at in plan.targets:
        target = refs[pos] if row is None else refs[pos].at[pl.ds(row, span)]
        stores.setdefault(name, []).append((at, target))
        pos += 1
    bufs = {}
    for name in plan.bufs:
        bufs[name] = refs[pos]
        pos += 1
    layer.held = Held(bufs, loads, stores, refs[pos], plan.pieces)
    layer.kept = plan.kept
    layer.heads_step = plan.heads_step

    @pl.when(layer.section == who)
    def _():
        for part in parts:
            part(layer, *[bufs[name] for name in uses(part)])
        layer.held.finish()


def stage(
    name, common, parts, who, slot, loads, stores, carried=None, after=(), kept=True, heads_step=3,
    pieces=None,
):
    carried = carried or {}
    span, width, hidden, count = common.sizes
    shapes = shapes_of(span, width, hidden, common.cores)
    bufs = []
    for part in parts:
        bufs += [item for item in uses(part) if item not in bufs]
    pair = lambda item: item if isinstance(item, tuple) else (item, None)
    args = list(common.args)
    in_specs = [pl.BlockSpec(memory_space=SMEM)] * 2 + [pl.BlockSpec(memory_space=VMEM)] * 5
    plan = Bag(sources=[], targets=[], bufs=bufs, kept=kept, heads_step=heads_step)
    plan["pieces"] = pieces or {}
    for item in loads:
        if item in bufs:
            array, row, *cols = pair(loads[item])
            args.append(array)
            plan.sources.append((item, row, cols[0] if cols else None))
    outs, aliases, extra = [], {}, []
    targets = []
    for item, key in stores.items():
        if item == "left":
            targets += [(item, key + "_send" * n, None, n) for n in range(common.cores)]
        else:
            targets.append((item, *pair(key), None))
    for i, (item, key, row, at) in enumerate(targets):
        shape, kind = shapes[item]
        if row is not None:
            shape = (common.tokens,) + shape[1:]
        if at is not None:
            shape = shape[1:]
        outs.append(jax.ShapeDtypeStruct(shape, kind))
        plan.targets.append((item, row, at))
        if key in carried:
            aliases[len(args) + len(extra)] = i
            extra.append(carried[key])
    extra += list(after)
    args += extra
    plan["extra"] = len(extra)
    in_specs += [pl.BlockSpec(memory_space=ANY)] * (len(args) - len(in_specs))
    results = pl.pallas_call(
        partial(stage_kernel, common.sizes, parts, who, slot, plan),
        out_shape=outs,
        in_specs=in_specs,
        out_specs=[pl.BlockSpec(memory_space=ANY)] * len(outs),
        input_output_aliases=aliases,
        scratch_shapes=[pltpu.VMEM(*shapes[item]) for item in bufs]
        + [pltpu.SemaphoreType.DMA((32,))],
        compiler_params=pltpu.CompilerParams(vmem_limit_bytes=62 * 1024 * 1024),
        name=name,
    )(*args)
    return Bag({key: value for (_, key, _, _), value in zip(targets, results)})


def bits_of(count):
    bits = count.bit_length() - 1
    assert 1 << bits == count
    return bits


class Chunk:
    def __init__(self, axis, bits, size, settled=()):
        self.axis = axis
        self.bits = list(range(bits - 1, 0, -1))
        self.size = size
        self.settled = list(settled)
        self.terms = []

    def add(self, term, start=0):
        left = [bit for bit in self.bits if bit not in self.settled]
        self.terms.append((term.reshape((2,) * len(left) + term.shape[-2:]), left, start))

    def take(self, term, start, left, flip):
        me = lax.axis_index(self.axis)
        side = lambda bit: 1 - ((me >> bit) & 1) if bit == flip else (me >> bit) & 1
        starts = [side(bit) if bit in self.settled else 0 for bit in left]
        sizes = [1 if bit in self.settled else 2 for bit in left]
        cols = term.shape[-1]
        piece = lax.dynamic_slice(term, starts + [start, 0], sizes + [self.size, cols])
        open_bits = [2] * (len(self.bits) - len(self.settled))
        return piece.reshape(open_bits + [self.size, cols]).astype(F32)

    def split(self, bit):
        self.settled.append(bit)
        return sum(self.take(term, start, left, bit) for term, left, start in self.terms).astype(
            BF16
        )

    def total(self):
        return sum(self.take(term, start, left, None) for term, left, start in self.terms)


def exchange(block, axis, bit):
    count = lax.axis_size(axis)
    return lax.ppermute(block, axis, [(i, i ^ (1 << bit)) for i in range(count)])


def join(*items):
    return lax.optimization_barrier(items)


def angle_table(span):
    half = HEAD // 2
    freqs = np.exp(-math.log(10000.0) * np.arange(half, dtype=np.float32) / half)
    phase = np.arange(span, dtype=np.float32)[:, None] * freqs.astype(np.float32)[None, :]
    cos_part, sin_part = np.cos(phase), np.sin(phase)
    return np.stack(
        [
            np.concatenate([cos_part] * 4, axis=1),
            np.concatenate([-sin_part, sin_part] * 2, axis=1),
        ]
    ).astype(np.float32)


def per_device(
    ends_in,
    lengths,
    times,
    norm_gain,
    attend_in,
    attend_out,
    time_weight,
    time_bias,
    expand_weight,
    expand_bias,
    reduce_weight,
    reduce_bias,
):
    local = ends_in[0]
    micro = lengths.shape[1]
    assert micro == 2
    width = local.shape[1]
    span = local.shape[0] // micro
    hidden = expand_weight.shape[2]
    count = lax.axis_size("rep")
    section = lax.axis_index("section")
    rank = lax.axis_index("rep")
    core = rank & 1
    steps = jnp.exp(-math.log(10000.0) * jnp.arange(EMB // 2, dtype=F32) / (EMB // 2))
    turn = times.reshape(micro * SEGS, 1).astype(F32) * steps
    embed = jnp.concatenate([jnp.cos(turn), jnp.sin(turn)], axis=1)
    mods = jnp.dot(
        embed, time_weight[0].astype(F32), precision=lax.Precision.HIGHEST
    ) + time_bias.astype(F32)
    fused = width // count % 16 == 0 and TILE % (hidden // count) == 0 and count >= 16
    common = Bag(
        args=(
            lengths[0],
            jnp.stack([section, core]),
            mods,
            jnp.asarray(angle_table(span)),
            norm_gain,
            expand_bias,
            reduce_bias,
        ),
        sizes=(span, width, hidden, count),
        tokens=local.shape[0],
        cores=2 if fused else 1,
    )
    weights = Bag(
        win=attend_in[0], wout=attend_out[0], wex=expand_weight[0], wre=reduce_weight[0]
    )
    rows = [(local, slot * span) for slot in range(micro)]
    same = lambda *names: {name: name for name in names}
    whole = same("left", "bg", "pa", "jg")
    run = partial(stage, common=common)
    both = (forward, output, mlp, copy_agrad, attend)
    over = lambda block, route: lax.ppermute(block, "section", route)
    swap = lambda block, bit: exchange(block, "rep", bit)
    a = run(
        "first_0",
        parts=(forward,),
        who=0,
        slot=0,
        loads=dict(xv=rows[0], **weights),
        stores=dict(result="leave"),
        kept=False,
    )
    came_0 = over(a.leave, [(0, 1)])
    after = (a.leave,)
    if fused:
        embeds = (embed.T, swap(embed.T, 0))
        after += (embeds[1],)
    b = run(
        "first_1",
        parts=(forward,),
        who=0,
        slot=1,
        loads=dict(xv=rows[1], **weights),
        stores=same("result", "left", "qkv", "probs", "middle", "slope", "branch"),
        after=after,
        heads_step=1,
    )
    came_1 = over(b.result, [(0, 1)])
    x = run(
        "second_0",
        parts=both,
        who=1,
        slot=0,
        loads=dict(xv=came_0, dyv=rows[0], **weights),
        stores=dict(whole, result=("ends", 0), leave="leave"),
        after=(b.result,),
    )
    back_0 = over(x.leave, [(1, 0)])
    y = run(
        "second_1",
        parts=both,
        who=1,
        slot=1,
        loads=dict(xv=came_1, dyv=rows[1], **weights),
        stores=dict(whole, result=("ends", span), leave="leave"),
        carried=dict(b, ends=x.ends),
        after=(x.leave,),
    )
    back_1 = over(y.leave, [(1, 0)])
    gates = mods[SEGS : 2 * SEGS, 2 * width :]
    gates = jnp.where(lengths[0, 1, 0] == span, gates[:1], gates)
    x = run(
        "back_0",
        parts=both,
        who=0,
        slot=0,
        loads=dict(xv=rows[0], dyv=back_0, **weights),
        stores=dict(whole, leave=("ends", 0)),
        carried=dict(x, ends=y.ends),
        after=(y.leave, gates),
    )
    if fused:
        y_left = swap(y.left_send, 0)
        back_1, x_send, x_bg = join(back_1, x.left_send, x.bg)
        lefts = [x.left, y.left, swap(x_send, 0), y_left]
        others = [swap(item, 0) for item in (x_bg, x.pa, x.jg)]
    cotan = back_1.astype(F32).reshape(SEGS, -1, width)
    made = (cotan * gates[:, None]).reshape(span, width).astype(BF16)
    bg_1 = jnp.where(section == 0, made, y.bg)
    after = ()
    if fused:
        bg_1_other = swap(bg_1, 0)
        after = (bg_1_other, others[0], lefts[2], lefts[3])
    part = run(
        "back_1_mlp",
        parts=(mlp,),
        who=0,
        slot=1,
        loads=dict(
            bg=bg_1,
            wre=weights.wre,
            slope=b.slope,
            wex=weights.wex,
            middle=b.middle,
            dyv=back_1,
            branch=b.branch,
        ),
        stores=same("pa", "middle_grad"),
        carried=y,
        after=after,
        pieces=dict(wre=(0, hidden // width), slope=(1, hidden // width), wex=(1, hidden // width)),
    )
    pa_1 = part.pa
    bits = bits_of(count)
    term = partial(term_call, sizes=common.sizes, core=core, rank=rank)
    lines = width // count
    deep = EMB // count
    sizes = (hidden // count, hidden // count + lines + 3 * deep + TAIL_ROWS, 3 * lines + GAIN_ROWS)
    bases = left_bases(width, hidden)

    def last_attend(after):
        return run(
            "back_1_attend",
            parts=(attend,),
            who=0,
            slot=1,
            loads=dict(
                agrad=(pa_1, None, (hidden, width)),
                wout=weights.wout,
                probs=b.probs,
                qkv=b.qkv,
                win=weights.win,
                xv=rows[1],
                middle_grad=part.middle_grad,
            ),
            stores=dict(jg="jg", leave=("ends", span)),
            carried=dict(y, ends=x.ends),
            after=after,
        )

    def pair_of(size, first):
        cut = size // 2 if fused else size // 32 * 16
        one = Chunk("rep", bits, cut, (1,) if fused else ())
        two = Chunk("rep", bits, size - cut, (2,) if fused else ())
        if fused:
            send_1, keep_1, send_2, keep_2 = first
            one.add(keep_1)
            two.add(keep_2)
            return one, two, send_1, send_2
        view = first.reshape((count // 2, 2) + first.shape[1:])
        cut = lambda at: lax.dynamic_index_in_dim(view, at, 1, keepdims=False)
        came = swap(cut(1 - core).astype(BF16), 0)
        for item in (cut(core), came):
            one.add(item)
            two.add(item, one.size)
        return one, two, one.split(1), two.split(2)

    if fused:
        pa_other = swap(pa_1, 0)
        sent = term(
            "term_reduce",
            term_reduce,
            lines=sizes[0],
            base=bases[0],
            rows=hidden // 2,
            lefts=lefts,
            rights=[x.bg, bg_1, others[0], bg_1_other],
            after=(pa_1,),
        )
        r1, r2, send_1, send_2 = pair_of(sizes[0], sent)
        came_r1, came_r2 = swap(send_1, 1), swap(send_2, 2)
        sent = term(
            "term_expand",
            term_expand,
            lines=sizes[1],
            base=bases[1],
            rows=width,
            lefts=lefts,
            rights=[x.pa, pa_1, others[1], pa_other],
            embeds=embeds,
            after=(send_1, send_2),
        )
        came_r1, came_r2, *sent = join(came_r1, came_r2, *sent)
        e1, e2, send_1, send_2 = pair_of(sizes[1], sent)
        came_e1, came_e2 = swap(send_1, 1), swap(send_2, 2)
        last = last_attend((send_1, send_2))
        jg_1 = last.jg
        jg_other = swap(jg_1, 0)
        came_r1, came_r2, _ = join(came_r1, came_r2, jg_1)
        r1.add(came_r1)
        r2.add(came_r2)
        send_3, send_4 = r1.split(2), r2.split(1)
        came_r1, came_r2 = swap(send_3, 2), swap(send_4, 1)
        came_e1, came_e2, _, _ = join(came_e1, came_e2, send_3, send_4)
        e1.add(came_e1)
        e2.add(came_e2)
        send_1, send_2 = e1.split(2), e2.split(1)
        came_e1, came_e2 = swap(send_1, 2), swap(send_2, 1)
        sent = term(
            "term_attend",
            term_attend,
            lines=sizes[2],
            base=bases[3],
            rows=width // 2,
            lefts=lefts,
            rights=[x.jg, jg_1, others[2], jg_other],
            after=(send_1, send_2, send_3, send_4),
        )
        came_r1, came_r2, *sent = join(came_r1, came_r2, *sent)
        a1, a2, send_1, send_2 = pair_of(sizes[2], sent)
    else:
        last = last_attend(())
        rights = [(x.bg, bg_1), (x.pa, pa_1), (x.jg, last.jg)]
        totals = plain_pieces((x.left, y.left), rights, embed.T, common.sizes)
        r1, r2, send_1, send_2 = pair_of(sizes[0], totals[0])
        r1.add(swap(send_1, 1))
        r2.add(swap(send_2, 2))
        came_r1, came_r2 = swap(r1.split(2), 2), swap(r2.split(1), 1)
        e1, e2, send_1, send_2 = pair_of(sizes[1], totals[1])
        e1.add(swap(send_1, 1))
        e2.add(swap(send_2, 2))
        came_e1, came_e2 = swap(e1.split(2), 2), swap(e2.split(1), 1)
        a1, a2, send_1, send_2 = pair_of(sizes[2], totals[2])
    ends = last.ends
    came_a1, came_a2 = swap(send_1, 1), swap(send_2, 2)
    r1.add(came_r1)
    r2.add(came_r2)
    block_r = jnp.concatenate([r1.split(3), r2.split(3)], axis=-2)
    came_r = swap(block_r, 3)
    came_e1, came_e2, _ = join(came_e1, came_e2, block_r)
    e1.add(came_e1)
    e2.add(came_e2)
    block_e = jnp.concatenate([e1.split(3), e2.split(3)], axis=-2)
    came_e = swap(block_e, 3)
    came_a1, came_a2, _ = join(came_a1, came_a2, block_e)
    a1.add(came_a1)
    a2.add(came_a2)
    send_1, send_2 = a1.split(2), a2.split(1)
    came_a1, came_a2 = swap(send_1, 2), swap(send_2, 1)
    a1.add(came_a1)
    a2.add(came_a2)
    block_a = jnp.concatenate([a1.split(3), a2.split(3)], axis=-2)
    came_a = swap(block_a, 3)
    came_r, _ = join(came_r, send_1)
    r1.add(came_r[..., : r1.size, :])
    r2.add(came_r[..., r1.size :, :])
    came_e, _ = join(came_e, block_a)
    e1.add(came_e[..., : e1.size, :])
    e2.add(came_e[..., e1.size :, :])
    a1.add(came_a[..., : a1.size, :])
    a2.add(came_a[..., a1.size :, :])
    for bit in range(4, bits):
        for chunk in (r1, r2, e1, e2, a1, a2):
            chunk.add(swap(chunk.split(bit), bit))
    share_r, share_e, share_a = (
        jnp.concatenate([one.total(), two.total()]) for one, two in ((r1, r2), (e1, e2), (a1, a2))
    )
    tall = hidden // width
    side = lambda item, n, size: jnp.concatenate(
        [item[i * size : (i + 1) * size] for i in range(n)], axis=1
    )
    at_o = tall * lines
    at_t = at_o + lines
    small = share_e[at_t + 3 * deep :]
    flat = lambda item, first, n: lax.dynamic_slice_in_dim(
        item[first : first + n].reshape(-1), rank * (n * width // count), n * width // count
    )
    results = (
        flat(share_a, 3 * lines, 1),
        side(share_a, 3, lines),
        share_e[at_o:at_t],
        side(share_e[at_t:], 3, deep),
        flat(small, 1, 3),
        side(share_e, tall, lines),
        flat(small, 4, tall),
        share_r,
        flat(small, 0, 1),
    )
    return (ends[None],) + tuple(piece[None] for piece in results)


def solution(mesh):
    return jax.shard_map(
        per_device,
        mesh=mesh,
        in_specs=(
            P("section", "rep", None),
            P("rep", None, None),
            P("rep", None, None),
            P("section", None),
            P("section", None, None),
            P("section", None, None),
            P("section", None, None),
            P("section", None),
            P("section", None, None),
            P("section", None),
            P("section", None, None),
            P("section", None),
        ),
        out_specs=(
            P("section", "rep", None),
            P("section", "rep"),
            P("section", "rep", None),
            P("section", "rep", None),
            P("section", "rep", None),
            P("section", "rep"),
            P("section", "rep", None),
            P("section", "rep"),
            P("section", "rep", None),
            P("section", "rep"),
        ),
        check_vma=False,
    )
```

```python
from functools import partial
import inspect
import math

import jax
import jax.numpy as jnp
import numpy as np
from jax import lax
from jax.experimental import pallas as pl
from jax.experimental.pallas import tpu as pltpu
from jax.sharding import PartitionSpec as P

HEADS = 12
HEAD = 64
EMB = 128
SEGS = 4
ANY = pl.ANY
VMEM = pltpu.MemorySpace.VMEM
SMEM = pltpu.MemorySpace.SMEM
F32 = jnp.float32
BF16 = jnp.bfloat16
ROOT_HALF = 0.7071067811865476
ROOT_TAU = 0.3989422804014327
TILE = 384
TAIL_ROWS = 24
GAIN_ROWS = 16
EXTRA = 16


class Bag(dict):
    __getattr__ = dict.__getitem__


def dot(left, right, left_dim=1, right_dim=0):
    return lax.dot_general(
        left, right, (((left_dim,), (right_dim,)), ((), ())), preferred_element_type=F32
    )


def repeat(count, body):
    for i in range(count):
        body(i)


def steps_of(count, size, body):
    def several(i, _):
        for j in range(size):
            body(size * i + j)
        return _

    lax.fori_loop(0, count // size, several, 0)


def lanes(index, size, start=0):
    if isinstance(index, int):
        return slice(start + index * size, start + (index + 1) * size)
    return pl.ds(pl.multiple_of(start + index * size, size), size)


def swap_halves(values, low_half):
    forth = pltpu.roll(values, 128 - HEAD // 2, 1)
    back = pltpu.roll(values, HEAD // 2, 1)
    return jnp.where(low_half, forth, back)


def norm_parts(values):
    center = values - jnp.mean(values, axis=-1, keepdims=True)
    spread = jnp.mean(center * center, axis=-1, keepdims=True)
    factor = lax.rsqrt(spread + 1e-05)
    return center * factor, factor


def norm_back(grad, unit, factor):
    return factor * (
        grad
        - jnp.mean(grad, axis=-1, keepdims=True)
        - unit * jnp.mean(grad * unit, axis=-1, keepdims=True)
    )


class Held:
    def __init__(self, bufs, loads, stores, sems, pieces):
        self.bufs = bufs
        self.loads = loads
        self.stores = stores
        self.sems = sems
        self.pieces = pieces
        self.names = {id(buf): name for name, buf in bufs.items()}
        keys = [(name, j) for name in loads for j in range(self.parts_of(name))]
        self.spots = {key: n for n, key in enumerate(keys)}
        self.waiting = set(keys)
        self.pending = set(keys)
        self.leaving = {}

    def parts_of(self, name):
        return self.pieces[name][1] if name in self.pieces else 1

    def load(self, name, j):
        source, target = self.loads[name], self.bufs[name]
        if name in self.pieces:
            axis, count = self.pieces[name]
            size = target.shape[axis] // count
            at = (slice(None),) * axis + (pl.ds(j * size, size),)
            source, target = source.at[at], target.at[at]
        return pltpu.make_async_copy(source, target, self.sems.at[self.spots[(name, j)]])

    def store(self, name, n):
        at, target = self.stores[name][n]
        source = self.bufs[name] if at is None else self.bufs[name].at[at]
        return pltpu.make_async_copy(source, target, self.sems.at[self.leaving[(name, n)]])

    def keys(self, bufs, part):
        for buf in bufs:
            name = self.names[id(buf)]
            for j in range(self.parts_of(name)):
                if part in (None, j):
                    yield name, j

    def begin(self, *bufs, part=None):
        for key in self.keys(bufs, part):
            if key in self.waiting:
                self.waiting.remove(key)
                self.load(*key).start()

    def need(self, *bufs, part=None):
        self.begin(*bufs, part=part)
        for key in self.keys(bufs, part):
            if key in self.pending:
                self.pending.remove(key)
                self.load(*key).wait()

    def done(self, *bufs):
        for buf in bufs:
            name = self.names[id(buf)]
            for n in range(len(self.stores.get(name, ()))):
                self.leaving[(name, n)] = len(self.spots) + len(self.leaving)
                self.store(name, n).start()

    def finish(self):
        for name, n in self.leaving:
            self.store(name, n).wait()


class Layer:
    def __init__(self, sizes, slot, refs):
        self.span, self.width, self.hidden, self.count = sizes
        self.slot = slot
        (
            lengths, section, core, self.mods, self.tbias, self.trig, self.gain, self.ebias,
            self.rbias,
        ) = refs
        self.section = section[0]
        self.core = core[0]
        self.single = lengths[slot, 0] == self.span
        self.pairs = self.width // 128
        self.seg = self.span // SEGS
        self.step = self.width
        self.tiles = self.hidden // self.step
        place = lax.broadcasted_iota(jnp.int32, (self.span, 128), 1)
        self.low_half = place % HEAD < HEAD // 2
        self.low_head = place < HEAD
        row = lax.broadcasted_iota(jnp.int32, (1, 128), 1) // HEAD
        self.head_row = [(row == i).astype(F32).astype(BF16) for i in range(2)]
        self.blocks = [(b, slice(b * self.seg, (b + 1) * self.seg)) for b in range(SEGS)]

    def trig_pair(self):
        cos_all, sin_all = self.trig[0], self.trig[1]
        cos_cut = jnp.concatenate([cos_all[: self.seg]] * SEGS, axis=0)
        sin_cut = jnp.concatenate([sin_all[: self.seg]] * SEGS, axis=0)
        return jnp.where(self.single, cos_all, cos_cut), jnp.where(self.single, sin_all, sin_cut)

    def mod_row(self, block, part):
        row = self.slot * SEGS + jnp.where(self.single, 0, block)
        at = slice(part * self.width, (part + 1) * self.width)
        return self.mods[pl.ds(row, 1), at] + self.tbias[:, at].astype(F32)

    def add_segment(self, small, block, at, sums):
        row = 2 + jnp.where(self.single, 0, block)
        small[pl.ds(row, 1), at * self.width : (at + 1) * self.width] += sums

    def side(self, block):
        return self.core if block % 2 == 0 else 1 - self.core

    def put_left(self, left, base, values):
        turned = values.T
        if left.shape[0] == 1:
            left[0, 2 * base : 2 * base + self.width] = turned
            return
        lines = self.width // self.count
        for block in range(self.count):
            to = base + block // 2 * lines
            left[self.side(block), to : to + lines] = turned[block * lines : (block + 1) * lines]

    def put_active(self, left, j, values):
        turned = values.T
        if left.shape[0] == 1:
            left[0, lanes(j, self.step)] = turned
            return
        lines = self.hidden // self.count
        per = self.step // lines
        for n in range(per):
            to = lanes(j, lines * (per // 2), n // 2 * lines)
            to = slice(to.start, to.start + lines) if isinstance(j, int) else pl.ds(to.start, lines)
            left[self.side(n), to] = turned[n * lines : (n + 1) * lines]

    def thirds(self, index):
        return [lanes(index, 128, p * self.width) for p in range(3)]


def left_bases(width, hidden):
    return 0, hidden // 2, (hidden + width) // 2, (hidden + 2 * width) // 2


def forward(
    k, xv, win, wout, wex, wre, left, qkv, probs, middle, slope, branch, result, bias, normed,
    mixed, modded,
):
    span, width, held = k.span, k.width, k.held
    _, at_modded, at_mixed, at_normed = left_bases(width, k.hidden)
    held.begin(xv, win)
    held.need(xv)
    unit, _ = norm_parts(xv[...].astype(F32))
    normed[...] = (unit * k.gain[...].astype(F32)).astype(BF16)
    across = lax.broadcasted_iota(jnp.int32, (span, span), 0) // k.seg
    down = lax.broadcasted_iota(jnp.int32, (span, span), 1) // k.seg
    bias[...] = jnp.where((across == down) | k.single, 0.0, -1e30)
    held.need(win)
    held.begin(wout, wex, wre)
    cos_part, sin_part = k.trig_pair()
    for tile, factor in ((0, 0.125), (1, 1.0)):
        for i in range(width // 256):
            at = lanes(i, 256, tile * width)
            joint = dot(normed[...], win[:, at])
            outs = []
            for piece in (joint[:, :128], joint[:, 128:]):
                turned = piece * cos_part + swap_halves(piece, k.low_half) * sin_part
                outs.append((turned * factor).astype(BF16))
            qkv[:, at] = jnp.concatenate(outs, axis=1)
    qkv[:, 2 * width :] = dot(normed[...], win[:, 2 * width :]).astype(BF16)
    held.done(qkv)
    if k.kept:
        k.put_left(left, at_normed, normed[...])

    def heads(i):
        at = k.thirds(i)
        query, key, value = (qkv[:, a] for a in at)
        outs = []
        for h in range(2):
            scores = dot(key * k.head_row[h], query, 1, 1) + bias[...]
            top = jnp.max(scores, axis=0, keepdims=True)
            raised = jnp.exp(scores - top)
            total = jnp.sum(raised, axis=0, keepdims=True)
            prob = raised * (1.0 / total)
            if k.kept:
                probs[2 * i + h] = prob
            outs.append(dot(prob.astype(BF16), value, 0, 0))
        mixed[:, at[0]] = jnp.where(k.low_head, outs[0], outs[1]).astype(BF16)

    steps_of(k.pairs, k.heads_step, heads)
    held.done(probs)
    held.need(wout)
    middle[...] = xv[...].astype(F32) + dot(mixed[...], wout[...])
    held.done(middle)
    if k.kept:
        k.put_left(left, at_mixed, mixed[...])
    for b, rows in k.blocks:
        unit, _ = norm_parts(middle[rows])
        modded[rows] = (unit * (1.0 + k.mod_row(b, 0)) + k.mod_row(b, 1)).astype(BF16)
    if k.kept:
        k.put_left(left, at_modded, modded[...])
    held.need(wex, wre)
    branch[...] = jnp.broadcast_to(k.rbias[...].astype(F32), (span, width))

    def feed(j):
        at = lanes(j, k.step)
        pre = dot(modded[...], wex[:, at]) + k.ebias[:, at].astype(F32)
        area = 0.5 + 0.5 * lax.erf(pre * ROOT_HALF)
        out = (pre * area).astype(BF16)
        if k.kept:
            slope[:, at] = area + pre * (jnp.exp(pre * pre * -0.5) * ROOT_TAU)
            k.put_active(left, j, out)
        branch[...] += dot(out, wre[at, :])

    if k.heads_step == 1:
        steps_of(k.tiles, 1, feed)
    else:
        repeat(k.tiles, feed)
    held.done(slope, left, branch)
    for b, rows in k.blocks:
        result[rows] = (middle[rows] + k.mod_row(b, 2) * branch[rows]).astype(BF16)
    held.done(result)


def output(k, dyv, bg):
    k.held.need(dyv)
    for b, rows in k.blocks:
        bg[rows] = (dyv[rows].astype(F32) * k.mod_row(b, 2)).astype(BF16)
    k.held.done(bg)


def mlp(k, wre, wex, bg, slope, middle, branch, dyv, pa, middle_grad, small, acc):
    span, width, hidden, held = k.span, k.width, k.hidden, k.held
    small[...] = jnp.zeros(small.shape, F32)
    acc[...] = jnp.zeros(acc.shape, F32)
    held.begin(bg)
    for j in range(k.tiles):
        held.begin(wre, slope, wex, part=j)
    held.begin(middle, dyv, branch)
    held.need(bg)

    def feed(j):
        at = lanes(j, k.step)
        held.need(wre, slope, wex, part=j)
        grad = dot(bg[...], wre[at, :], 1, 1)
        pre_grad = (slope[:, at] * grad).astype(BF16)
        pa[:span, at] = pre_grad
        small[0:1, at] = jnp.sum(pre_grad.astype(F32), axis=0, keepdims=True)
        acc[...] += dot(pre_grad, wex[:, at], 1, 1)

    repeat(k.tiles, feed)
    held.need(middle, dyv, branch)
    total = jnp.zeros((1, width), F32)
    for b, rows in k.blocks:
        cotan = dyv[rows].astype(F32)
        total += jnp.sum(bg[rows].astype(F32), axis=0, keepdims=True)
        grad = acc[rows]
        unit, factor = norm_parts(middle[rows])
        k.add_segment(small, b, 0, jnp.sum(grad * unit, axis=0, keepdims=True))
        k.add_segment(small, b, 1, jnp.sum(grad, axis=0, keepdims=True))
        k.add_segment(small, b, 2, jnp.sum(cotan * branch[rows], axis=0, keepdims=True))
        back = norm_back(grad * (1.0 + k.mod_row(b, 0)), unit, factor)
        full = cotan + back
        middle_grad[rows] = full
        pa[rows, hidden:] = full.astype(BF16)
    small[1:2, :width] = total
    pa[span:, :] = small[...].astype(BF16)
    held.done(pa, middle_grad)


def attend(
    k, wout, win, agrad, probs, qkv, xv, middle_grad, jg, leave, mixed_grad, acc
):
    span, held = k.span, k.held
    held.need(agrad, wout)
    held.begin(probs, qkv)
    mixed_grad[...] = dot(agrad[...], wout[...], 1, 1).astype(BF16)
    held.need(probs, qkv)
    held.begin(win, xv, middle_grad)
    cos_part, sin_part = k.trig_pair()

    def heads(i):
        at = k.thirds(i)
        query, key, value = (qkv[:, a] for a in at)
        out_grad = mixed_grad[:, at[0]]
        parts = []
        for h in range(2):
            prob = probs[2 * i + h]
            pull = dot(value * k.head_row[h], out_grad, 1, 1)
            shared = jnp.sum(prob * pull, axis=0, keepdims=True)
            score_grad = (prob * (pull - shared)).astype(BF16)
            parts.append(
                (
                    dot(score_grad, key, 0, 0),
                    dot(score_grad, query),
                    dot(prob.astype(BF16), out_grad),
                )
            )
        for p in range(3):
            grad = jnp.where(k.low_head, parts[0][p], parts[1][p])
            if p < 2:
                grad = grad * cos_part - swap_halves(grad, k.low_half) * sin_part
                if p == 0:
                    grad = grad * 0.125
            jg[:span, at[p]] = grad.astype(BF16)

    steps_of(k.pairs, k.heads_step, heads)
    held.need(win, xv, middle_grad)
    acc[...] = dot(jg[:span, :], win[...], 1, 1)
    total = jnp.zeros((1, k.width), F32)
    for b, rows in k.blocks:
        grad = acc[rows]
        unit, factor = norm_parts(xv[rows].astype(F32))
        total += jnp.sum(grad * unit, axis=0, keepdims=True)
        back = norm_back(grad * k.gain[...].astype(F32), unit, factor)
        leave[rows] = (middle_grad[rows] + back).astype(BF16)
    below = jnp.concatenate([total, jnp.zeros((EXTRA - 1, k.width), F32)], axis=0)
    jg[span:, : k.width] = below.astype(BF16)
    jg[span:, k.width :] = jnp.zeros((EXTRA, 2 * k.width), BF16)
    held.done(jg, leave)


def copy_agrad(k, pa, agrad):
    agrad[...] = pa[: k.span, k.hidden :]


class Sums:
    def __init__(self, ranks, full, outs, sems):
        self.full = full
        self.own = [((ranks[0] >> bit) & 1) == 0 for bit in (1, 2)]
        self.bufs = outs[:4]
        self.targets = outs[4:]
        self.sems = sems
        self.half = full.shape[1] // 2
        self.copies = []

    def put(self, block, at, values):
        self.full[block, at] = values

    def settle(self, which, groups):
        send, keep = self.bufs[2 * which : 2 * which + 2]
        at = slice(which * self.half, (which + 1) * self.half)
        apart = 1 + which
        for group in groups:
            for n in range(2):
                first = 4 * group + (2 * n if which == 0 else n)
                even, odd = self.full[first, at], self.full[first + apart, at]
                send[2 * group + n] = jnp.where(self.own[which], odd, even).astype(BF16)
                keep[2 * group + n] = jnp.where(self.own[which], even, odd)
            spot = pl.ds(2 * group, 2)
            for n in range(2 * which, 2 * which + 2):
                copy = pltpu.make_async_copy(
                    self.bufs[n].at[spot], self.targets[n].at[spot], self.sems.at[len(self.copies)]
                )
                copy.start()
                self.copies.append(copy)

    def finish(self):
        for copy in self.copies:
            copy.wait()


def term_reduce(k, sums, left, right):
    lines = k.hidden // k.count
    per = TILE // lines
    for tile in range(k.hidden // 2 // TILE):
        k.arrive(tile)
        total = dot(left[tile * TILE : (tile + 1) * TILE], right[...])
        for n in range(per):
            sums.put(tile * per + n, slice(0, lines), total[n * lines : (n + 1) * lines])
        if (tile + 1) * per % 4 == 0:
            group = ((tile + 1) * per // 4 - 1,)
            sums.settle(0, group)
            sums.settle(1, group)


def square_terms(k, sums, left, right, cols, part):
    lines = k.width // k.count
    total = dot(left, right[: 4 * k.span, cols])
    for n in range(k.count // 2):
        sums.put(n, slice(part * lines, (part + 1) * lines), total[n * lines : (n + 1) * lines])


def term_expand(k, sums, left, right):
    width, hidden, span = k.width, k.hidden, k.span
    groups = range(k.count // 8)
    tall = hidden // width
    lines = width // k.count
    rows = width // 2
    half = sums.half
    settled = False
    for col in range(tall + 1):
        k.arrive(col)
        part = left[:rows] if col < tall else left[rows:]
        square_terms(k, sums, part, right, slice(col * width, (col + 1) * width), col)
        if (col + 1) * lines >= half and not settled:
            sums.settle(0, groups)
            settled = True
    smalls = [k.small[n].astype(F32) for n in range(4)]
    angles = jnp.concatenate([embed[...] for embed in k.embeds], axis=1)
    pieces = []
    for _ in range(3):
        pieces.append(angles.astype(BF16))
        angles = angles - pieces[-1].astype(F32)
    seqs = jnp.concatenate([small[2 : 2 + SEGS, : 3 * width] for small in smalls]).astype(BF16)
    times = sum(dot(piece, seqs) for piece in pieces)
    both = sum(smalls)
    seq_sum = jnp.sum(both[2 : 2 + SEGS, : 3 * width], axis=0, keepdims=True)
    lines_v = k.lines
    lines_v[...] = jnp.zeros(lines_v.shape, F32)
    lines_v[0:1] = both[1:2, :width]
    for n in range(3):
        lines_v[1 + n : 2 + n] = seq_sum[:, n * width : (n + 1) * width]
    for n in range(tall):
        lines_v[4 + n : 5 + n] = both[0:1, n * width : (n + 1) * width]
    deep = EMB // k.count
    first = (tall + 1) * lines
    low = k.core == 0
    for g in range(k.count // 2):
        for p in range(3):
            at = slice(p * width, (p + 1) * width)
            even = times[2 * g * deep : (2 * g + 1) * deep, at]
            odd = times[(2 * g + 1) * deep : (2 * g + 2) * deep, at]
            to = first + p * deep
            sums.put(g, slice(to, to + deep), jnp.where(low, even, odd))
        sums.put(g, slice(first + 3 * deep, 2 * half), lines_v[...])
    sums.settle(1, groups)


def term_attend(k, sums, left, right):
    width = k.width
    groups = range(k.count // 8)
    lines = width // k.count
    settled = False
    for col in range(3):
        k.arrive(col)
        square_terms(k, sums, left[...], right, slice(col * width, (col + 1) * width), col)
        if (col + 1) * lines >= sums.half and not settled:
            sums.settle(0, groups)
            settled = True
    gain = sum(k.small[n].astype(F32) for n in range(4))[:, :width]
    for g in range(k.count // 2):
        sums.put(g, slice(3 * lines, 3 * lines + GAIN_ROWS), gain)
    sums.settle(1, groups)


def load_terms(k, refs, bufs, base, sems):
    left_v, right_v, small_v = bufs
    rows, cols = left_v.shape[0], right_v.shape[1]
    tall = rows // TILE if small_v is None else 1
    wide = cols // k.width
    groups = []
    for i in range(tall):
        for j in range(wide):
            copies = []
            for n, (left, right) in enumerate(zip(refs[:4], refs[4:8])):
                tokens = pl.ds(n * k.span, k.span)
                part = pl.ds(i * (rows // tall), rows // tall)
                from_part = pl.ds(base + i * (rows // tall), rows // tall)
                at = pl.ds(j * k.width, k.width)
                if j == 0:
                    copies.append((left.at[from_part], left_v.at[part, tokens]))
                if i == 0:
                    copies.append((right.at[pl.ds(0, k.span), at], right_v.at[tokens, at]))
                if small_v is not None and j == wide - 1:
                    copies.append((right.at[pl.ds(k.span, EXTRA)], small_v.at[n]))
            groups.append(copies)
    made, count = [], 0
    for copies in groups:
        made.append([])
        for pair in copies:
            made[-1].append(pltpu.make_async_copy(*pair, sems.at[count]))
            made[-1][-1].start()
            count += 1
    return made


class Terms:
    def __init__(self, sizes, core):
        self.span, self.width, self.hidden, self.count = sizes
        self.core = core[0]

    def arrive(self, group):
        for copy in self.groups[group]:
            copy.wait()


def term_kernel(sizes, body, base, extra, *refs):
    refs = list(refs)
    core, rank = refs[:2]
    k = Terms(sizes, core)
    pos = 2
    if body is term_expand:
        k.embeds = refs[pos : pos + 2]
        pos += 2
    sources = refs[pos : pos + 8]
    pos += 8 + extra
    targets = refs[pos : pos + 4]
    pos += 4
    left_v, right_v, full, *outs = refs[pos : pos + 7]
    pos += 7
    k.small = None
    if body is not term_reduce:
        k.small, k.lines = refs[pos : pos + 2]
        pos += 2
    sems, out_sems = refs[pos:]
    k.groups = load_terms(k, sources, (left_v, right_v, k.small), base, sems)
    sums = Sums(rank, full, outs + targets, out_sems)
    body(k, sums, left_v, right_v)
    sums.finish()


def term_call(name, body, sizes, lines, base, rows, core, rank, lefts, rights, embeds=(), after=()):
    span, width, hidden, count = sizes
    blocks = count // 2
    cols = rights[0].shape[1]
    half = lines // 2
    outs = [((blocks // 2, half, width), kind) for kind in (BF16, F32)] * 2
    scratch = [
        ((rows, 4 * span), BF16),
        ((4 * span, cols), BF16),
        ((blocks, lines, width), F32),
        *outs,
    ]
    if body is not term_reduce:
        scratch += [((4, EXTRA, cols), BF16), ((TAIL_ROWS, width), F32)]
    args = [core.reshape(1), rank.reshape(1), *embeds, *lefts, *rights, *after]
    in_specs = [pl.BlockSpec(memory_space=SMEM)] * 2
    in_specs += [pl.BlockSpec(memory_space=VMEM)] * len(embeds)
    in_specs += [pl.BlockSpec(memory_space=ANY)] * (8 + len(after))
    return pl.pallas_call(
        partial(term_kernel, sizes, body, base, len(after)),
        out_shape=[jax.ShapeDtypeStruct(*item) for item in outs],
        in_specs=in_specs,
        out_specs=[pl.BlockSpec(memory_space=ANY)] * 4,
        scratch_shapes=[pltpu.VMEM(*item) for item in scratch]
        + [pltpu.SemaphoreType.DMA((32,)), pltpu.SemaphoreType.DMA((8,))],
        compiler_params=pltpu.CompilerParams(vmem_limit_bytes=62 * 1024 * 1024),
        name=name,
    )(*args)


def plain_pieces(lefts, rights, embed, sizes):
    span, width, hidden, count = sizes
    bg, pa, jg = rights
    bases = [2 * base for base in left_bases(width, hidden)]

    def blocks(base, rows, right):
        total = sum(dot(a[base : base + rows], b) for a, b in zip(lefts, right))
        parts = [total[:, i : i + width] for i in range(0, total.shape[1], width)]
        return [part.reshape(count, -1, width) for part in parts]

    take = lambda items, cols: [item[:span, cols] for item in items]
    reduce = blocks(bases[0], hidden, bg)
    expand = blocks(bases[1], width, take(pa, slice(0, hidden)))
    expand += blocks(bases[2], width, take(pa, slice(hidden, hidden + width)))
    last = blocks(bases[3], width, take(jg, slice(None)))
    small = [item[span:].astype(F32) for item in pa]
    seqs = jnp.concatenate([item[2 : 2 + SEGS, : 3 * width] for item in small])
    times = jnp.dot(embed, seqs, precision=lax.Precision.HIGHEST)
    expand += [times[:, i * width : (i + 1) * width].reshape(count, -1, width) for i in range(3)]
    lines = jnp.concatenate(
        [
            sum(item[1:2, :width] for item in small),
            jnp.sum(seqs, axis=0).reshape(-1, width),
            sum(item[0, :hidden] for item in small).reshape(-1, width),
        ]
    )
    lines = jnp.pad(lines, ((0, TAIL_ROWS - lines.shape[0]), (0, 0)))
    gain = sum(item[span:, :width].astype(F32) for item in jg)
    expand.append(jnp.broadcast_to(lines, (count,) + lines.shape))
    last.append(jnp.broadcast_to(gain, (count,) + gain.shape))
    return [jnp.concatenate(item, axis=1) for item in (reduce, expand, last)]


def shapes_of(span, width, hidden, cores):
    tok = lambda cols, kind=BF16: ((span, cols), kind)
    below = lambda cols: ((span + EXTRA, cols), BF16)
    return dict(
        xv=tok(width),
        dyv=tok(width),
        win=((width, 3 * width), BF16),
        wout=((width, width), BF16),
        wex=((width, hidden), BF16),
        wre=((hidden, width), BF16),
        left=((cores, (hidden + 3 * width) // cores, span), BF16),
        normed=tok(width),
        qkv=tok(3 * width),
        probs=((HEADS, span, span), F32),
        mixed=tok(width),
        middle=tok(width, F32),
        modded=tok(width),
        slope=tok(hidden, F32),
        branch=tok(width, F32),
        result=tok(width),
        bg=tok(width),
        pa=below(hidden + width),
        jg=below(3 * width),
        agrad=tok(width),
        mixed_grad=tok(width),
        middle_grad=tok(width, F32),
        leave=tok(width),
        acc=tok(width, F32),
        bias=tok(span, F32),
        small=((EXTRA, hidden + width), F32),
    )


def uses(part):
    return list(inspect.signature(part).parameters)[1:]


def stage_kernel(sizes, parts, who, slot, plan, *refs):
    refs = list(refs)
    layer = Layer(sizes, slot, refs[:9])
    span = layer.span
    pos = 9
    loads = {}
    for name, row, cols in plan.sources:
        ref = refs[pos]
        if cols is not None:
            ref = ref.at[pl.ds(0, span), pl.ds(*cols)]
        elif row is not None:
            ref = ref.at[pl.ds(row, span)]
        loads[name] = ref
        pos += 1
    pos += plan.extra
    stores = {}
    for name, row, at in plan.targets:
        target = refs[pos] if row is None else refs[pos].at[pl.ds(row, span)]
        stores.setdefault(name, []).append((at, target))
        pos += 1
    bufs = {}
    for name in plan.bufs:
        bufs[name] = refs[pos]
        pos += 1
    layer.held = Held(bufs, loads, stores, refs[pos], plan.pieces)
    layer.kept = plan.kept
    layer.heads_step = plan.heads_step

    @pl.when(layer.section == who)
    def _():
        for part in parts:
            part(layer, *[bufs[name] for name in uses(part)])
        layer.held.finish()


def stage(
    name, common, parts, who, slot, loads, stores, carried=None, after=(), kept=True, heads_step=3,
    pieces=None,
):
    carried = carried or {}
    span, width, hidden, count = common.sizes
    shapes = shapes_of(span, width, hidden, common.cores)
    bufs = []
    for part in parts:
        bufs += [item for item in uses(part) if item not in bufs]
    pair = lambda item: item if isinstance(item, tuple) else (item, None)
    args = list(common.args)
    in_specs = [pl.BlockSpec(memory_space=SMEM)] * 3 + [pl.BlockSpec(memory_space=VMEM)] * 6
    plan = Bag(sources=[], targets=[], bufs=bufs, kept=kept, heads_step=heads_step)
    plan["pieces"] = pieces or {}
    for item in loads:
        if item in bufs:
            array, row, *cols = pair(loads[item])
            args.append(array)
            plan.sources.append((item, row, cols[0] if cols else None))
    outs, aliases, extra = [], {}, []
    targets = []
    for item, key in stores.items():
        if item == "left":
            targets += [(item, key + "_send" * n, None, n) for n in range(common.cores)]
        else:
            targets.append((item, *pair(key), None))
    for i, (item, key, row, at) in enumerate(targets):
        shape, kind = shapes[item]
        if row is not None:
            shape = (common.tokens,) + shape[1:]
        if at is not None:
            shape = shape[1:]
        outs.append(jax.ShapeDtypeStruct(shape, kind))
        plan.targets.append((item, row, at))
        if key in carried:
            aliases[len(args) + len(extra)] = i
            extra.append(carried[key])
    extra += list(after)
    args += extra
    plan["extra"] = len(extra)
    in_specs += [pl.BlockSpec(memory_space=ANY)] * (len(args) - len(in_specs))
    results = pl.pallas_call(
        partial(stage_kernel, common.sizes, parts, who, slot, plan),
        out_shape=outs,
        in_specs=in_specs,
        out_specs=[pl.BlockSpec(memory_space=ANY)] * len(outs),
        input_output_aliases=aliases,
        scratch_shapes=[pltpu.VMEM(*shapes[item]) for item in bufs]
        + [pltpu.SemaphoreType.DMA((32,))],
        compiler_params=pltpu.CompilerParams(vmem_limit_bytes=62 * 1024 * 1024),
        name=name,
    )(*args)
    return Bag({key: value for (_, key, _, _), value in zip(targets, results)})


def bits_of(count):
    bits = count.bit_length() - 1
    assert 1 << bits == count
    return bits


class Chunk:
    def __init__(self, axis, bits, size, settled=()):
        self.axis = axis
        self.bits = list(range(bits - 1, 0, -1))
        self.size = size
        self.settled = list(settled)
        self.terms = []

    def add(self, term, start=0):
        left = [bit for bit in self.bits if bit not in self.settled]
        self.terms.append((term.reshape((2,) * len(left) + term.shape[-2:]), left, start))

    def take(self, term, start, left, flip):
        me = lax.axis_index(self.axis)
        side = lambda bit: 1 - ((me >> bit) & 1) if bit == flip else (me >> bit) & 1
        starts = [side(bit) if bit in self.settled else 0 for bit in left]
        sizes = [1 if bit in self.settled else 2 for bit in left]
        cols = term.shape[-1]
        piece = lax.dynamic_slice(term, starts + [start, 0], sizes + [self.size, cols])
        open_bits = [2] * (len(self.bits) - len(self.settled))
        return piece.reshape(open_bits + [self.size, cols]).astype(F32)

    def split(self, bit):
        self.settled.append(bit)
        return sum(self.take(term, start, left, bit) for term, left, start in self.terms).astype(
            BF16
        )

    def total(self):
        return sum(self.take(term, start, left, None) for term, left, start in self.terms)


def exchange(block, axis, bit):
    count = lax.axis_size(axis)
    return lax.ppermute(block, axis, [(i, i ^ (1 << bit)) for i in range(count)])


def join(*items):
    return lax.optimization_barrier(items)


def angle_table(span):
    half = HEAD // 2
    freqs = np.exp(-math.log(10000.0) * np.arange(half, dtype=np.float32) / half)
    phase = np.arange(span, dtype=np.float32)[:, None] * freqs.astype(np.float32)[None, :]
    cos_part, sin_part = np.cos(phase), np.sin(phase)
    return np.stack(
        [
            np.concatenate([cos_part] * 4, axis=1),
            np.concatenate([-sin_part, sin_part] * 2, axis=1),
        ]
    ).astype(np.float32)


def per_device(
    ends_in,
    lengths,
    times,
    norm_gain,
    attend_in,
    attend_out,
    time_weight,
    time_bias,
    expand_weight,
    expand_bias,
    reduce_weight,
    reduce_bias,
):
    local = ends_in[0]
    micro = lengths.shape[1]
    assert micro == 2
    width = local.shape[1]
    span = local.shape[0] // micro
    hidden = expand_weight.shape[2]
    count = lax.axis_size("rep")
    section = lax.axis_index("section")
    rank = lax.axis_index("rep")
    core = rank & 1
    steps = jnp.exp(-math.log(10000.0) * jnp.arange(EMB // 2, dtype=F32) / (EMB // 2))
    turn = times.reshape(micro * SEGS, 1).astype(F32) * steps
    embed = jnp.concatenate([jnp.cos(turn), jnp.sin(turn)], axis=1)
    mods = jnp.dot(embed, time_weight[0].astype(F32), precision=lax.Precision.HIGHEST)
    fused = width // count % 16 == 0 and TILE % (hidden // count) == 0 and count >= 16
    common = Bag(
        args=(
            lengths[0],
            section.reshape(1),
            core.reshape(1),
            mods,
            time_bias,
            jnp.asarray(angle_table(span)),
            norm_gain,
            expand_bias,
            reduce_bias,
        ),
        sizes=(span, width, hidden, count),
        tokens=local.shape[0],
        cores=2 if fused else 1,
    )
    weights = Bag(
        win=attend_in[0], wout=attend_out[0], wex=expand_weight[0], wre=reduce_weight[0]
    )
    rows = [(local, slot * span) for slot in range(micro)]
    same = lambda *names: {name: name for name in names}
    whole = same("left", "bg", "pa", "jg")
    run = partial(stage, common=common)
    both = (forward, output, mlp, copy_agrad, attend)
    over = lambda block, route: lax.ppermute(block, "section", route)
    swap = lambda block, bit: exchange(block, "rep", bit)
    a = run(
        "first_0",
        parts=(forward,),
        who=0,
        slot=0,
        loads=dict(xv=rows[0], **weights),
        stores=dict(result="leave"),
        kept=False,
    )
    came_0 = over(a.leave, [(0, 1)])
    b = run(
        "first_1",
        parts=(forward,),
        who=0,
        slot=1,
        loads=dict(xv=rows[1], **weights),
        stores=same("result", "left", "qkv", "probs", "middle", "slope", "branch"),
        after=(a.leave,),
        heads_step=1,
    )
    came_1 = over(b.result, [(0, 1)])
    x = run(
        "second_0",
        parts=both,
        who=1,
        slot=0,
        loads=dict(xv=came_0, dyv=rows[0], **weights),
        stores=dict(whole, result=("ends", 0), leave="leave"),
        after=(b.result,),
    )
    back_0 = over(x.leave, [(1, 0)])
    y = run(
        "second_1",
        parts=both,
        who=1,
        slot=1,
        loads=dict(xv=came_1, dyv=rows[1], **weights),
        stores=dict(whole, result=("ends", span), leave="leave"),
        carried=dict(b, ends=x.ends),
        after=(x.leave,),
    )
    back_1 = over(y.leave, [(1, 0)])
    gates = mods[SEGS : 2 * SEGS, 2 * width :] + time_bias[:, 2 * width :].astype(F32)
    gates = jnp.where(lengths[0, 1, 0] == span, gates[:1], gates)
    after = (y.leave, gates)
    if fused:
        turned, _ = join(embed.T, y.leave)
        embeds = (turned, swap(turned, 0))
        after += (embeds[1],)
    x = run(
        "back_0",
        parts=both,
        who=0,
        slot=0,
        loads=dict(xv=rows[0], dyv=back_0, **weights),
        stores=dict(whole, leave=("ends", 0)),
        carried=dict(x, ends=y.ends),
        after=after,
    )
    if fused:
        y_left = swap(y.left_send, 0)
        back_1, x_send, x_bg = join(back_1, x.left_send, x.bg)
        lefts = [x.left, y.left, swap(x_send, 0), y_left]
        others = [swap(item, 0) for item in (x_bg, x.pa, x.jg)]
    cotan = back_1.astype(F32).reshape(SEGS, -1, width)
    made = (cotan * gates[:, None]).reshape(span, width).astype(BF16)
    bg_1 = jnp.where(section == 0, made, y.bg)
    after = ()
    if fused:
        bg_1_other = swap(bg_1, 0)
        after = (bg_1_other, others[0], lefts[2], lefts[3])
    part = run(
        "back_1_mlp",
        parts=(mlp,),
        who=0,
        slot=1,
        loads=dict(
            bg=bg_1,
            wre=weights.wre,
            slope=b.slope,
            wex=weights.wex,
            middle=b.middle,
            dyv=back_1,
            branch=b.branch,
        ),
        stores=same("pa", "middle_grad"),
        carried=y,
        after=after,
        pieces=dict(wre=(0, hidden // width), slope=(1, hidden // width), wex=(1, hidden // width)),
    )
    pa_1 = part.pa
    bits = bits_of(count)
    term = partial(term_call, sizes=common.sizes, core=core, rank=rank)
    lines = width // count
    deep = EMB // count
    sizes = (hidden // count, hidden // count + lines + 3 * deep + TAIL_ROWS, 3 * lines + GAIN_ROWS)
    bases = left_bases(width, hidden)

    def last_attend(after):
        return run(
            "back_1_attend",
            parts=(attend,),
            who=0,
            slot=1,
            loads=dict(
                agrad=(pa_1, None, (hidden, width)),
                wout=weights.wout,
                probs=b.probs,
                qkv=b.qkv,
                win=weights.win,
                xv=rows[1],
                middle_grad=part.middle_grad,
            ),
            stores=dict(jg="jg", leave=("ends", span)),
            carried=dict(y, ends=x.ends),
            after=after,
        )

    def pair_of(size, first):
        cut = size // 2 if fused else size // 32 * 16
        one = Chunk("rep", bits, cut, (1,) if fused else ())
        two = Chunk("rep", bits, size - cut, (2,) if fused else ())
        if fused:
            send_1, keep_1, send_2, keep_2 = first
            one.add(keep_1)
            two.add(keep_2)
            return one, two, send_1, send_2
        view = first.reshape((count // 2, 2) + first.shape[1:])
        cut = lambda at: lax.dynamic_index_in_dim(view, at, 1, keepdims=False)
        came = swap(cut(1 - core).astype(BF16), 0)
        for item in (cut(core), came):
            one.add(item)
            two.add(item, one.size)
        return one, two, one.split(1), two.split(2)

    if fused:
        pa_other = swap(pa_1, 0)
        sent = term(
            "term_reduce",
            term_reduce,
            lines=sizes[0],
            base=bases[0],
            rows=hidden // 2,
            lefts=lefts,
            rights=[x.bg, bg_1, others[0], bg_1_other],
            after=(pa_1,),
        )
        r1, r2, send_1, send_2 = pair_of(sizes[0], sent)
        came_r1, came_r2 = swap(send_1, 1), swap(send_2, 2)
        sent = term(
            "term_expand",
            term_expand,
            lines=sizes[1],
            base=bases[1],
            rows=width,
            lefts=lefts,
            rights=[x.pa, pa_1, others[1], pa_other],
            embeds=embeds,
            after=(send_1, send_2),
        )
        came_r1, came_r2, *sent = join(came_r1, came_r2, *sent)
        e1, e2, send_1, send_2 = pair_of(sizes[1], sent)
        came_e1, came_e2 = swap(send_1, 1), swap(send_2, 2)
        last = last_attend((send_1, send_2))
        jg_1 = last.jg
        jg_other = swap(jg_1, 0)
        came_r1, came_r2, _ = join(came_r1, came_r2, jg_1)
        r1.add(came_r1)
        r2.add(came_r2)
        send_3, send_4 = r1.split(2), r2.split(1)
        came_r1, came_r2 = swap(send_3, 2), swap(send_4, 1)
        came_e1, came_e2, _, _ = join(came_e1, came_e2, send_3, send_4)
        e1.add(came_e1)
        e2.add(came_e2)
        send_1, send_2 = e1.split(2), e2.split(1)
        came_e1, came_e2 = swap(send_1, 2), swap(send_2, 1)
        sent = term(
            "term_attend",
            term_attend,
            lines=sizes[2],
            base=bases[3],
            rows=width // 2,
            lefts=lefts,
            rights=[x.jg, jg_1, others[2], jg_other],
            after=(send_1, send_2, send_3, send_4),
        )
        came_r1, came_r2, *sent = join(came_r1, came_r2, *sent)
        a1, a2, send_1, send_2 = pair_of(sizes[2], sent)
    else:
        last = last_attend(())
        rights = [(x.bg, bg_1), (x.pa, pa_1), (x.jg, last.jg)]
        totals = plain_pieces((x.left, y.left), rights, embed.T, common.sizes)
        r1, r2, send_1, send_2 = pair_of(sizes[0], totals[0])
        r1.add(swap(send_1, 1))
        r2.add(swap(send_2, 2))
        came_r1, came_r2 = swap(r1.split(2), 2), swap(r2.split(1), 1)
        e1, e2, send_1, send_2 = pair_of(sizes[1], totals[1])
        e1.add(swap(send_1, 1))
        e2.add(swap(send_2, 2))
        came_e1, came_e2 = swap(e1.split(2), 2), swap(e2.split(1), 1)
        a1, a2, send_1, send_2 = pair_of(sizes[2], totals[2])
    ends = last.ends
    came_a1, came_a2 = swap(send_1, 1), swap(send_2, 2)
    r1.add(came_r1)
    r2.add(came_r2)
    block_r = jnp.concatenate([r1.split(3), r2.split(3)], axis=-2)
    came_r = swap(block_r, 3)
    came_e1, came_e2, _ = join(came_e1, came_e2, block_r)
    e1.add(came_e1)
    e2.add(came_e2)
    block_e = jnp.concatenate([e1.split(3), e2.split(3)], axis=-2)
    came_e = swap(block_e, 3)
    came_a1, came_a2, _ = join(came_a1, came_a2, block_e)
    a1.add(came_a1)
    a2.add(came_a2)
    send_1, send_2 = a1.split(2), a2.split(1)
    came_a1, came_a2 = swap(send_1, 2), swap(send_2, 1)
    a1.add(came_a1)
    a2.add(came_a2)
    block_a = jnp.concatenate([a1.split(3), a2.split(3)], axis=-2)
    came_a = swap(block_a, 3)
    came_r, _ = join(came_r, send_1)
    r1.add(came_r[..., : r1.size, :])
    r2.add(came_r[..., r1.size :, :])
    came_e, _ = join(came_e, block_a)
    e1.add(came_e[..., : e1.size, :])
    e2.add(came_e[..., e1.size :, :])
    a1.add(came_a[..., : a1.size, :])
    a2.add(came_a[..., a1.size :, :])
    for bit in range(4, bits):
        for chunk in (r1, r2, e1, e2, a1, a2):
            chunk.add(swap(chunk.split(bit), bit))
    share_r, share_e, share_a = (
        jnp.concatenate([one.total(), two.total()]) for one, two in ((r1, r2), (e1, e2), (a1, a2))
    )
    tall = hidden // width
    side = lambda item, n, size: jnp.concatenate(
        [item[i * size : (i + 1) * size] for i in range(n)], axis=1
    )
    at_o = tall * lines
    at_t = at_o + lines
    small = share_e[at_t + 3 * deep :]
    flat = lambda item, first, n: lax.dynamic_slice_in_dim(
        item[first : first + n].reshape(-1), rank * (n * width // count), n * width // count
    )
    results = (
        flat(share_a, 3 * lines, 1),
        side(share_a, 3, lines),
        share_e[at_o:at_t],
        side(share_e[at_t:], 3, deep),
        flat(small, 1, 3),
        side(share_e, tall, lines),
        flat(small, 4, tall),
        share_r,
        flat(small, 0, 1),
    )
    return (ends[None],) + tuple(piece[None] for piece in results)


def solution(mesh):
    return jax.shard_map(
        per_device,
        mesh=mesh,
        in_specs=(
            P("section", "rep", None),
            P("rep", None, None),
            P("rep", None, None),
            P("section", None),
            P("section", None, None),
            P("section", None, None),
            P("section", None, None),
            P("section", None),
            P("section", None, None),
            P("section", None),
            P("section", None, None),
            P("section", None),
        ),
        out_specs=(
            P("section", "rep", None),
            P("section", "rep"),
            P("section", "rep", None),
            P("section", "rep", None),
            P("section", "rep", None),
            P("section", "rep"),
            P("section", "rep", None),
            P("section", "rep"),
            P("section", "rep", None),
            P("section", "rep"),
        ),
        check_vma=False,
    )
```

```python
from functools import partial
import inspect
import math

import jax
import jax.numpy as jnp
import numpy as np
from jax import lax
from jax.experimental import pallas as pl
from jax.experimental.pallas import tpu as pltpu
from jax.sharding import PartitionSpec as P

HEADS = 12
HEAD = 64
EMB = 128
SEGS = 4
ANY = pl.ANY
VMEM = pltpu.MemorySpace.VMEM
SMEM = pltpu.MemorySpace.SMEM
F32 = jnp.float32
BF16 = jnp.bfloat16
ROOT_HALF = 0.7071067811865476
ROOT_TAU = 0.3989422804014327
TILE = 384
TAIL_ROWS = 24
GAIN_ROWS = 16
EXTRA = 16


class Bag(dict):
    __getattr__ = dict.__getitem__


def dot(left, right, left_dim=1, right_dim=0):
    return lax.dot_general(
        left, right, (((left_dim,), (right_dim,)), ((), ())), preferred_element_type=F32
    )


def repeat(count, body):
    for i in range(count):
        body(i)


def steps_of(count, size, body):
    def several(i, _):
        for j in range(size):
            body(size * i + j)
        return _

    lax.fori_loop(0, count // size, several, 0)


def lanes(index, size, start=0):
    if isinstance(index, int):
        return slice(start + index * size, start + (index + 1) * size)
    return pl.ds(pl.multiple_of(start + index * size, size), size)


def swap_halves(values, low_half):
    forth = pltpu.roll(values, 128 - HEAD // 2, 1)
    back = pltpu.roll(values, HEAD // 2, 1)
    return jnp.where(low_half, forth, back)


def norm_parts(values):
    center = values - jnp.mean(values, axis=-1, keepdims=True)
    spread = jnp.mean(center * center, axis=-1, keepdims=True)
    factor = lax.rsqrt(spread + 1e-05)
    return center * factor, factor


def norm_back(grad, unit, factor):
    return factor * (
        grad
        - jnp.mean(grad, axis=-1, keepdims=True)
        - unit * jnp.mean(grad * unit, axis=-1, keepdims=True)
    )


class Held:
    def __init__(self, bufs, loads, stores, sems, pieces):
        self.bufs = bufs
        self.loads = loads
        self.stores = stores
        self.sems = sems
        self.pieces = pieces
        self.names = {id(buf): name for name, buf in bufs.items()}
        keys = [(name, j) for name in loads for j in range(self.parts_of(name))]
        self.spots = {key: n for n, key in enumerate(keys)}
        self.waiting = set(keys)
        self.pending = set(keys)
        self.leaving = {}

    def parts_of(self, name):
        return self.pieces[name][1] if name in self.pieces else 1

    def load(self, name, j):
        source, target = self.loads[name], self.bufs[name]
        if name in self.pieces:
            axis, count = self.pieces[name]
            size = target.shape[axis] // count
            at = (slice(None),) * axis + (pl.ds(j * size, size),)
            source, target = source.at[at], target.at[at]
        return pltpu.make_async_copy(source, target, self.sems.at[self.spots[(name, j)]])

    def store(self, name, n):
        at, target = self.stores[name][n]
        source = self.bufs[name] if at is None else self.bufs[name].at[at]
        return pltpu.make_async_copy(source, target, self.sems.at[self.leaving[(name, n)]])

    def keys(self, bufs, part):
        for buf in bufs:
            name = self.names[id(buf)]
            for j in range(self.parts_of(name)):
                if part in (None, j):
                    yield name, j

    def begin(self, *bufs, part=None):
        for key in self.keys(bufs, part):
            if key in self.waiting:
                self.waiting.remove(key)
                self.load(*key).start()

    def need(self, *bufs, part=None):
        self.begin(*bufs, part=part)
        for key in self.keys(bufs, part):
            if key in self.pending:
                self.pending.remove(key)
                self.load(*key).wait()

    def done(self, *bufs):
        for buf in bufs:
            name = self.names[id(buf)]
            for n in range(len(self.stores.get(name, ()))):
                self.leaving[(name, n)] = len(self.spots) + len(self.leaving)
                self.store(name, n).start()

    def finish(self):
        for name, n in self.leaving:
            self.store(name, n).wait()


class Layer:
    def __init__(self, sizes, slot, refs):
        self.span, self.width, self.hidden, self.count = sizes
        self.slot = slot
        (
            lengths, section, core, self.mods, self.tbias, self.trig, self.gain, self.ebias,
            self.rbias,
        ) = refs
        self.section = section[0]
        self.core = core[0]
        self.single = lengths[slot, 0] == self.span
        self.pairs = self.width // 128
        self.seg = self.span // SEGS
        self.step = self.width
        self.tiles = self.hidden // self.step
        place = lax.broadcasted_iota(jnp.int32, (self.span, 128), 1)
        self.low_half = place % HEAD < HEAD // 2
        self.low_head = place < HEAD
        row = lax.broadcasted_iota(jnp.int32, (1, 128), 1) // HEAD
        self.head_row = [(row == i).astype(F32).astype(BF16) for i in range(2)]
        self.blocks = [(b, slice(b * self.seg, (b + 1) * self.seg)) for b in range(SEGS)]

    def trig_pair(self):
        cos_all, sin_all = self.trig[0], self.trig[1]
        cos_cut = jnp.concatenate([cos_all[: self.seg]] * SEGS, axis=0)
        sin_cut = jnp.concatenate([sin_all[: self.seg]] * SEGS, axis=0)
        return jnp.where(self.single, cos_all, cos_cut), jnp.where(self.single, sin_all, sin_cut)

    def mod_row(self, block, part):
        row = self.slot * SEGS + jnp.where(self.single, 0, block)
        at = slice(part * self.width, (part + 1) * self.width)
        return self.mods[pl.ds(row, 1), at] + self.tbias[:, at].astype(F32)

    def add_segment(self, small, block, at, sums):
        row = 2 + jnp.where(self.single, 0, block)
        small[pl.ds(row, 1), at * self.width : (at + 1) * self.width] += sums

    def side(self, block):
        return self.core if block % 2 == 0 else 1 - self.core

    def put_left(self, left, base, values):
        turned = values.T
        if left.shape[0] == 1:
            left[0, 2 * base : 2 * base + self.width] = turned
            return
        lines = self.width // self.count
        for block in range(self.count):
            to = base + block // 2 * lines
            left[self.side(block), to : to + lines] = turned[block * lines : (block + 1) * lines]

    def put_active(self, left, j, values):
        turned = values.T
        if left.shape[0] == 1:
            left[0, lanes(j, self.step)] = turned
            return
        lines = self.hidden // self.count
        per = self.step // lines
        for n in range(per):
            to = lanes(j, lines * (per // 2), n // 2 * lines)
            to = slice(to.start, to.start + lines) if isinstance(j, int) else pl.ds(to.start, lines)
            left[self.side(n), to] = turned[n * lines : (n + 1) * lines]

    def thirds(self, index):
        return [lanes(index, 128, p * self.width) for p in range(3)]


def left_bases(width, hidden):
    return 0, hidden // 2, (hidden + width) // 2, (hidden + 2 * width) // 2


def forward(
    k, xv, win, wout, wex, wre, left, qkv, probs, middle, slope, branch, result, bias, normed,
    mixed, modded,
):
    span, width, held = k.span, k.width, k.held
    _, at_modded, at_mixed, at_normed = left_bases(width, k.hidden)
    held.begin(xv, win)
    held.need(xv)
    unit, _ = norm_parts(xv[...].astype(F32))
    normed[...] = (unit * k.gain[...].astype(F32)).astype(BF16)
    across = lax.broadcasted_iota(jnp.int32, (span, span), 0) // k.seg
    down = lax.broadcasted_iota(jnp.int32, (span, span), 1) // k.seg
    bias[...] = jnp.where((across == down) | k.single, 0.0, -1e30)
    held.need(win)
    held.begin(wout, wex, wre)
    cos_part, sin_part = k.trig_pair()
    for tile, factor in ((0, 0.125), (1, 1.0)):
        for i in range(width // 256):
            at = lanes(i, 256, tile * width)
            joint = dot(normed[...], win[:, at])
            outs = []
            for piece in (joint[:, :128], joint[:, 128:]):
                turned = piece * cos_part + swap_halves(piece, k.low_half) * sin_part
                outs.append((turned * factor).astype(BF16))
            qkv[:, at] = jnp.concatenate(outs, axis=1)
    qkv[:, 2 * width :] = dot(normed[...], win[:, 2 * width :]).astype(BF16)
    held.done(qkv)
    if k.kept:
        k.put_left(left, at_normed, normed[...])

    def heads(i):
        at = k.thirds(i)
        query, key, value = (qkv[:, a] for a in at)
        outs = []
        for h in range(2):
            scores = dot(key * k.head_row[h], query, 1, 1) + bias[...]
            top = jnp.max(scores, axis=0, keepdims=True)
            raised = jnp.exp(scores - top)
            total = jnp.sum(raised, axis=0, keepdims=True)
            prob = raised * (1.0 / total)
            if k.kept:
                probs[2 * i + h] = prob
            outs.append(dot(prob.astype(BF16), value, 0, 0))
        mixed[:, at[0]] = jnp.where(k.low_head, outs[0], outs[1]).astype(BF16)

    steps_of(k.pairs, k.heads_step, heads)
    held.done(probs)
    held.need(wout)
    middle[...] = xv[...].astype(F32) + dot(mixed[...], wout[...])
    held.done(middle)
    if k.kept:
        k.put_left(left, at_mixed, mixed[...])
    for b, rows in k.blocks:
        unit, _ = norm_parts(middle[rows])
        modded[rows] = (unit * (1.0 + k.mod_row(b, 0)) + k.mod_row(b, 1)).astype(BF16)
    if k.kept:
        k.put_left(left, at_modded, modded[...])
    held.need(wex, wre)
    branch[...] = jnp.broadcast_to(k.rbias[...].astype(F32), (span, width))

    def feed(j):
        at = lanes(j, k.step)
        pre = dot(modded[...], wex[:, at]) + k.ebias[:, at].astype(F32)
        area = 0.5 + 0.5 * lax.erf(pre * ROOT_HALF)
        out = (pre * area).astype(BF16)
        if k.kept:
            slope[:, at] = area + pre * (jnp.exp(pre * pre * -0.5) * ROOT_TAU)
            k.put_active(left, j, out)
        branch[...] += dot(out, wre[at, :])

    if k.heads_step == 1:
        steps_of(k.tiles, 1, feed)
    else:
        repeat(k.tiles, feed)
    held.done(slope, left, branch)
    for b, rows in k.blocks:
        result[rows] = (middle[rows] + k.mod_row(b, 2) * branch[rows]).astype(BF16)
    held.done(result)


def output(k, dyv, bg):
    k.held.need(dyv)
    for b, rows in k.blocks:
        bg[rows] = (dyv[rows].astype(F32) * k.mod_row(b, 2)).astype(BF16)
    k.held.done(bg)


def mlp(k, wre, wex, bg, slope, middle, branch, dyv, pa, middle_grad, small, acc):
    span, width, hidden, held = k.span, k.width, k.hidden, k.held
    small[...] = jnp.zeros(small.shape, F32)
    acc[...] = jnp.zeros(acc.shape, F32)
    held.begin(bg)
    for j in range(k.tiles):
        held.begin(wre, slope, wex, part=j)
    held.begin(middle, dyv, branch)
    held.need(bg)

    def feed(j):
        at = lanes(j, k.step)
        held.need(wre, slope, wex, part=j)
        grad = dot(bg[...], wre[at, :], 1, 1)
        pre_grad = (slope[:, at] * grad).astype(BF16)
        pa[:span, at] = pre_grad
        small[0:1, at] = jnp.sum(pre_grad.astype(F32), axis=0, keepdims=True)
        acc[...] += dot(pre_grad, wex[:, at], 1, 1)

    repeat(k.tiles, feed)
    held.need(middle, dyv, branch)
    total = jnp.zeros((1, width), F32)
    for b, rows in k.blocks:
        cotan = dyv[rows].astype(F32)
        total += jnp.sum(bg[rows].astype(F32), axis=0, keepdims=True)
        grad = acc[rows]
        unit, factor = norm_parts(middle[rows])
        k.add_segment(small, b, 0, jnp.sum(grad * unit, axis=0, keepdims=True))
        k.add_segment(small, b, 1, jnp.sum(grad, axis=0, keepdims=True))
        k.add_segment(small, b, 2, jnp.sum(cotan * branch[rows], axis=0, keepdims=True))
        back = norm_back(grad * (1.0 + k.mod_row(b, 0)), unit, factor)
        full = cotan + back
        middle_grad[rows] = full
        pa[rows, hidden:] = full.astype(BF16)
    small[1:2, :width] = total
    pa[span:, :] = small[...].astype(BF16)
    held.done(pa, middle_grad)


def attend(
    k, wout, win, agrad, probs, qkv, xv, middle_grad, jg, leave, mixed_grad, acc
):
    span, held = k.span, k.held
    held.need(agrad, wout)
    held.begin(probs, qkv)
    mixed_grad[...] = dot(agrad[...], wout[...], 1, 1).astype(BF16)
    held.need(probs, qkv)
    held.begin(win, xv, middle_grad)
    cos_part, sin_part = k.trig_pair()

    def heads(i):
        at = k.thirds(i)
        query, key, value = (qkv[:, a] for a in at)
        out_grad = mixed_grad[:, at[0]]
        parts = []
        for h in range(2):
            prob = probs[2 * i + h]
            pull = dot(value * k.head_row[h], out_grad, 1, 1)
            shared = jnp.sum(prob * pull, axis=0, keepdims=True)
            score_grad = (prob * (pull - shared)).astype(BF16)
            parts.append(
                (
                    dot(score_grad, key, 0, 0),
                    dot(score_grad, query),
                    dot(prob.astype(BF16), out_grad),
                )
            )
        for p in range(3):
            grad = jnp.where(k.low_head, parts[0][p], parts[1][p])
            if p < 2:
                grad = grad * cos_part - swap_halves(grad, k.low_half) * sin_part
                if p == 0:
                    grad = grad * 0.125
            jg[:span, at[p]] = grad.astype(BF16)

    steps_of(k.pairs, k.heads_step, heads)
    held.need(win, xv, middle_grad)
    acc[...] = dot(jg[:span, :], win[...], 1, 1)
    total = jnp.zeros((1, k.width), F32)
    for b, rows in k.blocks:
        grad = acc[rows]
        unit, factor = norm_parts(xv[rows].astype(F32))
        total += jnp.sum(grad * unit, axis=0, keepdims=True)
        back = norm_back(grad * k.gain[...].astype(F32), unit, factor)
        leave[rows] = (middle_grad[rows] + back).astype(BF16)
    below = jnp.concatenate([total, jnp.zeros((EXTRA - 1, k.width), F32)], axis=0)
    jg[span:, : k.width] = below.astype(BF16)
    jg[span:, k.width :] = jnp.zeros((EXTRA, 2 * k.width), BF16)
    held.done(jg, leave)


def copy_agrad(k, pa, agrad):
    agrad[...] = pa[: k.span, k.hidden :]


class Sums:
    def __init__(self, ranks, full, outs, sems):
        self.full = full
        self.own = [((ranks[0] >> bit) & 1) == 0 for bit in (1, 2)]
        self.bufs = outs[:4]
        self.targets = outs[4:]
        self.sems = sems
        self.half = full.shape[1] // 2
        self.copies = []

    def put(self, block, at, values):
        self.full[block, at] = values

    def settle(self, which, groups):
        send, keep = self.bufs[2 * which : 2 * which + 2]
        at = slice(which * self.half, (which + 1) * self.half)
        apart = 1 + which
        for group in groups:
            for n in range(2):
                first = 4 * group + (2 * n if which == 0 else n)
                even, odd = self.full[first, at], self.full[first + apart, at]
                send[2 * group + n] = jnp.where(self.own[which], odd, even).astype(BF16)
                keep[2 * group + n] = jnp.where(self.own[which], even, odd)
            spot = pl.ds(2 * group, 2)
            for n in range(2 * which, 2 * which + 2):
                copy = pltpu.make_async_copy(
                    self.bufs[n].at[spot], self.targets[n].at[spot], self.sems.at[len(self.copies)]
                )
                copy.start()
                self.copies.append(copy)

    def finish(self):
        for copy in self.copies:
            copy.wait()


def term_reduce(k, sums, left, right):
    lines = k.hidden // k.count
    per = TILE // lines
    for tile in range(k.hidden // 2 // TILE):
        k.arrive(tile)
        total = dot(left[tile * TILE : (tile + 1) * TILE], right[...])
        for n in range(per):
            sums.put(tile * per + n, slice(0, lines), total[n * lines : (n + 1) * lines])
        if (tile + 1) * per % 4 == 0:
            group = ((tile + 1) * per // 4 - 1,)
            sums.settle(0, group)
            sums.settle(1, group)


def square_terms(k, sums, left, right, cols, part):
    lines = k.width // k.count
    total = dot(left, right[: 4 * k.span, cols])
    for n in range(k.count // 2):
        sums.put(n, slice(part * lines, (part + 1) * lines), total[n * lines : (n + 1) * lines])


def term_expand(k, sums, left, right):
    width, hidden, span = k.width, k.hidden, k.span
    groups = range(k.count // 8)
    tall = hidden // width
    lines = width // k.count
    rows = width // 2
    half = sums.half
    settled = False
    for col in range(tall + 1):
        k.arrive(col)
        part = left[:rows] if col < tall else left[rows:]
        square_terms(k, sums, part, right, slice(col * width, (col + 1) * width), col)
        if (col + 1) * lines >= half and not settled:
            sums.settle(0, groups)
            settled = True
    smalls = [k.small[n].astype(F32) for n in range(4)]
    angles = jnp.concatenate([embed[...] for embed in k.embeds], axis=1)
    pieces = []
    for _ in range(3):
        pieces.append(angles.astype(BF16))
        angles = angles - pieces[-1].astype(F32)
    seqs = jnp.concatenate([small[2 : 2 + SEGS, : 3 * width] for small in smalls]).astype(BF16)
    times = sum(dot(piece, seqs) for piece in pieces)
    both = sum(smalls)
    seq_sum = jnp.sum(both[2 : 2 + SEGS, : 3 * width], axis=0, keepdims=True)
    lines_v = k.lines
    lines_v[...] = jnp.zeros(lines_v.shape, F32)
    lines_v[0:1] = both[1:2, :width]
    for n in range(3):
        lines_v[1 + n : 2 + n] = seq_sum[:, n * width : (n + 1) * width]
    for n in range(tall):
        lines_v[4 + n : 5 + n] = both[0:1, n * width : (n + 1) * width]
    deep = EMB // k.count
    first = (tall + 1) * lines
    low = k.core == 0
    for g in range(k.count // 2):
        for p in range(3):
            at = slice(p * width, (p + 1) * width)
            even = times[2 * g * deep : (2 * g + 1) * deep, at]
            odd = times[(2 * g + 1) * deep : (2 * g + 2) * deep, at]
            to = first + p * deep
            sums.put(g, slice(to, to + deep), jnp.where(low, even, odd))
        sums.put(g, slice(first + 3 * deep, 2 * half), lines_v[...])
    sums.settle(1, groups)


def term_attend(k, sums, left, right):
    width = k.width
    groups = range(k.count // 8)
    lines = width // k.count
    settled = False
    for col in range(3):
        k.arrive(col)
        square_terms(k, sums, left[...], right, slice(col * width, (col + 1) * width), col)
        if (col + 1) * lines >= sums.half and not settled:
            sums.settle(0, groups)
            settled = True
    gain = sum(k.small[n].astype(F32) for n in range(4))[:, :width]
    for g in range(k.count // 2):
        sums.put(g, slice(3 * lines, 3 * lines + GAIN_ROWS), gain)
    sums.settle(1, groups)


def load_terms(k, refs, bufs, base, sems):
    left_v, right_v, small_v = bufs
    rows, cols = left_v.shape[0], right_v.shape[1]
    tall = rows // TILE if small_v is None else 1
    wide = cols // k.width
    groups = []
    for i in range(tall):
        for j in range(wide):
            copies = []
            for n, (left, right) in enumerate(zip(refs[:4], refs[4:8])):
                tokens = pl.ds(n * k.span, k.span)
                part = pl.ds(i * (rows // tall), rows // tall)
                from_part = pl.ds(base + i * (rows // tall), rows // tall)
                at = pl.ds(j * k.width, k.width)
                if j == 0:
                    copies.append((left.at[from_part], left_v.at[part, tokens]))
                if i == 0:
                    copies.append((right.at[pl.ds(0, k.span), at], right_v.at[tokens, at]))
                if small_v is not None and j == wide - 1:
                    copies.append((right.at[pl.ds(k.span, EXTRA)], small_v.at[n]))
            groups.append(copies)
    made, count = [], 0
    for copies in groups:
        made.append([])
        for pair in copies:
            made[-1].append(pltpu.make_async_copy(*pair, sems.at[count]))
            made[-1][-1].start()
            count += 1
    return made


class Terms:
    def __init__(self, sizes, core):
        self.span, self.width, self.hidden, self.count = sizes
        self.core = core[0]

    def arrive(self, group):
        for copy in self.groups[group]:
            copy.wait()


def term_kernel(sizes, body, base, extra, *refs):
    refs = list(refs)
    core, rank = refs[:2]
    k = Terms(sizes, core)
    pos = 2
    if body is term_expand:
        k.embeds = refs[pos : pos + 2]
        pos += 2
    sources = refs[pos : pos + 8]
    pos += 8 + extra
    targets = refs[pos : pos + 4]
    pos += 4
    left_v, right_v, full, *outs = refs[pos : pos + 7]
    pos += 7
    k.small = None
    if body is not term_reduce:
        k.small, k.lines = refs[pos : pos + 2]
        pos += 2
    sems, out_sems = refs[pos:]
    k.groups = load_terms(k, sources, (left_v, right_v, k.small), base, sems)
    sums = Sums(rank, full, outs + targets, out_sems)
    body(k, sums, left_v, right_v)
    sums.finish()


def term_call(name, body, sizes, lines, base, rows, core, rank, lefts, rights, embeds=(), after=()):
    span, width, hidden, count = sizes
    blocks = count // 2
    cols = rights[0].shape[1]
    half = lines // 2
    outs = [((blocks // 2, half, width), kind) for kind in (BF16, F32)] * 2
    scratch = [
        ((rows, 4 * span), BF16),
        ((4 * span, cols), BF16),
        ((blocks, lines, width), F32),
        *outs,
    ]
    if body is not term_reduce:
        scratch += [((4, EXTRA, cols), BF16), ((TAIL_ROWS, width), F32)]
    args = [core.reshape(1), rank.reshape(1), *embeds, *lefts, *rights, *after]
    in_specs = [pl.BlockSpec(memory_space=SMEM)] * 2
    in_specs += [pl.BlockSpec(memory_space=VMEM)] * len(embeds)
    in_specs += [pl.BlockSpec(memory_space=ANY)] * (8 + len(after))
    return pl.pallas_call(
        partial(term_kernel, sizes, body, base, len(after)),
        out_shape=[jax.ShapeDtypeStruct(*item) for item in outs],
        in_specs=in_specs,
        out_specs=[pl.BlockSpec(memory_space=ANY)] * 4,
        scratch_shapes=[pltpu.VMEM(*item) for item in scratch]
        + [pltpu.SemaphoreType.DMA((32,)), pltpu.SemaphoreType.DMA((8,))],
        compiler_params=pltpu.CompilerParams(vmem_limit_bytes=62 * 1024 * 1024),
        name=name,
    )(*args)


def plain_pieces(lefts, rights, embed, sizes):
    span, width, hidden, count = sizes
    bg, pa, jg = rights
    bases = [2 * base for base in left_bases(width, hidden)]

    def blocks(base, rows, right):
        total = sum(dot(a[base : base + rows], b) for a, b in zip(lefts, right))
        parts = [total[:, i : i + width] for i in range(0, total.shape[1], width)]
        return [part.reshape(count, -1, width) for part in parts]

    take = lambda items, cols: [item[:span, cols] for item in items]
    reduce = blocks(bases[0], hidden, bg)
    expand = blocks(bases[1], width, take(pa, slice(0, hidden)))
    expand += blocks(bases[2], width, take(pa, slice(hidden, hidden + width)))
    last = blocks(bases[3], width, take(jg, slice(None)))
    small = [item[span:].astype(F32) for item in pa]
    seqs = jnp.concatenate([item[2 : 2 + SEGS, : 3 * width] for item in small])
    times = jnp.dot(embed, seqs, precision=lax.Precision.HIGHEST)
    expand += [times[:, i * width : (i + 1) * width].reshape(count, -1, width) for i in range(3)]
    lines = jnp.concatenate(
        [
            sum(item[1:2, :width] for item in small),
            jnp.sum(seqs, axis=0).reshape(-1, width),
            sum(item[0, :hidden] for item in small).reshape(-1, width),
        ]
    )
    lines = jnp.pad(lines, ((0, TAIL_ROWS - lines.shape[0]), (0, 0)))
    gain = sum(item[span:, :width].astype(F32) for item in jg)
    expand.append(jnp.broadcast_to(lines, (count,) + lines.shape))
    last.append(jnp.broadcast_to(gain, (count,) + gain.shape))
    return [jnp.concatenate(item, axis=1) for item in (reduce, expand, last)]


def shapes_of(span, width, hidden, cores):
    tok = lambda cols, kind=BF16: ((span, cols), kind)
    below = lambda cols: ((span + EXTRA, cols), BF16)
    return dict(
        xv=tok(width),
        dyv=tok(width),
        win=((width, 3 * width), BF16),
        wout=((width, width), BF16),
        wex=((width, hidden), BF16),
        wre=((hidden, width), BF16),
        left=((cores, (hidden + 3 * width) // cores, span), BF16),
        normed=tok(width),
        qkv=tok(3 * width),
        probs=((HEADS, span, span), F32),
        mixed=tok(width),
        middle=tok(width, F32),
        modded=tok(width),
        slope=tok(hidden, F32),
        branch=tok(width, F32),
        result=tok(width),
        bg=tok(width),
        pa=below(hidden + width),
        jg=below(3 * width),
        agrad=tok(width),
        mixed_grad=tok(width),
        middle_grad=tok(width, F32),
        leave=tok(width),
        acc=tok(width, F32),
        bias=tok(span, F32),
        small=((EXTRA, hidden + width), F32),
    )


def uses(part):
    return list(inspect.signature(part).parameters)[1:]


def stage_kernel(sizes, parts, who, slot, plan, *refs):
    refs = list(refs)
    layer = Layer(sizes, slot, refs[:9])
    span = layer.span
    pos = 9
    loads = {}
    for name, row, cols in plan.sources:
        ref = refs[pos]
        if cols is not None:
            ref = ref.at[pl.ds(0, span), pl.ds(*cols)]
        elif row is not None:
            ref = ref.at[pl.ds(row, span)]
        loads[name] = ref
        pos += 1
    pos += plan.extra
    stores = {}
    for name, row, at in plan.targets:
        target = refs[pos] if row is None else refs[pos].at[pl.ds(row, span)]
        stores.setdefault(name, []).append((at, target))
        pos += 1
    bufs = {}
    for name in plan.bufs:
        bufs[name] = refs[pos]
        pos += 1
    layer.held = Held(bufs, loads, stores, refs[pos], plan.pieces)
    layer.kept = plan.kept
    layer.heads_step = plan.heads_step

    @pl.when(layer.section == who)
    def _():
        for part in parts:
            part(layer, *[bufs[name] for name in uses(part)])
        layer.held.finish()


def stage(
    name, common, parts, who, slot, loads, stores, carried=None, after=(), kept=True, heads_step=3,
    pieces=None,
):
    carried = carried or {}
    span, width, hidden, count = common.sizes
    shapes = shapes_of(span, width, hidden, common.cores)
    bufs = []
    for part in parts:
        bufs += [item for item in uses(part) if item not in bufs]
    pair = lambda item: item if isinstance(item, tuple) else (item, None)
    args = list(common.args)
    in_specs = [pl.BlockSpec(memory_space=SMEM)] * 3 + [pl.BlockSpec(memory_space=VMEM)] * 6
    plan = Bag(sources=[], targets=[], bufs=bufs, kept=kept, heads_step=heads_step)
    plan["pieces"] = pieces or {}
    for item in loads:
        if item in bufs:
            array, row, *cols = pair(loads[item])
            args.append(array)
            plan.sources.append((item, row, cols[0] if cols else None))
    outs, aliases, extra = [], {}, []
    targets = []
    for item, key in stores.items():
        if item == "left":
            targets += [(item, key + "_send" * n, None, n) for n in range(common.cores)]
        else:
            targets.append((item, *pair(key), None))
    for i, (item, key, row, at) in enumerate(targets):
        shape, kind = shapes[item]
        if row is not None:
            shape = (common.tokens,) + shape[1:]
        if at is not None:
            shape = shape[1:]
        outs.append(jax.ShapeDtypeStruct(shape, kind))
        plan.targets.append((item, row, at))
        if key in carried:
            aliases[len(args) + len(extra)] = i
            extra.append(carried[key])
    extra += list(after)
    args += extra
    plan["extra"] = len(extra)
    in_specs += [pl.BlockSpec(memory_space=ANY)] * (len(args) - len(in_specs))
    results = pl.pallas_call(
        partial(stage_kernel, common.sizes, parts, who, slot, plan),
        out_shape=outs,
        in_specs=in_specs,
        out_specs=[pl.BlockSpec(memory_space=ANY)] * len(outs),
        input_output_aliases=aliases,
        scratch_shapes=[pltpu.VMEM(*shapes[item]) for item in bufs]
        + [pltpu.SemaphoreType.DMA((32,))],
        compiler_params=pltpu.CompilerParams(vmem_limit_bytes=62 * 1024 * 1024),
        name=name,
    )(*args)
    return Bag({key: value for (_, key, _, _), value in zip(targets, results)})


def bits_of(count):
    bits = count.bit_length() - 1
    assert 1 << bits == count
    return bits


class Chunk:
    def __init__(self, axis, bits, size, settled=()):
        self.axis = axis
        self.bits = list(range(bits - 1, 0, -1))
        self.size = size
        self.settled = list(settled)
        self.terms = []

    def add(self, term, start=0):
        left = [bit for bit in self.bits if bit not in self.settled]
        self.terms.append((term.reshape((2,) * len(left) + term.shape[-2:]), left, start))

    def take(self, term, start, left, flip):
        me = lax.axis_index(self.axis)
        side = lambda bit: 1 - ((me >> bit) & 1) if bit == flip else (me >> bit) & 1
        starts = [side(bit) if bit in self.settled else 0 for bit in left]
        sizes = [1 if bit in self.settled else 2 for bit in left]
        cols = term.shape[-1]
        piece = lax.dynamic_slice(term, starts + [start, 0], sizes + [self.size, cols])
        open_bits = [2] * (len(self.bits) - len(self.settled))
        return piece.reshape(open_bits + [self.size, cols]).astype(F32)

    def split(self, bit):
        self.settled.append(bit)
        return sum(self.take(term, start, left, bit) for term, left, start in self.terms).astype(
            BF16
        )

    def total(self):
        return sum(self.take(term, start, left, None) for term, left, start in self.terms)


def exchange(block, axis, bit):
    count = lax.axis_size(axis)
    return lax.ppermute(block, axis, [(i, i ^ (1 << bit)) for i in range(count)])


def join(*items):
    return lax.optimization_barrier(items)


def angle_table(span):
    half = HEAD // 2
    freqs = np.exp(-math.log(10000.0) * np.arange(half, dtype=np.float32) / half)
    phase = np.arange(span, dtype=np.float32)[:, None] * freqs.astype(np.float32)[None, :]
    cos_part, sin_part = np.cos(phase), np.sin(phase)
    return np.stack(
        [
            np.concatenate([cos_part] * 4, axis=1),
            np.concatenate([-sin_part, sin_part] * 2, axis=1),
        ]
    ).astype(np.float32)


def per_device(
    ends_in,
    lengths,
    times,
    norm_gain,
    attend_in,
    attend_out,
    time_weight,
    time_bias,
    expand_weight,
    expand_bias,
    reduce_weight,
    reduce_bias,
):
    local = ends_in[0]
    micro = lengths.shape[1]
    assert micro == 2
    width = local.shape[1]
    span = local.shape[0] // micro
    hidden = expand_weight.shape[2]
    count = lax.axis_size("rep")
    section = lax.axis_index("section")
    rank = lax.axis_index("rep")
    core = rank & 1
    steps = jnp.exp(-math.log(10000.0) * jnp.arange(EMB // 2, dtype=F32) / (EMB // 2))
    turn = times.reshape(micro * SEGS, 1).astype(F32) * steps
    embed = jnp.concatenate([jnp.cos(turn), jnp.sin(turn)], axis=1)
    mods = jnp.dot(embed, time_weight[0].astype(F32), precision=lax.Precision.HIGHEST)
    fused = width // count % 16 == 0 and TILE % (hidden // count) == 0 and count >= 16
    common = Bag(
        args=(
            lengths[0],
            section.reshape(1),
            core.reshape(1),
            mods,
            time_bias,
            jnp.asarray(angle_table(span)),
            norm_gain,
            expand_bias,
            reduce_bias,
        ),
        sizes=(span, width, hidden, count),
        tokens=local.shape[0],
        cores=2 if fused else 1,
    )
    weights = Bag(
        win=attend_in[0], wout=attend_out[0], wex=expand_weight[0], wre=reduce_weight[0]
    )
    rows = [(local, slot * span) for slot in range(micro)]
    same = lambda *names: {name: name for name in names}
    whole = same("left", "bg", "pa", "jg")
    run = partial(stage, common=common)
    both = (forward, output, mlp, copy_agrad, attend)
    over = lambda block, route: lax.ppermute(block, "section", route)
    swap = lambda block, bit: exchange(block, "rep", bit)
    a = run(
        "first_0",
        parts=(forward,),
        who=0,
        slot=0,
        loads=dict(xv=rows[0], **weights),
        stores=dict(result="leave"),
        kept=False,
    )
    came_0 = over(a.leave, [(0, 1)])
    b = run(
        "first_1",
        parts=(forward,),
        who=0,
        slot=1,
        loads=dict(xv=rows[1], **weights),
        stores=same("result", "left", "qkv", "probs", "middle", "slope", "branch"),
        after=(a.leave,),
        heads_step=1,
    )
    came_1 = over(b.result, [(0, 1)])
    x = run(
        "second_0",
        parts=both,
        who=1,
        slot=0,
        loads=dict(xv=came_0, dyv=rows[0], **weights),
        stores=dict(whole, result=("ends", 0), leave="leave"),
        after=(b.result,),
        heads_step=6,
    )
    back_0 = over(x.leave, [(1, 0)])
    y = run(
        "second_1",
        parts=both,
        who=1,
        slot=1,
        loads=dict(xv=came_1, dyv=rows[1], **weights),
        stores=dict(whole, result=("ends", span), leave="leave"),
        carried=dict(b, ends=x.ends),
        after=(x.leave,),
        heads_step=6,
    )
    back_1 = over(y.leave, [(1, 0)])
    gates = mods[SEGS : 2 * SEGS, 2 * width :] + time_bias[:, 2 * width :].astype(F32)
    gates = jnp.where(lengths[0, 1, 0] == span, gates[:1], gates)
    after = (y.leave, gates)
    if fused:
        turned, _ = join(embed.T, y.leave)
        embeds = (turned, swap(turned, 0))
        after += (embeds[1],)
    x = run(
        "back_0",
        parts=both,
        who=0,
        slot=0,
        loads=dict(xv=rows[0], dyv=back_0, **weights),
        stores=dict(whole, leave=("ends", 0)),
        carried=dict(x, ends=y.ends),
        after=after,
        heads_step=2,
    )
    if fused:
        y_left = swap(y.left_send, 0)
        back_1, x_send, x_bg = join(back_1, x.left_send, x.bg)
        lefts = [x.left, y.left, swap(x_send, 0), y_left]
        others = [swap(item, 0) for item in (x_bg, x.pa, x.jg)]
    cotan = back_1.astype(F32).reshape(SEGS, -1, width)
    made = (cotan * gates[:, None]).reshape(span, width).astype(BF16)
    bg_1 = jnp.where(section == 0, made, y.bg)
    after = ()
    if fused:
        bg_1_other = swap(bg_1, 0)
        after = (bg_1_other, others[0], lefts[2], lefts[3])
    part = run(
        "back_1_mlp",
        parts=(mlp,),
        who=0,
        slot=1,
        loads=dict(
            bg=bg_1,
            wre=weights.wre,
            slope=b.slope,
            wex=weights.wex,
            middle=b.middle,
            dyv=back_1,
            branch=b.branch,
        ),
        stores=same("pa", "middle_grad"),
        carried=y,
        after=after,
        pieces=dict(wre=(0, hidden // width), slope=(1, hidden // width), wex=(1, hidden // width)),
    )
    pa_1 = part.pa
    bits = bits_of(count)
    term = partial(term_call, sizes=common.sizes, core=core, rank=rank)
    lines = width // count
    deep = EMB // count
    sizes = (hidden // count, hidden // count + lines + 3 * deep + TAIL_ROWS, 3 * lines + GAIN_ROWS)
    bases = left_bases(width, hidden)

    def last_attend(after):
        return run(
            "back_1_attend",
            parts=(attend,),
            who=0,
            slot=1,
            loads=dict(
                agrad=(pa_1, None, (hidden, width)),
                wout=weights.wout,
                probs=b.probs,
                qkv=b.qkv,
                win=weights.win,
                xv=rows[1],
                middle_grad=part.middle_grad,
            ),
            stores=dict(jg="jg", leave=("ends", span)),
            carried=dict(y, ends=x.ends),
            after=after,
            heads_step=6,
        )

    def pair_of(size, first):
        cut = size // 2 if fused else size // 32 * 16
        one = Chunk("rep", bits, cut, (1,) if fused else ())
        two = Chunk("rep", bits, size - cut, (2,) if fused else ())
        if fused:
            send_1, keep_1, send_2, keep_2 = first
            one.add(keep_1)
            two.add(keep_2)
            return one, two, send_1, send_2
        view = first.reshape((count // 2, 2) + first.shape[1:])
        cut = lambda at: lax.dynamic_index_in_dim(view, at, 1, keepdims=False)
        came = swap(cut(1 - core).astype(BF16), 0)
        for item in (cut(core), came):
            one.add(item)
            two.add(item, one.size)
        return one, two, one.split(1), two.split(2)

    if fused:
        pa_other = swap(pa_1, 0)
        sent = term(
            "term_reduce",
            term_reduce,
            lines=sizes[0],
            base=bases[0],
            rows=hidden // 2,
            lefts=lefts,
            rights=[x.bg, bg_1, others[0], bg_1_other],
            after=(pa_1,),
        )
        r1, r2, send_1, send_2 = pair_of(sizes[0], sent)
        came_r1, came_r2 = swap(send_1, 1), swap(send_2, 2)
        sent = term(
            "term_expand",
            term_expand,
            lines=sizes[1],
            base=bases[1],
            rows=width,
            lefts=lefts,
            rights=[x.pa, pa_1, others[1], pa_other],
            embeds=embeds,
            after=(send_1, send_2),
        )
        came_r1, came_r2, *sent = join(came_r1, came_r2, *sent)
        e1, e2, send_1, send_2 = pair_of(sizes[1], sent)
        came_e1, came_e2 = swap(send_1, 1), swap(send_2, 2)
        last = last_attend((send_1, send_2))
        jg_1 = last.jg
        jg_other = swap(jg_1, 0)
        came_r1, came_r2, _ = join(came_r1, came_r2, jg_1)
        r1.add(came_r1)
        r2.add(came_r2)
        send_3, send_4 = r1.split(2), r2.split(1)
        came_r1, came_r2 = swap(send_3, 2), swap(send_4, 1)
        came_e1, came_e2, _, _ = join(came_e1, came_e2, send_3, send_4)
        e1.add(came_e1)
        e2.add(came_e2)
        send_1, send_2 = e1.split(2), e2.split(1)
        came_e1, came_e2 = swap(send_1, 2), swap(send_2, 1)
        sent = term(
            "term_attend",
            term_attend,
            lines=sizes[2],
            base=bases[3],
            rows=width // 2,
            lefts=lefts,
            rights=[x.jg, jg_1, others[2], jg_other],
            after=(send_1, send_2, send_3, send_4),
        )
        came_r1, came_r2, *sent = join(came_r1, came_r2, *sent)
        a1, a2, send_1, send_2 = pair_of(sizes[2], sent)
    else:
        last = last_attend(())
        rights = [(x.bg, bg_1), (x.pa, pa_1), (x.jg, last.jg)]
        totals = plain_pieces((x.left, y.left), rights, embed.T, common.sizes)
        r1, r2, send_1, send_2 = pair_of(sizes[0], totals[0])
        r1.add(swap(send_1, 1))
        r2.add(swap(send_2, 2))
        came_r1, came_r2 = swap(r1.split(2), 2), swap(r2.split(1), 1)
        e1, e2, send_1, send_2 = pair_of(sizes[1], totals[1])
        e1.add(swap(send_1, 1))
        e2.add(swap(send_2, 2))
        came_e1, came_e2 = swap(e1.split(2), 2), swap(e2.split(1), 1)
        a1, a2, send_1, send_2 = pair_of(sizes[2], totals[2])
    ends = last.ends
    came_a1, came_a2 = swap(send_1, 1), swap(send_2, 2)
    r1.add(came_r1)
    r2.add(came_r2)
    block_r = jnp.concatenate([r1.split(3), r2.split(3)], axis=-2)
    came_r = swap(block_r, 3)
    came_e1, came_e2, _ = join(came_e1, came_e2, block_r)
    e1.add(came_e1)
    e2.add(came_e2)
    block_e = jnp.concatenate([e1.split(3), e2.split(3)], axis=-2)
    came_e = swap(block_e, 3)
    came_a1, came_a2, _ = join(came_a1, came_a2, block_e)
    a1.add(came_a1)
    a2.add(came_a2)
    send_1, send_2 = a1.split(2), a2.split(1)
    came_a1, came_a2 = swap(send_1, 2), swap(send_2, 1)
    a1.add(came_a1)
    a2.add(came_a2)
    block_a = jnp.concatenate([a1.split(3), a2.split(3)], axis=-2)
    came_a = swap(block_a, 3)
    came_r, _ = join(came_r, send_1)
    r1.add(came_r[..., : r1.size, :])
    r2.add(came_r[..., r1.size :, :])
    came_e, _ = join(came_e, block_a)
    e1.add(came_e[..., : e1.size, :])
    e2.add(came_e[..., e1.size :, :])
    a1.add(came_a[..., : a1.size, :])
    a2.add(came_a[..., a1.size :, :])
    for bit in range(4, bits):
        for chunk in (r1, r2, e1, e2, a1, a2):
            chunk.add(swap(chunk.split(bit), bit))
    share_r, share_e, share_a = (
        jnp.concatenate([one.total(), two.total()]) for one, two in ((r1, r2), (e1, e2), (a1, a2))
    )
    tall = hidden // width
    side = lambda item, n, size: jnp.concatenate(
        [item[i * size : (i + 1) * size] for i in range(n)], axis=1
    )
    at_o = tall * lines
    at_t = at_o + lines
    small = share_e[at_t + 3 * deep :]
    flat = lambda item, first, n: lax.dynamic_slice_in_dim(
        item[first : first + n].reshape(-1), rank * (n * width // count), n * width // count
    )
    results = (
        flat(share_a, 3 * lines, 1),
        side(share_a, 3, lines),
        share_e[at_o:at_t],
        side(share_e[at_t:], 3, deep),
        flat(small, 1, 3),
        side(share_e, tall, lines),
        flat(small, 4, tall),
        share_r,
        flat(small, 0, 1),
    )
    return (ends[None],) + tuple(piece[None] for piece in results)


def solution(mesh):
    return jax.shard_map(
        per_device,
        mesh=mesh,
        in_specs=(
            P("section", "rep", None),
            P("rep", None, None),
            P("rep", None, None),
            P("section", None),
            P("section", None, None),
            P("section", None, None),
            P("section", None, None),
            P("section", None),
            P("section", None, None),
            P("section", None),
            P("section", None, None),
            P("section", None),
        ),
        out_specs=(
            P("section", "rep", None),
            P("section", "rep"),
            P("section", "rep", None),
            P("section", "rep", None),
            P("section", "rep", None),
            P("section", "rep"),
            P("section", "rep", None),
            P("section", "rep"),
            P("section", "rep", None),
            P("section", "rep"),
        ),
        check_vma=False,
    )
```

```python
from functools import partial
import inspect
import math

import jax
import jax.numpy as jnp
import numpy as np
from jax import lax
from jax.experimental import pallas as pl
from jax.experimental.pallas import tpu as pltpu
from jax.sharding import PartitionSpec as P

HEADS = 12
HEAD = 64
EMB = 128
SEGS = 4
ANY = pl.ANY
VMEM = pltpu.MemorySpace.VMEM
SMEM = pltpu.MemorySpace.SMEM
F32 = jnp.float32
BF16 = jnp.bfloat16
ROOT_HALF = 0.7071067811865476
ROOT_TAU = 0.3989422804014327
TILE = 384
TAIL_ROWS = 24
GAIN_ROWS = 16
EXTRA = 16


class Bag(dict):
    __getattr__ = dict.__getitem__


def dot(left, right, left_dim=1, right_dim=0):
    return lax.dot_general(
        left, right, (((left_dim,), (right_dim,)), ((), ())), preferred_element_type=F32
    )


def repeat(count, body):
    for i in range(count):
        body(i)


def steps_of(count, size, body):
    def several(i, _):
        for j in range(size):
            body(size * i + j)
        return _

    lax.fori_loop(0, count // size, several, 0)


def lanes(index, size, start=0):
    if isinstance(index, int):
        return slice(start + index * size, start + (index + 1) * size)
    return pl.ds(pl.multiple_of(start + index * size, size), size)


def swap_halves(values, low_half):
    forth = pltpu.roll(values, 128 - HEAD // 2, 1)
    back = pltpu.roll(values, HEAD // 2, 1)
    return jnp.where(low_half, forth, back)


def norm_parts(values):
    center = values - jnp.mean(values, axis=-1, keepdims=True)
    spread = jnp.mean(center * center, axis=-1, keepdims=True)
    factor = lax.rsqrt(spread + 1e-05)
    return center * factor, factor


def norm_back(grad, unit, factor):
    return factor * (
        grad
        - jnp.mean(grad, axis=-1, keepdims=True)
        - unit * jnp.mean(grad * unit, axis=-1, keepdims=True)
    )


class Held:
    def __init__(self, bufs, loads, stores, sems, pieces):
        self.bufs = bufs
        self.loads = loads
        self.stores = stores
        self.sems = sems
        self.pieces = pieces
        self.names = {id(buf): name for name, buf in bufs.items()}
        keys = [(name, j) for name in loads for j in range(self.parts_of(name))]
        self.spots = {key: n for n, key in enumerate(keys)}
        self.waiting = set(keys)
        self.pending = set(keys)
        self.leaving = {}

    def parts_of(self, name):
        return self.pieces[name][1] if name in self.pieces else 1

    def load(self, name, j):
        source, target = self.loads[name], self.bufs[name]
        if name in self.pieces:
            axis, count = self.pieces[name]
            size = target.shape[axis] // count
            at = (slice(None),) * axis + (pl.ds(j * size, size),)
            source, target = source.at[at], target.at[at]
        return pltpu.make_async_copy(source, target, self.sems.at[self.spots[(name, j)]])

    def store(self, name, n):
        at, target = self.stores[name][n]
        source = self.bufs[name] if at is None else self.bufs[name].at[at]
        return pltpu.make_async_copy(source, target, self.sems.at[self.leaving[(name, n)]])

    def keys(self, bufs, part):
        for buf in bufs:
            name = self.names[id(buf)]
            for j in range(self.parts_of(name)):
                if part in (None, j):
                    yield name, j

    def begin(self, *bufs, part=None):
        for key in self.keys(bufs, part):
            if key in self.waiting:
                self.waiting.remove(key)
                self.load(*key).start()

    def need(self, *bufs, part=None):
        self.begin(*bufs, part=part)
        for key in self.keys(bufs, part):
            if key in self.pending:
                self.pending.remove(key)
                self.load(*key).wait()

    def done(self, *bufs):
        for buf in bufs:
            name = self.names[id(buf)]
            for n in range(len(self.stores.get(name, ()))):
                self.leaving[(name, n)] = len(self.spots) + len(self.leaving)
                self.store(name, n).start()

    def finish(self):
        for name, n in self.leaving:
            self.store(name, n).wait()


class Layer:
    def __init__(self, sizes, slot, refs):
        self.span, self.width, self.hidden, self.count = sizes
        self.slot = slot
        (
            lengths, section, core, self.mods, self.tbias, self.trig, self.gain, self.ebias,
            self.rbias,
        ) = refs
        self.section = section[0]
        self.core = core[0]
        self.single = lengths[slot, 0] == self.span
        self.pairs = self.width // 128
        self.seg = self.span // SEGS
        self.step = self.width
        self.tiles = self.hidden // self.step
        place = lax.broadcasted_iota(jnp.int32, (self.span, 128), 1)
        self.low_half = place % HEAD < HEAD // 2
        self.low_head = place < HEAD
        row = lax.broadcasted_iota(jnp.int32, (1, 128), 1) // HEAD
        self.head_row = [(row == i).astype(F32).astype(BF16) for i in range(2)]
        self.blocks = [(b, slice(b * self.seg, (b + 1) * self.seg)) for b in range(SEGS)]

    def trig_pair(self):
        cos_all, sin_all = self.trig[0], self.trig[1]
        cos_cut = jnp.concatenate([cos_all[: self.seg]] * SEGS, axis=0)
        sin_cut = jnp.concatenate([sin_all[: self.seg]] * SEGS, axis=0)
        return jnp.where(self.single, cos_all, cos_cut), jnp.where(self.single, sin_all, sin_cut)

    def mod_row(self, block, part):
        row = self.slot * SEGS + jnp.where(self.single, 0, block)
        at = slice(part * self.width, (part + 1) * self.width)
        return self.mods[pl.ds(row, 1), at] + self.tbias[:, at].astype(F32)

    def add_segment(self, small, block, at, sums):
        row = 2 + jnp.where(self.single, 0, block)
        small[pl.ds(row, 1), at * self.width : (at + 1) * self.width] += sums

    def side(self, block):
        return self.core if block % 2 == 0 else 1 - self.core

    def put_left(self, left, base, values):
        turned = values.T
        if left.shape[0] == 1:
            left[0, 2 * base : 2 * base + self.width] = turned
            return
        lines = self.width // self.count
        for block in range(self.count):
            to = base + block // 2 * lines
            left[self.side(block), to : to + lines] = turned[block * lines : (block + 1) * lines]

    def put_active(self, left, j, values):
        turned = values.T
        if left.shape[0] == 1:
            left[0, lanes(j, self.step)] = turned
            return
        lines = self.hidden // self.count
        per = self.step // lines
        for n in range(per):
            to = lanes(j, lines * (per // 2), n // 2 * lines)
            to = slice(to.start, to.start + lines) if isinstance(j, int) else pl.ds(to.start, lines)
            left[self.side(n), to] = turned[n * lines : (n + 1) * lines]

    def thirds(self, index):
        return [lanes(index, 128, p * self.width) for p in range(3)]


def left_bases(width, hidden):
    return 0, hidden // 2, (hidden + width) // 2, (hidden + 2 * width) // 2


def forward(
    k, xv, win, wout, wex, wre, left, qkv, probs, middle, slope, branch, result, bias, normed,
    mixed, modded,
):
    span, width, held = k.span, k.width, k.held
    _, at_modded, at_mixed, at_normed = left_bases(width, k.hidden)
    held.begin(xv, win)
    held.need(xv)
    unit, _ = norm_parts(xv[...].astype(F32))
    normed[...] = (unit * k.gain[...].astype(F32)).astype(BF16)
    across = lax.broadcasted_iota(jnp.int32, (span, span), 0) // k.seg
    down = lax.broadcasted_iota(jnp.int32, (span, span), 1) // k.seg
    bias[...] = jnp.where((across == down) | k.single, 0.0, -1e30)
    held.need(win)
    held.begin(wout, wex, wre)
    cos_part, sin_part = k.trig_pair()
    for tile, factor in ((0, 0.125), (1, 1.0)):
        for i in range(width // 256):
            at = lanes(i, 256, tile * width)
            joint = dot(normed[...], win[:, at])
            outs = []
            for piece in (joint[:, :128], joint[:, 128:]):
                turned = piece * cos_part + swap_halves(piece, k.low_half) * sin_part
                outs.append((turned * factor).astype(BF16))
            qkv[:, at] = jnp.concatenate(outs, axis=1)
    qkv[:, 2 * width :] = dot(normed[...], win[:, 2 * width :]).astype(BF16)
    held.done(qkv)
    if k.kept:
        k.put_left(left, at_normed, normed[...])

    def heads(i):
        at = k.thirds(i)
        query, key, value = (qkv[:, a] for a in at)
        outs = []
        for h in range(2):
            scores = dot(key * k.head_row[h], query, 1, 1) + bias[...]
            top = jnp.max(scores, axis=0, keepdims=True)
            raised = jnp.exp(scores - top)
            total = jnp.sum(raised, axis=0, keepdims=True)
            prob = raised * (1.0 / total)
            if k.kept:
                probs[2 * i + h] = prob
            outs.append(dot(prob.astype(BF16), value, 0, 0))
        mixed[:, at[0]] = jnp.where(k.low_head, outs[0], outs[1]).astype(BF16)

    steps_of(k.pairs, k.heads_step, heads)
    held.done(probs)
    held.need(wout)
    middle[...] = xv[...].astype(F32) + dot(mixed[...], wout[...])
    held.done(middle)
    if k.kept:
        k.put_left(left, at_mixed, mixed[...])
    for b, rows in k.blocks:
        unit, _ = norm_parts(middle[rows])
        modded[rows] = (unit * (1.0 + k.mod_row(b, 0)) + k.mod_row(b, 1)).astype(BF16)
    if k.kept:
        k.put_left(left, at_modded, modded[...])
    held.need(wex, wre)
    branch[...] = jnp.broadcast_to(k.rbias[...].astype(F32), (span, width))

    def feed(j):
        at = lanes(j, k.step)
        pre = dot(modded[...], wex[:, at]) + k.ebias[:, at].astype(F32)
        area = 0.5 + 0.5 * lax.erf(pre * ROOT_HALF)
        out = (pre * area).astype(BF16)
        if k.kept:
            slope[:, at] = area + pre * (jnp.exp(pre * pre * -0.5) * ROOT_TAU)
            k.put_active(left, j, out)
        branch[...] += dot(out, wre[at, :])

    if k.heads_step == 1:
        steps_of(k.tiles, 1, feed)
    else:
        repeat(k.tiles, feed)
    held.done(slope, left, branch)
    for b, rows in k.blocks:
        result[rows] = (middle[rows] + k.mod_row(b, 2) * branch[rows]).astype(BF16)
    held.done(result)


def output(k, dyv, bg):
    k.held.need(dyv)
    for b, rows in k.blocks:
        bg[rows] = (dyv[rows].astype(F32) * k.mod_row(b, 2)).astype(BF16)
    k.held.done(bg)


def mlp(k, wre, wex, bg, slope, middle, branch, dyv, pa, middle_grad, small, acc):
    span, width, hidden, held = k.span, k.width, k.hidden, k.held
    small[...] = jnp.zeros(small.shape, F32)
    acc[...] = jnp.zeros(acc.shape, F32)
    held.begin(bg)
    for j in range(k.tiles):
        held.begin(wre, slope, wex, part=j)
    held.begin(middle, dyv, branch)
    held.need(bg)

    def feed(j):
        at = lanes(j, k.step)
        held.need(wre, slope, wex, part=j)
        grad = dot(bg[...], wre[at, :], 1, 1)
        pre_grad = (slope[:, at] * grad).astype(BF16)
        pa[:span, at] = pre_grad
        small[0:1, at] = jnp.sum(pre_grad.astype(F32), axis=0, keepdims=True)
        acc[...] += dot(pre_grad, wex[:, at], 1, 1)

    repeat(k.tiles, feed)
    held.need(middle, dyv, branch)
    total = jnp.zeros((1, width), F32)
    for b, rows in k.blocks:
        cotan = dyv[rows].astype(F32)
        total += jnp.sum(bg[rows].astype(F32), axis=0, keepdims=True)
        grad = acc[rows]
        unit, factor = norm_parts(middle[rows])
        k.add_segment(small, b, 0, jnp.sum(grad * unit, axis=0, keepdims=True))
        k.add_segment(small, b, 1, jnp.sum(grad, axis=0, keepdims=True))
        k.add_segment(small, b, 2, jnp.sum(cotan * branch[rows], axis=0, keepdims=True))
        back = norm_back(grad * (1.0 + k.mod_row(b, 0)), unit, factor)
        full = cotan + back
        middle_grad[rows] = full
        pa[rows, hidden:] = full.astype(BF16)
    small[1:2, :width] = total
    pa[span:, :] = small[...].astype(BF16)
    held.done(pa, middle_grad)


def attend(
    k, wout, win, agrad, probs, qkv, xv, middle_grad, jg, leave, mixed_grad, acc
):
    span, held = k.span, k.held
    held.need(agrad, wout)
    held.begin(probs, qkv)
    mixed_grad[...] = dot(agrad[...], wout[...], 1, 1).astype(BF16)
    held.need(probs, qkv)
    held.begin(win, xv, middle_grad)
    cos_part, sin_part = k.trig_pair()

    def heads(i):
        at = k.thirds(i)
        query, key, value = (qkv[:, a] for a in at)
        out_grad = mixed_grad[:, at[0]]
        parts = []
        for h in range(2):
            prob = probs[2 * i + h]
            pull = dot(value * k.head_row[h], out_grad, 1, 1)
            shared = jnp.sum(prob * pull, axis=0, keepdims=True)
            score_grad = (prob * (pull - shared)).astype(BF16)
            parts.append(
                (
                    dot(score_grad, key, 0, 0),
                    dot(score_grad, query),
                    dot(prob.astype(BF16), out_grad),
                )
            )
        for p in range(3):
            grad = jnp.where(k.low_head, parts[0][p], parts[1][p])
            if p < 2:
                grad = grad * cos_part - swap_halves(grad, k.low_half) * sin_part
                if p == 0:
                    grad = grad * 0.125
            jg[:span, at[p]] = grad.astype(BF16)

    steps_of(k.pairs, k.heads_step, heads)
    held.need(win, xv, middle_grad)
    acc[...] = dot(jg[:span, :], win[...], 1, 1)
    total = jnp.zeros((1, k.width), F32)
    for b, rows in k.blocks:
        grad = acc[rows]
        unit, factor = norm_parts(xv[rows].astype(F32))
        total += jnp.sum(grad * unit, axis=0, keepdims=True)
        back = norm_back(grad * k.gain[...].astype(F32), unit, factor)
        leave[rows] = (middle_grad[rows] + back).astype(BF16)
    below = jnp.concatenate([total, jnp.zeros((EXTRA - 1, k.width), F32)], axis=0)
    jg[span:, : k.width] = below.astype(BF16)
    jg[span:, k.width :] = jnp.zeros((EXTRA, 2 * k.width), BF16)
    held.done(jg, leave)


def copy_agrad(k, pa, agrad):
    agrad[...] = pa[: k.span, k.hidden :]


class Sums:
    def __init__(self, ranks, full, outs, sems):
        self.full = full
        self.own = [((ranks[0] >> bit) & 1) == 0 for bit in (1, 2)]
        self.bufs = outs[:4]
        self.targets = outs[4:]
        self.sems = sems
        self.half = full.shape[1] // 2
        self.copies = []

    def put(self, block, at, values):
        self.full[block, at] = values

    def settle(self, which, groups):
        send, keep = self.bufs[2 * which : 2 * which + 2]
        at = slice(which * self.half, (which + 1) * self.half)
        apart = 1 + which
        for group in groups:
            for n in range(2):
                first = 4 * group + (2 * n if which == 0 else n)
                even, odd = self.full[first, at], self.full[first + apart, at]
                send[2 * group + n] = jnp.where(self.own[which], odd, even).astype(BF16)
                keep[2 * group + n] = jnp.where(self.own[which], even, odd)
            spot = pl.ds(2 * group, 2)
            for n in range(2 * which, 2 * which + 2):
                copy = pltpu.make_async_copy(
                    self.bufs[n].at[spot], self.targets[n].at[spot], self.sems.at[len(self.copies)]
                )
                copy.start()
                self.copies.append(copy)

    def finish(self):
        for copy in self.copies:
            copy.wait()


def term_reduce(k, sums, left, right):
    lines = k.hidden // k.count
    per = TILE // lines
    for tile in range(k.hidden // 2 // TILE):
        k.arrive(tile)
        total = dot(left[tile * TILE : (tile + 1) * TILE], right[...])
        for n in range(per):
            sums.put(tile * per + n, slice(0, lines), total[n * lines : (n + 1) * lines])
        if (tile + 1) * per % 4 == 0:
            group = ((tile + 1) * per // 4 - 1,)
            sums.settle(0, group)
            sums.settle(1, group)


def square_terms(k, sums, left, right, cols, part):
    lines = k.width // k.count
    total = dot(left, right[: 4 * k.span, cols])
    for n in range(k.count // 2):
        sums.put(n, slice(part * lines, (part + 1) * lines), total[n * lines : (n + 1) * lines])


def term_expand(k, sums, left, right):
    width, hidden, span = k.width, k.hidden, k.span
    groups = range(k.count // 8)
    tall = hidden // width
    lines = width // k.count
    rows = width // 2
    half = sums.half
    settled = False
    for col in range(tall + 1):
        k.arrive(col)
        part = left[:rows] if col < tall else left[rows:]
        square_terms(k, sums, part, right, slice(col * width, (col + 1) * width), col)
        if (col + 1) * lines >= half and not settled:
            sums.settle(0, groups)
            settled = True
    smalls = [k.small[n].astype(F32) for n in range(4)]
    angles = jnp.concatenate([embed[...] for embed in k.embeds], axis=1)
    pieces = []
    for _ in range(3):
        pieces.append(angles.astype(BF16))
        angles = angles - pieces[-1].astype(F32)
    seqs = jnp.concatenate([small[2 : 2 + SEGS, : 3 * width] for small in smalls]).astype(BF16)
    times = sum(dot(piece, seqs) for piece in pieces)
    both = sum(smalls)
    seq_sum = jnp.sum(both[2 : 2 + SEGS, : 3 * width], axis=0, keepdims=True)
    lines_v = k.lines
    lines_v[...] = jnp.zeros(lines_v.shape, F32)
    lines_v[0:1] = both[1:2, :width]
    for n in range(3):
        lines_v[1 + n : 2 + n] = seq_sum[:, n * width : (n + 1) * width]
    for n in range(tall):
        lines_v[4 + n : 5 + n] = both[0:1, n * width : (n + 1) * width]
    deep = EMB // k.count
    first = (tall + 1) * lines
    low = k.core == 0
    for g in range(k.count // 2):
        for p in range(3):
            at = slice(p * width, (p + 1) * width)
            even = times[2 * g * deep : (2 * g + 1) * deep, at]
            odd = times[(2 * g + 1) * deep : (2 * g + 2) * deep, at]
            to = first + p * deep
            sums.put(g, slice(to, to + deep), jnp.where(low, even, odd))
        sums.put(g, slice(first + 3 * deep, 2 * half), lines_v[...])
    sums.settle(1, groups)


def term_attend(k, sums, left, right):
    width = k.width
    groups = range(k.count // 8)
    lines = width // k.count
    settled = False
    for col in range(3):
        k.arrive(col)
        square_terms(k, sums, left[...], right, slice(col * width, (col + 1) * width), col)
        if (col + 1) * lines >= sums.half and not settled:
            sums.settle(0, groups)
            settled = True
    gain = sum(k.small[n].astype(F32) for n in range(4))[:, :width]
    for g in range(k.count // 2):
        sums.put(g, slice(3 * lines, 3 * lines + GAIN_ROWS), gain)
    sums.settle(1, groups)


def load_terms(k, refs, bufs, base, sems):
    left_v, right_v, small_v = bufs
    rows, cols = left_v.shape[0], right_v.shape[1]
    tall = rows // TILE if small_v is None else 1
    wide = cols // k.width
    groups = []
    for i in range(tall):
        for j in range(wide):
            copies = []
            for n, (left, right) in enumerate(zip(refs[:4], refs[4:8])):
                tokens = pl.ds(n * k.span, k.span)
                part = pl.ds(i * (rows // tall), rows // tall)
                from_part = pl.ds(base + i * (rows // tall), rows // tall)
                at = pl.ds(j * k.width, k.width)
                if j == 0:
                    copies.append((left.at[from_part], left_v.at[part, tokens]))
                if i == 0:
                    copies.append((right.at[pl.ds(0, k.span), at], right_v.at[tokens, at]))
                if small_v is not None and j == wide - 1:
                    copies.append((right.at[pl.ds(k.span, EXTRA)], small_v.at[n]))
            groups.append(copies)
    made, count = [], 0
    for copies in groups:
        made.append([])
        for pair in copies:
            made[-1].append(pltpu.make_async_copy(*pair, sems.at[count]))
            made[-1][-1].start()
            count += 1
    return made


class Terms:
    def __init__(self, sizes, core):
        self.span, self.width, self.hidden, self.count = sizes
        self.core = core[0]

    def arrive(self, group):
        for copy in self.groups[group]:
            copy.wait()


def term_kernel(sizes, body, base, extra, *refs):
    refs = list(refs)
    core, rank = refs[:2]
    k = Terms(sizes, core)
    pos = 2
    if body is term_expand:
        k.embeds = refs[pos : pos + 2]
        pos += 2
    sources = refs[pos : pos + 8]
    pos += 8 + extra
    targets = refs[pos : pos + 4]
    pos += 4
    left_v, right_v, full, *outs = refs[pos : pos + 7]
    pos += 7
    k.small = None
    if body is not term_reduce:
        k.small, k.lines = refs[pos : pos + 2]
        pos += 2
    sems, out_sems = refs[pos:]
    k.groups = load_terms(k, sources, (left_v, right_v, k.small), base, sems)
    sums = Sums(rank, full, outs + targets, out_sems)
    body(k, sums, left_v, right_v)
    sums.finish()


def term_call(name, body, sizes, lines, base, rows, core, rank, lefts, rights, embeds=(), after=()):
    span, width, hidden, count = sizes
    blocks = count // 2
    cols = rights[0].shape[1]
    half = lines // 2
    outs = [((blocks // 2, half, width), kind) for kind in (BF16, F32)] * 2
    scratch = [
        ((rows, 4 * span), BF16),
        ((4 * span, cols), BF16),
        ((blocks, lines, width), F32),
        *outs,
    ]
    if body is not term_reduce:
        scratch += [((4, EXTRA, cols), BF16), ((TAIL_ROWS, width), F32)]
    args = [core.reshape(1), rank.reshape(1), *embeds, *lefts, *rights, *after]
    in_specs = [pl.BlockSpec(memory_space=SMEM)] * 2
    in_specs += [pl.BlockSpec(memory_space=VMEM)] * len(embeds)
    in_specs += [pl.BlockSpec(memory_space=ANY)] * (8 + len(after))
    return pl.pallas_call(
        partial(term_kernel, sizes, body, base, len(after)),
        out_shape=[jax.ShapeDtypeStruct(*item) for item in outs],
        in_specs=in_specs,
        out_specs=[pl.BlockSpec(memory_space=ANY)] * 4,
        scratch_shapes=[pltpu.VMEM(*item) for item in scratch]
        + [pltpu.SemaphoreType.DMA((32,)), pltpu.SemaphoreType.DMA((8,))],
        compiler_params=pltpu.CompilerParams(vmem_limit_bytes=62 * 1024 * 1024),
        name=name,
    )(*args)


def plain_pieces(lefts, rights, embed, sizes):
    span, width, hidden, count = sizes
    bg, pa, jg = rights
    bases = [2 * base for base in left_bases(width, hidden)]

    def blocks(base, rows, right):
        total = sum(dot(a[base : base + rows], b) for a, b in zip(lefts, right))
        parts = [total[:, i : i + width] for i in range(0, total.shape[1], width)]
        return [part.reshape(count, -1, width) for part in parts]

    take = lambda items, cols: [item[:span, cols] for item in items]
    reduce = blocks(bases[0], hidden, bg)
    expand = blocks(bases[1], width, take(pa, slice(0, hidden)))
    expand += blocks(bases[2], width, take(pa, slice(hidden, hidden + width)))
    last = blocks(bases[3], width, take(jg, slice(None)))
    small = [item[span:].astype(F32) for item in pa]
    seqs = jnp.concatenate([item[2 : 2 + SEGS, : 3 * width] for item in small])
    times = jnp.dot(embed, seqs, precision=lax.Precision.HIGHEST)
    expand += [times[:, i * width : (i + 1) * width].reshape(count, -1, width) for i in range(3)]
    lines = jnp.concatenate(
        [
            sum(item[1:2, :width] for item in small),
            jnp.sum(seqs, axis=0).reshape(-1, width),
            sum(item[0, :hidden] for item in small).reshape(-1, width),
        ]
    )
    lines = jnp.pad(lines, ((0, TAIL_ROWS - lines.shape[0]), (0, 0)))
    gain = sum(item[span:, :width].astype(F32) for item in jg)
    expand.append(jnp.broadcast_to(lines, (count,) + lines.shape))
    last.append(jnp.broadcast_to(gain, (count,) + gain.shape))
    return [jnp.concatenate(item, axis=1) for item in (reduce, expand, last)]


def shapes_of(span, width, hidden, cores):
    tok = lambda cols, kind=BF16: ((span, cols), kind)
    below = lambda cols: ((span + EXTRA, cols), BF16)
    return dict(
        xv=tok(width),
        dyv=tok(width),
        win=((width, 3 * width), BF16),
        wout=((width, width), BF16),
        wex=((width, hidden), BF16),
        wre=((hidden, width), BF16),
        left=((cores, (hidden + 3 * width) // cores, span), BF16),
        normed=tok(width),
        qkv=tok(3 * width),
        probs=((HEADS, span, span), F32),
        mixed=tok(width),
        middle=tok(width, F32),
        modded=tok(width),
        slope=tok(hidden, F32),
        branch=tok(width, F32),
        result=tok(width),
        bg=tok(width),
        pa=below(hidden + width),
        jg=below(3 * width),
        agrad=tok(width),
        mixed_grad=tok(width),
        middle_grad=tok(width, F32),
        leave=tok(width),
        acc=tok(width, F32),
        bias=tok(span, F32),
        small=((EXTRA, hidden + width), F32),
    )


def uses(part):
    return list(inspect.signature(part).parameters)[1:]


def stage_kernel(sizes, parts, who, slot, plan, *refs):
    refs = list(refs)
    layer = Layer(sizes, slot, refs[:9])
    span = layer.span
    pos = 9
    loads = {}
    for name, row, cols in plan.sources:
        ref = refs[pos]
        if cols is not None:
            ref = ref.at[pl.ds(0, span), pl.ds(*cols)]
        elif row is not None:
            ref = ref.at[pl.ds(row, span)]
        loads[name] = ref
        pos += 1
    pos += plan.extra
    stores = {}
    for name, row, at in plan.targets:
        target = refs[pos] if row is None else refs[pos].at[pl.ds(row, span)]
        stores.setdefault(name, []).append((at, target))
        pos += 1
    bufs = {}
    for name in plan.bufs:
        bufs[name] = refs[pos]
        pos += 1
    layer.held = Held(bufs, loads, stores, refs[pos], plan.pieces)
    layer.kept = plan.kept
    layer.heads_step = plan.heads_step

    @pl.when(layer.section == who)
    def _():
        for part in parts:
            part(layer, *[bufs[name] for name in uses(part)])
        layer.held.finish()


def stage(
    name, common, parts, who, slot, loads, stores, carried=None, after=(), kept=True, heads_step=3,
    pieces=None,
):
    carried = carried or {}
    span, width, hidden, count = common.sizes
    shapes = shapes_of(span, width, hidden, common.cores)
    bufs = []
    for part in parts:
        bufs += [item for item in uses(part) if item not in bufs]
    pair = lambda item: item if isinstance(item, tuple) else (item, None)
    args = list(common.args)
    in_specs = [pl.BlockSpec(memory_space=SMEM)] * 3 + [pl.BlockSpec(memory_space=VMEM)] * 6
    plan = Bag(sources=[], targets=[], bufs=bufs, kept=kept, heads_step=heads_step)
    plan["pieces"] = pieces or {}
    for item in loads:
        if item in bufs:
            array, row, *cols = pair(loads[item])
            args.append(array)
            plan.sources.append((item, row, cols[0] if cols else None))
    outs, aliases, extra = [], {}, []
    targets = []
    for item, key in stores.items():
        if item == "left":
            targets += [(item, key + "_send" * n, None, n) for n in range(common.cores)]
        else:
            targets.append((item, *pair(key), None))
    for i, (item, key, row, at) in enumerate(targets):
        shape, kind = shapes[item]
        if row is not None:
            shape = (common.tokens,) + shape[1:]
        if at is not None:
            shape = shape[1:]
        outs.append(jax.ShapeDtypeStruct(shape, kind))
        plan.targets.append((item, row, at))
        if key in carried:
            aliases[len(args) + len(extra)] = i
            extra.append(carried[key])
    extra += list(after)
    args += extra
    plan["extra"] = len(extra)
    in_specs += [pl.BlockSpec(memory_space=ANY)] * (len(args) - len(in_specs))
    results = pl.pallas_call(
        partial(stage_kernel, common.sizes, parts, who, slot, plan),
        out_shape=outs,
        in_specs=in_specs,
        out_specs=[pl.BlockSpec(memory_space=ANY)] * len(outs),
        input_output_aliases=aliases,
        scratch_shapes=[pltpu.VMEM(*shapes[item]) for item in bufs]
        + [pltpu.SemaphoreType.DMA((32,))],
        compiler_params=pltpu.CompilerParams(vmem_limit_bytes=62 * 1024 * 1024),
        name=name,
    )(*args)
    return Bag({key: value for (_, key, _, _), value in zip(targets, results)})


def bits_of(count):
    bits = count.bit_length() - 1
    assert 1 << bits == count
    return bits


class Chunk:
    def __init__(self, axis, bits, size, settled=()):
        self.axis = axis
        self.bits = list(range(bits - 1, 0, -1))
        self.size = size
        self.settled = list(settled)
        self.terms = []

    def add(self, term, start=0):
        left = [bit for bit in self.bits if bit not in self.settled]
        self.terms.append((term.reshape((2,) * len(left) + term.shape[-2:]), left, start))

    def take(self, term, start, left, flip):
        me = lax.axis_index(self.axis)
        side = lambda bit: 1 - ((me >> bit) & 1) if bit == flip else (me >> bit) & 1
        starts = [side(bit) if bit in self.settled else 0 for bit in left]
        sizes = [1 if bit in self.settled else 2 for bit in left]
        cols = term.shape[-1]
        piece = lax.dynamic_slice(term, starts + [start, 0], sizes + [self.size, cols])
        open_bits = [2] * (len(self.bits) - len(self.settled))
        return piece.reshape(open_bits + [self.size, cols]).astype(F32)

    def split(self, bit):
        self.settled.append(bit)
        return sum(self.take(term, start, left, bit) for term, left, start in self.terms).astype(
            BF16
        )

    def total(self):
        return sum(self.take(term, start, left, None) for term, left, start in self.terms)


def exchange(block, axis, bit):
    count = lax.axis_size(axis)
    return lax.ppermute(block, axis, [(i, i ^ (1 << bit)) for i in range(count)])


def join(*items):
    return lax.optimization_barrier(items)


def angle_table(span):
    half = HEAD // 2
    freqs = np.exp(-math.log(10000.0) * np.arange(half, dtype=np.float32) / half)
    phase = np.arange(span, dtype=np.float32)[:, None] * freqs.astype(np.float32)[None, :]
    cos_part, sin_part = np.cos(phase), np.sin(phase)
    return np.stack(
        [
            np.concatenate([cos_part] * 4, axis=1),
            np.concatenate([-sin_part, sin_part] * 2, axis=1),
        ]
    ).astype(np.float32)


def per_device(
    ends_in,
    lengths,
    times,
    norm_gain,
    attend_in,
    attend_out,
    time_weight,
    time_bias,
    expand_weight,
    expand_bias,
    reduce_weight,
    reduce_bias,
):
    local = ends_in[0]
    micro = lengths.shape[1]
    assert micro == 2
    width = local.shape[1]
    span = local.shape[0] // micro
    hidden = expand_weight.shape[2]
    count = lax.axis_size("rep")
    section = lax.axis_index("section")
    rank = lax.axis_index("rep")
    core = rank & 1
    steps = jnp.exp(-math.log(10000.0) * jnp.arange(EMB // 2, dtype=F32) / (EMB // 2))
    turn = times.reshape(micro * SEGS, 1).astype(F32) * steps
    embed = jnp.concatenate([jnp.cos(turn), jnp.sin(turn)], axis=1)
    mods = jnp.dot(embed, time_weight[0].astype(F32), precision=lax.Precision.HIGHEST)
    fused = width // count % 16 == 0 and TILE % (hidden // count) == 0 and count >= 16
    common = Bag(
        args=(
            lengths[0],
            section.reshape(1),
            core.reshape(1),
            mods,
            time_bias,
            jnp.asarray(angle_table(span)),
            norm_gain,
            expand_bias,
            reduce_bias,
        ),
        sizes=(span, width, hidden, count),
        tokens=local.shape[0],
        cores=2 if fused else 1,
    )
    weights = Bag(
        win=attend_in[0], wout=attend_out[0], wex=expand_weight[0], wre=reduce_weight[0]
    )
    rows = [(local, slot * span) for slot in range(micro)]
    same = lambda *names: {name: name for name in names}
    whole = same("left", "bg", "pa", "jg")
    run = partial(stage, common=common)
    both = (forward, output, mlp, copy_agrad, attend)
    over = lambda block, route: lax.ppermute(block, "section", route)
    swap = lambda block, bit: exchange(block, "rep", bit)
    a = run(
        "first_0",
        parts=(forward,),
        who=0,
        slot=0,
        loads=dict(xv=rows[0], **weights),
        stores=dict(result="leave"),
        kept=False,
        heads_step=6,
    )
    came_0 = over(a.leave, [(0, 1)])
    b = run(
        "first_1",
        parts=(forward,),
        who=0,
        slot=1,
        loads=dict(xv=rows[1], **weights),
        stores=same("result", "left", "qkv", "probs", "middle", "slope", "branch"),
        after=(a.leave,),
        heads_step=1,
    )
    came_1 = over(b.result, [(0, 1)])
    x = run(
        "second_0",
        parts=both,
        who=1,
        slot=0,
        loads=dict(xv=came_0, dyv=rows[0], **weights),
        stores=dict(whole, result=("ends", 0), leave="leave"),
        after=(b.result,),
        heads_step=6,
    )
    back_0 = over(x.leave, [(1, 0)])
    y = run(
        "second_1",
        parts=both,
        who=1,
        slot=1,
        loads=dict(xv=came_1, dyv=rows[1], **weights),
        stores=dict(whole, result=("ends", span), leave="leave"),
        carried=dict(b, ends=x.ends),
        after=(x.leave,),
        heads_step=6,
    )
    back_1 = over(y.leave, [(1, 0)])
    gates = mods[SEGS : 2 * SEGS, 2 * width :] + time_bias[:, 2 * width :].astype(F32)
    gates = jnp.where(lengths[0, 1, 0] == span, gates[:1], gates)
    after = (y.leave, gates)
    if fused:
        turned, _ = join(embed.T, y.leave)
        embeds = (turned, swap(turned, 0))
        after += (embeds[1],)
    x = run(
        "back_0",
        parts=both,
        who=0,
        slot=0,
        loads=dict(xv=rows[0], dyv=back_0, **weights),
        stores=dict(whole, leave=("ends", 0)),
        carried=dict(x, ends=y.ends),
        after=after,
        heads_step=3,
    )
    if fused:
        y_left = swap(y.left_send, 0)
        back_1, x_send, x_bg = join(back_1, x.left_send, x.bg)
        lefts = [x.left, y.left, swap(x_send, 0), y_left]
        others = [swap(item, 0) for item in (x_bg, x.pa, x.jg)]
    cotan = back_1.astype(F32).reshape(SEGS, -1, width)
    made = (cotan * gates[:, None]).reshape(span, width).astype(BF16)
    bg_1 = jnp.where(section == 0, made, y.bg)
    after = ()
    if fused:
        bg_1_other = swap(bg_1, 0)
        after = (bg_1_other, others[0], lefts[2], lefts[3])
    part = run(
        "back_1_mlp",
        parts=(mlp,),
        who=0,
        slot=1,
        loads=dict(
            bg=bg_1,
            wre=weights.wre,
            slope=b.slope,
            wex=weights.wex,
            middle=b.middle,
            dyv=back_1,
            branch=b.branch,
        ),
        stores=same("pa", "middle_grad"),
        carried=y,
        after=after,
        pieces=dict(wre=(0, hidden // width), slope=(1, hidden // width), wex=(1, hidden // width)),
    )
    pa_1 = part.pa
    bits = bits_of(count)
    term = partial(term_call, sizes=common.sizes, core=core, rank=rank)
    lines = width // count
    deep = EMB // count
    sizes = (hidden // count, hidden // count + lines + 3 * deep + TAIL_ROWS, 3 * lines + GAIN_ROWS)
    bases = left_bases(width, hidden)

    def last_attend(after):
        return run(
            "back_1_attend",
            parts=(attend,),
            who=0,
            slot=1,
            loads=dict(
                agrad=(pa_1, None, (hidden, width)),
                wout=weights.wout,
                probs=b.probs,
                qkv=b.qkv,
                win=weights.win,
                xv=rows[1],
                middle_grad=part.middle_grad,
            ),
            stores=dict(jg="jg", leave=("ends", span)),
            carried=dict(y, ends=x.ends),
            after=after,
            heads_step=6,
        )

    def pair_of(size, first):
        cut = size // 2 if fused else size // 32 * 16
        one = Chunk("rep", bits, cut, (1,) if fused else ())
        two = Chunk("rep", bits, size - cut, (2,) if fused else ())
        if fused:
            send_1, keep_1, send_2, keep_2 = first
            one.add(keep_1)
            two.add(keep_2)
            return one, two, send_1, send_2
        view = first.reshape((count // 2, 2) + first.shape[1:])
        cut = lambda at: lax.dynamic_index_in_dim(view, at, 1, keepdims=False)
        came = swap(cut(1 - core).astype(BF16), 0)
        for item in (cut(core), came):
            one.add(item)
            two.add(item, one.size)
        return one, two, one.split(1), two.split(2)

    if fused:
        pa_other = swap(pa_1, 0)
        sent = term(
            "term_reduce",
            term_reduce,
            lines=sizes[0],
            base=bases[0],
            rows=hidden // 2,
            lefts=lefts,
            rights=[x.bg, bg_1, others[0], bg_1_other],
            after=(pa_1,),
        )
        r1, r2, send_1, send_2 = pair_of(sizes[0], sent)
        came_r1, came_r2 = swap(send_1, 1), swap(send_2, 2)
        sent = term(
            "term_expand",
            term_expand,
            lines=sizes[1],
            base=bases[1],
            rows=width,
            lefts=lefts,
            rights=[x.pa, pa_1, others[1], pa_other],
            embeds=embeds,
            after=(send_1, send_2),
        )
        came_r1, came_r2, *sent = join(came_r1, came_r2, *sent)
        e1, e2, send_1, send_2 = pair_of(sizes[1], sent)
        came_e1, came_e2 = swap(send_1, 1), swap(send_2, 2)
        last = last_attend((send_1, send_2))
        jg_1 = last.jg
        jg_other = swap(jg_1, 0)
        came_r1, came_r2, _ = join(came_r1, came_r2, jg_1)
        r1.add(came_r1)
        r2.add(came_r2)
        send_3, send_4 = r1.split(2), r2.split(1)
        came_r1, came_r2 = swap(send_3, 2), swap(send_4, 1)
        came_e1, came_e2, _, _ = join(came_e1, came_e2, send_3, send_4)
        e1.add(came_e1)
        e2.add(came_e2)
        send_1, send_2 = e1.split(2), e2.split(1)
        came_e1, came_e2 = swap(send_1, 2), swap(send_2, 1)
        sent = term(
            "term_attend",
            term_attend,
            lines=sizes[2],
            base=bases[3],
            rows=width // 2,
            lefts=lefts,
            rights=[x.jg, jg_1, others[2], jg_other],
            after=(send_1, send_2, send_3, send_4),
        )
        came_r1, came_r2, *sent = join(came_r1, came_r2, *sent)
        a1, a2, send_1, send_2 = pair_of(sizes[2], sent)
    else:
        last = last_attend(())
        rights = [(x.bg, bg_1), (x.pa, pa_1), (x.jg, last.jg)]
        totals = plain_pieces((x.left, y.left), rights, embed.T, common.sizes)
        r1, r2, send_1, send_2 = pair_of(sizes[0], totals[0])
        r1.add(swap(send_1, 1))
        r2.add(swap(send_2, 2))
        came_r1, came_r2 = swap(r1.split(2), 2), swap(r2.split(1), 1)
        e1, e2, send_1, send_2 = pair_of(sizes[1], totals[1])
        e1.add(swap(send_1, 1))
        e2.add(swap(send_2, 2))
        came_e1, came_e2 = swap(e1.split(2), 2), swap(e2.split(1), 1)
        a1, a2, send_1, send_2 = pair_of(sizes[2], totals[2])
    ends = last.ends
    came_a1, came_a2 = swap(send_1, 1), swap(send_2, 2)
    r1.add(came_r1)
    r2.add(came_r2)
    block_r = jnp.concatenate([r1.split(3), r2.split(3)], axis=-2)
    came_r = swap(block_r, 3)
    came_e1, came_e2, _ = join(came_e1, came_e2, block_r)
    e1.add(came_e1)
    e2.add(came_e2)
    block_e = jnp.concatenate([e1.split(3), e2.split(3)], axis=-2)
    came_e = swap(block_e, 3)
    came_a1, came_a2, _ = join(came_a1, came_a2, block_e)
    a1.add(came_a1)
    a2.add(came_a2)
    send_1, send_2 = a1.split(2), a2.split(1)
    came_a1, came_a2 = swap(send_1, 2), swap(send_2, 1)
    a1.add(came_a1)
    a2.add(came_a2)
    block_a = jnp.concatenate([a1.split(3), a2.split(3)], axis=-2)
    came_a = swap(block_a, 3)
    came_r, _ = join(came_r, send_1)
    r1.add(came_r[..., : r1.size, :])
    r2.add(came_r[..., r1.size :, :])
    came_e, _ = join(came_e, block_a)
    e1.add(came_e[..., : e1.size, :])
    e2.add(came_e[..., e1.size :, :])
    a1.add(came_a[..., : a1.size, :])
    a2.add(came_a[..., a1.size :, :])
    for bit in range(4, bits):
        for chunk in (r1, r2, e1, e2, a1, a2):
            chunk.add(swap(chunk.split(bit), bit))
    share_r, share_e, share_a = (
        jnp.concatenate([one.total(), two.total()]) for one, two in ((r1, r2), (e1, e2), (a1, a2))
    )
    tall = hidden // width
    side = lambda item, n, size: jnp.concatenate(
        [item[i * size : (i + 1) * size] for i in range(n)], axis=1
    )
    at_o = tall * lines
    at_t = at_o + lines
    small = share_e[at_t + 3 * deep :]
    flat = lambda item, first, n: lax.dynamic_slice_in_dim(
        item[first : first + n].reshape(-1), rank * (n * width // count), n * width // count
    )
    results = (
        flat(share_a, 3 * lines, 1),
        side(share_a, 3, lines),
        share_e[at_o:at_t],
        side(share_e[at_t:], 3, deep),
        flat(small, 1, 3),
        side(share_e, tall, lines),
        flat(small, 4, tall),
        share_r,
        flat(small, 0, 1),
    )
    return (ends[None],) + tuple(piece[None] for piece in results)


def solution(mesh):
    return jax.shard_map(
        per_device,
        mesh=mesh,
        in_specs=(
            P("section", "rep", None),
            P("rep", None, None),
            P("rep", None, None),
            P("section", None),
            P("section", None, None),
            P("section", None, None),
            P("section", None, None),
            P("section", None),
            P("section", None, None),
            P("section", None),
            P("section", None, None),
            P("section", None),
        ),
        out_specs=(
            P("section", "rep", None),
            P("section", "rep"),
            P("section", "rep", None),
            P("section", "rep", None),
            P("section", "rep", None),
            P("section", "rep"),
            P("section", "rep", None),
            P("section", "rep"),
            P("section", "rep", None),
            P("section", "rep"),
        ),
        check_vma=False,
    )
```
